32 devices in a mesh: leaf: 2 (over core), row: 4 (over y, x), col: 4 (over z).
Axes of the slice: x: 2, y: 2, z: 4, core: 2. Of those that a mesh axis runs over, the one named last changes fastest.
Arguments:
- child_rhs: float32 [64, 256, 256], P(('leaf', 'row', 'col')), may hold values from -6 to 6
- child_diag: float32 [64, 256, 256], P(('leaf', 'row', 'col')), may hold values from -0.375 to 0.375
- child_off: float32 [64, 256, 256], P(('leaf', 'row', 'col')), may hold values from -0.125 to 0.125
- live: int32 [64], P(('leaf', 'row', 'col')), may hold values from 1 to 256, 10240 in all
- targets: int32 [64, 256], P(('leaf', 'row', 'col')), may hold values from 0 to 2047
- top_rhs: float32 [2048, 256], P('row'), may hold values from -6 to 6
- top_factor: float32 [2048, 2048], P('row', 'col'), may hold values from -0.125 to 0.125
- top_diag: float32 [2048, 512], P('row'), may hold values from -0.25 to 0.25
Outputs:
- child_sol: float32 [64, 256, 256], P(('leaf', 'row', 'col'))
- top_sol: float32 [2048, 256], P('row')
The draws below stay inside these ranges and needn't reach their ends.
All inputs are finite; a program needn't handle non-finite values. No bound on the sum of `live` on one device may be relied on, other than what follows from the above.
Results may differ from the reference program's by a relative error of at most 0.0003.
Values sent between devices are 32-bit elements; how exact they have to be, the bound alone decides.
No kernel may reach another device: no remote copies, remote signals or barrier semaphores. Data moves between devices by JAX's collectives and lax.ppermute only.
A program may use at most 64 MiB of HBM per device.

```python
import math
import jax
import jax.numpy as jnp
import numpy as np
from jax import lax

W = 256
NRHS = 256
TILE = 256
TB = 512
CH_DEV = 2
NTOP = 2048
CHILD = 64
FAN = 2048


def set_ends(values, own_key, smallest, top_value):
    longest = values.shape.index(max(values.shape))
    spots = []
    for shift in (0, 1):
        where = [jax.random.randint(jax.random.fold_in(own_key, axis), (), 0, length) for axis, length in enumerate(values.shape)]
        where[longest] = (where[longest] + shift) % values.shape[longest]
        spots.append(tuple(where))
    return values.at[spots[0]].set(smallest).at[spots[1]].set(top_value)


def levels(key, dims, split, smallest, top_value):
    level = 1.0
    for axis_at, shards_of in split:
        steps = jax.random.uniform(jax.random.fold_in(jax.random.fold_in(key, 6), axis_at), (shards_of,), jnp.float32, smallest / len(split), top_value / len(split))
        level = level * jnp.repeat(jnp.exp(steps), dims[axis_at] // shards_of).reshape((-1,) + (1,) * (len(dims) - 1 - axis_at))
    return level


def rank_table(number_of, skew):
    portions = [(1 << 20) // math.isqrt(standing ** skew) + 1 for standing in range(1, number_of + 1)]
    width = 1 + sum(portions) // (1 << 30)
    return np.cumsum(np.array([max(1, weight // width) for weight in portions]))


def ranked_ids(stream_key, shape, amount, skew):
    table = rank_table(amount, skew)
    ticket = jax.random.randint(jax.random.fold_in(stream_key, 1), shape, 0, int(table[amount - 1]))
    standing = jnp.searchsorted(jnp.asarray(table, jnp.int32), ticket, side="right")
    return jax.random.permutation(jax.random.fold_in(stream_key, 2), amount)[standing].astype(jnp.int32)


def profile(number_of, total, reach, skew):
    loads = [(1 << 20) // math.isqrt(grade ** skew) + 1 for grade in range(2, number_of + 1)]
    surplus, holding = total - reach - (number_of - 1), [1] * (number_of - 1)
    while surplus > 0:
        movable = [i for i in range(number_of - 1) if holding[i] < reach]
        mass, budget = sum([loads[i] for i in movable]), surplus
        for i in movable:
            more = min(reach - holding[i], max(1, budget * loads[i] // mass), surplus)
            holding[i] = holding[i] + more
            surplus = surplus - more
    return np.array([reach] + holding)


def uneven(stream_key, count, total, limit, skew):
    if count == 2:
        one = jax.random.randint(stream_key, (), max(1, total - limit), min(limit, total - 1) + 1)
        return jnp.stack([one, total - one])
    tallies = jnp.asarray(profile(count, total, limit, skew), jnp.int32)
    pairs = (count - 1) // 2
    donor, sink = tallies[1:1 + 2 * pairs:2], tallies[2:2 + 2 * pairs:2]
    margin = jnp.minimum(donor - 1, limit - sink)
    passed = jax.random.randint(jax.random.fold_in(stream_key, 1), (pairs,), 0, 1 << 20) % (margin + 1)
    tallies = tallies.at[1:1 + 2 * pairs:2].set(donor - passed).at[2:2 + 2 * pairs:2].set(sink + passed)
    return tallies[jax.random.permutation(jax.random.fold_in(stream_key, 2), count)]


def gaussian(stream_key, extent, spread, most, split=(), held_as=jnp.bfloat16):
    result = jax.random.normal(stream_key, extent, jnp.float32) * spread
    if len(split) > 0:
        result = levels(stream_key, extent, split, -0.22, 0.18) * result
    return jnp.clip(result, min=-most, max=most).astype(held_as)


def setup_inputs(seed: int = 0) -> dict:
    arg_keys = jax.random.split(jax.random.key(seed), 9)
    child_rhs = gaussian(arg_keys[0], (CHILD, W, NRHS), 1.0, 6.0, ((0, 32),), jnp.float32)
    child_diag = gaussian(arg_keys[1], (CHILD, W, W), W ** -0.5, 0.375, ((0, 32),), jnp.float32)
    child_off = gaussian(arg_keys[2], (CHILD, TILE, W), FAN ** -0.5, 0.125, ((0, 32),), jnp.float32)
    live = uneven(arg_keys[3], CHILD, CHILD * TILE * 5 // 8, TILE, 0).astype(jnp.int32)
    targets = set_ends(ranked_ids(arg_keys[4], (CHILD, TILE), NTOP, 2), jax.random.fold_in(arg_keys[4], 3), 0, NTOP - 1).astype(jnp.int32)
    top_rhs = gaussian(arg_keys[5], (NTOP, NRHS), 1.0, 6.0, ((0, 4),), jnp.float32)
    top_factor = gaussian(arg_keys[6], (NTOP, NTOP), NTOP ** -0.5, 0.125, ((0, 4), (1, 4)), jnp.float32)
    top_diag = gaussian(arg_keys[7], (NTOP, TB), TB ** -0.5, 0.25, ((0, 4),), jnp.float32)
    return {"child_rhs": child_rhs, "child_diag": child_diag, "child_off": child_off, "live": live, "targets": targets, "top_rhs": top_rhs, "top_factor": top_factor, "top_diag": top_diag}


def unit_lower(matrix):
    return jnp.tril(matrix) + jnp.eye(matrix.shape[-1], dtype=matrix.dtype)


def reference(child_rhs, child_diag, child_off, live, targets, top_rhs, top_factor, top_diag):
    blocks = CHILD // CH_DEV
    highest = lax.Precision.HIGHEST
    slot_index = jnp.arange(TILE, dtype=jnp.int32)

    def child_step(contrib, pieces):
        rhs_part, diag_part, off_part, live_part, target_part = pieces
        solved = jnp.einsum("bij,bjr->bir", unit_lower(diag_part), rhs_part, precision=highest)
        tiles = jnp.einsum("btj,bjr->btr", off_part, solved, precision=highest)
        keep = slot_index[None, :] < live_part[:, None]
        tiles = jnp.where(keep[:, :, None], tiles, jnp.zeros_like(tiles))
        contrib = contrib.at[target_part.reshape(-1)].add(tiles.reshape(-1, NRHS))
        return contrib, solved

    pieces = (child_rhs.reshape(blocks, CH_DEV, W, NRHS), child_diag.reshape(blocks, CH_DEV, W, W),
              child_off.reshape(blocks, CH_DEV, TILE, W), live.reshape(blocks, CH_DEV),
              targets.reshape(blocks, CH_DEV, TILE))
    updates, solved_all = lax.scan(child_step, jnp.zeros((NTOP, NRHS), jnp.float32), pieces)
    child_sol = solved_all.reshape(CHILD, W, NRHS)
    reduced = top_rhs - updates
    block_of = jnp.arange(NTOP, dtype=jnp.int32) // TB

    def top_step(block, solution):
        start = (block * TB).astype(jnp.int32)
        factor_rows = lax.dynamic_slice_in_dim(top_factor, start, TB, 0)
        factor_rows = jnp.where((block_of < block)[None, :], factor_rows, jnp.zeros_like(factor_rows))
        before = jnp.dot(factor_rows, solution, precision=highest, preferred_element_type=jnp.float32)
        inverse = unit_lower(lax.dynamic_slice_in_dim(top_diag, start, TB, 0))
        rhs_block = lax.dynamic_slice_in_dim(reduced, start, TB, 0)
        solved = jnp.dot(inverse, rhs_block - before, precision=highest, preferred_element_type=jnp.float32)
        return lax.dynamic_update_slice_in_dim(solution, solved, start, 0)

    top_sol = lax.fori_loop(0, NTOP // TB, top_step, jnp.zeros((NTOP, NRHS), jnp.float32))
    return child_sol, top_sol
```

```python
import functools

import jax
import jax.numpy as jnp
from jax import lax
from jax.experimental import pallas as pl
from jax.experimental.pallas import tpu as pltpu
from jax.sharding import PartitionSpec as P

F32 = jnp.float32
BF16 = jnp.bfloat16
NT = (((1,), (1,)), ((), ()))
NN = (((1,), (0,)), ((), ()))
VM = pl.BlockSpec(memory_space=pltpu.VMEM)
SM = pl.BlockSpec(memory_space=pltpu.SMEM)


def spread(value, axis, source):
    kept = jnp.where(lax.axis_index(axis) == source, value, 0).astype(value.dtype)
    return lax.psum(kept, axis)


def unit_lower(matrix):
    return jnp.tril(matrix) + jnp.eye(matrix.shape[-1], dtype=matrix.dtype)


def any_mesh(child_rhs, child_diag, child_off, live, targets, top_rhs, top_factor, top_diag):
    highest = lax.Precision.HIGHEST
    owned_rows = top_rhs.shape[0]
    right_count = top_rhs.shape[1]
    block_size = top_diag.shape[1]
    owned_blocks = owned_rows // block_size
    row_count = lax.axis_size("row")
    top_order = owned_rows * row_count
    col_width = top_factor.shape[1]
    my_row = lax.axis_index("row")
    my_col = lax.axis_index("col")
    child_sol = jnp.einsum("bij,bjr->bir", unit_lower(child_diag), child_rhs, precision=highest)
    tiles = jnp.einsum("btj,bjr->btr", child_off, child_sol, precision=highest)
    slot_index = jnp.arange(child_off.shape[1], dtype=jnp.int32)
    keep = slot_index[None, :] < live[:, None]
    tiles = jnp.where(keep[:, :, None], tiles, jnp.zeros_like(tiles))
    contrib = jnp.zeros((top_order, right_count), F32)
    contrib = contrib.at[targets.reshape(-1)].add(tiles.reshape(-1, right_count))
    row_part = lax.psum_scatter(contrib, "row", scatter_dimension=0, tiled=True)
    share = lax.psum_scatter(row_part, ("leaf", "col"), scatter_dimension=0, tiled=True)
    updates = lax.all_gather(share, ("leaf", "col"), axis=0, tiled=True)
    reduced = top_rhs - updates
    inverse_all = unit_lower(top_diag.reshape(owned_blocks, block_size, block_size))
    col_global = my_col * col_width + jnp.arange(col_width, dtype=jnp.int32)

    def step(block, solution):
        local = block % owned_blocks
        owner = block // owned_blocks
        factor_rows = jnp.where(
            (col_global < block * block_size)[None, :], top_factor, jnp.zeros_like(top_factor)
        )
        columns = lax.dynamic_slice_in_dim(solution, my_col * col_width, col_width, 0)
        partial_value = jnp.dot(
            factor_rows, columns, precision=highest, preferred_element_type=F32
        )
        block_inverse = lax.dynamic_index_in_dim(inverse_all, local, 0, keepdims=False)
        before = lax.psum(partial_value, "col")
        solved = jnp.dot(
            block_inverse, reduced - before, precision=highest, preferred_element_type=F32
        )
        solved = spread(solved, "row", owner)
        return lax.dynamic_update_slice_in_dim(solution, solved, block * block_size, 0)

    solution = lax.fori_loop(
        0, row_count * owned_blocks, step, jnp.zeros((top_order, right_count), F32)
    )
    top_sol = lax.dynamic_slice_in_dim(solution, my_row * owned_rows, owned_rows, 0)
    return (child_sol, top_sol)


def split(value):
    high = value.astype(BF16)
    return high, (value - high.astype(F32)).astype(BF16)


def dot3(left, right, dims):
    left_high, left_low = split(left)
    right_high, right_low = split(right)
    rows = left.shape[0]
    both = lax.dot_general(
        jnp.concatenate([left_high, left_low], axis=0), right_high, dims, preferred_element_type=F32
    )
    cross = lax.dot_general(left_high, right_low, dims, preferred_element_type=F32)
    return both[:rows] + both[rows:] + cross


def lower(matrix):
    row = lax.broadcasted_iota(jnp.int32, matrix.shape, 0)
    col = lax.broadcasted_iota(jnp.int32, matrix.shape, 1)
    return jnp.where(col <= row, matrix, 0.0)


def child_kernel(where_ref, live_ref, rhs_ref, diag_ref, off_ref, tgt_ref, sol_ref, keep_ref, send_ref, tiles_ref):
    leaf = where_ref[0]
    children, slots = off_ref.shape[0], off_ref.shape[1]
    half = keep_ref.shape[0]
    for s in range(children):
        rhs = rhs_ref[s]
        sol = rhs + dot3(lower(diag_ref[s]), rhs, NN)
        sol_ref[s] = sol
        tiles = dot3(sol.T, off_ref[s], NT)
        slot = lax.broadcasted_iota(jnp.int32, tiles.shape, 1)
        tiles_ref[:, s * slots:(s + 1) * slots] = jnp.where(slot < live_ref[s], tiles, 0.0)
        send_ref[half:half + 8, s * slots:(s + 1) * slots] = jnp.broadcast_to(
            tgt_ref[s:s + 1, :].astype(F32), (8, slots)
        )
    keep_ref[...] = tiles_ref[pl.ds(pl.multiple_of(leaf * half, half), half), :]
    send_ref[0:half, :] = tiles_ref[pl.ds(pl.multiple_of((1 - leaf) * half, half), half), :]


def scatter_kernel(where_ref, keep_ref, recv_ref, tgt_ref, *out_refs):
    row = where_ref[1]
    half, slots_all = keep_ref.shape
    size = out_refs[0].shape[1]
    children, slots = tgt_ref.shape
    mine = [split(keep_ref[...]), split(recv_ref[0:half, :])]
    stacked = [jnp.concatenate(pair, axis=0) for pair in mine]
    mine_targets = jnp.concatenate([tgt_ref[s:s + 1, :] for s in range(children)], axis=1)
    target = [mine_targets, recv_ref[half:half + 1, :].astype(jnp.int32)]
    for s, out_ref in enumerate(out_refs):
        block = jnp.bitwise_xor(row, s)
        index = lax.broadcasted_iota(jnp.int32, (size, slots_all), 0) + block * size
        total = None
        for t, value in zip(target, stacked):
            hot = jnp.where(index == t, 1.0, 0.0).astype(BF16)
            product = lax.dot_general(value, hot, NT, preferred_element_type=F32)
            total = product if total is None else total + product
        out_ref[...] = total[:half] + total[half:]


def pieces_kernel(where_ref, a_ref, b_ref, c_ref, d_ref, first_ref, second_ref, sum_ref):
    odd = where_ref[2] % 2
    piece = first_ref.shape[0]
    sum_ref[...] = (a_ref[...] + b_ref[...]) + (c_ref[...] + d_ref[...])
    first_ref[...] = sum_ref[pl.ds(pl.multiple_of(odd * piece, piece), piece), :]
    second_ref[...] = sum_ref[pl.ds(pl.multiple_of((1 - odd) * piece, piece), piece), :]


def first_kernel(rhs_ref, a_ref, b_ref, c_ref, d_ref, diag_ref, res_ref, x_ref):
    res = rhs_ref[...] - ((a_ref[...] + b_ref[...]) + (c_ref[...] + d_ref[...]))
    res_ref[...] = res
    x_ref[...] = res + dot3(res, lower(diag_ref[...]), NT)


def step_kernel(count, *refs):
    res_ref, diag_ref = refs[0], refs[1]
    given, factors = refs[2:2 + count], refs[2 + count:2 + 2 * count]
    res_out, x_out = refs[2 + 2 * count], refs[3 + 2 * count]
    res = res_ref[...]
    for x_ref, factor_ref in zip(given, factors):
        res = res - dot3(x_ref[...], factor_ref[...], NT)
    res_out[...] = res
    x_out[...] = res + dot3(res, lower(diag_ref[...]), NT)


def half_kernel(where_ref, x_ref, a_ref, b_ref, c_ref, out_ref):
    z = where_ref[2]
    piece = x_ref.shape[0]
    x, a, b, c = x_ref[...], a_ref[...], b_ref[...], c_ref[...]
    out_ref[0:piece, :] = jnp.where(z == 0, a, jnp.where(z == 1, x, jnp.where(z == 2, b, c)))
    out_ref[piece:2 * piece, :] = jnp.where(z == 0, c, jnp.where(z == 1, b, jnp.where(z == 2, x, a)))


def last_kernel(where_ref, own_ref, other_ref, out_ref):
    leaf = where_ref[0]
    half = own_ref.shape[0]
    own, other = own_ref[...].T, other_ref[...].T
    out_ref[:, 0:half] = jnp.where(leaf == 0, own, other)
    out_ref[:, half:2 * half] = jnp.where(leaf == 0, other, own)


def call(kernel, ins, outs, scratch=(), flops=0):
    return pl.pallas_call(
        kernel,
        out_shape=[jax.ShapeDtypeStruct(shape, F32) for shape in outs],
        in_specs=[SM if a.ndim == 1 else VM for a in ins],
        out_specs=[VM] * len(outs),
        scratch_shapes=list(scratch),
        cost_estimate=pl.CostEstimate(flops=flops, bytes_accessed=4 * sum(a.size for a in ins), transcendentals=0),
        compiler_params=pltpu.CompilerParams(vmem_limit_bytes=40 * 1024 * 1024),
    )(*ins)


def central(child_rhs, child_diag, child_off, live, targets, top_rhs, top_factor, top_diag):
    leaf, row, col = (lax.axis_index(a) for a in ("leaf", "row", "col"))
    where = jnp.stack([leaf, row, col]).astype(jnp.int32)
    rows, cols = lax.axis_size("row"), lax.axis_size("col")
    size = top_diag.shape[1]
    right = top_rhs.shape[1]
    half, piece = right // 2, right // 4
    children, slots = targets.shape

    def swap(value):
        return lax.ppermute(value, "leaf", [(0, 1), (1, 0)])

    def along_row(value, pairs):
        return lax.ppermute(value, "row", pairs)

    def along_col(value, pairs):
        return lax.ppermute(value, "col", pairs)

    def at(r, c):
        return r * cols + c

    part = lax.dynamic_slice_in_dim(top_factor, leaf * (size // 2), size // 2, 0)
    near = [(at(k, 0), at(k, 1)) for k in (1, 2, 3)] + [(at(k, 1), at(k, 2)) for k in (2, 3)]
    far = [(at(k, 0), at(k, 2)) for k in (1, 2, 3)] + [(at(3, 2), at(3, 1))]
    near_part = lax.ppermute(part, ("row", "col"), near)
    far_part = lax.ppermute(part, ("row", "col"), far)

    start = leaf * half + (col // 2) * piece
    rhs_piece = lax.dynamic_slice_in_dim(top_rhs, start, piece, 1).T

    child_sol, keep, send = call(
        child_kernel,
        [where, live, child_rhs, child_diag, child_off, targets],
        [child_rhs.shape, (half, children * slots), (half + 8, children * slots)],
        [pltpu.VMEM((right, children * slots), F32)],
    )
    recv = swap(send)
    sums = call(scatter_kernel, [where, keep, recv, targets], [(half, size)] * rows)
    got = [along_row(sums[s], [(i, i ^ s) for i in range(rows)]) for s in (1, 2, 3)]

    near_other, far_other = swap(near_part), swap(far_part)

    def whole(mine, other):
        return jnp.where(
            leaf == 0, jnp.concatenate([mine, other], 0), jnp.concatenate([other, mine], 0)
        )

    near_whole, far_whole = whole(near_part, near_other), whole(far_part, far_other)
    factor0 = jnp.where(col == 1, near_whole, far_whole)
    factor1 = jnp.where(col == 1, top_factor, near_whole)
    factor2 = jnp.where(col == 1, far_whole, top_factor)

    first, second = call(
        pieces_kernel, [where, sums[0]] + got, [(piece, size)] * 2, [pltpu.VMEM((half, size), F32)]
    )
    q = [
        along_col(first, [(0, 1), (3, 2)]),
        along_col(first, [(1, 2), (2, 1)]),
        along_col(second, [(0, 2), (3, 1)]),
    ]
    shape = (piece, size)
    res, x = call(first_kernel, [rhs_piece, second] + q + [top_diag], [shape] * 2)
    x0 = along_row(x, [(0, 1)]) + along_row(x, [(0, 2)])
    res, x = call(
        functools.partial(step_kernel, 1), [res, top_diag, x0, factor0], [shape] * 2
    )
    on = along_row(jnp.where(row == 2, x0, x), [(1, 2), (2, 3)])
    x1 = along_row(x, [(1, 3)])
    x0 = jnp.where(row == 3, on, 0.0)
    x1 = jnp.where(row == 2, on, x1)
    res, x = call(
        functools.partial(step_kernel, 2), [res, top_diag, x0, x1, factor0, factor1], [shape] * 2
    )
    x2 = along_row(x, [(2, 3)])
    res, x = call(
        functools.partial(step_kernel, 1), [res, top_diag, x2, factor2], [shape] * 2
    )
    z = [
        along_col(x, [(1, 0), (2, 3)]),
        along_col(x, [(1, 2), (2, 1)]),
        along_col(x, [(1, 3), (2, 0)]),
    ]
    (own,) = call(half_kernel, [where, x] + z, [(half, size)])
    (top_sol,) = call(last_kernel, [where, own, swap(own)], [top_rhs.shape])
    return (child_sol, top_sol)


def solution(mesh):
    in_specs = (
        P(("leaf", "row", "col"), None, None),
        P(("leaf", "row", "col"), None, None),
        P(("leaf", "row", "col"), None, None),
        P(("leaf", "row", "col")),
        P(("leaf", "row", "col"), None),
        P("row", None),
        P("row", "col"),
        P("row", None),
    )
    out_specs = (P(("leaf", "row", "col"), None, None), P("row", None))
    axes = tuple(mesh.shape[a] for a in ("leaf", "row", "col"))

    def shards(*args):
        top_rhs, top_factor, top_diag = args[5:]
        size = top_diag.shape[1]
        fits = axes == (2, 4, 4) and top_rhs.shape[0] == size and top_factor.shape[1] == size
        return (central if fits else any_mesh)(*args)

    return jax.shard_map(shards, mesh=mesh, in_specs=in_specs, out_specs=out_specs, check_vma=False)
```

```python
import functools

import jax
import jax.numpy as jnp
from jax import lax
from jax.experimental import pallas as pl
from jax.experimental.pallas import tpu as pltpu
from jax.sharding import PartitionSpec as P

F32 = jnp.float32
BF16 = jnp.bfloat16
NT = (((1,), (1,)), ((), ()))
NN = (((1,), (0,)), ((), ()))
VM = pl.BlockSpec(memory_space=pltpu.VMEM)
SM = pl.BlockSpec(memory_space=pltpu.SMEM)


def spread(value, axis, source):
    kept = jnp.where(lax.axis_index(axis) == source, value, 0).astype(value.dtype)
    return lax.psum(kept, axis)


def unit_lower(matrix):
    return jnp.tril(matrix) + jnp.eye(matrix.shape[-1], dtype=matrix.dtype)


def any_mesh(child_rhs, child_diag, child_off, live, targets, top_rhs, top_factor, top_diag):
    highest = lax.Precision.HIGHEST
    owned_rows = top_rhs.shape[0]
    right_count = top_rhs.shape[1]
    block_size = top_diag.shape[1]
    owned_blocks = owned_rows // block_size
    row_count = lax.axis_size("row")
    top_order = owned_rows * row_count
    col_width = top_factor.shape[1]
    my_row = lax.axis_index("row")
    my_col = lax.axis_index("col")
    child_sol = jnp.einsum("bij,bjr->bir", unit_lower(child_diag), child_rhs, precision=highest)
    tiles = jnp.einsum("btj,bjr->btr", child_off, child_sol, precision=highest)
    slot_index = jnp.arange(child_off.shape[1], dtype=jnp.int32)
    keep = slot_index[None, :] < live[:, None]
    tiles = jnp.where(keep[:, :, None], tiles, jnp.zeros_like(tiles))
    contrib = jnp.zeros((top_order, right_count), F32)
    contrib = contrib.at[targets.reshape(-1)].add(tiles.reshape(-1, right_count))
    row_part = lax.psum_scatter(contrib, "row", scatter_dimension=0, tiled=True)
    share = lax.psum_scatter(row_part, ("leaf", "col"), scatter_dimension=0, tiled=True)
    updates = lax.all_gather(share, ("leaf", "col"), axis=0, tiled=True)
    reduced = top_rhs - updates
    inverse_all = unit_lower(top_diag.reshape(owned_blocks, block_size, block_size))
    col_global = my_col * col_width + jnp.arange(col_width, dtype=jnp.int32)

    def step(block, solution):
        local = block % owned_blocks
        owner = block // owned_blocks
        factor_rows = jnp.where(
            (col_global < block * block_size)[None, :], top_factor, jnp.zeros_like(top_factor)
        )
        columns = lax.dynamic_slice_in_dim(solution, my_col * col_width, col_width, 0)
        partial_value = jnp.dot(
            factor_rows, columns, precision=highest, preferred_element_type=F32
        )
        block_inverse = lax.dynamic_index_in_dim(inverse_all, local, 0, keepdims=False)
        before = lax.psum(partial_value, "col")
        solved = jnp.dot(
            block_inverse, reduced - before, precision=highest, preferred_element_type=F32
        )
        solved = spread(solved, "row", owner)
        return lax.dynamic_update_slice_in_dim(solution, solved, block * block_size, 0)

    solution = lax.fori_loop(
        0, row_count * owned_blocks, step, jnp.zeros((top_order, right_count), F32)
    )
    top_sol = lax.dynamic_slice_in_dim(solution, my_row * owned_rows, owned_rows, 0)
    return (child_sol, top_sol)


def split(value):
    high = value.astype(BF16)
    return high, (value - high.astype(F32)).astype(BF16)


def dot3(left, right, dims):
    left_high, left_low = split(left)
    right_high, right_low = split(right)
    rows = left.shape[0]
    both = lax.dot_general(
        jnp.concatenate([left_high, left_low], axis=0), right_high, dims, preferred_element_type=F32
    )
    cross = lax.dot_general(left_high, right_low, dims, preferred_element_type=F32)
    return both[:rows] + both[rows:] + cross


def lower(matrix, first_row=0):
    row = lax.broadcasted_iota(jnp.int32, matrix.shape, 0) + first_row
    col = lax.broadcasted_iota(jnp.int32, matrix.shape, 1)
    return jnp.where(col <= row, matrix, 0.0)


def pack_kernel(where_ref, factor_ref, diag_ref, rhs_ref, out_ref, turned_ref):
    leaf, row, z = where_ref[0], where_ref[1], where_ref[2]
    part = factor_ref.shape[0] // 2
    half = rhs_ref.shape[1] // 2
    piece = half // 2
    mine = pl.ds(pl.multiple_of(leaf * part, part), part)

    @pl.when(row == 0)
    def _():
        out_ref[0:part, :] = diag_ref[mine, :]

    @pl.when(row != 0)
    def _():
        out_ref[0:part, :] = factor_ref[mine, :]

    turned_ref[...] = rhs_ref[:, pl.ds(pl.multiple_of(leaf * half, half), half)].T
    out_ref[part:part + piece, :] = turned_ref[pl.ds(pl.multiple_of((z // 2) * piece, piece), piece), :]


def child_kernel(live_ref, rhs_ref, diag_ref, off_ref, tgt_ref, sol_ref, send_ref):
    children, slots = off_ref.shape[0], off_ref.shape[1]
    right = rhs_ref.shape[2]
    groups = send_ref.shape[0]
    lanes = send_ref.shape[2]
    width = right // groups
    rows = groups // 2
    tiles_each = slots // lanes
    count = children * tiles_each
    for s in range(children):
        rhs = rhs_ref[s]
        sol = rhs + dot3(lower(diag_ref[s]), rhs, NN)
        sol_ref[s] = sol
        tiles = dot3(sol.T, off_ref[s], NT)
        slot = lax.broadcasted_iota(jnp.int32, tiles.shape, 1)
        tiles = jnp.where(slot < live_ref[s], tiles, 0.0)
        for g in range(groups):
            leaf, row = g // rows, g % rows
            for h in range(2):
                start = leaf * (right // 2) + h * (right // 4) + row * (width // 2)
                for t in range(tiles_each):
                    at = (s * tiles_each + t) * width + h * (width // 2)
                    send_ref[g, at:at + width // 2, :] = tiles[
                        start:start + width // 2, t * lanes:(t + 1) * lanes
                    ]
    target = jnp.concatenate(
        [tgt_ref[s:s + 1, t * lanes:(t + 1) * lanes] for s in range(children) for t in range(tiles_each)]
        + [jnp.zeros((send_ref.shape[1] - count * width - count, lanes), jnp.int32)],
        axis=0,
    ).astype(F32)
    for g in range(groups):
        send_ref[g, count * width:, :] = target


def scatter_kernel(blocks, where_ref, recv_ref, first_ref, second_ref, sum_ref):
    odd = where_ref[2] % 2
    groups, lanes = recv_ref.shape[0], recv_ref.shape[2]
    width = sum_ref.shape[0]
    size = sum_ref.shape[1] // blocks
    piece = first_ref.shape[0]
    count = (recv_ref.shape[1] - 1) // width
    total = None
    for g in range(groups):
        lefts, targets = [], []
        for t in range(count):
            target = recv_ref[g, count * width + t:count * width + t + 1, :].astype(jnp.int32)
            value = recv_ref[g, t * width:(t + 1) * width, :]
            parts = []
            for b in range(blocks):
                inside = (target >= b * size) & (target < (b + 1) * size)
                parts.append(jnp.where(inside, value, 0.0))
            lefts.append(jnp.concatenate(parts, axis=0))
            targets.append(target)
        left = jnp.concatenate(lefts, axis=1)
        target = jnp.concatenate(targets, axis=1)
        within = target
        for b in range(1, blocks):
            within = jnp.where(target >= b * size, target - b * size, within)
        index = lax.broadcasted_iota(jnp.int32, (size, count * lanes), 0)
        hot = jnp.where(index == within, 1.0, 0.0).astype(BF16)
        high, low = split(left)
        product = lax.dot_general(
            jnp.concatenate([high, low], axis=0), hot, NT, preferred_element_type=F32
        )
        total = product if total is None else total + product
    total = total[:blocks * width] + total[blocks * width:]
    for b in range(blocks):
        sum_ref[:, b * size:(b + 1) * size] = total[b * width:(b + 1) * width]
    first_ref[...] = sum_ref[pl.ds(pl.multiple_of(odd * piece, piece), piece), :]
    second_ref[...] = sum_ref[pl.ds(pl.multiple_of((1 - odd) * piece, piece), piece), :]


def add_kernel(a_ref, b_ref, c_ref, d_ref, out_ref):
    out_ref[...] = (a_ref[...] + b_ref[...]) + (c_ref[...] + d_ref[...])


def halves(x, mine_ref, other_ref, leaf, out_ref, tri=False):
    part = out_ref.shape[1] // 2
    for ref, at in ((mine_ref, leaf), (other_ref, 1 - leaf)):
        start = pl.multiple_of(at * part, part)
        block = ref[0:part, :]
        if tri:
            block = lower(block, start)
        out_ref[:, pl.ds(start, part)] = dot3(x, block, NT)
    return out_ref[...]


def first_kernel(where_ref, pack_ref, a_ref, b_ref, c_ref, d_ref, diag_ref, nm_ref, no_ref, fm_ref, fo_ref,
                 res_ref, x_ref, sum_ref, tmp_ref):
    leaf, row, z = where_ref[0], where_ref[1], where_ref[2]
    size = diag_ref.shape[0]
    part = size // 2
    piece = a_ref.shape[0]
    for s, ref in enumerate((a_ref, b_ref, c_ref, d_ref)):
        at = jnp.bitwise_xor(row, s) * piece
        sum_ref[pl.ds(pl.multiple_of(at, piece), piece), :] = ref[...]
    res = pack_ref[part:, :] - sum_ref[:, pl.ds(pl.multiple_of(row * size, size), size)]
    res_ref[...] = res
    x_ref[...] = res

    def solve(value):
        x_ref[...] = value + dot3(value, lower(diag_ref[...]), NT)

    @pl.when(row == 0)
    def _():
        solve(res)

    def both(factor_mine, factor_other, diag_mine, diag_other):
        before = diag_mine[part:, :] - sum_ref[:, 0:size]
        x0 = before + halves(before, diag_mine, diag_other, leaf, tmp_ref, tri=True)
        solve(res_ref[...] - halves(x0, factor_mine, factor_other, leaf, tmp_ref))

    @pl.when((row == 1) & (z == 1))
    def _():
        both(nm_ref, no_ref, fm_ref, fo_ref)

    @pl.when((row == 1) & (z == 2))
    def _():
        both(fm_ref, fo_ref, nm_ref, no_ref)


def earlier(res, x0, x1, leaf, z, refs, out_ref, tmp_ref):
    factor_ref, nm_ref, no_ref, fm_ref, fo_ref = refs

    @pl.when(z == 1)
    def _():
        value = res - halves(x0, nm_ref, no_ref, leaf, tmp_ref)
        out_ref[...] = value - dot3(x1, factor_ref[...], NT)

    @pl.when(z == 2)
    def _():
        value = res - halves(x0, fm_ref, fo_ref, leaf, tmp_ref)
        out_ref[...] = value - halves(x1, nm_ref, no_ref, leaf, tmp_ref)


def second_kernel(where_ref, res_ref, x_ref, diag_ref, hb_ref, ha_ref, factor_ref, nm_ref, no_ref, fm_ref, fo_ref,
                  out_ref, left_ref, tmp_ref):
    leaf, row, z = where_ref[0], where_ref[1], where_ref[2]
    out_ref[...] = x_ref[...]

    @pl.when((row == 2) & ((z == 1) | (z == 2)))
    def _():
        refs = (factor_ref, nm_ref, no_ref, fm_ref, fo_ref)
        earlier(res_ref[...], ha_ref[...], hb_ref[...], leaf, z, refs, left_ref, tmp_ref)
        value = left_ref[...]
        out_ref[...] = value + dot3(value, lower(diag_ref[...]), NT)


def third_kernel(where_ref, res_ref, hb_ref, ha_ref, factor_ref, nm_ref, no_ref, fm_ref, fo_ref, out_ref, tmp_ref):
    leaf, row, z = where_ref[0], where_ref[1], where_ref[2]
    out_ref[...] = res_ref[...]

    @pl.when(row == 3)
    def _():
        refs = (factor_ref, nm_ref, no_ref, fm_ref, fo_ref)
        earlier(res_ref[...], hb_ref[...], ha_ref[...], leaf, z, refs, out_ref, tmp_ref)


def fourth_kernel(where_ref, res_ref, x_ref, diag_ref, h_ref, factor_ref, fm_ref, fo_ref, out_ref, left_ref, tmp_ref):
    leaf, row, z = where_ref[0], where_ref[1], where_ref[2]
    out_ref[...] = x_ref[...]

    @pl.when((row == 3) & ((z == 1) | (z == 2)))
    def _():
        @pl.when(z == 1)
        def _():
            left_ref[...] = res_ref[...] - halves(h_ref[...], fm_ref, fo_ref, leaf, tmp_ref)

        @pl.when(z == 2)
        def _():
            left_ref[...] = res_ref[...] - dot3(h_ref[...], factor_ref[...], NT)

        value = left_ref[...]
        out_ref[...] = value + dot3(value, lower(diag_ref[...]), NT)


def half_kernel(where_ref, x_ref, a_ref, b_ref, c_ref, out_ref):
    z = where_ref[2]
    x, a, b, c = x_ref[...], a_ref[...], b_ref[...], c_ref[...]
    low = jnp.where(z == 0, a, jnp.where(z == 1, x, jnp.where(z == 2, b, c)))
    high = jnp.where(z == 0, c, jnp.where(z == 1, b, jnp.where(z == 2, x, a)))
    out_ref[...] = jnp.concatenate([low, high], axis=0).T


def last_kernel(where_ref, own_ref, other_ref, out_ref):
    leaf = where_ref[0]
    half = own_ref.shape[1]
    own, other = own_ref[...], other_ref[...]
    out_ref[:, 0:half] = jnp.where(leaf == 0, own, other)
    out_ref[:, half:2 * half] = jnp.where(leaf == 0, other, own)


def call(kernel, ins, outs, scratch=(), flops=0):
    return pl.pallas_call(
        kernel,
        out_shape=[jax.ShapeDtypeStruct(shape, F32) for shape in outs],
        in_specs=[SM if a.ndim == 1 else VM for a in ins],
        out_specs=[VM] * len(outs),
        scratch_shapes=[pltpu.VMEM(shape, F32) for shape in scratch],
        cost_estimate=pl.CostEstimate(
            flops=flops, bytes_accessed=4 * sum(a.size for a in ins), transcendentals=0
        ),
        compiler_params=pltpu.CompilerParams(vmem_limit_bytes=40 * 1024 * 1024),
    )(*ins)


def central(child_rhs, child_diag, child_off, live, targets, top_rhs, top_factor, top_diag):
    leaf, row, col = (lax.axis_index(a) for a in ("leaf", "row", "col"))
    where = jnp.stack([leaf, row, col]).astype(jnp.int32)
    rows, cols = lax.axis_size("row"), lax.axis_size("col")
    size = top_diag.shape[1]
    right = top_rhs.shape[1]
    half, piece = right // 2, right // 4
    children, slots = targets.shape
    lanes = 128
    groups = 2 * rows
    width = right // groups

    def at(r, c):
        return r * cols + c

    def swap(value):
        return lax.ppermute(value, "leaf", [(0, 1), (1, 0)])

    def plane(value, pairs):
        return lax.ppermute(value, ("row", "col"), pairs)

    def hop(value, pairs):
        return plane(value, [(at(a, z), at(b, z)) for a, b in pairs for z in (1, 2)])

    def along_col(value, pairs):
        return lax.ppermute(value, "col", pairs)

    (pack,) = call(
        pack_kernel, [where, top_factor, top_diag, top_rhs], [(size // 2 + piece, size)], [(half, size)]
    )
    near = plane(
        pack,
        [(at(k, 0), at(k, 1)) for k in (1, 2, 3)]
        + [(at(k, 1), at(k, 2)) for k in (2, 3)]
        + [(at(0, 2), at(1, 2))],
    )
    far = plane(
        pack, [(at(k, 0), at(k, 2)) for k in (1, 2, 3)] + [(at(3, 2), at(3, 1)), (at(0, 1), at(1, 1))]
    )

    tiles = children * slots // lanes
    child_sol, send = call(
        child_kernel,
        [live, child_rhs, child_diag, child_off, targets],
        [child_rhs.shape, (groups, tiles * width + 8 * pl.cdiv(tiles, 8), lanes)],
    )
    recv = lax.all_to_all(send, ("leaf", "row"), 0, 0, tiled=True)
    first, second = call(
        functools.partial(scatter_kernel, rows),
        [where, recv],
        [(width // 2, rows * size)] * 2,
        [(width, rows * size)],
    )
    q = [
        along_col(first, [(0, 1), (3, 2)]),
        along_col(first, [(1, 2), (2, 1)]),
        along_col(second, [(0, 2), (3, 1)]),
    ]
    (sums,) = call(add_kernel, [second] + q, [second.shape])
    got = [hop(sums, [(i, i ^ s) for i in range(rows)]) for s in (1, 2, 3)]
    moved = [near, swap(near), far, swap(far)]

    shape = (piece, size)
    res, x = call(
        first_kernel,
        [where, pack, sums] + got + [top_diag] + moved,
        [shape] * 2,
        [(piece, rows * size), shape],
    )
    hb = hop(x, [(1, 2), (0, 3)])
    ha = hop(x, [(0, 2), (1, 3)])
    (x,) = call(
        second_kernel, [where, res, x, top_diag, hb, ha, top_factor] + moved, [shape], [shape] * 2
    )
    h = hop(x, [(2, 3)])
    (res,) = call(third_kernel, [where, res, hb, ha, top_factor] + moved, [shape], [shape])
    (x,) = call(
        fourth_kernel, [where, res, x, top_diag, h, top_factor] + moved[2:], [shape], [shape] * 2
    )
    z = [
        along_col(x, [(1, 0), (2, 3)]),
        along_col(x, [(1, 2), (2, 1)]),
        along_col(x, [(1, 3), (2, 0)]),
    ]
    (own,) = call(half_kernel, [where, x] + z, [(size, half)])
    (top_sol,) = call(last_kernel, [where, own, swap(own)], [top_rhs.shape])
    return (child_sol, top_sol)


def solution(mesh):
    in_specs = (
        P(("leaf", "row", "col"), None, None),
        P(("leaf", "row", "col"), None, None),
        P(("leaf", "row", "col"), None, None),
        P(("leaf", "row", "col")),
        P(("leaf", "row", "col"), None),
        P("row", None),
        P("row", "col"),
        P("row", None),
    )
    out_specs = (P(("leaf", "row", "col"), None, None), P("row", None))
    axes = tuple(mesh.shape[a] for a in ("leaf", "row", "col"))

    def shards(*args):
        top_rhs, top_factor, top_diag = args[5:]
        size = top_diag.shape[1]
        fits = axes == (2, 4, 4) and top_rhs.shape[0] == size and top_factor.shape[1] == size
        return (central if fits else any_mesh)(*args)

    return jax.shard_map(shards, mesh=mesh, in_specs=in_specs, out_specs=out_specs, check_vma=False)
```

```python
import functools

import jax
import jax.numpy as jnp
from jax import lax
from jax.experimental import pallas as pl
from jax.experimental.pallas import tpu as pltpu
from jax.sharding import PartitionSpec as P

F32 = jnp.float32
BF16 = jnp.bfloat16
NT = (((1,), (1,)), ((), ()))
NN = (((1,), (0,)), ((), ()))
VM = pl.BlockSpec(memory_space=pltpu.VMEM)
ANY = pl.BlockSpec(memory_space=pl.ANY)
SM = pl.BlockSpec(memory_space=pltpu.SMEM)


def spread(value, axis, source):
    kept = jnp.where(lax.axis_index(axis) == source, value, 0).astype(value.dtype)
    return lax.psum(kept, axis)


def unit_lower(matrix):
    return jnp.tril(matrix) + jnp.eye(matrix.shape[-1], dtype=matrix.dtype)


def any_mesh(child_rhs, child_diag, child_off, live, targets, top_rhs, top_factor, top_diag):
    highest = lax.Precision.HIGHEST
    owned_rows = top_rhs.shape[0]
    right_count = top_rhs.shape[1]
    block_size = top_diag.shape[1]
    owned_blocks = owned_rows // block_size
    row_count = lax.axis_size("row")
    top_order = owned_rows * row_count
    col_width = top_factor.shape[1]
    my_row = lax.axis_index("row")
    my_col = lax.axis_index("col")
    child_sol = jnp.einsum("bij,bjr->bir", unit_lower(child_diag), child_rhs, precision=highest)
    tiles = jnp.einsum("btj,bjr->btr", child_off, child_sol, precision=highest)
    slot_index = jnp.arange(child_off.shape[1], dtype=jnp.int32)
    keep = slot_index[None, :] < live[:, None]
    tiles = jnp.where(keep[:, :, None], tiles, jnp.zeros_like(tiles))
    contrib = jnp.zeros((top_order, right_count), F32)
    contrib = contrib.at[targets.reshape(-1)].add(tiles.reshape(-1, right_count))
    row_part = lax.psum_scatter(contrib, "row", scatter_dimension=0, tiled=True)
    share = lax.psum_scatter(row_part, ("leaf", "col"), scatter_dimension=0, tiled=True)
    updates = lax.all_gather(share, ("leaf", "col"), axis=0, tiled=True)
    reduced = top_rhs - updates
    inverse_all = unit_lower(top_diag.reshape(owned_blocks, block_size, block_size))
    col_global = my_col * col_width + jnp.arange(col_width, dtype=jnp.int32)

    def step(block, solution):
        local = block % owned_blocks
        owner = block // owned_blocks
        factor_rows = jnp.where(
            (col_global < block * block_size)[None, :], top_factor, jnp.zeros_like(top_factor)
        )
        columns = lax.dynamic_slice_in_dim(solution, my_col * col_width, col_width, 0)
        partial_value = jnp.dot(
            factor_rows, columns, precision=highest, preferred_element_type=F32
        )
        block_inverse = lax.dynamic_index_in_dim(inverse_all, local, 0, keepdims=False)
        before = lax.psum(partial_value, "col")
        solved = jnp.dot(
            block_inverse, reduced - before, precision=highest, preferred_element_type=F32
        )
        solved = spread(solved, "row", owner)
        return lax.dynamic_update_slice_in_dim(solution, solved, block * block_size, 0)

    solution = lax.fori_loop(
        0, row_count * owned_blocks, step, jnp.zeros((top_order, right_count), F32)
    )
    top_sol = lax.dynamic_slice_in_dim(solution, my_row * owned_rows, owned_rows, 0)
    return (child_sol, top_sol)


def split(value):
    high = value.astype(BF16)
    return high, (value - high.astype(F32)).astype(BF16)


def dot3(left, right, dims):
    left_high, left_low = split(left)
    right_high, right_low = split(right)
    rows = left.shape[0]
    both = lax.dot_general(
        jnp.concatenate([left_high, left_low], axis=0), right_high, dims, preferred_element_type=F32
    )
    cross = lax.dot_general(left_high, right_low, dims, preferred_element_type=F32)
    return both[:rows] + both[rows:] + cross


def lower(matrix, first_row=0):
    row = lax.broadcasted_iota(jnp.int32, matrix.shape, 0) + first_row
    col = lax.broadcasted_iota(jnp.int32, matrix.shape, 1)
    return jnp.where(col <= row, matrix, 0.0)


def pack_kernel(where_ref, factor_ref, rhs_ref, after_ref, part_ref, rhs_out_ref, turned_ref):
    leaf, z = where_ref[0], where_ref[2]
    part, half, piece = part_ref.shape[0], turned_ref.shape[0], rhs_out_ref.shape[0]
    part_ref[...] = factor_ref[pl.ds(pl.multiple_of(leaf * part, part), part), :]
    turned_ref[...] = rhs_ref[:, pl.ds(pl.multiple_of(leaf * half, half), half)].T
    rhs_out_ref[...] = turned_ref[pl.ds(pl.multiple_of((z // 2) * piece, piece), piece), :]


def child_kernel(where_ref, live_ref, rhs_hbm, diag_hbm, off_hbm, tgt_ref, sol_ref, keep_ref, send_ref,
                 rhs_ref, diag_ref, off_ref, tiles_ref, sems):
    leaf = where_ref[0]
    children, slots = off_ref.shape[0], off_ref.shape[1]
    half = keep_ref.shape[0]
    pairs = ((rhs_hbm, rhs_ref), (diag_hbm, diag_ref), (off_hbm, off_ref))
    copies = [
        [pltpu.make_async_copy(source.at[s], target.at[s], sems.at[i, s]) for i, (source, target) in enumerate(pairs)]
        for s in range(children)
    ]
    for s in range(children):
        for copy in copies[s]:
            copy.start()
    for s in range(children):
        copies[s][0].wait()
        copies[s][1].wait()
        rhs = rhs_ref[s]
        sol = rhs + dot3(lower(diag_ref[s]), rhs, NN)
        sol_ref[s] = sol
        copies[s][2].wait()
        tiles = dot3(sol.T, off_ref[s], NT)
        slot = lax.broadcasted_iota(jnp.int32, tiles.shape, 1)
        tiles_ref[:, s * slots:(s + 1) * slots] = jnp.where(slot < live_ref[s], tiles, 0.0)
        send_ref[half:half + 8, s * slots:(s + 1) * slots] = jnp.broadcast_to(
            tgt_ref[s:s + 1, :].astype(F32), (8, slots)
        )
    keep_ref[...] = tiles_ref[pl.ds(pl.multiple_of(leaf * half, half), half), :]
    send_ref[0:half, :] = tiles_ref[pl.ds(pl.multiple_of((1 - leaf) * half, half), half), :]


def scatter_kernel(where_ref, keep_ref, recv_ref, tgt_ref, *out_refs):
    row = where_ref[1]
    half, slots_all = keep_ref.shape
    size = out_refs[0].shape[1]
    children, slots = tgt_ref.shape
    mine = [split(keep_ref[...]), split(recv_ref[0:half, :])]
    stacked = [jnp.concatenate(pair, axis=0) for pair in mine]
    mine_targets = jnp.concatenate([tgt_ref[s:s + 1, :] for s in range(children)], axis=1)
    target = [mine_targets, recv_ref[half:half + 1, :].astype(jnp.int32)]
    for s, out_ref in enumerate(out_refs):
        block = jnp.bitwise_xor(row, s)
        index = lax.broadcasted_iota(jnp.int32, (size, slots_all), 0) + block * size
        total = None
        for t, value in zip(target, stacked):
            hot = jnp.where(index == t, 1.0, 0.0).astype(BF16)
            product = lax.dot_general(value, hot, NT, preferred_element_type=F32)
            total = product if total is None else total + product
        out_ref[...] = total[:half] + total[half:]


def pieces_kernel(where_ref, a_ref, b_ref, c_ref, d_ref, first_ref, second_ref, sum_ref):
    odd = where_ref[2] % 2
    piece = first_ref.shape[0]
    sum_ref[...] = (a_ref[...] + b_ref[...]) + (c_ref[...] + d_ref[...])
    first_ref[...] = sum_ref[pl.ds(pl.multiple_of(odd * piece, piece), piece), :]
    second_ref[...] = sum_ref[pl.ds(pl.multiple_of((1 - odd) * piece, piece), piece), :]


def halves(x, mine_ref, other_ref, leaf, out_ref):
    part = out_ref.shape[1] // 2
    for ref, at in ((mine_ref, leaf), (other_ref, 1 - leaf)):
        start = pl.multiple_of(at * part, part)
        block = ref[0:part, :]
        out_ref[:, pl.ds(start, part)] = dot3(x, block, NT)
    return out_ref[...]


def zeroth_kernel(where_ref, rhs_ref, a_ref, b_ref, c_ref, d_ref, diag_ref, res_ref, x_ref):
    row = where_ref[1]
    res = rhs_ref[...] - ((a_ref[...] + b_ref[...]) + (c_ref[...] + d_ref[...]))
    res_ref[...] = res
    x_ref[...] = res

    @pl.when(row == 0)
    def _():
        x_ref[...] = res + dot3(res, lower(diag_ref[...]), NT)


def first_kernel(where_ref, res_ref, x_ref, diag_ref, h_ref, nm_ref, no_ref, fm_ref, fo_ref, out_ref, left_ref, tmp_ref):
    leaf, row, z = where_ref[0], where_ref[1], where_ref[2]
    out_ref[...] = x_ref[...]

    @pl.when((row == 1) & ((z == 1) | (z == 2)))
    def _():
        @pl.when(z == 1)
        def _():
            left_ref[...] = res_ref[...] - halves(h_ref[...], nm_ref, no_ref, leaf, tmp_ref)

        @pl.when(z == 2)
        def _():
            left_ref[...] = res_ref[...] - halves(h_ref[...], fm_ref, fo_ref, leaf, tmp_ref)

        value = left_ref[...]
        out_ref[...] = value + dot3(value, lower(diag_ref[...]), NT)


def earlier(res, x0, x1, leaf, z, refs, out_ref, tmp_ref):
    factor_ref, nm_ref, no_ref, fm_ref, fo_ref = refs

    @pl.when(z == 1)
    def _():
        value = res - halves(x0, nm_ref, no_ref, leaf, tmp_ref)
        out_ref[...] = value - dot3(x1, factor_ref[...], NT)

    @pl.when(z == 2)
    def _():
        value = res - halves(x0, fm_ref, fo_ref, leaf, tmp_ref)
        out_ref[...] = value - halves(x1, nm_ref, no_ref, leaf, tmp_ref)


def second_kernel(where_ref, res_ref, x_ref, diag_ref, hb_ref, ha_ref, factor_ref, nm_ref, no_ref, fm_ref, fo_ref,
                  out_ref, left_ref, tmp_ref):
    leaf, row, z = where_ref[0], where_ref[1], where_ref[2]
    out_ref[...] = x_ref[...]

    @pl.when((row == 2) & ((z == 1) | (z == 2)))
    def _():
        refs = (factor_ref, nm_ref, no_ref, fm_ref, fo_ref)
        earlier(res_ref[...], ha_ref[...], hb_ref[...], leaf, z, refs, left_ref, tmp_ref)
        value = left_ref[...]
        out_ref[...] = value + dot3(value, lower(diag_ref[...]), NT)


def third_kernel(where_ref, res_ref, hb_ref, ha_ref, factor_ref, nm_ref, no_ref, fm_ref, fo_ref, out_ref, tmp_ref):
    leaf, row, z = where_ref[0], where_ref[1], where_ref[2]
    out_ref[...] = res_ref[...]

    @pl.when(row == 3)
    def _():
        refs = (factor_ref, nm_ref, no_ref, fm_ref, fo_ref)
        earlier(res_ref[...], hb_ref[...], ha_ref[...], leaf, z, refs, out_ref, tmp_ref)


def fourth_kernel(where_ref, res_ref, x_ref, diag_ref, h_ref, factor_ref, fm_ref, fo_ref, out_ref, left_ref, tmp_ref):
    leaf, row, z = where_ref[0], where_ref[1], where_ref[2]
    out_ref[...] = x_ref[...]

    @pl.when((row == 3) & ((z == 1) | (z == 2)))
    def _():
        @pl.when(z == 1)
        def _():
            left_ref[...] = res_ref[...] - halves(h_ref[...], fm_ref, fo_ref, leaf, tmp_ref)

        @pl.when(z == 2)
        def _():
            left_ref[...] = res_ref[...] - dot3(h_ref[...], factor_ref[...], NT)

        value = left_ref[...]
        out_ref[...] = value + dot3(value, lower(diag_ref[...]), NT)


def half_kernel(where_ref, x_ref, a_ref, b_ref, c_ref, out_ref):
    z = where_ref[2]
    x, a, b, c = x_ref[...], a_ref[...], b_ref[...], c_ref[...]
    low = jnp.where(z == 0, a, jnp.where(z == 1, x, jnp.where(z == 2, b, c)))
    high = jnp.where(z == 0, c, jnp.where(z == 1, b, jnp.where(z == 2, x, a)))
    out_ref[...] = jnp.concatenate([low, high], axis=0).T


def last_kernel(where_ref, own_ref, other_ref, out_ref):
    leaf = where_ref[0]
    half = own_ref.shape[1]
    own, other = own_ref[...], other_ref[...]
    out_ref[:, 0:half] = jnp.where(leaf == 0, own, other)
    out_ref[:, half:2 * half] = jnp.where(leaf == 0, other, own)


def call(kernel, ins, outs, scratch=(), outside=(), limit=40):
    def spec(i, a):
        return ANY if i in outside else SM if a.ndim == 1 else VM

    return pl.pallas_call(
        kernel,
        out_shape=[jax.ShapeDtypeStruct(shape, F32) for shape in outs],
        in_specs=[spec(i, a) for i, a in enumerate(ins)],
        out_specs=[VM] * len(outs),
        scratch_shapes=[pltpu.VMEM(s, F32) if isinstance(s, tuple) else s for s in scratch],
        cost_estimate=pl.CostEstimate(flops=0, bytes_accessed=4 * sum(a.size for a in ins), transcendentals=0),
        compiler_params=pltpu.CompilerParams(vmem_limit_bytes=limit * 1024 * 1024),
    )(*ins)


def central(child_rhs, child_diag, child_off, live, targets, top_rhs, top_factor, top_diag):
    leaf, row, col = (lax.axis_index(a) for a in ("leaf", "row", "col"))
    where = jnp.stack([leaf, row, col]).astype(jnp.int32)
    rows, cols = lax.axis_size("row"), lax.axis_size("col")
    size = top_diag.shape[1]
    right = top_rhs.shape[1]
    half, piece = right // 2, right // 4
    children, slots = targets.shape

    def at(r, c):
        return r * cols + c

    def swap(value):
        return lax.ppermute(value, "leaf", [(0, 1), (1, 0)])

    def plane(value, pairs):
        return lax.ppermute(value, ("row", "col"), pairs)

    def hop(value, pairs):
        return plane(value, [(at(a, z), at(b, z)) for a, b in pairs for z in (1, 2)])

    def along_row(value, pairs):
        return lax.ppermute(value, "row", pairs)

    def along_col(value, pairs):
        return lax.ppermute(value, "col", pairs)

    child_sol, keep, send = call(
        child_kernel,
        [where, live, child_rhs, child_diag, child_off, targets],
        [child_rhs.shape, (half, children * slots), (half + 8, children * slots)],
        [child_rhs.shape, child_diag.shape, child_off.shape, (right, children * slots),
         pltpu.SemaphoreType.DMA((3, children))],
        outside=(2, 3, 4),
        limit=56,
    )
    sums = call(scatter_kernel, [where, keep, swap(send), targets], [(half, size)] * rows)
    got = [along_row(sums[s], [(i, i ^ s) for i in range(rows)]) for s in (1, 2, 3)]

    part, rhs_piece = call(
        pack_kernel,
        [where, top_factor, top_rhs, got[0]],
        [(size // 2, size), (piece, size)],
        [(half, size)],
        outside=(3,),
    )
    near = plane(
        part,
        [(at(k, 0), at(k, 1)) for k in (1, 2, 3)] + [(at(k, 1), at(k, 2)) for k in (2, 3)],
    )
    far = plane(part, [(at(k, 0), at(k, 2)) for k in (1, 2, 3)] + [(at(3, 2), at(3, 1))])

    first, second = call(
        pieces_kernel, [where, sums[0]] + got, [(piece, size)] * 2, [(half, size)]
    )
    q = [
        along_col(first, [(0, 1), (3, 2)]),
        along_col(first, [(1, 2), (2, 1)]),
        along_col(second, [(0, 2), (3, 1)]),
    ]
    shape = (piece, size)
    res, x = call(zeroth_kernel, [where, rhs_piece, second] + q + [top_diag], [shape] * 2)
    h = hop(x, [(0, 1)])
    near, far, x = lax.optimization_barrier((near, far, x))
    moved = [near, swap(near), far, swap(far)]
    (x,) = call(
        first_kernel, [where, res, x, top_diag, h] + moved, [shape], [shape] * 2
    )
    hb = hop(x, [(1, 2), (0, 3)])
    ha = hop(x, [(0, 2), (1, 3)])
    (x,) = call(
        second_kernel, [where, res, x, top_diag, hb, ha, top_factor] + moved, [shape], [shape] * 2
    )
    h = hop(x, [(2, 3)])
    (res,) = call(third_kernel, [where, res, hb, ha, top_factor] + moved, [shape], [shape])
    (x,) = call(
        fourth_kernel, [where, res, x, top_diag, h, top_factor] + moved[2:], [shape], [shape] * 2
    )
    z = [
        along_col(x, [(1, 0), (2, 3)]),
        along_col(x, [(1, 2), (2, 1)]),
        along_col(x, [(1, 3), (2, 0)]),
    ]
    (own,) = call(half_kernel, [where, x] + z, [(size, half)])
    (top_sol,) = call(last_kernel, [where, own, swap(own)], [top_rhs.shape])
    return (child_sol, top_sol)


def solution(mesh):
    in_specs = (
        P(("leaf", "row", "col"), None, None),
        P(("leaf", "row", "col"), None, None),
        P(("leaf", "row", "col"), None, None),
        P(("leaf", "row", "col")),
        P(("leaf", "row", "col"), None),
        P("row", None),
        P("row", "col"),
        P("row", None),
    )
    out_specs = (P(("leaf", "row", "col"), None, None), P("row", None))
    axes = tuple(mesh.shape[a] for a in ("leaf", "row", "col"))

    def shards(*args):
        top_rhs, top_factor, top_diag = args[5:]
        size = top_diag.shape[1]
        fits = axes == (2, 4, 4) and top_rhs.shape[0] == size and top_factor.shape[1] == size
        return (central if fits else any_mesh)(*args)

    return jax.shard_map(shards, mesh=mesh, in_specs=in_specs, out_specs=out_specs, check_vma=False)
```

```python
import functools

import jax
import jax.numpy as jnp
from jax import lax
from jax.experimental import pallas as pl
from jax.experimental.pallas import tpu as pltpu
from jax.sharding import PartitionSpec as P

F32 = jnp.float32
BF16 = jnp.bfloat16
NT = (((1,), (1,)), ((), ()))
NN = (((1,), (0,)), ((), ()))
VM = pl.BlockSpec(memory_space=pltpu.VMEM)
ANY = pl.BlockSpec(memory_space=pl.ANY)
SM = pl.BlockSpec(memory_space=pltpu.SMEM)


def spread(value, axis, source):
    kept = jnp.where(lax.axis_index(axis) == source, value, 0).astype(value.dtype)
    return lax.psum(kept, axis)


def unit_lower(matrix):
    return jnp.tril(matrix) + jnp.eye(matrix.shape[-1], dtype=matrix.dtype)


def any_mesh(child_rhs, child_diag, child_off, live, targets, top_rhs, top_factor, top_diag):
    highest = lax.Precision.HIGHEST
    owned_rows = top_rhs.shape[0]
    right_count = top_rhs.shape[1]
    block_size = top_diag.shape[1]
    owned_blocks = owned_rows // block_size
    row_count = lax.axis_size("row")
    top_order = owned_rows * row_count
    col_width = top_factor.shape[1]
    my_row = lax.axis_index("row")
    my_col = lax.axis_index("col")
    child_sol = jnp.einsum("bij,bjr->bir", unit_lower(child_diag), child_rhs, precision=highest)
    tiles = jnp.einsum("btj,bjr->btr", child_off, child_sol, precision=highest)
    slot_index = jnp.arange(child_off.shape[1], dtype=jnp.int32)
    keep = slot_index[None, :] < live[:, None]
    tiles = jnp.where(keep[:, :, None], tiles, jnp.zeros_like(tiles))
    contrib = jnp.zeros((top_order, right_count), F32)
    contrib = contrib.at[targets.reshape(-1)].add(tiles.reshape(-1, right_count))
    row_part = lax.psum_scatter(contrib, "row", scatter_dimension=0, tiled=True)
    share = lax.psum_scatter(row_part, ("leaf", "col"), scatter_dimension=0, tiled=True)
    updates = lax.all_gather(share, ("leaf", "col"), axis=0, tiled=True)
    reduced = top_rhs - updates
    inverse_all = unit_lower(top_diag.reshape(owned_blocks, block_size, block_size))
    col_global = my_col * col_width + jnp.arange(col_width, dtype=jnp.int32)

    def step(block, solution):
        local = block % owned_blocks
        owner = block // owned_blocks
        factor_rows = jnp.where(
            (col_global < block * block_size)[None, :], top_factor, jnp.zeros_like(top_factor)
        )
        columns = lax.dynamic_slice_in_dim(solution, my_col * col_width, col_width, 0)
        partial_value = jnp.dot(
            factor_rows, columns, precision=highest, preferred_element_type=F32
        )
        block_inverse = lax.dynamic_index_in_dim(inverse_all, local, 0, keepdims=False)
        before = lax.psum(partial_value, "col")
        solved = jnp.dot(
            block_inverse, reduced - before, precision=highest, preferred_element_type=F32
        )
        solved = spread(solved, "row", owner)
        return lax.dynamic_update_slice_in_dim(solution, solved, block * block_size, 0)

    solution = lax.fori_loop(
        0, row_count * owned_blocks, step, jnp.zeros((top_order, right_count), F32)
    )
    top_sol = lax.dynamic_slice_in_dim(solution, my_row * owned_rows, owned_rows, 0)
    return (child_sol, top_sol)


def split(value):
    high = value.astype(BF16)
    return high, (value - high.astype(F32)).astype(BF16)


def dot3(left, right, dims):
    left_high, left_low = split(left)
    right_high, right_low = split(right)
    rows = left.shape[0]
    both = lax.dot_general(
        jnp.concatenate([left_high, left_low], axis=0), right_high, dims, preferred_element_type=F32
    )
    cross = lax.dot_general(left_high, right_low, dims, preferred_element_type=F32)
    return both[:rows] + both[rows:] + cross


def lower(matrix, first_row=0):
    row = lax.broadcasted_iota(jnp.int32, matrix.shape, 0) + first_row
    col = lax.broadcasted_iota(jnp.int32, matrix.shape, 1)
    return jnp.where(col <= row, matrix, 0.0)


def turn_kernel(where_ref, rhs_ref, out_ref, turned_ref):
    leaf, z = where_ref[0], where_ref[2]
    half, piece = turned_ref.shape[0], out_ref.shape[0]
    turned_ref[...] = rhs_ref[:, pl.ds(pl.multiple_of(leaf * half, half), half)].T
    out_ref[...] = turned_ref[pl.ds(pl.multiple_of((z // 2) * piece, piece), piece), :]


def child_kernel(where_ref, live_ref, rhs_hbm, diag_hbm, off_hbm, tgt_ref, sol_ref, keep_ref, send_ref,
                 rhs_ref, diag_ref, off_ref, tiles_ref, sems):
    leaf = where_ref[0]
    children, slots = off_ref.shape[0], off_ref.shape[1]
    half = keep_ref.shape[0]
    pairs = ((rhs_hbm, rhs_ref), (diag_hbm, diag_ref), (off_hbm, off_ref))
    copies = [
        [pltpu.make_async_copy(source.at[s], target.at[s], sems.at[i, s]) for i, (source, target) in enumerate(pairs)]
        for s in range(children)
    ]
    for s in range(children):
        for copy in copies[s]:
            copy.start()
    for s in range(children):
        copies[s][0].wait()
        copies[s][1].wait()
        rhs = rhs_ref[s]
        sol = rhs + dot3(lower(diag_ref[s]), rhs, NN)
        sol_ref[s] = sol
        copies[s][2].wait()
        tiles = dot3(sol.T, off_ref[s], NT)
        slot = lax.broadcasted_iota(jnp.int32, tiles.shape, 1)
        tiles_ref[:, s * slots:(s + 1) * slots] = jnp.where(slot < live_ref[s], tiles, 0.0)
        send_ref[half:half + 8, s * slots:(s + 1) * slots] = jnp.broadcast_to(
            tgt_ref[s:s + 1, :].astype(F32), (8, slots)
        )
    keep_ref[...] = tiles_ref[pl.ds(pl.multiple_of(leaf * half, half), half), :]
    send_ref[0:half, :] = tiles_ref[pl.ds(pl.multiple_of((1 - leaf) * half, half), half), :]


def scatter_kernel(where_ref, keep_ref, recv_ref, tgt_ref, *out_refs):
    row = where_ref[1]
    half, slots_all = keep_ref.shape
    size = out_refs[0].shape[1]
    children, slots = tgt_ref.shape
    mine = [split(keep_ref[...]), split(recv_ref[0:half, :])]
    stacked = [jnp.concatenate(pair, axis=0) for pair in mine]
    mine_targets = jnp.concatenate([tgt_ref[s:s + 1, :] for s in range(children)], axis=1)
    target = [mine_targets, recv_ref[half:half + 1, :].astype(jnp.int32)]
    for s, out_ref in enumerate(out_refs):
        block = jnp.bitwise_xor(row, s)
        index = lax.broadcasted_iota(jnp.int32, (size, slots_all), 0) + block * size
        total = None
        for t, value in zip(target, stacked):
            hot = jnp.where(index == t, 1.0, 0.0).astype(BF16)
            product = lax.dot_general(value, hot, NT, preferred_element_type=F32)
            total = product if total is None else total + product
        out_ref[...] = total[:half] + total[half:]


def pieces_kernel(where_ref, a_ref, b_ref, c_ref, d_ref, first_ref, second_ref, sum_ref):
    odd = where_ref[2] % 2
    piece = first_ref.shape[0]
    sum_ref[...] = (a_ref[...] + b_ref[...]) + (c_ref[...] + d_ref[...])
    first_ref[...] = sum_ref[pl.ds(pl.multiple_of(odd * piece, piece), piece), :]
    second_ref[...] = sum_ref[pl.ds(pl.multiple_of((1 - odd) * piece, piece), piece), :]


def zeroth_kernel(where_ref, rhs_ref, a_ref, b_ref, c_ref, d_ref, diag_ref, res_ref, x_ref):
    row = where_ref[1]
    res = rhs_ref[...] - ((a_ref[...] + b_ref[...]) + (c_ref[...] + d_ref[...]))
    res_ref[...] = res
    x_ref[...] = res

    @pl.when(row == 0)
    def _():
        x_ref[...] = res + dot3(res, lower(diag_ref[...]), NT)


def column(where_ref, block, own_ref, got_ref, other_ref):
    leaf, z = where_ref[0], where_ref[2]
    if block == 0:
        return jnp.where((leaf == 0) == (z == 1), got_ref[...], other_ref[...])
    sent = jnp.where((leaf == 0) == (block == 1), got_ref[...], other_ref[...])
    return jnp.where(z == block, own_ref[...], sent)


def first_kernel(where_ref, res_ref, x_ref, diag_ref, h_ref, *refs):
    row, z = where_ref[1], where_ref[2]
    blocks, out_ref = refs[:3], refs[3]
    out_ref[...] = x_ref[...]

    @pl.when((row == 1) & ((z == 1) | (z == 2)))
    def _():
        value = res_ref[...] - dot3(h_ref[...], column(where_ref, 0, *blocks), NT)
        out_ref[...] = value + dot3(value, lower(diag_ref[...]), NT)


def second_kernel(where_ref, res_ref, x_ref, diag_ref, hb_ref, ha_ref, *refs):
    row, z = where_ref[1], where_ref[2]
    blocks, out_ref = refs[:3], refs[3]
    out_ref[...] = x_ref[...]

    @pl.when((row == 2) & ((z == 1) | (z == 2)))
    def _():
        value = res_ref[...] - dot3(ha_ref[...], column(where_ref, 0, *blocks), NT)
        value = value - dot3(hb_ref[...], column(where_ref, 1, *blocks), NT)
        out_ref[...] = value + dot3(value, lower(diag_ref[...]), NT)


def third_kernel(where_ref, res_ref, hb_ref, ha_ref, *refs):
    row, z = where_ref[1], where_ref[2]
    blocks, out_ref = refs[:3], refs[3]
    out_ref[...] = res_ref[...]

    @pl.when((row == 3) & ((z == 1) | (z == 2)))
    def _():
        value = res_ref[...] - dot3(hb_ref[...], column(where_ref, 0, *blocks), NT)
        out_ref[...] = value - dot3(ha_ref[...], column(where_ref, 1, *blocks), NT)


def fourth_kernel(where_ref, res_ref, x_ref, diag_ref, h_ref, *refs):
    row, z = where_ref[1], where_ref[2]
    blocks, out_ref = refs[:3], refs[3]
    out_ref[...] = x_ref[...]

    @pl.when((row == 3) & ((z == 1) | (z == 2)))
    def _():
        value = res_ref[...] - dot3(h_ref[...], column(where_ref, 2, *blocks), NT)
        out_ref[...] = value + dot3(value, lower(diag_ref[...]), NT)


def half_kernel(where_ref, x_ref, a_ref, b_ref, c_ref, out_ref):
    z = where_ref[2]
    x, a, b, c = x_ref[...], a_ref[...], b_ref[...], c_ref[...]
    low = jnp.where(z == 0, a, jnp.where(z == 1, x, jnp.where(z == 2, b, c)))
    high = jnp.where(z == 0, c, jnp.where(z == 1, b, jnp.where(z == 2, x, a)))
    out_ref[...] = jnp.concatenate([low, high], axis=0).T


def last_kernel(where_ref, own_ref, other_ref, out_ref):
    leaf = where_ref[0]
    half = own_ref.shape[1]
    own, other = own_ref[...], other_ref[...]
    out_ref[:, 0:half] = jnp.where(leaf == 0, own, other)
    out_ref[:, half:2 * half] = jnp.where(leaf == 0, other, own)


def call(kernel, ins, outs, scratch=(), outside=(), limit=40):
    def spec(i, a):
        return ANY if i in outside else SM if a.ndim == 1 else VM

    return pl.pallas_call(
        kernel,
        out_shape=[jax.ShapeDtypeStruct(shape, F32) for shape in outs],
        in_specs=[spec(i, a) for i, a in enumerate(ins)],
        out_specs=[VM] * len(outs),
        scratch_shapes=[pltpu.VMEM(s, F32) if isinstance(s, tuple) else s for s in scratch],
        cost_estimate=pl.CostEstimate(flops=0, bytes_accessed=4 * sum(a.size for a in ins), transcendentals=0),
        compiler_params=pltpu.CompilerParams(vmem_limit_bytes=limit * 1024 * 1024),
    )(*ins)


def central(child_rhs, child_diag, child_off, live, targets, top_rhs, top_factor, top_diag):
    leaf, row, col = (lax.axis_index(a) for a in ("leaf", "row", "col"))
    where = jnp.stack([leaf, row, col]).astype(jnp.int32)
    rows, cols = lax.axis_size("row"), lax.axis_size("col")
    size = top_diag.shape[1]
    right = top_rhs.shape[1]
    half, piece = right // 2, right // 4
    children, slots = targets.shape

    def at(r, c):
        return r * cols + c

    def swap(value):
        return lax.ppermute(value, "leaf", [(0, 1), (1, 0)])

    def plane(value, pairs):
        return lax.ppermute(value, ("row", "col"), pairs)

    def hop(value, pairs):
        return plane(value, [(at(a, z), at(b, z)) for a, b in pairs for z in (1, 2)])

    def along_row(value, pairs):
        return lax.ppermute(value, "row", pairs)

    def along_col(value, pairs):
        return lax.ppermute(value, "col", pairs)

    near = [(at(k, 0), at(k, 1)) for k in (1, 2, 3)] + [(at(k, 1), at(k, 2)) for k in (2, 3)]
    far = [(at(k, 0), at(k, 2)) for k in (1, 2, 3)] + [(at(3, 2), at(3, 1))]
    shift = rows * cols
    sent = lax.ppermute(
        top_factor, ("leaf", "row", "col"), near + [(a + shift, b + shift) for a, b in far]
    )
    child_sol, keep, send = call(
        child_kernel,
        [where, live, child_rhs, child_diag, child_off, targets],
        [child_rhs.shape, (half, children * slots), (half + 8, children * slots)],
        [child_rhs.shape, child_diag.shape, child_off.shape, (right, children * slots),
         pltpu.SemaphoreType.DMA((3, children))],
        outside=(2, 3, 4),
        limit=56,
    )
    sums = call(scatter_kernel, [where, keep, swap(send), targets], [(half, size)] * rows)
    got = [along_row(sums[s], [(i, i ^ s) for i in range(rows)]) for s in (1, 2, 3)]

    (rhs_piece,) = call(turn_kernel, [where, top_rhs], [(piece, size)], [(half, size)])
    first, second = call(
        pieces_kernel, [where, sums[0]] + got, [(piece, size)] * 2, [(half, size)]
    )
    q = [
        along_col(first, [(0, 1), (3, 2)]),
        along_col(first, [(1, 2), (2, 1)]),
        along_col(second, [(0, 2), (3, 1)]),
    ]
    shape = (piece, size)
    res, x = call(zeroth_kernel, [where, rhs_piece, second] + q + [top_diag], [shape] * 2)
    h = hop(x, [(0, 1)])
    sent, x = lax.optimization_barrier((sent, x))
    blocks = [top_factor, sent, swap(sent)]
    (x,) = call(first_kernel, [where, res, x, top_diag, h] + blocks, [shape])
    hb = hop(x, [(1, 2), (0, 3)])
    ha = hop(x, [(0, 2), (1, 3)])
    (x,) = call(second_kernel, [where, res, x, top_diag, hb, ha] + blocks, [shape])
    h = hop(x, [(2, 3)])
    (res,) = call(third_kernel, [where, res, hb, ha] + blocks, [shape])
    (x,) = call(fourth_kernel, [where, res, x, top_diag, h] + blocks, [shape])
    z = [
        along_col(x, [(1, 0), (2, 3)]),
        along_col(x, [(1, 2), (2, 1)]),
        along_col(x, [(1, 3), (2, 0)]),
    ]
    (own,) = call(half_kernel, [where, x] + z, [(size, half)])
    (top_sol,) = call(last_kernel, [where, own, swap(own)], [top_rhs.shape])
    return (child_sol, top_sol)


def solution(mesh):
    in_specs = (
        P(("leaf", "row", "col"), None, None),
        P(("leaf", "row", "col"), None, None),
        P(("leaf", "row", "col"), None, None),
        P(("leaf", "row", "col")),
        P(("leaf", "row", "col"), None),
        P("row", None),
        P("row", "col"),
        P("row", None),
    )
    out_specs = (P(("leaf", "row", "col"), None, None), P("row", None))
    axes = tuple(mesh.shape[a] for a in ("leaf", "row", "col"))

    def shards(*args):
        top_rhs, top_factor, top_diag = args[5:]
        size = top_diag.shape[1]
        fits = axes == (2, 4, 4) and top_rhs.shape[0] == size and top_factor.shape[1] == size
        return (central if fits else any_mesh)(*args)

    return jax.shard_map(shards, mesh=mesh, in_specs=in_specs, out_specs=out_specs, check_vma=False)
```

```python
import functools

import jax
import jax.numpy as jnp
from jax import lax
from jax.experimental import pallas as pl
from jax.experimental.pallas import tpu as pltpu
from jax.sharding import PartitionSpec as P

F32 = jnp.float32
BF16 = jnp.bfloat16
NT = (((1,), (1,)), ((), ()))
NN = (((1,), (0,)), ((), ()))
VM = pl.BlockSpec(memory_space=pltpu.VMEM)
ANY = pl.BlockSpec(memory_space=pl.ANY)
SM = pl.BlockSpec(memory_space=pltpu.SMEM)


def spread(value, axis, source):
    kept = jnp.where(lax.axis_index(axis) == source, value, 0).astype(value.dtype)
    return lax.psum(kept, axis)


def unit_lower(matrix):
    return jnp.tril(matrix) + jnp.eye(matrix.shape[-1], dtype=matrix.dtype)


def any_mesh(child_rhs, child_diag, child_off, live, targets, top_rhs, top_factor, top_diag):
    highest = lax.Precision.HIGHEST
    owned_rows = top_rhs.shape[0]
    right_count = top_rhs.shape[1]
    block_size = top_diag.shape[1]
    owned_blocks = owned_rows // block_size
    row_count = lax.axis_size("row")
    top_order = owned_rows * row_count
    col_width = top_factor.shape[1]
    my_row = lax.axis_index("row")
    my_col = lax.axis_index("col")
    child_sol = jnp.einsum("bij,bjr->bir", unit_lower(child_diag), child_rhs, precision=highest)
    tiles = jnp.einsum("btj,bjr->btr", child_off, child_sol, precision=highest)
    slot_index = jnp.arange(child_off.shape[1], dtype=jnp.int32)
    keep = slot_index[None, :] < live[:, None]
    tiles = jnp.where(keep[:, :, None], tiles, jnp.zeros_like(tiles))
    contrib = jnp.zeros((top_order, right_count), F32)
    contrib = contrib.at[targets.reshape(-1)].add(tiles.reshape(-1, right_count))
    row_part = lax.psum_scatter(contrib, "row", scatter_dimension=0, tiled=True)
    share = lax.psum_scatter(row_part, ("leaf", "col"), scatter_dimension=0, tiled=True)
    updates = lax.all_gather(share, ("leaf", "col"), axis=0, tiled=True)
    reduced = top_rhs - updates
    inverse_all = unit_lower(top_diag.reshape(owned_blocks, block_size, block_size))
    col_global = my_col * col_width + jnp.arange(col_width, dtype=jnp.int32)

    def step(block, solution):
        local = block % owned_blocks
        owner = block // owned_blocks
        factor_rows = jnp.where(
            (col_global < block * block_size)[None, :], top_factor, jnp.zeros_like(top_factor)
        )
        columns = lax.dynamic_slice_in_dim(solution, my_col * col_width, col_width, 0)
        partial_value = jnp.dot(
            factor_rows, columns, precision=highest, preferred_element_type=F32
        )
        block_inverse = lax.dynamic_index_in_dim(inverse_all, local, 0, keepdims=False)
        before = lax.psum(partial_value, "col")
        solved = jnp.dot(
            block_inverse, reduced - before, precision=highest, preferred_element_type=F32
        )
        solved = spread(solved, "row", owner)
        return lax.dynamic_update_slice_in_dim(solution, solved, block * block_size, 0)

    solution = lax.fori_loop(
        0, row_count * owned_blocks, step, jnp.zeros((top_order, right_count), F32)
    )
    top_sol = lax.dynamic_slice_in_dim(solution, my_row * owned_rows, owned_rows, 0)
    return (child_sol, top_sol)


def place():
    return tuple(lax.axis_index(a) for a in ("leaf", "row", "col"))


def split(value):
    high = value.astype(BF16)
    return high, (value - high.astype(F32)).astype(BF16)


def dot3(left, high, low, dims):
    left_high, left_low = split(left)
    rows = left.shape[0]
    both = lax.dot_general(
        jnp.concatenate([left_high, left_low], axis=0), high, dims, preferred_element_type=F32
    )
    cross = lax.dot_general(left_high, low, dims, preferred_element_type=F32)
    return both[:rows] + both[rows:] + cross


def lower(matrix):
    row = lax.broadcasted_iota(jnp.int32, matrix.shape, 0)
    col = lax.broadcasted_iota(jnp.int32, matrix.shape, 1)
    return jnp.where(col <= row, matrix, 0.0)


def turn_kernel(rhs_ref, diag_ref, out_ref, high_ref, low_ref, turned_ref):
    leaf, _, z = place()
    half, piece = turned_ref.shape[0], out_ref.shape[0]
    turned_ref[...] = rhs_ref[:, pl.ds(pl.multiple_of(leaf * half, half), half)].T
    out_ref[...] = turned_ref[pl.ds(pl.multiple_of((z // 2) * piece, piece), piece), :]
    high_ref[...], low_ref[...] = split(lower(diag_ref[...]).T)


def child_kernel(live_ref, rhs_hbm, diag_hbm, off_hbm, tgt_ref, sol_hbm, keep_ref, send_ref,
                 rhs_ref, diag_ref, off_ref, sol_ref, tiles_ref, sems):
    leaf, _, _ = place()
    children, slots = off_ref.shape[0], off_ref.shape[1]
    half = keep_ref.shape[0]
    pairs = ((rhs_hbm, rhs_ref), (diag_hbm, diag_ref), (off_hbm, off_ref))
    copies = [
        [pltpu.make_async_copy(source.at[s], target.at[s], sems.at[i, s]) for i, (source, target) in enumerate(pairs)]
        for s in range(children)
    ]
    back = [pltpu.make_async_copy(sol_ref.at[s], sol_hbm.at[s], sems.at[3, s]) for s in range(children)]
    for s in range(children):
        for copy in copies[s]:
            copy.start()
    for s in range(children):
        copies[s][0].wait()
        copies[s][1].wait()
        rhs = rhs_ref[s]
        sol = rhs + dot3(lower(diag_ref[s]), *split(rhs), NN)
        sol_ref[s] = sol
        back[s].start()
        copies[s][2].wait()
        tiles = dot3(sol.T, *split(off_ref[s]), NT)
        slot = lax.broadcasted_iota(jnp.int32, tiles.shape, 1)
        tiles_ref[:, s * slots:(s + 1) * slots] = jnp.where(slot < live_ref[s], tiles, 0.0)
        send_ref[half:half + 8, s * slots:(s + 1) * slots] = jnp.broadcast_to(
            tgt_ref[s:s + 1, :].astype(F32), (8, slots)
        )
    keep_ref[...] = tiles_ref[pl.ds(pl.multiple_of(leaf * half, half), half), :]
    send_ref[0:half, :] = tiles_ref[pl.ds(pl.multiple_of((1 - leaf) * half, half), half), :]
    for copy in back:
        copy.wait()


def scatter_kernel(keep_ref, recv_ref, tgt_ref, *out_refs):
    _, row, _ = place()
    half, slots_all = keep_ref.shape
    size = out_refs[0].shape[1]
    children, slots = tgt_ref.shape
    mine = [split(keep_ref[...]), split(recv_ref[0:half, :])]
    stacked = [jnp.concatenate(pair, axis=0) for pair in mine]
    mine_targets = jnp.concatenate([tgt_ref[s:s + 1, :] for s in range(children)], axis=1)
    target = [mine_targets, recv_ref[half:half + 1, :].astype(jnp.int32)]
    for s, out_ref in enumerate(out_refs):
        block = jnp.bitwise_xor(row, s)
        index = lax.broadcasted_iota(jnp.int32, (size, slots_all), 0) + block * size
        total = None
        for t, value in zip(target, stacked):
            hot = jnp.where(index == t, 1.0, 0.0).astype(BF16)
            product = lax.dot_general(value, hot, NT, preferred_element_type=F32)
            total = product if total is None else total + product
        out_ref[...] = total[:half] + total[half:]


def pieces_kernel(a_ref, b_ref, c_ref, d_ref, first_ref, second_ref, sum_ref):
    _, _, z = place()
    odd = z % 2
    piece = first_ref.shape[0]
    sum_ref[...] = (a_ref[...] + b_ref[...]) + (c_ref[...] + d_ref[...])
    first_ref[...] = sum_ref[pl.ds(pl.multiple_of(odd * piece, piece), piece), :]
    second_ref[...] = sum_ref[pl.ds(pl.multiple_of((1 - odd) * piece, piece), piece), :]


def factor_kernel(own_ref, sent_ref, other_ref, *out_refs):
    leaf, row, z = place()
    for block in range(3):
        high_ref, low_ref = out_refs[2 * block], out_refs[2 * block + 1]

        @pl.when((row > block) & ((z == 1) | (z == 2)))
        def _():
            if block == 0:
                value = jnp.where((leaf == 0) == (z == 1), sent_ref[...], other_ref[...])
            else:
                sent = jnp.where((leaf == 0) == (block == 1), sent_ref[...], other_ref[...])
                value = jnp.where(z == block, own_ref[...], sent)
            high_ref[...], low_ref[...] = split(value.T)


def chain_kernel(owner, has_sums, solves, *refs):
    refs = list(refs)
    out_refs = [refs.pop()]
    if has_sums:
        out_refs.insert(0, refs.pop())
    _, row, z = place()
    given_ref = refs[0]
    if has_sums:
        value = given_ref[...] - ((refs[1][...] + refs[2][...]) + (refs[3][...] + refs[4][...]))
        out_refs[0][...] = value
        out_refs[1][...] = value
        refs = refs[5:]
    else:
        out_refs[0][...] = refs[1][...]
        refs = refs[2:]

    @pl.when((row == owner) & ((z == 1) | (z == 2)))
    def _():
        left = out_refs[0][...] if has_sums else given_ref[...]
        used = refs[2:] if solves else refs
        for i in range(0, len(used), 3):
            left = left - dot3(used[i][...], used[i + 1][...], used[i + 2][...], NN)
        if solves:
            left = left + dot3(left, refs[0][...], refs[1][...], NN)
        out_refs[-1][...] = left


def half_kernel(x_ref, a_ref, b_ref, c_ref, out_ref):
    _, _, z = place()
    x, a, b, c = x_ref[...], a_ref[...], b_ref[...], c_ref[...]
    low = jnp.where(z == 0, a, jnp.where(z == 1, x, jnp.where(z == 2, b, c)))
    high = jnp.where(z == 0, c, jnp.where(z == 1, b, jnp.where(z == 2, x, a)))
    out_ref[...] = jnp.concatenate([low, high], axis=0).T


def write_kernel(mine, part_ref, *refs):
    out_hbm, sem = refs[-2:]
    leaf, _, _ = place()
    half = part_ref.shape[1]
    at = leaf if mine else 1 - leaf
    copy = pltpu.make_async_copy(part_ref, out_hbm.at[:, pl.ds(pl.multiple_of(at * half, half), half)], sem)
    copy.start()
    copy.wait()


def call(kernel, ins, outs, scratch=(), outside=(), outs_outside=(), pinned=(), aliases=None, limit=24):
    def spec(i, a):
        return ANY if i in outside else SM if a.ndim == 1 else VM

    def shape(i, out):
        dims, dtype = out if isinstance(out[0], tuple) else (out, F32)
        return pltpu.VMEM(dims, dtype) if i in pinned else jax.ShapeDtypeStruct(dims, dtype)

    outs = pl.pallas_call(
        kernel,
        out_shape=[shape(i, out) for i, out in enumerate(outs)],
        in_specs=[spec(i, a) for i, a in enumerate(ins)],
        out_specs=[ANY if i in outs_outside else VM for i in range(len(outs))],
        scratch_shapes=[pltpu.VMEM(s, F32) if isinstance(s, tuple) else s for s in scratch],
        input_output_aliases=aliases or {},
        cost_estimate=pl.CostEstimate(flops=0, bytes_accessed=4 * sum(a.size for a in ins), transcendentals=0),
        compiler_params=pltpu.CompilerParams(vmem_limit_bytes=limit * 1024 * 1024),
    )(*ins)
    return list(outs)


def central(child_rhs, child_diag, child_off, live, targets, top_rhs, top_factor, top_diag):
    rows, cols = lax.axis_size("row"), lax.axis_size("col")
    size = top_diag.shape[1]
    right = top_rhs.shape[1]
    half, piece = right // 2, right // 4
    children, slots = targets.shape
    shape = (piece, size)
    block = ((size, size), BF16)
    dma = pltpu.SemaphoreType.DMA

    def at(r, c):
        return r * cols + c

    def swap(value):
        return lax.ppermute(value, "leaf", [(0, 1), (1, 0)])

    def hop(value, pairs):
        pairs = [(at(a, z), at(b, z)) for a, b in pairs for z in (1, 2)]
        return lax.ppermute(value, ("row", "col"), pairs)

    def along_row(value, pairs):
        return lax.ppermute(value, "row", pairs)

    def along_col(value, pairs):
        return lax.ppermute(value, "col", pairs)

    near = [(at(k, 0), at(k, 1)) for k in (1, 2, 3)] + [(at(k, 1), at(k, 2)) for k in (2, 3)]
    far = [(at(k, 0), at(k, 2)) for k in (1, 2, 3)] + [(at(3, 2), at(3, 1))]
    shift = rows * cols
    sent = lax.ppermute(
        top_factor, ("leaf", "row", "col"), near + [(a + shift, b + shift) for a, b in far]
    )
    child_sol, keep, send = call(
        child_kernel,
        [live, child_rhs, child_diag, child_off, targets],
        [child_rhs.shape, (half, children * slots), (half + 8, children * slots)],
        [child_rhs.shape, child_diag.shape, child_off.shape, child_rhs.shape, (right, children * slots),
         dma((4, children))],
        outside=(1, 2, 3),
        outs_outside=(0,),
        pinned=(1, 2),
        limit=56,
    )
    sums = call(scatter_kernel, [keep, swap(send), targets], [(half, size)] * rows)
    got = [along_row(sums[s], [(i, i ^ s) for i in range(rows)]) for s in (1, 2, 3)]
    rhs_piece, diag_high, diag_low = call(
        turn_kernel, [top_rhs, top_diag], [shape, block, block], [(half, size)]
    )
    diag = [diag_high, diag_low]
    first, second = call(pieces_kernel, [sums[0]] + got, [shape] * 2, [(half, size)])
    sent, first, second = lax.optimization_barrier((sent, first, second))
    q = [
        along_col(first, [(0, 1), (3, 2)]),
        along_col(first, [(1, 2), (2, 1)]),
        along_col(second, [(0, 2), (3, 1)]),
    ]
    factor = call(factor_kernel, [top_factor, sent, swap(sent)], [block] * 6)
    factor = [factor[0:2], factor[2:4], factor[4:6]]

    def chain(owner, ins, has_sums=False, solves=True):
        outs = call(
            functools.partial(chain_kernel, owner, has_sums, solves), ins, [shape] * (1 + has_sums)
        )
        return outs if has_sums else outs[0]

    res, x = chain(0, [rhs_piece, second] + q + diag, has_sums=True)
    to1 = hop(x, [(0, 1)])
    to2 = hop(x, [(0, 2)])
    x = chain(1, [res, x] + diag + [to1] + factor[0])
    on = hop(x, [(1, 2), (0, 3)])
    res = chain(2, [res, res, to2] + factor[0], solves=False)
    x = chain(2, [res, x] + diag + [on] + factor[1])
    to3 = hop(x, [(2, 3)])
    late = hop(x, [(1, 3)])
    res = chain(3, [res, res, on] + factor[0], solves=False)
    x = chain(3, [res, x] + diag + [late] + factor[1] + [to3] + factor[2])

    both = along_col(x, [(1, 2), (2, 1)])
    step = along_col(x, [(1, 0), (2, 3)])
    over = along_col(x, [(1, 3), (2, 0)])
    (own,) = call(half_kernel, [x, step, both, over], [(size, half)])
    (top_sol,) = call(
        functools.partial(write_kernel, True), [own], [top_rhs.shape], [dma(())], outs_outside=(0,)
    )
    (top_sol,) = call(
        functools.partial(write_kernel, False),
        [swap(own), top_sol],
        [top_rhs.shape],
        [dma(())],
        outside=(1,),
        outs_outside=(0,),
        aliases={1: 0},
    )
    return (child_sol, top_sol)


def solution(mesh):
    in_specs = (
        P(("leaf", "row", "col"), None, None),
        P(("leaf", "row", "col"), None, None),
        P(("leaf", "row", "col"), None, None),
        P(("leaf", "row", "col")),
        P(("leaf", "row", "col"), None),
        P("row", None),
        P("row", "col"),
        P("row", None),
    )
    out_specs = (P(("leaf", "row", "col"), None, None), P("row", None))
    axes = tuple(mesh.shape[a] for a in ("leaf", "row", "col"))

    def shards(*args):
        top_rhs, top_factor, top_diag = args[5:]
        size = top_diag.shape[1]
        fits = axes == (2, 4, 4) and top_rhs.shape[0] == size and top_factor.shape[1] == size
        return (central if fits else any_mesh)(*args)

    return jax.shard_map(shards, mesh=mesh, in_specs=in_specs, out_specs=out_specs, check_vma=False)
```

```python
import functools

import jax
import jax.numpy as jnp
from jax import lax
from jax.experimental import pallas as pl
from jax.experimental.pallas import tpu as pltpu
from jax.sharding import PartitionSpec as P

F32 = jnp.float32
BF16 = jnp.bfloat16
NT = (((1,), (1,)), ((), ()))
NN = (((1,), (0,)), ((), ()))
VM = pl.BlockSpec(memory_space=pltpu.VMEM)
ANY = pl.BlockSpec(memory_space=pl.ANY)
SM = pl.BlockSpec(memory_space=pltpu.SMEM)


def spread(value, axis, source):
    kept = jnp.where(lax.axis_index(axis) == source, value, 0).astype(value.dtype)
    return lax.psum(kept, axis)


def unit_lower(matrix):
    return jnp.tril(matrix) + jnp.eye(matrix.shape[-1], dtype=matrix.dtype)


def any_mesh(child_rhs, child_diag, child_off, live, targets, top_rhs, top_factor, top_diag):
    highest = lax.Precision.HIGHEST
    owned_rows = top_rhs.shape[0]
    right_count = top_rhs.shape[1]
    block_size = top_diag.shape[1]
    owned_blocks = owned_rows // block_size
    row_count = lax.axis_size("row")
    top_order = owned_rows * row_count
    col_width = top_factor.shape[1]
    my_row = lax.axis_index("row")
    my_col = lax.axis_index("col")
    child_sol = jnp.einsum("bij,bjr->bir", unit_lower(child_diag), child_rhs, precision=highest)
    tiles = jnp.einsum("btj,bjr->btr", child_off, child_sol, precision=highest)
    slot_index = jnp.arange(child_off.shape[1], dtype=jnp.int32)
    keep = slot_index[None, :] < live[:, None]
    tiles = jnp.where(keep[:, :, None], tiles, jnp.zeros_like(tiles))
    contrib = jnp.zeros((top_order, right_count), F32)
    contrib = contrib.at[targets.reshape(-1)].add(tiles.reshape(-1, right_count))
    row_part = lax.psum_scatter(contrib, "row", scatter_dimension=0, tiled=True)
    share = lax.psum_scatter(row_part, ("leaf", "col"), scatter_dimension=0, tiled=True)
    updates = lax.all_gather(share, ("leaf", "col"), axis=0, tiled=True)
    reduced = top_rhs - updates
    inverse_all = unit_lower(top_diag.reshape(owned_blocks, block_size, block_size))
    col_global = my_col * col_width + jnp.arange(col_width, dtype=jnp.int32)

    def step(block, solution):
        local = block % owned_blocks
        owner = block // owned_blocks
        factor_rows = jnp.where(
            (col_global < block * block_size)[None, :], top_factor, jnp.zeros_like(top_factor)
        )
        columns = lax.dynamic_slice_in_dim(solution, my_col * col_width, col_width, 0)
        partial_value = jnp.dot(
            factor_rows, columns, precision=highest, preferred_element_type=F32
        )
        block_inverse = lax.dynamic_index_in_dim(inverse_all, local, 0, keepdims=False)
        before = lax.psum(partial_value, "col")
        solved = jnp.dot(
            block_inverse, reduced - before, precision=highest, preferred_element_type=F32
        )
        solved = spread(solved, "row", owner)
        return lax.dynamic_update_slice_in_dim(solution, solved, block * block_size, 0)

    solution = lax.fori_loop(
        0, row_count * owned_blocks, step, jnp.zeros((top_order, right_count), F32)
    )
    top_sol = lax.dynamic_slice_in_dim(solution, my_row * owned_rows, owned_rows, 0)
    return (child_sol, top_sol)


def place():
    return tuple(lax.axis_index(a) for a in ("leaf", "row", "col"))


def split(value):
    high = value.astype(BF16)
    return high, (value - high.astype(F32)).astype(BF16)


def dot3(left, high, low, dims):
    left_high, left_low = split(left)
    rows = left.shape[0]
    both = lax.dot_general(
        jnp.concatenate([left_high, left_low], axis=0), high, dims, preferred_element_type=F32
    )
    cross = lax.dot_general(left_high, low, dims, preferred_element_type=F32)
    return both[:rows] + both[rows:] + cross


def lower(matrix):
    row = lax.broadcasted_iota(jnp.int32, matrix.shape, 0)
    col = lax.broadcasted_iota(jnp.int32, matrix.shape, 1)
    return jnp.where(col <= row, matrix, 0.0)


def turn_kernel(rhs_ref, diag_ref, out_ref, high_ref, low_ref, turned_ref):
    leaf, _, z = place()
    half, piece = turned_ref.shape[0], out_ref.shape[0]
    turned_ref[...] = rhs_ref[:, pl.ds(pl.multiple_of(leaf * half, half), half)].T
    out_ref[...] = turned_ref[pl.ds(pl.multiple_of((z // 2) * piece, piece), piece), :]
    high_ref[...], low_ref[...] = split(lower(diag_ref[...]).T)


def child_kernel(live_ref, rhs_hbm, diag_hbm, off_hbm, tgt_ref, sol_hbm, keep_ref, send_ref,
                 rhs_ref, diag_ref, off_ref, sol_ref, tiles_ref, sems):
    leaf, _, _ = place()
    children, slots = off_ref.shape[0], off_ref.shape[1]
    half = keep_ref.shape[0]
    pairs = ((rhs_hbm, rhs_ref), (diag_hbm, diag_ref), (off_hbm, off_ref))
    copies = [
        [pltpu.make_async_copy(source.at[s], target.at[s], sems.at[i, s]) for i, (source, target) in enumerate(pairs)]
        for s in range(children)
    ]
    back = [pltpu.make_async_copy(sol_ref.at[s], sol_hbm.at[s], sems.at[3, s]) for s in range(children)]
    for s in range(children):
        for copy in copies[s]:
            copy.start()
    for s in range(children):
        copies[s][0].wait()
        copies[s][1].wait()
        rhs = rhs_ref[s]
        sol = rhs + dot3(lower(diag_ref[s]), *split(rhs), NN)
        sol_ref[s] = sol
        back[s].start()
        copies[s][2].wait()
        tiles = dot3(sol.T, *split(off_ref[s]), NT)
        slot = lax.broadcasted_iota(jnp.int32, tiles.shape, 1)
        tiles_ref[:, s * slots:(s + 1) * slots] = jnp.where(slot < live_ref[s], tiles, 0.0)
        send_ref[half:half + 8, s * slots:(s + 1) * slots] = jnp.broadcast_to(
            tgt_ref[s:s + 1, :].astype(F32), (8, slots)
        )
    keep_ref[...] = tiles_ref[pl.ds(pl.multiple_of(leaf * half, half), half), :]
    send_ref[0:half, :] = tiles_ref[pl.ds(pl.multiple_of((1 - leaf) * half, half), half), :]
    for copy in back:
        copy.wait()


def scatter_kernel(keep_ref, recv_ref, tgt_ref, *out_refs):
    _, row, _ = place()
    half, slots_all = keep_ref.shape
    size = out_refs[0].shape[1]
    children, slots = tgt_ref.shape
    mine = [split(keep_ref[...]), split(recv_ref[0:half, :])]
    stacked = [jnp.concatenate(pair, axis=0) for pair in mine]
    mine_targets = jnp.concatenate([tgt_ref[s:s + 1, :] for s in range(children)], axis=1)
    target = [mine_targets, recv_ref[half:half + 1, :].astype(jnp.int32)]
    for s, out_ref in enumerate(out_refs):
        block = jnp.bitwise_xor(row, s)
        index = lax.broadcasted_iota(jnp.int32, (size, slots_all), 0) + block * size
        total = None
        for t, value in zip(target, stacked):
            hot = jnp.where(index == t, 1.0, 0.0).astype(BF16)
            product = lax.dot_general(value, hot, NT, preferred_element_type=F32)
            total = product if total is None else total + product
        out_ref[...] = total[:half] + total[half:]


def pieces_kernel(a_ref, b_ref, c_ref, d_ref, first_ref, second_ref, sum_ref):
    _, _, z = place()
    odd = z % 2
    piece = first_ref.shape[0]
    sum_ref[...] = (a_ref[...] + b_ref[...]) + (c_ref[...] + d_ref[...])
    first_ref[...] = sum_ref[pl.ds(pl.multiple_of(odd * piece, piece), piece), :]
    second_ref[...] = sum_ref[pl.ds(pl.multiple_of((1 - odd) * piece, piece), piece), :]


def factor_kernel(own_ref, sent_ref, other_ref, *out_refs):
    leaf, row, z = place()
    for block in range(3):
        high_ref, low_ref = out_refs[2 * block], out_refs[2 * block + 1]

        @pl.when((row > block) & ((z == 1) | (z == 2)))
        def _():
            if block == 0:
                value = jnp.where((leaf == 0) == (z == 1), sent_ref[...], other_ref[...])
            else:
                sent = jnp.where((leaf == 0) == (block == 1), sent_ref[...], other_ref[...])
                value = jnp.where(z == block, own_ref[...], sent)
            high_ref[...], low_ref[...] = split(value.T)


def chain_kernel(owner, has_sums, solves, *refs):
    refs = list(refs)
    out_refs = [refs.pop()]
    if has_sums:
        out_refs.insert(0, refs.pop())
    _, row, z = place()
    given_ref = refs[0]
    if has_sums:
        value = given_ref[...] - ((refs[1][...] + refs[2][...]) + (refs[3][...] + refs[4][...]))
        out_refs[0][...] = value
        out_refs[1][...] = value
        refs = refs[5:]
    else:
        out_refs[0][...] = refs[1][...]
        refs = refs[2:]

    @pl.when((row == owner) & ((z == 1) | (z == 2)))
    def _():
        left = out_refs[0][...] if has_sums else given_ref[...]
        used = refs[2:] if solves else refs
        for i in range(0, len(used), 3):
            left = left - dot3(used[i][...], used[i + 1][...], used[i + 2][...], NN)
        if solves:
            left = left + dot3(left, refs[0][...], refs[1][...], NN)
        out_refs[-1][...] = left


def half_kernel(c_ref, a_ref, b_ref, x_ref, out_ref):
    _, _, z = place()
    x, a, b, c = x_ref[...], a_ref[...], b_ref[...], c_ref[...]
    low = jnp.where(z == 0, a, jnp.where(z == 1, x, jnp.where(z == 2, b, c)))
    high = jnp.where(z == 0, c, jnp.where(z == 1, b, jnp.where(z == 2, x, a)))
    out_ref[...] = jnp.concatenate([low, high], axis=0).T


def write_kernel(mine, part_ref, *refs):
    out_hbm, sem = refs[-2:]
    leaf, _, _ = place()
    half = part_ref.shape[1]
    at = leaf if mine else 1 - leaf
    copy = pltpu.make_async_copy(part_ref, out_hbm.at[:, pl.ds(pl.multiple_of(at * half, half), half)], sem)
    copy.start()
    copy.wait()


def call(kernel, ins, outs, scratch=(), outside=(), outs_outside=(), pinned=(), aliases=None, limit=24):
    def spec(i, a):
        return ANY if i in outside else SM if a.ndim == 1 else VM

    def shape(i, out):
        dims, dtype = out if isinstance(out[0], tuple) else (out, F32)
        return pltpu.VMEM(dims, dtype) if i in pinned else jax.ShapeDtypeStruct(dims, dtype)

    outs = pl.pallas_call(
        kernel,
        out_shape=[shape(i, out) for i, out in enumerate(outs)],
        in_specs=[spec(i, a) for i, a in enumerate(ins)],
        out_specs=[ANY if i in outs_outside else VM for i in range(len(outs))],
        scratch_shapes=[pltpu.VMEM(s, F32) if isinstance(s, tuple) else s for s in scratch],
        input_output_aliases=aliases or {},
        cost_estimate=pl.CostEstimate(flops=0, bytes_accessed=4 * sum(a.size for a in ins), transcendentals=0),
        compiler_params=pltpu.CompilerParams(vmem_limit_bytes=limit * 1024 * 1024),
    )(*ins)
    return list(outs)


def central(child_rhs, child_diag, child_off, live, targets, top_rhs, top_factor, top_diag):
    rows, cols = lax.axis_size("row"), lax.axis_size("col")
    size = top_diag.shape[1]
    right = top_rhs.shape[1]
    half, piece = right // 2, right // 4
    children, slots = targets.shape
    shape = (piece, size)
    block = ((size, size), BF16)
    dma = pltpu.SemaphoreType.DMA

    def at(r, c):
        return r * cols + c

    def swap(value):
        return lax.ppermute(value, "leaf", [(0, 1), (1, 0)])

    def hop(value, pairs):
        pairs = [(at(a, z), at(b, z)) for a, b in pairs for z in (1, 2)]
        return lax.ppermute(value, ("row", "col"), pairs)

    def along_row(value, pairs):
        return lax.ppermute(value, "row", pairs)

    def along_col(value, pairs):
        return lax.ppermute(value, "col", pairs)

    near = [(at(k, 0), at(k, 1)) for k in (1, 2, 3)] + [(at(k, 1), at(k, 2)) for k in (2, 3)]
    far = [(at(k, 0), at(k, 2)) for k in (1, 2, 3)] + [(at(3, 2), at(3, 1))]
    shift = rows * cols
    sent = lax.ppermute(
        top_factor, ("leaf", "row", "col"), near + [(a + shift, b + shift) for a, b in far]
    )
    child_sol, keep, send = call(
        child_kernel,
        [live, child_rhs, child_diag, child_off, targets],
        [child_rhs.shape, (half, children * slots), (half + 8, children * slots)],
        [child_rhs.shape, child_diag.shape, child_off.shape, child_rhs.shape, (right, children * slots),
         dma((4, children))],
        outside=(1, 2, 3),
        outs_outside=(0,),
        pinned=(1, 2),
        limit=56,
    )
    sums = call(scatter_kernel, [keep, swap(send), targets], [(half, size)] * rows)
    got = [along_row(sums[s], [(i, i ^ s) for i in range(rows)]) for s in (1, 2, 3)]
    rhs_piece, diag_high, diag_low = call(
        turn_kernel, [top_rhs, top_diag], [shape, block, block], [(half, size)]
    )
    diag = [diag_high, diag_low]
    first, second = call(pieces_kernel, [sums[0]] + got, [shape] * 2, [(half, size)])
    q = [
        along_col(second, [(0, 2), (3, 1)]),
        along_col(first, [(1, 2), (2, 1)]),
        along_col(first, [(0, 1), (3, 2)]),
    ]

    def chain(owner, ins, has_sums=False, solves=True):
        outs = call(
            functools.partial(chain_kernel, owner, has_sums, solves), ins, [shape] * (1 + has_sums)
        )
        return outs if has_sums else outs[0]

    res, x = chain(0, [rhs_piece, second] + q + diag, has_sums=True)
    sent, res = lax.optimization_barrier((sent, res))
    factor = call(factor_kernel, [top_factor, sent, swap(sent)], [block] * 6)
    factor = [factor[0:2], factor[2:4], factor[4:6]]
    to1 = hop(x, [(0, 1)])
    to2 = hop(x, [(0, 2)])
    x = chain(1, [res, x] + diag + [to1] + factor[0])
    on = hop(x, [(1, 2), (0, 3)])
    res = chain(2, [res, res, to2] + factor[0], solves=False)
    x = chain(2, [res, x] + diag + [on] + factor[1])
    to3 = hop(x, [(2, 3)])
    late = hop(x, [(1, 3)])
    res = chain(3, [res, res, on] + factor[0], solves=False)
    x = chain(3, [res, x] + diag + [to3] + factor[2] + [late] + factor[1])

    both = along_col(x, [(1, 2), (2, 1)])
    step = along_col(x, [(1, 0), (2, 3)])
    over = along_col(x, [(1, 3), (2, 0)])
    (own,) = call(half_kernel, [over, step, both, x], [(size, half)])
    (top_sol,) = call(
        functools.partial(write_kernel, True), [own], [top_rhs.shape], [dma(())], outs_outside=(0,)
    )
    (top_sol,) = call(
        functools.partial(write_kernel, False),
        [swap(own), top_sol],
        [top_rhs.shape],
        [dma(())],
        outside=(1,),
        outs_outside=(0,),
        aliases={1: 0},
    )
    return (child_sol, top_sol)


def solution(mesh):
    in_specs = (
        P(("leaf", "row", "col"), None, None),
        P(("leaf", "row", "col"), None, None),
        P(("leaf", "row", "col"), None, None),
        P(("leaf", "row", "col")),
        P(("leaf", "row", "col"), None),
        P("row", None),
        P("row", "col"),
        P("row", None),
    )
    out_specs = (P(("leaf", "row", "col"), None, None), P("row", None))
    axes = tuple(mesh.shape[a] for a in ("leaf", "row", "col"))

    def shards(*args):
        top_rhs, top_factor, top_diag = args[5:]
        size = top_diag.shape[1]
        fits = axes == (2, 4, 4) and top_rhs.shape[0] == size and top_factor.shape[1] == size
        return (central if fits else any_mesh)(*args)

    return jax.shard_map(shards, mesh=mesh, in_specs=in_specs, out_specs=out_specs, check_vma=False)
```

```python
import functools

import jax
import jax.numpy as jnp
from jax import lax
from jax.experimental import pallas as pl
from jax.experimental.pallas import tpu as pltpu
from jax.sharding import PartitionSpec as P

F32 = jnp.float32
BF16 = jnp.bfloat16
NT = (((1,), (1,)), ((), ()))
NN = (((1,), (0,)), ((), ()))
VM = pl.BlockSpec(memory_space=pltpu.VMEM)
ANY = pl.BlockSpec(memory_space=pl.ANY)
SM = pl.BlockSpec(memory_space=pltpu.SMEM)


def spread(value, axis, source):
    kept = jnp.where(lax.axis_index(axis) == source, value, 0).astype(value.dtype)
    return lax.psum(kept, axis)


def unit_lower(matrix):
    return jnp.tril(matrix) + jnp.eye(matrix.shape[-1], dtype=matrix.dtype)


def any_mesh(child_rhs, child_diag, child_off, live, targets, top_rhs, top_factor, top_diag):
    highest = lax.Precision.HIGHEST
    owned_rows = top_rhs.shape[0]
    right_count = top_rhs.shape[1]
    block_size = top_diag.shape[1]
    owned_blocks = owned_rows // block_size
    row_count = lax.axis_size("row")
    top_order = owned_rows * row_count
    col_width = top_factor.shape[1]
    my_row = lax.axis_index("row")
    my_col = lax.axis_index("col")
    child_sol = jnp.einsum("bij,bjr->bir", unit_lower(child_diag), child_rhs, precision=highest)
    tiles = jnp.einsum("btj,bjr->btr", child_off, child_sol, precision=highest)
    slot_index = jnp.arange(child_off.shape[1], dtype=jnp.int32)
    keep = slot_index[None, :] < live[:, None]
    tiles = jnp.where(keep[:, :, None], tiles, jnp.zeros_like(tiles))
    contrib = jnp.zeros((top_order, right_count), F32)
    contrib = contrib.at[targets.reshape(-1)].add(tiles.reshape(-1, right_count))
    row_part = lax.psum_scatter(contrib, "row", scatter_dimension=0, tiled=True)
    share = lax.psum_scatter(row_part, ("leaf", "col"), scatter_dimension=0, tiled=True)
    updates = lax.all_gather(share, ("leaf", "col"), axis=0, tiled=True)
    reduced = top_rhs - updates
    inverse_all = unit_lower(top_diag.reshape(owned_blocks, block_size, block_size))
    col_global = my_col * col_width + jnp.arange(col_width, dtype=jnp.int32)

    def step(block, solution):
        local = block % owned_blocks
        owner = block // owned_blocks
        factor_rows = jnp.where(
            (col_global < block * block_size)[None, :], top_factor, jnp.zeros_like(top_factor)
        )
        columns = lax.dynamic_slice_in_dim(solution, my_col * col_width, col_width, 0)
        partial_value = jnp.dot(
            factor_rows, columns, precision=highest, preferred_element_type=F32
        )
        block_inverse = lax.dynamic_index_in_dim(inverse_all, local, 0, keepdims=False)
        before = lax.psum(partial_value, "col")
        solved = jnp.dot(
            block_inverse, reduced - before, precision=highest, preferred_element_type=F32
        )
        solved = spread(solved, "row", owner)
        return lax.dynamic_update_slice_in_dim(solution, solved, block * block_size, 0)

    solution = lax.fori_loop(
        0, row_count * owned_blocks, step, jnp.zeros((top_order, right_count), F32)
    )
    top_sol = lax.dynamic_slice_in_dim(solution, my_row * owned_rows, owned_rows, 0)
    return (child_sol, top_sol)


def place():
    return tuple(lax.axis_index(a) for a in ("leaf", "row", "col"))


def split(value):
    high = value.astype(BF16)
    return high, (value - high.astype(F32)).astype(BF16)


def dot3(left, high, low, dims):
    left_high, left_low = split(left)
    rows = left.shape[0]
    both = lax.dot_general(
        jnp.concatenate([left_high, left_low], axis=0), high, dims, preferred_element_type=F32
    )
    cross = lax.dot_general(left_high, low, dims, preferred_element_type=F32)
    return both[:rows] + both[rows:] + cross


def lower(matrix):
    row = lax.broadcasted_iota(jnp.int32, matrix.shape, 0)
    col = lax.broadcasted_iota(jnp.int32, matrix.shape, 1)
    return jnp.where(col <= row, matrix, 0.0)


def turn_kernel(rhs_ref, diag_ref, out_ref, high_ref, low_ref, turned_ref):
    leaf, _, z = place()
    half, piece = turned_ref.shape[0], out_ref.shape[0]
    turned_ref[...] = rhs_ref[:, pl.ds(pl.multiple_of(leaf * half, half), half)].T
    out_ref[...] = turned_ref[pl.ds(pl.multiple_of((z // 2) * piece, piece), piece), :]
    high_ref[...], low_ref[...] = split(lower(diag_ref[...]).T)


def child_kernel(live_ref, rhs_hbm, diag_hbm, off_hbm, tgt_ref, sol_hbm, keep_ref, send_ref,
                 rhs_ref, diag_ref, off_ref, sol_ref, tiles_ref, sems):
    leaf, _, _ = place()
    children, slots = off_ref.shape[0], off_ref.shape[1]
    half = keep_ref.shape[0]
    pairs = ((rhs_hbm, rhs_ref), (diag_hbm, diag_ref), (off_hbm, off_ref))
    copies = [
        [pltpu.make_async_copy(source.at[s], target.at[s], sems.at[i, s]) for i, (source, target) in enumerate(pairs)]
        for s in range(children)
    ]
    back = [pltpu.make_async_copy(sol_ref.at[s], sol_hbm.at[s], sems.at[3, s]) for s in range(children)]
    for s in range(children):
        for copy in copies[s]:
            copy.start()
    for s in range(children):
        copies[s][0].wait()
        copies[s][1].wait()
        rhs = rhs_ref[s]
        sol = rhs + dot3(lower(diag_ref[s]), *split(rhs), NN)
        sol_ref[s] = sol
        back[s].start()
        copies[s][2].wait()
        tiles = dot3(sol.T, *split(off_ref[s]), NT)
        slot = lax.broadcasted_iota(jnp.int32, tiles.shape, 1)
        tiles_ref[:, s * slots:(s + 1) * slots] = jnp.where(slot < live_ref[s], tiles, 0.0)
        send_ref[half:half + 8, s * slots:(s + 1) * slots] = jnp.broadcast_to(
            tgt_ref[s:s + 1, :].astype(F32), (8, slots)
        )
    keep_ref[...] = tiles_ref[pl.ds(pl.multiple_of(leaf * half, half), half), :]
    send_ref[0:half, :] = tiles_ref[pl.ds(pl.multiple_of((1 - leaf) * half, half), half), :]
    for copy in back:
        copy.wait()


def scatter_kernel(keep_ref, recv_ref, tgt_ref, *out_refs):
    _, row, _ = place()
    half, slots_all = keep_ref.shape
    size = out_refs[0].shape[1]
    children, slots = tgt_ref.shape
    mine = [split(keep_ref[...]), split(recv_ref[0:half, :])]
    stacked = [jnp.concatenate(pair, axis=0) for pair in mine]
    mine_targets = jnp.concatenate([tgt_ref[s:s + 1, :] for s in range(children)], axis=1)
    target = [mine_targets, recv_ref[half:half + 1, :].astype(jnp.int32)]
    for s, out_ref in enumerate(out_refs):
        block = jnp.bitwise_xor(row, s)
        index = lax.broadcasted_iota(jnp.int32, (size, slots_all), 0) + block * size
        total = None
        for t, value in zip(target, stacked):
            hot = jnp.where(index == t, 1.0, 0.0).astype(BF16)
            product = lax.dot_general(value, hot, NT, preferred_element_type=F32)
            total = product if total is None else total + product
        out_ref[...] = total[:half] + total[half:]


def pieces_kernel(a_ref, b_ref, c_ref, d_ref, first_ref, second_ref, sum_ref):
    _, _, z = place()
    odd = z % 2
    piece = first_ref.shape[0]
    sum_ref[...] = (a_ref[...] + b_ref[...]) + (c_ref[...] + d_ref[...])
    first_ref[...] = sum_ref[pl.ds(pl.multiple_of(odd * piece, piece), piece), :]
    second_ref[...] = sum_ref[pl.ds(pl.multiple_of((1 - odd) * piece, piece), piece), :]


def factor_kernel(own_ref, sent_ref, other_ref, *out_refs):
    leaf, row, z = place()
    for block in range(3):
        high_ref, low_ref = out_refs[2 * block], out_refs[2 * block + 1]

        @pl.when((row > block) & ((z == 1) | (z == 2)))
        def _():
            if block == 0:
                value = jnp.where((leaf == 0) == (z == 1), sent_ref[...], other_ref[...])
            else:
                sent = jnp.where((leaf == 0) == (block == 1), sent_ref[...], other_ref[...])
                value = jnp.where(z == block, own_ref[...], sent)
            high_ref[...], low_ref[...] = split(value.T)


def chain_kernel(owner, has_sums, solves, *refs):
    refs = list(refs)
    out_refs = [refs.pop()]
    if has_sums:
        out_refs.insert(0, refs.pop())
    _, row, z = place()
    given_ref = refs[0]
    if has_sums:
        value = given_ref[...] - ((refs[1][...] + refs[2][...]) + (refs[3][...] + refs[4][...]))
        out_refs[0][...] = value
        out_refs[1][...] = value
        refs = refs[5:]
    else:
        out_refs[0][...] = refs[1][...]
        refs = refs[2:]

    @pl.when((row == owner) & ((z == 1) | (z == 2)))
    def _():
        left = out_refs[0][...] if has_sums else given_ref[...]
        used = refs[2:] if solves else refs
        for i in range(0, len(used), 3):
            left = left - dot3(used[i][...], used[i + 1][...], used[i + 2][...], NN)
        if solves:
            left = left + dot3(left, refs[0][...], refs[1][...], NN)
        out_refs[-1][...] = left


def half_kernel(c_ref, a_ref, b_ref, x_ref, out_ref):
    _, _, z = place()
    x, a, b, c = x_ref[...], a_ref[...], b_ref[...], c_ref[...]
    low = jnp.where(z == 0, a, jnp.where(z == 1, x, jnp.where(z == 2, b, c)))
    high = jnp.where(z == 0, c, jnp.where(z == 1, b, jnp.where(z == 2, x, a)))
    out_ref[...] = jnp.concatenate([low, high], axis=0).T


def write_kernel(mine, part_ref, *refs):
    out_hbm, sem = refs[-2:]
    leaf, _, _ = place()
    half = part_ref.shape[1]
    at = leaf if mine else 1 - leaf
    copy = pltpu.make_async_copy(part_ref, out_hbm.at[:, pl.ds(pl.multiple_of(at * half, half), half)], sem)
    copy.start()
    copy.wait()


def call(kernel, ins, outs, scratch=(), outside=(), outs_outside=(), pinned=(), aliases=None, limit=24, flops=0):
    def spec(i, a):
        return ANY if i in outside else SM if a.ndim == 1 else VM

    def shape(i, out):
        dims, dtype = out if isinstance(out[0], tuple) else (out, F32)
        return pltpu.VMEM(dims, dtype) if i in pinned else jax.ShapeDtypeStruct(dims, dtype)

    outs = pl.pallas_call(
        kernel,
        out_shape=[shape(i, out) for i, out in enumerate(outs)],
        in_specs=[spec(i, a) for i, a in enumerate(ins)],
        out_specs=[ANY if i in outs_outside else VM for i in range(len(outs))],
        scratch_shapes=[pltpu.VMEM(s, F32) if isinstance(s, tuple) else s for s in scratch],
        input_output_aliases=aliases or {},
        cost_estimate=pl.CostEstimate(flops=flops, bytes_accessed=4 * sum(a.size for a in ins), transcendentals=0),
        compiler_params=pltpu.CompilerParams(vmem_limit_bytes=limit * 1024 * 1024),
    )(*ins)
    return list(outs)


def central(child_rhs, child_diag, child_off, live, targets, top_rhs, top_factor, top_diag):
    rows, cols = lax.axis_size("row"), lax.axis_size("col")
    size = top_diag.shape[1]
    right = top_rhs.shape[1]
    half, piece = right // 2, right // 4
    children, slots = targets.shape
    shape = (piece, size)
    block = ((size, size), BF16)
    dma = pltpu.SemaphoreType.DMA

    def at(r, c):
        return r * cols + c

    def swap(value):
        return lax.ppermute(value, "leaf", [(0, 1), (1, 0)])

    def hop(value, pairs):
        pairs = [(at(a, z), at(b, z)) for a, b in pairs for z in (1, 2)]
        return lax.ppermute(value, ("row", "col"), pairs)

    def along_row(value, pairs):
        return lax.ppermute(value, "row", pairs)

    def along_col(value, pairs):
        return lax.ppermute(value, "col", pairs)

    near = [(at(k, 0), at(k, 1)) for k in (1, 2, 3)] + [(at(k, 1), at(k, 2)) for k in (2, 3)]
    far = [(at(k, 0), at(k, 2)) for k in (1, 2, 3)] + [(at(3, 2), at(3, 1))]
    shift = rows * cols
    sent = lax.ppermute(
        top_factor, ("leaf", "row", "col"), near + [(a + shift, b + shift) for a, b in far]
    )
    child_sol, keep, send = call(
        child_kernel,
        [live, child_rhs, child_diag, child_off, targets],
        [child_rhs.shape, (half, children * slots), (half + 8, children * slots)],
        [child_rhs.shape, child_diag.shape, child_off.shape, child_rhs.shape, (right, children * slots),
         dma((4, children))],
        outside=(1, 2, 3),
        outs_outside=(0,),
        pinned=(1, 2),
        limit=56,
    )
    sums = call(scatter_kernel, [keep, swap(send), targets], [(half, size)] * rows)
    got = [along_row(sums[s], [(i, i ^ s) for i in range(rows)]) for s in (1, 2, 3)]
    rhs_piece, diag_high, diag_low = call(
        turn_kernel, [top_rhs, top_diag], [shape, block, block], [(half, size)]
    )
    diag = [diag_high, diag_low]
    first, second = call(pieces_kernel, [sums[0]] + got, [shape] * 2, [(half, size)], flops=10 ** 11)
    q = [
        along_col(second, [(0, 2), (3, 1)]),
        along_col(first, [(1, 2), (2, 1)]),
        along_col(first, [(0, 1), (3, 2)]),
    ]

    def chain(owner, ins, has_sums=False, solves=True):
        outs = call(
            functools.partial(chain_kernel, owner, has_sums, solves), ins, [shape] * (1 + has_sums)
        )
        return outs if has_sums else outs[0]

    res, x = chain(0, [rhs_piece, second] + q + diag, has_sums=True)
    sent, res = lax.optimization_barrier((sent, res))
    middle = [at(k, z) for k in (1, 2, 3) for z in (1, 2)]
    other = lax.ppermute(
        sent, ("leaf", "row", "col"), [(a + b, a + shift - b) for a in middle for b in (0, shift)]
    )
    factor = call(factor_kernel, [top_factor, sent, other], [block] * 6)
    factor = [factor[0:2], factor[2:4], factor[4:6]]
    to1 = hop(x, [(0, 1)])
    to2 = hop(x, [(0, 2)])
    x = chain(1, [res, x] + diag + [to1] + factor[0])
    on = hop(x, [(1, 2), (0, 3)])
    res = chain(2, [res, res, to2] + factor[0], solves=False)
    x = chain(2, [res, x] + diag + [on] + factor[1])
    to3 = hop(x, [(2, 3)])
    late = hop(x, [(1, 3)])
    res = chain(3, [res, res, on] + factor[0], solves=False)
    x = chain(3, [res, x] + diag + [to3] + factor[2] + [late] + factor[1])

    both = along_col(x, [(1, 2), (2, 1)])
    step = along_col(x, [(1, 0), (2, 3)])
    over = along_col(x, [(1, 3), (2, 0)])
    (own,) = call(half_kernel, [over, step, both, x], [(size, half)])
    (top_sol,) = call(
        functools.partial(write_kernel, True), [own], [top_rhs.shape], [dma(())], outs_outside=(0,)
    )
    (top_sol,) = call(
        functools.partial(write_kernel, False),
        [swap(own), top_sol],
        [top_rhs.shape],
        [dma(())],
        outside=(1,),
        outs_outside=(0,),
        aliases={1: 0},
    )
    return (child_sol, top_sol)


def solution(mesh):
    in_specs = (
        P(("leaf", "row", "col"), None, None),
        P(("leaf", "row", "col"), None, None),
        P(("leaf", "row", "col"), None, None),
        P(("leaf", "row", "col")),
        P(("leaf", "row", "col"), None),
        P("row", None),
        P("row", "col"),
        P("row", None),
    )
    out_specs = (P(("leaf", "row", "col"), None, None), P("row", None))
    axes = tuple(mesh.shape[a] for a in ("leaf", "row", "col"))

    def shards(*args):
        top_rhs, top_factor, top_diag = args[5:]
        size = top_diag.shape[1]
        fits = axes == (2, 4, 4) and top_rhs.shape[0] == size and top_factor.shape[1] == size
        return (central if fits else any_mesh)(*args)

    return jax.shard_map(shards, mesh=mesh, in_specs=in_specs, out_specs=out_specs, check_vma=False)
```

```python
import functools

import jax
import jax.numpy as jnp
from jax import lax
from jax.experimental import pallas as pl
from jax.experimental.pallas import tpu as pltpu
from jax.sharding import PartitionSpec as P

F32 = jnp.float32
BF16 = jnp.bfloat16
NT = (((1,), (1,)), ((), ()))
NN = (((1,), (0,)), ((), ()))
VM = pl.BlockSpec(memory_space=pltpu.VMEM)
ANY = pl.BlockSpec(memory_space=pl.ANY)
SM = pl.BlockSpec(memory_space=pltpu.SMEM)


def spread(value, axis, source):
    kept = jnp.where(lax.axis_index(axis) == source, value, 0).astype(value.dtype)
    return lax.psum(kept, axis)


def unit_lower(matrix):
    return jnp.tril(matrix) + jnp.eye(matrix.shape[-1], dtype=matrix.dtype)


def any_mesh(child_rhs, child_diag, child_off, live, targets, top_rhs, top_factor, top_diag):
    highest = lax.Precision.HIGHEST
    owned_rows = top_rhs.shape[0]
    right_count = top_rhs.shape[1]
    block_size = top_diag.shape[1]
    owned_blocks = owned_rows // block_size
    row_count = lax.axis_size("row")
    top_order = owned_rows * row_count
    col_width = top_factor.shape[1]
    my_row = lax.axis_index("row")
    my_col = lax.axis_index("col")
    child_sol = jnp.einsum("bij,bjr->bir", unit_lower(child_diag), child_rhs, precision=highest)
    tiles = jnp.einsum("btj,bjr->btr", child_off, child_sol, precision=highest)
    slot_index = jnp.arange(child_off.shape[1], dtype=jnp.int32)
    keep = slot_index[None, :] < live[:, None]
    tiles = jnp.where(keep[:, :, None], tiles, jnp.zeros_like(tiles))
    contrib = jnp.zeros((top_order, right_count), F32)
    contrib = contrib.at[targets.reshape(-1)].add(tiles.reshape(-1, right_count))
    row_part = lax.psum_scatter(contrib, "row", scatter_dimension=0, tiled=True)
    share = lax.psum_scatter(row_part, ("leaf", "col"), scatter_dimension=0, tiled=True)
    updates = lax.all_gather(share, ("leaf", "col"), axis=0, tiled=True)
    reduced = top_rhs - updates
    inverse_all = unit_lower(top_diag.reshape(owned_blocks, block_size, block_size))
    col_global = my_col * col_width + jnp.arange(col_width, dtype=jnp.int32)

    def step(block, solution):
        local = block % owned_blocks
        owner = block // owned_blocks
        factor_rows = jnp.where(
            (col_global < block * block_size)[None, :], top_factor, jnp.zeros_like(top_factor)
        )
        columns = lax.dynamic_slice_in_dim(solution, my_col * col_width, col_width, 0)
        partial_value = jnp.dot(
            factor_rows, columns, precision=highest, preferred_element_type=F32
        )
        block_inverse = lax.dynamic_index_in_dim(inverse_all, local, 0, keepdims=False)
        before = lax.psum(partial_value, "col")
        solved = jnp.dot(
            block_inverse, reduced - before, precision=highest, preferred_element_type=F32
        )
        solved = spread(solved, "row", owner)
        return lax.dynamic_update_slice_in_dim(solution, solved, block * block_size, 0)

    solution = lax.fori_loop(
        0, row_count * owned_blocks, step, jnp.zeros((top_order, right_count), F32)
    )
    top_sol = lax.dynamic_slice_in_dim(solution, my_row * owned_rows, owned_rows, 0)
    return (child_sol, top_sol)


def place():
    return tuple(lax.axis_index(a) for a in ("leaf", "row", "col"))


def split(value):
    high = value.astype(BF16)
    return high, (value - high.astype(F32)).astype(BF16)


def dot3(left, high, low, dims):
    left_high, left_low = split(left)
    rows = left.shape[0]
    both = lax.dot_general(
        jnp.concatenate([left_high, left_low], axis=0), high, dims, preferred_element_type=F32
    )
    cross = lax.dot_general(left_high, low, dims, preferred_element_type=F32)
    return both[:rows] + both[rows:] + cross


def lower(matrix):
    row = lax.broadcasted_iota(jnp.int32, matrix.shape, 0)
    col = lax.broadcasted_iota(jnp.int32, matrix.shape, 1)
    return jnp.where(col <= row, matrix, 0.0)


def turn_kernel(rhs_ref, diag_ref, out_ref, high_ref, low_ref, turned_ref):
    leaf, _, z = place()
    half, piece = turned_ref.shape[0], out_ref.shape[0]
    turned_ref[...] = rhs_ref[:, pl.ds(pl.multiple_of(leaf * half, half), half)].T
    out_ref[...] = turned_ref[pl.ds(pl.multiple_of((z // 2) * piece, piece), piece), :]
    high_ref[...], low_ref[...] = split(lower(diag_ref[...]).T)


def child_kernel(live_ref, rhs_hbm, diag_hbm, off_hbm, tgt_ref, sol_hbm, keep_ref, send_ref,
                 rhs_ref, diag_ref, off_ref, sol_ref, tiles_ref, sems):
    leaf, _, _ = place()
    children, slots = off_ref.shape[0], off_ref.shape[1]
    half = keep_ref.shape[0]
    pairs = ((rhs_hbm, rhs_ref), (diag_hbm, diag_ref), (off_hbm, off_ref))
    copies = [
        [pltpu.make_async_copy(source.at[s], target.at[s], sems.at[i, s]) for i, (source, target) in enumerate(pairs)]
        for s in range(children)
    ]
    back = [pltpu.make_async_copy(sol_ref.at[s], sol_hbm.at[s], sems.at[3, s]) for s in range(children)]
    for s in range(children):
        for copy in copies[s]:
            copy.start()
    for s in range(children):
        copies[s][0].wait()
        copies[s][1].wait()
        rhs = rhs_ref[s]
        sol = rhs + dot3(lower(diag_ref[s]), *split(rhs), NN)
        sol_ref[s] = sol
        back[s].start()
        copies[s][2].wait()
        tiles = dot3(sol.T, *split(off_ref[s]), NT)
        slot = lax.broadcasted_iota(jnp.int32, tiles.shape, 1)
        tiles_ref[:, s * slots:(s + 1) * slots] = jnp.where(slot < live_ref[s], tiles, 0.0)
        send_ref[half:half + 8, s * slots:(s + 1) * slots] = jnp.broadcast_to(
            tgt_ref[s:s + 1, :].astype(F32), (8, slots)
        )
    keep_ref[...] = tiles_ref[pl.ds(pl.multiple_of(leaf * half, half), half), :]
    send_ref[0:half, :] = tiles_ref[pl.ds(pl.multiple_of((1 - leaf) * half, half), half), :]
    for copy in back:
        copy.wait()


def scatter(value, target, size, start):
    index = lax.broadcasted_iota(jnp.int32, (size, value.shape[1]), 0) + start
    hot = jnp.where(index == target, 1.0, 0.0).astype(BF16)
    product = lax.dot_general(value, hot, NT, preferred_element_type=F32)
    half = value.shape[0] // 2
    return product[:half] + product[half:]


def own_kernel(keep_ref, tgt_ref, *out_refs):
    _, row, _ = place()
    size = out_refs[0].shape[1]
    value = jnp.concatenate(split(keep_ref[...]), axis=0)
    target = jnp.concatenate([tgt_ref[s:s + 1, :] for s in range(tgt_ref.shape[0])], axis=1)
    for s, out_ref in enumerate(out_refs):
        out_ref[...] = scatter(value, target, size, jnp.bitwise_xor(row, s) * size)


def other_kernel(recv_ref, *refs):
    _, row, _ = place()
    own_refs, out_refs = refs[:4], refs[4:]
    half, size = out_refs[0].shape
    value = jnp.concatenate(split(recv_ref[0:half, :]), axis=0)
    target = recv_ref[half:half + 1, :].astype(jnp.int32)
    for s, (own_ref, out_ref) in enumerate(zip(own_refs, out_refs)):
        out_ref[...] = own_ref[...] + scatter(value, target, size, jnp.bitwise_xor(row, s) * size)


def pieces_kernel(a_ref, b_ref, c_ref, d_ref, first_ref, second_ref, sum_ref):
    _, _, z = place()
    odd = z % 2
    piece = first_ref.shape[0]
    sum_ref[...] = (a_ref[...] + b_ref[...]) + (c_ref[...] + d_ref[...])
    first_ref[...] = sum_ref[pl.ds(pl.multiple_of(odd * piece, piece), piece), :]
    second_ref[...] = sum_ref[pl.ds(pl.multiple_of((1 - odd) * piece, piece), piece), :]


def factor_kernel(own_ref, sent_ref, other_ref, *out_refs):
    leaf, row, z = place()
    for block in range(3):
        high_ref, low_ref = out_refs[2 * block], out_refs[2 * block + 1]

        @pl.when((row > block) & ((z == 1) | (z == 2)))
        def _():
            if block == 0:
                value = jnp.where((leaf == 0) == (z == 1), sent_ref[...], other_ref[...])
            else:
                sent = jnp.where((leaf == 0) == (block == 1), sent_ref[...], other_ref[...])
                value = jnp.where(z == block, own_ref[...], sent)
            high_ref[...], low_ref[...] = split(value.T)


def chain_kernel(owner, has_sums, solves, *refs):
    refs = list(refs)
    out_refs = [refs.pop()]
    if has_sums:
        out_refs.insert(0, refs.pop())
    _, row, z = place()
    given_ref = refs[0]
    if has_sums:
        value = given_ref[...] - ((refs[1][...] + refs[2][...]) + (refs[3][...] + refs[4][...]))
        out_refs[0][...] = value
        out_refs[1][...] = value
        refs = refs[5:]
    else:
        out_refs[0][...] = refs[1][...]
        refs = refs[2:]

    @pl.when((row == owner) & ((z == 1) | (z == 2)))
    def _():
        left = out_refs[0][...] if has_sums else given_ref[...]
        used = refs[2:] if solves else refs
        for i in range(0, len(used), 3):
            left = left - dot3(used[i][...], used[i + 1][...], used[i + 2][...], NN)
        if solves:
            left = left + dot3(left, refs[0][...], refs[1][...], NN)
        out_refs[-1][...] = left


def half_kernel(c_ref, a_ref, b_ref, x_ref, out_ref):
    _, _, z = place()
    x, a, b, c = x_ref[...], a_ref[...], b_ref[...], c_ref[...]
    low = jnp.where(z == 0, a, jnp.where(z == 1, x, jnp.where(z == 2, b, c)))
    high = jnp.where(z == 0, c, jnp.where(z == 1, b, jnp.where(z == 2, x, a)))
    out_ref[...] = jnp.concatenate([low, high], axis=0).T


def write_kernel(mine, part_ref, *refs):
    out_hbm, sem = refs[-2:]
    leaf, _, _ = place()
    half = part_ref.shape[1]
    at = leaf if mine else 1 - leaf
    copy = pltpu.make_async_copy(part_ref, out_hbm.at[:, pl.ds(pl.multiple_of(at * half, half), half)], sem)
    copy.start()
    copy.wait()


def call(kernel, ins, outs, scratch=(), outside=(), outs_outside=(), pinned=(), aliases=None, limit=24):
    def spec(i, a):
        return ANY if i in outside else SM if a.ndim == 1 else VM

    def shape(i, out):
        dims, dtype = out if isinstance(out[0], tuple) else (out, F32)
        return pltpu.VMEM(dims, dtype) if i in pinned else jax.ShapeDtypeStruct(dims, dtype)

    outs = pl.pallas_call(
        kernel,
        out_shape=[shape(i, out) for i, out in enumerate(outs)],
        in_specs=[spec(i, a) for i, a in enumerate(ins)],
        out_specs=[ANY if i in outs_outside else VM for i in range(len(outs))],
        scratch_shapes=[pltpu.VMEM(s, F32) if isinstance(s, tuple) else s for s in scratch],
        input_output_aliases=aliases or {},
        cost_estimate=pl.CostEstimate(flops=0, bytes_accessed=4 * sum(a.size for a in ins), transcendentals=0),
        compiler_params=pltpu.CompilerParams(vmem_limit_bytes=limit * 1024 * 1024),
    )(*ins)
    return list(outs)


def central(child_rhs, child_diag, child_off, live, targets, top_rhs, top_factor, top_diag):
    rows, cols = lax.axis_size("row"), lax.axis_size("col")
    size = top_diag.shape[1]
    right = top_rhs.shape[1]
    half, piece = right // 2, right // 4
    children, slots = targets.shape
    shape = (piece, size)
    block = ((size, size), BF16)
    dma = pltpu.SemaphoreType.DMA

    def at(r, c):
        return r * cols + c

    def swap(value):
        return lax.ppermute(value, "leaf", [(0, 1), (1, 0)])

    def hop(value, pairs):
        pairs = [(at(a, z), at(b, z)) for a, b in pairs for z in (1, 2)]
        return lax.ppermute(value, ("row", "col"), pairs)

    def along_row(value, pairs):
        return lax.ppermute(value, "row", pairs)

    def along_col(value, pairs):
        return lax.ppermute(value, "col", pairs)

    near = [(at(k, 0), at(k, 1)) for k in (1, 2, 3)] + [(at(k, 1), at(k, 2)) for k in (2, 3)]
    far = [(at(k, 0), at(k, 2)) for k in (1, 2, 3)] + [(at(3, 2), at(3, 1))]
    shift = rows * cols
    sent = lax.ppermute(
        top_factor, ("leaf", "row", "col"), near + [(a + shift, b + shift) for a, b in far]
    )
    child_sol, keep, send = call(
        child_kernel,
        [live, child_rhs, child_diag, child_off, targets],
        [child_rhs.shape, (half, children * slots), (half + 8, children * slots)],
        [child_rhs.shape, child_diag.shape, child_off.shape, child_rhs.shape, (right, children * slots),
         dma((4, children))],
        outside=(1, 2, 3),
        outs_outside=(0,),
        pinned=(1, 2),
        limit=56,
    )
    sums = call(own_kernel, [keep, targets], [(half, size)] * rows)
    sums = call(other_kernel, [swap(send)] + sums, [(half, size)] * rows)
    got = [along_row(sums[s], [(i, i ^ s) for i in range(rows)]) for s in (1, 2, 3)]
    rhs_piece, diag_high, diag_low = call(
        turn_kernel, [top_rhs, top_diag], [shape, block, block], [(half, size)]
    )
    diag = [diag_high, diag_low]
    first, second = call(pieces_kernel, [sums[0]] + got, [shape] * 2, [(half, size)])
    q = [
        along_col(second, [(0, 2), (3, 1)]),
        along_col(first, [(0, 1), (3, 2)]),
        along_col(first, [(1, 2), (2, 1)]),
    ]

    def chain(owner, ins, has_sums=False, solves=True):
        outs = call(
            functools.partial(chain_kernel, owner, has_sums, solves), ins, [shape] * (1 + has_sums)
        )
        return outs if has_sums else outs[0]

    res, x = chain(0, [rhs_piece, second] + q + diag, has_sums=True)
    sent, res = lax.optimization_barrier((sent, res))
    middle = [at(k, z) for k in (1, 2, 3) for z in (1, 2)]
    other = lax.ppermute(
        sent, ("leaf", "row", "col"), [(a + b, a + shift - b) for a in middle for b in (0, shift)]
    )
    factor = call(factor_kernel, [top_factor, sent, other], [block] * 6)
    factor = [factor[0:2], factor[2:4], factor[4:6]]
    to1 = hop(x, [(0, 1)])
    to2 = hop(x, [(0, 2)])
    x = chain(1, [res, x] + diag + [to1] + factor[0])
    on = hop(x, [(1, 2), (0, 3)])
    res = chain(2, [res, res, to2] + factor[0], solves=False)
    x = chain(2, [res, x] + diag + [on] + factor[1])
    to3 = hop(x, [(2, 3)])
    late = hop(x, [(1, 3)])
    res = chain(3, [res, res, on] + factor[0], solves=False)
    x = chain(3, [res, x] + diag + [to3] + factor[2] + [late] + factor[1])

    both = along_col(x, [(1, 2), (2, 1)])
    step = along_col(x, [(1, 0), (2, 3)])
    over = along_col(x, [(1, 3), (2, 0)])
    (own,) = call(half_kernel, [over, step, both, x], [(size, half)])
    (top_sol,) = call(
        functools.partial(write_kernel, True), [own], [top_rhs.shape], [dma(())], outs_outside=(0,)
    )
    (top_sol,) = call(
        functools.partial(write_kernel, False),
        [swap(own), top_sol],
        [top_rhs.shape],
        [dma(())],
        outside=(1,),
        outs_outside=(0,),
        aliases={1: 0},
    )
    return (child_sol, top_sol)


def solution(mesh):
    in_specs = (
        P(("leaf", "row", "col"), None, None),
        P(("leaf", "row", "col"), None, None),
        P(("leaf", "row", "col"), None, None),
        P(("leaf", "row", "col")),
        P(("leaf", "row", "col"), None),
        P("row", None),
        P("row", "col"),
        P("row", None),
    )
    out_specs = (P(("leaf", "row", "col"), None, None), P("row", None))
    axes = tuple(mesh.shape[a] for a in ("leaf", "row", "col"))

    def shards(*args):
        top_rhs, top_factor, top_diag = args[5:]
        size = top_diag.shape[1]
        fits = axes == (2, 4, 4) and top_rhs.shape[0] == size and top_factor.shape[1] == size
        return (central if fits else any_mesh)(*args)

    return jax.shard_map(shards, mesh=mesh, in_specs=in_specs, out_specs=out_specs, check_vma=False)
```

```python
import functools

import jax
import jax.numpy as jnp
from jax import lax
from jax.experimental import pallas as pl
from jax.experimental.pallas import tpu as pltpu
from jax.sharding import PartitionSpec as P

F32 = jnp.float32
BF16 = jnp.bfloat16
NT = (((1,), (1,)), ((), ()))
NN = (((1,), (0,)), ((), ()))
VM = pl.BlockSpec(memory_space=pltpu.VMEM)
ANY = pl.BlockSpec(memory_space=pl.ANY)
SM = pl.BlockSpec(memory_space=pltpu.SMEM)


def spread(value, axis, source):
    kept = jnp.where(lax.axis_index(axis) == source, value, 0).astype(value.dtype)
    return lax.psum(kept, axis)


def unit_lower(matrix):
    return jnp.tril(matrix) + jnp.eye(matrix.shape[-1], dtype=matrix.dtype)


def any_mesh(child_rhs, child_diag, child_off, live, targets, top_rhs, top_factor, top_diag):
    highest = lax.Precision.HIGHEST
    owned_rows = top_rhs.shape[0]
    right_count = top_rhs.shape[1]
    block_size = top_diag.shape[1]
    owned_blocks = owned_rows // block_size
    row_count = lax.axis_size("row")
    top_order = owned_rows * row_count
    col_width = top_factor.shape[1]
    my_row = lax.axis_index("row")
    my_col = lax.axis_index("col")
    child_sol = jnp.einsum("bij,bjr->bir", unit_lower(child_diag), child_rhs, precision=highest)
    tiles = jnp.einsum("btj,bjr->btr", child_off, child_sol, precision=highest)
    slot_index = jnp.arange(child_off.shape[1], dtype=jnp.int32)
    keep = slot_index[None, :] < live[:, None]
    tiles = jnp.where(keep[:, :, None], tiles, jnp.zeros_like(tiles))
    contrib = jnp.zeros((top_order, right_count), F32)
    contrib = contrib.at[targets.reshape(-1)].add(tiles.reshape(-1, right_count))
    row_part = lax.psum_scatter(contrib, "row", scatter_dimension=0, tiled=True)
    share = lax.psum_scatter(row_part, ("leaf", "col"), scatter_dimension=0, tiled=True)
    updates = lax.all_gather(share, ("leaf", "col"), axis=0, tiled=True)
    reduced = top_rhs - updates
    inverse_all = unit_lower(top_diag.reshape(owned_blocks, block_size, block_size))
    col_global = my_col * col_width + jnp.arange(col_width, dtype=jnp.int32)

    def step(block, solution):
        local = block % owned_blocks
        owner = block // owned_blocks
        factor_rows = jnp.where(
            (col_global < block * block_size)[None, :], top_factor, jnp.zeros_like(top_factor)
        )
        columns = lax.dynamic_slice_in_dim(solution, my_col * col_width, col_width, 0)
        partial_value = jnp.dot(
            factor_rows, columns, precision=highest, preferred_element_type=F32
        )
        block_inverse = lax.dynamic_index_in_dim(inverse_all, local, 0, keepdims=False)
        before = lax.psum(partial_value, "col")
        solved = jnp.dot(
            block_inverse, reduced - before, precision=highest, preferred_element_type=F32
        )
        solved = spread(solved, "row", owner)
        return lax.dynamic_update_slice_in_dim(solution, solved, block * block_size, 0)

    solution = lax.fori_loop(
        0, row_count * owned_blocks, step, jnp.zeros((top_order, right_count), F32)
    )
    top_sol = lax.dynamic_slice_in_dim(solution, my_row * owned_rows, owned_rows, 0)
    return (child_sol, top_sol)


def place():
    return tuple(lax.axis_index(a) for a in ("leaf", "row", "col"))


def split(value):
    high = value.astype(BF16)
    return high, (value - high.astype(F32)).astype(BF16)


def dot3(left, high, low, dims):
    left_high, left_low = split(left)
    rows = left.shape[0]
    both = lax.dot_general(
        jnp.concatenate([left_high, left_low], axis=0), high, dims, preferred_element_type=F32
    )
    cross = lax.dot_general(left_high, low, dims, preferred_element_type=F32)
    return both[:rows] + both[rows:] + cross


def lower(matrix):
    row = lax.broadcasted_iota(jnp.int32, matrix.shape, 0)
    col = lax.broadcasted_iota(jnp.int32, matrix.shape, 1)
    return jnp.where(col <= row, matrix, 0.0)


def turn_kernel(rhs_ref, diag_ref, out_ref, high_ref, low_ref, turned_ref):
    leaf, _, z = place()
    half, piece = turned_ref.shape[0], out_ref.shape[0]
    turned_ref[...] = rhs_ref[:, pl.ds(pl.multiple_of(leaf * half, half), half)].T
    out_ref[...] = turned_ref[pl.ds(pl.multiple_of((z // 2) * piece, piece), piece), :]
    high_ref[...], low_ref[...] = split(lower(diag_ref[...]).T)


def child_kernel(live_ref, rhs_hbm, diag_hbm, off_hbm, tgt_ref, sol_hbm, keep_ref, send_ref,
                 rhs_ref, diag_ref, off_ref, sol_ref, tiles_ref, sems):
    leaf, _, _ = place()
    children, slots = off_ref.shape[0], off_ref.shape[1]
    half = keep_ref.shape[0]
    pairs = ((rhs_hbm, rhs_ref), (diag_hbm, diag_ref), (off_hbm, off_ref))
    copies = [
        [pltpu.make_async_copy(source.at[s], target.at[s], sems.at[i, s]) for i, (source, target) in enumerate(pairs)]
        for s in range(children)
    ]
    back = [pltpu.make_async_copy(sol_ref.at[s], sol_hbm.at[s], sems.at[3, s]) for s in range(children)]
    for s in range(children):
        for copy in copies[s]:
            copy.start()
    for s in range(children):
        copies[s][0].wait()
        copies[s][1].wait()
        rhs = rhs_ref[s]
        sol = rhs + dot3(lower(diag_ref[s]), *split(rhs), NN)
        sol_ref[s] = sol
        back[s].start()
        copies[s][2].wait()
        tiles = dot3(sol.T, *split(off_ref[s]), NT)
        slot = lax.broadcasted_iota(jnp.int32, tiles.shape, 1)
        tiles_ref[:, s * slots:(s + 1) * slots] = jnp.where(slot < live_ref[s], tiles, 0.0)
        send_ref[half:half + 8, s * slots:(s + 1) * slots] = jnp.broadcast_to(
            tgt_ref[s:s + 1, :].astype(F32), (8, slots)
        )
    keep_ref[...] = tiles_ref[pl.ds(pl.multiple_of(leaf * half, half), half), :]
    send_ref[0:half, :] = tiles_ref[pl.ds(pl.multiple_of((1 - leaf) * half, half), half), :]
    for copy in back:
        copy.wait()


def scatter(value, target, size, start):
    index = lax.broadcasted_iota(jnp.int32, (size, value.shape[1]), 0) + start
    hot = jnp.where(index == target, 1.0, 0.0).astype(BF16)
    product = lax.dot_general(value, hot, NT, preferred_element_type=F32)
    half = value.shape[0] // 2
    return product[:half] + product[half:]


def own_kernel(keep_ref, tgt_ref, *out_refs):
    _, row, _ = place()
    size = out_refs[0].shape[1]
    value = jnp.concatenate(split(keep_ref[...]), axis=0)
    target = jnp.concatenate([tgt_ref[s:s + 1, :] for s in range(tgt_ref.shape[0])], axis=1)
    for s, out_ref in enumerate(out_refs):
        out_ref[...] = scatter(value, target, size, jnp.bitwise_xor(row, s) * size)


def other_kernel(recv_ref, *refs):
    _, row, _ = place()
    own_refs, out_refs = refs[:4], refs[4:]
    half, size = out_refs[0].shape
    value = jnp.concatenate(split(recv_ref[0:half, :]), axis=0)
    target = recv_ref[half:half + 1, :].astype(jnp.int32)
    for s, (own_ref, out_ref) in enumerate(zip(own_refs, out_refs)):
        out_ref[...] = own_ref[...] + scatter(value, target, size, jnp.bitwise_xor(row, s) * size)


def pieces_kernel(a_ref, b_ref, c_ref, d_ref, first_ref, second_ref, sum_ref):
    _, _, z = place()
    odd = z % 2
    piece = first_ref.shape[0]
    sum_ref[...] = (a_ref[...] + b_ref[...]) + (c_ref[...] + d_ref[...])
    first_ref[...] = sum_ref[pl.ds(pl.multiple_of(odd * piece, piece), piece), :]
    second_ref[...] = sum_ref[pl.ds(pl.multiple_of((1 - odd) * piece, piece), piece), :]


def factor_kernel(own_ref, sent_ref, other_ref, *out_refs):
    leaf, row, z = place()
    for block in range(3):
        high_ref, low_ref = out_refs[2 * block], out_refs[2 * block + 1]

        @pl.when((row > block) & ((z == 1) | (z == 2)))
        def _():
            if block == 0:
                value = jnp.where((leaf == 0) == (z == 1), sent_ref[...], other_ref[...])
            else:
                sent = jnp.where((leaf == 0) == (block == 1), sent_ref[...], other_ref[...])
                value = jnp.where(z == block, own_ref[...], sent)
            high_ref[...], low_ref[...] = split(value.T)


def chain_kernel(owner, has_sums, solves, *refs):
    refs = list(refs)
    out_refs = [refs.pop()]
    if has_sums:
        out_refs.insert(0, refs.pop())
    _, row, z = place()
    given_ref = refs[0]
    if has_sums:
        value = given_ref[...] - ((refs[1][...] + refs[2][...]) + (refs[3][...] + refs[4][...]))
        out_refs[0][...] = value
        out_refs[1][...] = value
        refs = refs[5:]
    else:
        out_refs[0][...] = refs[1][...]
        refs = refs[2:]

    @pl.when((row == owner) & ((z == 1) | (z == 2)))
    def _():
        left = out_refs[0][...] if has_sums else given_ref[...]
        used = refs[2:] if solves else refs
        for i in range(0, len(used), 3):
            left = left - dot3(used[i][...], used[i + 1][...], used[i + 2][...], NN)
        if solves:
            left = left + dot3(left, refs[0][...], refs[1][...], NN)
        out_refs[-1][...] = left


def half_kernel(c_ref, a_ref, b_ref, x_ref, out_ref):
    _, _, z = place()
    x, a, b, c = x_ref[...], a_ref[...], b_ref[...], c_ref[...]
    low = jnp.where(z == 0, a, jnp.where(z == 1, x, jnp.where(z == 2, b, c)))
    high = jnp.where(z == 0, c, jnp.where(z == 1, b, jnp.where(z == 2, x, a)))
    out_ref[...] = jnp.concatenate([low, high], axis=0).T


def write_kernel(mine, part_ref, *refs):
    out_hbm, sem = refs[-2:]
    leaf, _, _ = place()
    half = part_ref.shape[1]
    at = leaf if mine else 1 - leaf
    copy = pltpu.make_async_copy(part_ref, out_hbm.at[:, pl.ds(pl.multiple_of(at * half, half), half)], sem)
    copy.start()
    copy.wait()


def call(kernel, ins, outs, scratch=(), outside=(), outs_outside=(), pinned=(), aliases=None, limit=24):
    def spec(i, a):
        return ANY if i in outside else SM if a.ndim == 1 else VM

    def shape(i, out):
        dims, dtype = out if isinstance(out[0], tuple) else (out, F32)
        return pltpu.VMEM(dims, dtype) if i in pinned else jax.ShapeDtypeStruct(dims, dtype)

    outs = pl.pallas_call(
        kernel,
        out_shape=[shape(i, out) for i, out in enumerate(outs)],
        in_specs=[spec(i, a) for i, a in enumerate(ins)],
        out_specs=[ANY if i in outs_outside else VM for i in range(len(outs))],
        scratch_shapes=[pltpu.VMEM(s, F32) if isinstance(s, tuple) else s for s in scratch],
        input_output_aliases=aliases or {},
        cost_estimate=pl.CostEstimate(flops=0, bytes_accessed=4 * sum(a.size for a in ins), transcendentals=0),
        compiler_params=pltpu.CompilerParams(vmem_limit_bytes=limit * 1024 * 1024),
    )(*ins)
    return list(outs)


def central(child_rhs, child_diag, child_off, live, targets, top_rhs, top_factor, top_diag):
    rows, cols = lax.axis_size("row"), lax.axis_size("col")
    size = top_diag.shape[1]
    right = top_rhs.shape[1]
    half, piece = right // 2, right // 4
    children, slots = targets.shape
    shape = (piece, size)
    block = ((size, size), BF16)
    dma = pltpu.SemaphoreType.DMA

    def at(r, c):
        return r * cols + c

    def swap(value):
        return lax.ppermute(value, "leaf", [(0, 1), (1, 0)])

    def along_row(value, step):
        return lax.ppermute(value, "row", [(r, r ^ step) for r in range(rows)])

    def along_col(value, pairs):
        rest = [a for a in range(cols) if a not in [p[0] for p in pairs]]
        open_ends = [b for b in range(cols) if b not in [p[1] for p in pairs]]
        return lax.ppermute(value, "col", pairs + list(zip(rest, open_ends)))

    near = [(at(k, 0), at(k, 1)) for k in (1, 2, 3)] + [(at(k, 1), at(k, 2)) for k in (2, 3)]
    far = [(at(k, 0), at(k, 2)) for k in (1, 2, 3)] + [(at(3, 2), at(3, 1))]
    shift = rows * cols
    pairs = near + [(a + shift, b + shift) for a, b in far]
    for k in range(2 * rows):
        here = range(k * cols, (k + 1) * cols)
        rest = [a for a in here if a not in [p[0] for p in pairs]]
        open_ends = [b for b in here if b not in [p[1] for p in pairs]]
        stay = [a for a in rest if a in open_ends]
        pairs = pairs + [(a, a) for a in stay]
        pairs = pairs + list(zip([a for a in rest if a not in stay], [b for b in open_ends if b not in stay]))
    sent = lax.ppermute(top_factor, ("leaf", "row", "col"), pairs)
    child_sol, keep, send = call(
        child_kernel,
        [live, child_rhs, child_diag, child_off, targets],
        [child_rhs.shape, (half, children * slots), (half + 8, children * slots)],
        [child_rhs.shape, child_diag.shape, child_off.shape, child_rhs.shape, (right, children * slots),
         dma((4, children))],
        outside=(1, 2, 3),
        outs_outside=(0,),
        pinned=(1, 2),
        limit=56,
    )
    sums = call(own_kernel, [keep, targets], [(half, size)] * rows)
    sums = call(other_kernel, [swap(send)] + sums, [(half, size)] * rows)
    got = [along_row(sums[s], s) for s in (1, 2, 3)]
    rhs_piece, diag_high, diag_low = call(
        turn_kernel, [top_rhs, top_diag], [shape, block, block], [(half, size)]
    )
    diag = [diag_high, diag_low]
    first, second = call(pieces_kernel, [sums[0]] + got, [shape] * 2, [(half, size)])
    q = [
        along_col(second, [(0, 2), (3, 1)]),
        along_col(first, [(1, 2), (2, 1)]),
        along_col(first, [(0, 1), (3, 2)]),
    ]

    def chain(owner, ins, has_sums=False, solves=True):
        outs = call(
            functools.partial(chain_kernel, owner, has_sums, solves), ins, [shape] * (1 + has_sums)
        )
        return outs if has_sums else outs[0]

    res, x = chain(0, [rhs_piece, second] + q + diag, has_sums=True)
    sent, res = lax.optimization_barrier((sent, res))
    factor = call(factor_kernel, [top_factor, sent, swap(sent)], [block] * 6)
    factor = [factor[0:2], factor[2:4], factor[4:6]]
    to1 = along_row(x, 1)
    to2 = along_row(x, 2)
    x = chain(1, [res, x] + diag + [to1] + factor[0])
    on = along_row(x, 3)
    res = chain(2, [res, res, to2] + factor[0], solves=False)
    x = chain(2, [res, x] + diag + [on] + factor[1])
    to3 = along_row(x, 1)
    late = along_row(x, 2)
    res = chain(3, [res, res, on] + factor[0], solves=False)
    x = chain(3, [res, x] + diag + [to3] + factor[2] + [late] + factor[1])

    both = along_col(x, [(1, 2), (2, 1)])
    step = along_col(x, [(1, 0), (2, 3)])
    over = along_col(x, [(1, 3), (2, 0)])
    (own,) = call(half_kernel, [over, step, both, x], [(size, half)])
    (top_sol,) = call(
        functools.partial(write_kernel, True), [own], [top_rhs.shape], [dma(())], outs_outside=(0,)
    )
    (top_sol,) = call(
        functools.partial(write_kernel, False),
        [swap(own), top_sol],
        [top_rhs.shape],
        [dma(())],
        outside=(1,),
        outs_outside=(0,),
        aliases={1: 0},
    )
    return (child_sol, top_sol)


def solution(mesh):
    in_specs = (
        P(("leaf", "row", "col"), None, None),
        P(("leaf", "row", "col"), None, None),
        P(("leaf", "row", "col"), None, None),
        P(("leaf", "row", "col")),
        P(("leaf", "row", "col"), None),
        P("row", None),
        P("row", "col"),
        P("row", None),
    )
    out_specs = (P(("leaf", "row", "col"), None, None), P("row", None))
    axes = tuple(mesh.shape[a] for a in ("leaf", "row", "col"))

    def shards(*args):
        top_rhs, top_factor, top_diag = args[5:]
        size = top_diag.shape[1]
        fits = axes == (2, 4, 4) and top_rhs.shape[0] == size and top_factor.shape[1] == size
        return (central if fits else any_mesh)(*args)

    return jax.shard_map(shards, mesh=mesh, in_specs=in_specs, out_specs=out_specs, check_vma=False)
```

```python
import functools

import jax
import jax.numpy as jnp
from jax import lax
from jax.experimental import pallas as pl
from jax.experimental.pallas import tpu as pltpu
from jax.sharding import PartitionSpec as P

F32 = jnp.float32
BF16 = jnp.bfloat16
NT = (((1,), (1,)), ((), ()))
NN = (((1,), (0,)), ((), ()))
VM = pl.BlockSpec(memory_space=pltpu.VMEM)
ANY = pl.BlockSpec(memory_space=pl.ANY)
SM = pl.BlockSpec(memory_space=pltpu.SMEM)


def spread(value, axis, source):
    kept = jnp.where(lax.axis_index(axis) == source, value, 0).astype(value.dtype)
    return lax.psum(kept, axis)


def unit_lower(matrix):
    return jnp.tril(matrix) + jnp.eye(matrix.shape[-1], dtype=matrix.dtype)


def any_mesh(child_rhs, child_diag, child_off, live, targets, top_rhs, top_factor, top_diag):
    highest = lax.Precision.HIGHEST
    owned_rows = top_rhs.shape[0]
    right_count = top_rhs.shape[1]
    block_size = top_diag.shape[1]
    owned_blocks = owned_rows // block_size
    row_count = lax.axis_size("row")
    top_order = owned_rows * row_count
    col_width = top_factor.shape[1]
    my_row = lax.axis_index("row")
    my_col = lax.axis_index("col")
    child_sol = jnp.einsum("bij,bjr->bir", unit_lower(child_diag), child_rhs, precision=highest)
    tiles = jnp.einsum("btj,bjr->btr", child_off, child_sol, precision=highest)
    slot_index = jnp.arange(child_off.shape[1], dtype=jnp.int32)
    keep = slot_index[None, :] < live[:, None]
    tiles = jnp.where(keep[:, :, None], tiles, jnp.zeros_like(tiles))
    contrib = jnp.zeros((top_order, right_count), F32)
    contrib = contrib.at[targets.reshape(-1)].add(tiles.reshape(-1, right_count))
    row_part = lax.psum_scatter(contrib, "row", scatter_dimension=0, tiled=True)
    share = lax.psum_scatter(row_part, ("leaf", "col"), scatter_dimension=0, tiled=True)
    updates = lax.all_gather(share, ("leaf", "col"), axis=0, tiled=True)
    reduced = top_rhs - updates
    inverse_all = unit_lower(top_diag.reshape(owned_blocks, block_size, block_size))
    col_global = my_col * col_width + jnp.arange(col_width, dtype=jnp.int32)

    def step(block, solution):
        local = block % owned_blocks
        owner = block // owned_blocks
        factor_rows = jnp.where(
            (col_global < block * block_size)[None, :], top_factor, jnp.zeros_like(top_factor)
        )
        columns = lax.dynamic_slice_in_dim(solution, my_col * col_width, col_width, 0)
        partial_value = jnp.dot(
            factor_rows, columns, precision=highest, preferred_element_type=F32
        )
        block_inverse = lax.dynamic_index_in_dim(inverse_all, local, 0, keepdims=False)
        before = lax.psum(partial_value, "col")
        solved = jnp.dot(
            block_inverse, reduced - before, precision=highest, preferred_element_type=F32
        )
        solved = spread(solved, "row", owner)
        return lax.dynamic_update_slice_in_dim(solution, solved, block * block_size, 0)

    solution = lax.fori_loop(
        0, row_count * owned_blocks, step, jnp.zeros((top_order, right_count), F32)
    )
    top_sol = lax.dynamic_slice_in_dim(solution, my_row * owned_rows, owned_rows, 0)
    return (child_sol, top_sol)


def place():
    return tuple(lax.axis_index(a) for a in ("leaf", "row", "col"))


def split(value):
    high = value.astype(BF16)
    return high, (value - high.astype(F32)).astype(BF16)


def dot3(left, high, low, dims):
    left_high, left_low = split(left)
    rows = left.shape[0]
    both = lax.dot_general(
        jnp.concatenate([left_high, left_low], axis=0), high, dims, preferred_element_type=F32
    )
    cross = lax.dot_general(left_high, low, dims, preferred_element_type=F32)
    return both[:rows] + both[rows:] + cross


def lower(matrix):
    row = lax.broadcasted_iota(jnp.int32, matrix.shape, 0)
    col = lax.broadcasted_iota(jnp.int32, matrix.shape, 1)
    return jnp.where(col <= row, matrix, 0.0)


def turn_kernel(rhs_ref, diag_ref, out_ref, high_ref, low_ref, turned_ref):
    leaf, _, z = place()
    half, piece = turned_ref.shape[0], out_ref.shape[0]
    turned_ref[...] = rhs_ref[:, pl.ds(pl.multiple_of(leaf * half, half), half)].T
    out_ref[...] = turned_ref[pl.ds(pl.multiple_of((z // 2) * piece, piece), piece), :]
    high_ref[...], low_ref[...] = split(lower(diag_ref[...]).T)


def child_kernel(live_ref, rhs_hbm, diag_hbm, off_hbm, tgt_ref, sol_hbm, keep_ref, send_ref,
                 rhs_ref, diag_ref, off_ref, sol_ref, tiles_ref, sems):
    leaf, _, _ = place()
    children, slots = off_ref.shape[0], off_ref.shape[1]
    half = keep_ref.shape[0]
    pairs = ((rhs_hbm, rhs_ref), (diag_hbm, diag_ref), (off_hbm, off_ref))
    copies = [
        [pltpu.make_async_copy(source.at[s], target.at[s], sems.at[i, s]) for i, (source, target) in enumerate(pairs)]
        for s in range(children)
    ]
    back = [pltpu.make_async_copy(sol_ref.at[s], sol_hbm.at[s], sems.at[3, s]) for s in range(children)]
    for s in range(children):
        for copy in copies[s]:
            copy.start()
    for s in range(children):
        copies[s][0].wait()
        copies[s][1].wait()
        rhs = rhs_ref[s]
        sol = rhs + dot3(lower(diag_ref[s]), *split(rhs), NN)
        sol_ref[s] = sol
        back[s].start()
        copies[s][2].wait()
        tiles = dot3(sol.T, *split(off_ref[s]), NT)
        slot = lax.broadcasted_iota(jnp.int32, tiles.shape, 1)
        tiles_ref[:, s * slots:(s + 1) * slots] = jnp.where(slot < live_ref[s], tiles, 0.0)
        send_ref[half:half + 8, s * slots:(s + 1) * slots] = jnp.broadcast_to(
            tgt_ref[s:s + 1, :].astype(F32), (8, slots)
        )
    keep_ref[...] = tiles_ref[pl.ds(pl.multiple_of(leaf * half, half), half), :]
    send_ref[0:half, :] = tiles_ref[pl.ds(pl.multiple_of((1 - leaf) * half, half), half), :]
    for copy in back:
        copy.wait()


def scatter(value, target, size, start):
    index = lax.broadcasted_iota(jnp.int32, (size, value.shape[1]), 0) + start
    hot = jnp.where(index == target, 1.0, 0.0).astype(BF16)
    product = lax.dot_general(value, hot, NT, preferred_element_type=F32)
    half = value.shape[0] // 2
    return product[:half] + product[half:]


def own_kernel(keep_ref, send_ref, *out_refs):
    _, row, _ = place()
    half, size = out_refs[0].shape
    value = jnp.concatenate(split(keep_ref[...]), axis=0)
    target = send_ref[half:half + 1, :].astype(jnp.int32)
    for s, out_ref in enumerate(out_refs):
        out_ref[...] = scatter(value, target, size, jnp.bitwise_xor(row, s) * size)


def other_kernel(recv_ref, *refs):
    _, row, _ = place()
    own_refs, out_refs = refs[:4], refs[4:]
    half, size = out_refs[0].shape
    value = jnp.concatenate(split(recv_ref[0:half, :]), axis=0)
    target = recv_ref[half:half + 1, :].astype(jnp.int32)
    for s, (own_ref, out_ref) in enumerate(zip(own_refs, out_refs)):
        out_ref[...] = own_ref[...] + scatter(value, target, size, jnp.bitwise_xor(row, s) * size)


def pieces_kernel(a_ref, b_ref, c_ref, d_ref, first_ref, second_ref, sum_ref):
    _, _, z = place()
    odd = z % 2
    piece = first_ref.shape[0]
    sum_ref[...] = (a_ref[...] + b_ref[...]) + (c_ref[...] + d_ref[...])
    first_ref[...] = sum_ref[pl.ds(pl.multiple_of(odd * piece, piece), piece), :]
    second_ref[...] = sum_ref[pl.ds(pl.multiple_of((1 - odd) * piece, piece), piece), :]


def factor_kernel(own_ref, sent_ref, other_ref, *out_refs):
    leaf, row, z = place()
    for block in range(3):
        high_ref, low_ref = out_refs[2 * block], out_refs[2 * block + 1]

        @pl.when((row > block) & ((z == 1) | (z == 2)))
        def _():
            if block == 0:
                value = jnp.where((leaf == 0) == (z == 1), sent_ref[...], other_ref[...])
            else:
                sent = jnp.where((leaf == 0) == (block == 1), sent_ref[...], other_ref[...])
                value = jnp.where(z == block, own_ref[...], sent)
            high_ref[...], low_ref[...] = split(value.T)


def chain_kernel(owner, has_sums, solves, *refs):
    refs = list(refs)
    out_refs = [refs.pop()]
    if has_sums:
        out_refs.insert(0, refs.pop())
    _, row, z = place()
    given_ref = refs[0]
    if has_sums:
        value = given_ref[...] - ((refs[1][...] + refs[2][...]) + (refs[3][...] + refs[4][...]))
        out_refs[0][...] = value
        out_refs[1][...] = value
        refs = refs[5:]
    else:
        out_refs[0][...] = refs[1][...]
        refs = refs[2:]

    @pl.when((row == owner) & ((z == 1) | (z == 2)))
    def _():
        left = out_refs[0][...] if has_sums else given_ref[...]
        used = refs[2:] if solves else refs
        for i in range(0, len(used), 3):
            left = left - dot3(used[i][...], used[i + 1][...], used[i + 2][...], NN)
        if solves:
            left = left + dot3(left, refs[0][...], refs[1][...], NN)
        out_refs[-1][...] = left


def half_kernel(c_ref, a_ref, b_ref, x_ref, out_ref):
    _, _, z = place()
    x, a, b, c = x_ref[...], a_ref[...], b_ref[...], c_ref[...]
    low = jnp.where(z == 0, a, jnp.where(z == 1, x, jnp.where(z == 2, b, c)))
    high = jnp.where(z == 0, c, jnp.where(z == 1, b, jnp.where(z == 2, x, a)))
    out_ref[...] = jnp.concatenate([low, high], axis=0).T


def write_kernel(mine, part_ref, *refs):
    out_hbm, sem = refs[-2:]
    leaf, _, _ = place()
    half = part_ref.shape[1]
    at = leaf if mine else 1 - leaf
    copy = pltpu.make_async_copy(part_ref, out_hbm.at[:, pl.ds(pl.multiple_of(at * half, half), half)], sem)
    copy.start()
    copy.wait()


def call(kernel, ins, outs, scratch=(), outside=(), outs_outside=(), pinned=(), aliases=None, limit=24, flops=0):
    def spec(i, a):
        return ANY if i in outside else SM if a.ndim == 1 else VM

    def shape(i, out):
        dims, dtype = out if isinstance(out[0], tuple) else (out, F32)
        return pltpu.VMEM(dims, dtype) if i in pinned else jax.ShapeDtypeStruct(dims, dtype)

    outs = pl.pallas_call(
        kernel,
        out_shape=[shape(i, out) for i, out in enumerate(outs)],
        in_specs=[spec(i, a) for i, a in enumerate(ins)],
        out_specs=[ANY if i in outs_outside else VM for i in range(len(outs))],
        scratch_shapes=[pltpu.VMEM(s, F32) if isinstance(s, tuple) else s for s in scratch],
        input_output_aliases=aliases or {},
        cost_estimate=pl.CostEstimate(flops=flops, bytes_accessed=4 * sum(a.size for a in ins), transcendentals=0),
        compiler_params=pltpu.CompilerParams(vmem_limit_bytes=limit * 1024 * 1024),
    )(*ins)
    return list(outs)


def central(child_rhs, child_diag, child_off, live, targets, top_rhs, top_factor, top_diag):
    rows, cols = lax.axis_size("row"), lax.axis_size("col")
    size = top_diag.shape[1]
    right = top_rhs.shape[1]
    half, piece = right // 2, right // 4
    children, slots = targets.shape
    shape = (piece, size)
    block = ((size, size), BF16)
    dma = pltpu.SemaphoreType.DMA

    def at(r, c):
        return r * cols + c

    def swap(value):
        return lax.ppermute(value, "leaf", [(0, 1), (1, 0)])

    def along_row(value, step):
        return lax.ppermute(value, "row", [(r, r ^ step) for r in range(rows)])

    def along_col(value, pairs):
        rest = [a for a in range(cols) if a not in [p[0] for p in pairs]]
        open_ends = [b for b in range(cols) if b not in [p[1] for p in pairs]]
        return lax.ppermute(value, "col", pairs + list(zip(rest, open_ends)))

    near = [(at(k, 0), at(k, 1)) for k in (1, 2, 3)] + [(at(k, 1), at(k, 2)) for k in (2, 3)]
    far = [(at(k, 0), at(k, 2)) for k in (1, 2, 3)] + [(at(3, 2), at(3, 1))]
    shift = rows * cols
    pairs = near + [(a + shift, b + shift) for a, b in far]
    for k in range(2 * rows):
        here = range(k * cols, (k + 1) * cols)
        rest = [a for a in here if a not in [p[0] for p in pairs]]
        open_ends = [b for b in here if b not in [p[1] for p in pairs]]
        stay = [a for a in rest if a in open_ends]
        pairs = pairs + [(a, a) for a in stay]
        pairs = pairs + list(zip([a for a in rest if a not in stay], [b for b in open_ends if b not in stay]))
    sent = lax.ppermute(top_factor, ("leaf", "row", "col"), pairs)
    child_sol, keep, send = call(
        child_kernel,
        [live, child_rhs, child_diag, child_off, targets],
        [child_rhs.shape, (half, children * slots), (half + 8, children * slots)],
        [child_rhs.shape, child_diag.shape, child_off.shape, child_rhs.shape, (right, children * slots),
         dma((4, children))],
        outside=(1, 2, 3),
        outs_outside=(0,),
        pinned=(1, 2),
        limit=56,
    )
    sums = call(own_kernel, [keep, send], [(half, size)] * rows)
    sums = call(other_kernel, [swap(send)] + sums, [(half, size)] * rows)
    got = [along_row(sums[s], s) for s in (1, 2, 3)]
    rhs_piece, diag_high, diag_low = call(
        turn_kernel, [top_rhs, top_diag], [shape, block, block], [(half, size)]
    )
    diag = [diag_high, diag_low]
    first, second = call(pieces_kernel, [sums[0]] + got, [shape] * 2, [(half, size)])
    q = [
        along_col(second, [(0, 2), (3, 1)]),
        along_col(first, [(0, 1), (3, 2)]),
        along_col(first, [(1, 2), (2, 1)]),
    ]

    def chain(owner, ins, has_sums=False, solves=True, flops=0):
        outs = call(
            functools.partial(chain_kernel, owner, has_sums, solves), ins, [shape] * (1 + has_sums), flops=flops
        )
        return outs if has_sums else outs[0]

    res, x = chain(0, [rhs_piece, second] + q + diag, has_sums=True, flops=10 ** 10)
    factor = call(factor_kernel, [top_factor, sent, swap(sent)], [block] * 6)
    factor = [factor[0:2], factor[2:4], factor[4:6]]
    to1 = along_row(x, 1)
    to2 = along_row(x, 2)
    x = chain(1, [res, x] + diag + [to1] + factor[0])
    on = along_row(x, 3)
    res = chain(2, [res, res, to2] + factor[0], solves=False)
    x = chain(2, [res, x] + diag + [on] + factor[1])
    to3 = along_row(x, 1)
    late = along_row(x, 2)
    res = chain(3, [res, res, on] + factor[0], solves=False)
    x = chain(3, [res, x] + diag + [to3] + factor[2] + [late] + factor[1])

    both = along_col(x, [(1, 2), (2, 1)])
    step = along_col(x, [(1, 0), (2, 3)])
    over = along_col(x, [(1, 3), (2, 0)])
    (own,) = call(half_kernel, [over, step, both, x], [(size, half)])
    (top_sol,) = call(
        functools.partial(write_kernel, True), [own], [top_rhs.shape], [dma(())], outs_outside=(0,)
    )
    (top_sol,) = call(
        functools.partial(write_kernel, False),
        [swap(own), top_sol],
        [top_rhs.shape],
        [dma(())],
        outside=(1,),
        outs_outside=(0,),
        aliases={1: 0},
    )
    return (child_sol, top_sol)


def solution(mesh):
    in_specs = (
        P(("leaf", "row", "col"), None, None),
        P(("leaf", "row", "col"), None, None),
        P(("leaf", "row", "col"), None, None),
        P(("leaf", "row", "col")),
        P(("leaf", "row", "col"), None),
        P("row", None),
        P("row", "col"),
        P("row", None),
    )
    out_specs = (P(("leaf", "row", "col"), None, None), P("row", None))
    axes = tuple(mesh.shape[a] for a in ("leaf", "row", "col"))

    def shards(*args):
        top_rhs, top_factor, top_diag = args[5:]
        size = top_diag.shape[1]
        fits = axes == (2, 4, 4) and top_rhs.shape[0] == size and top_factor.shape[1] == size
        return (central if fits else any_mesh)(*args)

    return jax.shard_map(shards, mesh=mesh, in_specs=in_specs, out_specs=out_specs, check_vma=False)
```

```python
import functools

import jax
import jax.numpy as jnp
from jax import lax
from jax.experimental import pallas as pl
from jax.experimental.pallas import tpu as pltpu
from jax.sharding import PartitionSpec as P

F32 = jnp.float32
BF16 = jnp.bfloat16
NT = (((1,), (1,)), ((), ()))
NN = (((1,), (0,)), ((), ()))
VM = pl.BlockSpec(memory_space=pltpu.VMEM)
ANY = pl.BlockSpec(memory_space=pl.ANY)
SM = pl.BlockSpec(memory_space=pltpu.SMEM)


def spread(value, axis, source):
    kept = jnp.where(lax.axis_index(axis) == source, value, 0).astype(value.dtype)
    return lax.psum(kept, axis)


def unit_lower(matrix):
    return jnp.tril(matrix) + jnp.eye(matrix.shape[-1], dtype=matrix.dtype)


def any_mesh(child_rhs, child_diag, child_off, live, targets, top_rhs, top_factor, top_diag):
    highest = lax.Precision.HIGHEST
    owned_rows = top_rhs.shape[0]
    right_count = top_rhs.shape[1]
    block_size = top_diag.shape[1]
    owned_blocks = owned_rows // block_size
    row_count = lax.axis_size("row")
    top_order = owned_rows * row_count
    col_width = top_factor.shape[1]
    my_row = lax.axis_index("row")
    my_col = lax.axis_index("col")
    child_sol = jnp.einsum("bij,bjr->bir", unit_lower(child_diag), child_rhs, precision=highest)
    tiles = jnp.einsum("btj,bjr->btr", child_off, child_sol, precision=highest)
    slot_index = jnp.arange(child_off.shape[1], dtype=jnp.int32)
    keep = slot_index[None, :] < live[:, None]
    tiles = jnp.where(keep[:, :, None], tiles, jnp.zeros_like(tiles))
    contrib = jnp.zeros((top_order, right_count), F32)
    contrib = contrib.at[targets.reshape(-1)].add(tiles.reshape(-1, right_count))
    row_part = lax.psum_scatter(contrib, "row", scatter_dimension=0, tiled=True)
    share = lax.psum_scatter(row_part, ("leaf", "col"), scatter_dimension=0, tiled=True)
    updates = lax.all_gather(share, ("leaf", "col"), axis=0, tiled=True)
    reduced = top_rhs - updates
    inverse_all = unit_lower(top_diag.reshape(owned_blocks, block_size, block_size))
    col_global = my_col * col_width + jnp.arange(col_width, dtype=jnp.int32)

    def step(block, solution):
        local = block % owned_blocks
        owner = block // owned_blocks
        factor_rows = jnp.where(
            (col_global < block * block_size)[None, :], top_factor, jnp.zeros_like(top_factor)
        )
        columns = lax.dynamic_slice_in_dim(solution, my_col * col_width, col_width, 0)
        partial_value = jnp.dot(
            factor_rows, columns, precision=highest, preferred_element_type=F32
        )
        block_inverse = lax.dynamic_index_in_dim(inverse_all, local, 0, keepdims=False)
        before = lax.psum(partial_value, "col")
        solved = jnp.dot(
            block_inverse, reduced - before, precision=highest, preferred_element_type=F32
        )
        solved = spread(solved, "row", owner)
        return lax.dynamic_update_slice_in_dim(solution, solved, block * block_size, 0)

    solution = lax.fori_loop(
        0, row_count * owned_blocks, step, jnp.zeros((top_order, right_count), F32)
    )
    top_sol = lax.dynamic_slice_in_dim(solution, my_row * owned_rows, owned_rows, 0)
    return (child_sol, top_sol)


def place():
    return tuple(lax.axis_index(a) for a in ("leaf", "row", "col"))


def split(value):
    high = value.astype(BF16)
    return high, (value - high.astype(F32)).astype(BF16)


def dot3(left, high, low, dims):
    left_high, left_low = split(left)
    rows = left.shape[0]
    both = lax.dot_general(
        jnp.concatenate([left_high, left_low], axis=0), high, dims, preferred_element_type=F32
    )
    cross = lax.dot_general(left_high, low, dims, preferred_element_type=F32)
    return both[:rows] + both[rows:] + cross


def lower(matrix):
    row = lax.broadcasted_iota(jnp.int32, matrix.shape, 0)
    col = lax.broadcasted_iota(jnp.int32, matrix.shape, 1)
    return jnp.where(col <= row, matrix, 0.0)


def turn_kernel(rhs_ref, diag_ref, out_ref, high_ref, low_ref, turned_ref):
    leaf, _, z = place()
    half, piece = turned_ref.shape[0], out_ref.shape[0]
    turned_ref[...] = rhs_ref[:, pl.ds(pl.multiple_of(leaf * half, half), half)].T
    out_ref[...] = turned_ref[pl.ds(pl.multiple_of((z // 2) * piece, piece), piece), :]
    high_ref[...], low_ref[...] = split(lower(diag_ref[...]).T)


def child_kernel(live_hbm, rhs_hbm, diag_hbm, off_hbm, tgt_hbm, sol_hbm, keep_ref, send_ref,
                 live_ref, tgt_ref, rhs_ref, diag_ref, off_ref, sol_ref, tiles_ref, sems):
    leaf, _, _ = place()
    children, slots = off_ref.shape[0], off_ref.shape[1]
    half = keep_ref.shape[0]
    pairs = ((rhs_hbm, rhs_ref), (diag_hbm, diag_ref), (off_hbm, off_ref))
    copies = [
        [pltpu.make_async_copy(source.at[s], target.at[s], sems.at[i, s]) for i, (source, target) in enumerate(pairs)]
        for s in range(children)
    ]
    back = [pltpu.make_async_copy(sol_ref.at[s], sol_hbm.at[s], sems.at[3, s]) for s in range(children)]
    small = [
        pltpu.make_async_copy(live_hbm, live_ref, sems.at[4, 0]),
        pltpu.make_async_copy(tgt_hbm, tgt_ref, sems.at[4, 1]),
    ]
    for s in range(children):
        for copy in copies[s]:
            copy.start()
    for copy in small:
        copy.start()
    for s in range(children):
        copies[s][0].wait()
        copies[s][1].wait()
        rhs = rhs_ref[s]
        sol = rhs + dot3(lower(diag_ref[s]), *split(rhs), NN)
        sol_ref[s] = sol
        back[s].start()
        copies[s][2].wait()
        if s == 0:
            for copy in small:
                copy.wait()
        tiles = dot3(sol.T, *split(off_ref[s]), NT)
        slot = lax.broadcasted_iota(jnp.int32, tiles.shape, 1)
        tiles_ref[:, s * slots:(s + 1) * slots] = jnp.where(slot < live_ref[s], tiles, 0.0)
        send_ref[half:half + 8, s * slots:(s + 1) * slots] = jnp.broadcast_to(
            tgt_ref[s:s + 1, :].astype(F32), (8, slots)
        )
    keep_ref[...] = tiles_ref[pl.ds(pl.multiple_of(leaf * half, half), half), :]
    send_ref[0:half, :] = tiles_ref[pl.ds(pl.multiple_of((1 - leaf) * half, half), half), :]
    for copy in back:
        copy.wait()


def scatter(value, target, size, start):
    index = lax.broadcasted_iota(jnp.int32, (size, value.shape[1]), 0) + start
    hot = jnp.where(index == target, 1.0, 0.0).astype(BF16)
    product = lax.dot_general(value, hot, NT, preferred_element_type=F32)
    half = value.shape[0] // 2
    return product[:half] + product[half:]


def own_kernel(keep_ref, send_ref, *out_refs):
    _, row, _ = place()
    half, size = out_refs[0].shape
    value = jnp.concatenate(split(keep_ref[...]), axis=0)
    target = send_ref[half:half + 1, :].astype(jnp.int32)
    for s, out_ref in enumerate(out_refs):
        out_ref[...] = scatter(value, target, size, jnp.bitwise_xor(row, s) * size)


def other_kernel(recv_ref, *refs):
    _, row, _ = place()
    own_refs, out_refs = refs[:4], refs[4:]
    half, size = out_refs[0].shape
    value = jnp.concatenate(split(recv_ref[0:half, :]), axis=0)
    target = recv_ref[half:half + 1, :].astype(jnp.int32)
    for s, (own_ref, out_ref) in enumerate(zip(own_refs, out_refs)):
        out_ref[...] = own_ref[...] + scatter(value, target, size, jnp.bitwise_xor(row, s) * size)


def pieces_kernel(a_ref, b_ref, c_ref, d_ref, first_ref, second_ref, sum_ref):
    _, _, z = place()
    odd = z % 2
    piece = first_ref.shape[0]
    sum_ref[...] = (a_ref[...] + b_ref[...]) + (c_ref[...] + d_ref[...])
    first_ref[...] = sum_ref[pl.ds(pl.multiple_of(odd * piece, piece), piece), :]
    second_ref[...] = sum_ref[pl.ds(pl.multiple_of((1 - odd) * piece, piece), piece), :]


def factor_kernel(own_ref, sent_ref, other_ref, *out_refs):
    leaf, row, z = place()
    for block in range(3):
        high_ref, low_ref = out_refs[2 * block], out_refs[2 * block + 1]

        @pl.when((row > block) & ((z == 1) | (z == 2)))
        def _():
            if block == 0:
                value = jnp.where((leaf == 0) == (z == 1), sent_ref[...], other_ref[...])
            else:
                sent = jnp.where((leaf == 0) == (block == 1), sent_ref[...], other_ref[...])
                value = jnp.where(z == block, own_ref[...], sent)
            high_ref[...], low_ref[...] = split(value.T)


def chain_kernel(owner, has_sums, solves, *refs):
    refs = list(refs)
    out_refs = [refs.pop()]
    if has_sums:
        out_refs.insert(0, refs.pop())
    _, row, z = place()
    given_ref = refs[0]
    if has_sums:
        value = given_ref[...] - ((refs[1][...] + refs[2][...]) + (refs[3][...] + refs[4][...]))
        out_refs[0][...] = value
        out_refs[1][...] = value
        refs = refs[5:]
    else:
        out_refs[0][...] = refs[1][...]
        refs = refs[2:]

    @pl.when((row == owner) & ((z == 1) | (z == 2)))
    def _():
        left = out_refs[0][...] if has_sums else given_ref[...]
        used = refs[2:] if solves else refs
        for i in range(0, len(used), 3):
            left = left - dot3(used[i][...], used[i + 1][...], used[i + 2][...], NN)
        if solves:
            left = left + dot3(left, refs[0][...], refs[1][...], NN)
        out_refs[-1][...] = left


def half_kernel(b_ref, a_ref, c_ref, x_ref, out_ref):
    _, _, z = place()
    x, a, b, c = x_ref[...], a_ref[...], b_ref[...], c_ref[...]
    low = jnp.where(z == 0, a, jnp.where(z == 1, x, jnp.where(z == 2, b, c)))
    high = jnp.where(z == 0, c, jnp.where(z == 1, b, jnp.where(z == 2, x, a)))
    out_ref[...] = jnp.concatenate([low, high], axis=0).T


def write_kernel(mine, part_ref, *refs):
    out_hbm, sem = refs[-2:]
    leaf, _, _ = place()
    half = part_ref.shape[1]
    at = leaf if mine else 1 - leaf
    copy = pltpu.make_async_copy(part_ref, out_hbm.at[:, pl.ds(pl.multiple_of(at * half, half), half)], sem)
    copy.start()
    copy.wait()


def call(kernel, ins, outs, scratch=(), outside=(), outs_outside=(), pinned=(), aliases=None, limit=24, flops=0):
    def spec(i, a):
        return ANY if i in outside else SM if a.ndim == 1 else VM

    def shape(i, out):
        dims, dtype = out if isinstance(out[0], tuple) else (out, F32)
        return pltpu.VMEM(dims, dtype) if i in pinned else jax.ShapeDtypeStruct(dims, dtype)

    outs = pl.pallas_call(
        kernel,
        out_shape=[shape(i, out) for i, out in enumerate(outs)],
        in_specs=[spec(i, a) for i, a in enumerate(ins)],
        out_specs=[ANY if i in outs_outside else VM for i in range(len(outs))],
        scratch_shapes=[pltpu.VMEM(s, F32) if isinstance(s, tuple) else s for s in scratch],
        input_output_aliases=aliases or {},
        cost_estimate=pl.CostEstimate(flops=flops, bytes_accessed=4 * sum(a.size for a in ins), transcendentals=0),
        compiler_params=pltpu.CompilerParams(vmem_limit_bytes=limit * 1024 * 1024),
    )(*ins)
    return list(outs)


def central(child_rhs, child_diag, child_off, live, targets, top_rhs, top_factor, top_diag):
    rows, cols = lax.axis_size("row"), lax.axis_size("col")
    size = top_diag.shape[1]
    right = top_rhs.shape[1]
    half, piece = right // 2, right // 4
    children, slots = targets.shape
    shape = (piece, size)
    block = ((size, size), BF16)
    dma = pltpu.SemaphoreType.DMA

    def at(r, c):
        return r * cols + c

    def swap(value):
        return lax.ppermute(value, "leaf", [(0, 1), (1, 0)])

    def along_row(value, step):
        return lax.ppermute(value, "row", [(r, r ^ step) for r in range(rows)])

    def along_col(value, pairs):
        rest = [a for a in range(cols) if a not in [p[0] for p in pairs]]
        open_ends = [b for b in range(cols) if b not in [p[1] for p in pairs]]
        return lax.ppermute(value, "col", pairs + list(zip(rest, open_ends)))

    near = [(at(k, 0), at(k, 1)) for k in (1, 2, 3)] + [(at(k, 1), at(k, 2)) for k in (2, 3)]
    far = [(at(k, 0), at(k, 2)) for k in (1, 2, 3)] + [(at(3, 2), at(3, 1))]
    shift = rows * cols
    pairs = near + [(a + shift, b + shift) for a, b in far]
    for k in range(2 * rows):
        here = range(k * cols, (k + 1) * cols)
        rest = [a for a in here if a not in [p[0] for p in pairs]]
        open_ends = [b for b in here if b not in [p[1] for p in pairs]]
        stay = [a for a in rest if a in open_ends]
        pairs = pairs + [(a, a) for a in stay]
        pairs = pairs + list(zip([a for a in rest if a not in stay], [b for b in open_ends if b not in stay]))
    sent = lax.ppermute(top_factor, ("leaf", "row", "col"), pairs)
    child_sol, keep, send = call(
        child_kernel,
        [live, child_rhs, child_diag, child_off, targets],
        [child_rhs.shape, (half, children * slots), (half + 8, children * slots)],
        [pltpu.SMEM(live.shape, jnp.int32), pltpu.VMEM(targets.shape, jnp.int32), child_rhs.shape,
         child_diag.shape, child_off.shape, child_rhs.shape, (right, children * slots), dma((5, max(2, children)))],
        outside=(0, 1, 2, 3, 4),
        outs_outside=(0,),
        pinned=(1, 2),
        limit=56,
    )
    sums = call(own_kernel, [keep, send], [(half, size)] * rows)
    sums = call(other_kernel, [swap(send)] + sums, [(half, size)] * rows)
    got = [along_row(sums[s], s) for s in (1, 2, 3)]
    rhs_piece, diag_high, diag_low = call(
        turn_kernel, [top_rhs, top_diag], [shape, block, block], [(half, size)]
    )
    diag = [diag_high, diag_low]
    first, second = call(pieces_kernel, [sums[0]] + got, [shape] * 2, [(half, size)])
    q = [
        along_col(second, [(0, 2), (3, 1)]),
        along_col(first, [(0, 1), (3, 2)]),
        along_col(first, [(1, 2), (2, 1)]),
    ]

    def chain(owner, ins, has_sums=False, solves=True, flops=0):
        outs = call(
            functools.partial(chain_kernel, owner, has_sums, solves), ins, [shape] * (1 + has_sums), flops=flops
        )
        return outs if has_sums else outs[0]

    res, x = chain(0, [rhs_piece, second] + q + diag, has_sums=True, flops=10 ** 10)
    factor = call(factor_kernel, [top_factor, sent, swap(sent)], [block] * 6)
    factor = [factor[0:2], factor[2:4], factor[4:6]]
    to1 = along_row(x, 1)
    to2 = along_row(x, 2)
    x = chain(1, [res, x] + diag + [to1] + factor[0])
    on = along_row(x, 3)
    res = chain(2, [res, res, to2] + factor[0], solves=False)
    x = chain(2, [res, x] + diag + [on] + factor[1])
    to3 = along_row(x, 1)
    late = along_row(x, 2)
    res = chain(3, [res, res, on] + factor[0], solves=False)
    x = chain(3, [res, x] + diag + [late] + factor[1] + [to3] + factor[2])

    both = along_col(x, [(1, 2), (2, 1)])
    step = along_col(x, [(1, 0), (2, 3)])
    over = along_col(x, [(1, 3), (2, 0)])
    (own,) = call(half_kernel, [both, step, over, x], [(size, half)])
    (top_sol,) = call(
        functools.partial(write_kernel, True), [own], [top_rhs.shape], [dma(())], outs_outside=(0,)
    )
    (top_sol,) = call(
        functools.partial(write_kernel, False),
        [swap(own), top_sol],
        [top_rhs.shape],
        [dma(())],
        outside=(1,),
        outs_outside=(0,),
        aliases={1: 0},
    )
    return (child_sol, top_sol)


def solution(mesh):
    in_specs = (
        P(("leaf", "row", "col"), None, None),
        P(("leaf", "row", "col"), None, None),
        P(("leaf", "row", "col"), None, None),
        P(("leaf", "row", "col")),
        P(("leaf", "row", "col"), None),
        P("row", None),
        P("row", "col"),
        P("row", None),
    )
    out_specs = (P(("leaf", "row", "col"), None, None), P("row", None))
    axes = tuple(mesh.shape[a] for a in ("leaf", "row", "col"))

    def shards(*args):
        top_rhs, top_factor, top_diag = args[5:]
        size = top_diag.shape[1]
        fits = axes == (2, 4, 4) and top_rhs.shape[0] == size and top_factor.shape[1] == size
        return (central if fits else any_mesh)(*args)

    return jax.shard_map(shards, mesh=mesh, in_specs=in_specs, out_specs=out_specs, check_vma=False)
```

```python
import functools

import jax
import jax.numpy as jnp
from jax import lax
from jax.experimental import pallas as pl
from jax.experimental.pallas import tpu as pltpu
from jax.sharding import PartitionSpec as P

F32 = jnp.float32
BF16 = jnp.bfloat16
NT = (((1,), (1,)), ((), ()))
NN = (((1,), (0,)), ((), ()))
VM = pl.BlockSpec(memory_space=pltpu.VMEM)
ANY = pl.BlockSpec(memory_space=pl.ANY)
SM = pl.BlockSpec(memory_space=pltpu.SMEM)


def spread(value, axis, source):
    kept = jnp.where(lax.axis_index(axis) == source, value, 0).astype(value.dtype)
    return lax.psum(kept, axis)


def unit_lower(matrix):
    return jnp.tril(matrix) + jnp.eye(matrix.shape[-1], dtype=matrix.dtype)


def any_mesh(child_rhs, child_diag, child_off, live, targets, top_rhs, top_factor, top_diag):
    highest = lax.Precision.HIGHEST
    owned_rows = top_rhs.shape[0]
    right_count = top_rhs.shape[1]
    block_size = top_diag.shape[1]
    owned_blocks = owned_rows // block_size
    row_count = lax.axis_size("row")
    top_order = owned_rows * row_count
    col_width = top_factor.shape[1]
    my_row = lax.axis_index("row")
    my_col = lax.axis_index("col")
    child_sol = jnp.einsum("bij,bjr->bir", unit_lower(child_diag), child_rhs, precision=highest)
    tiles = jnp.einsum("btj,bjr->btr", child_off, child_sol, precision=highest)
    slot_index = jnp.arange(child_off.shape[1], dtype=jnp.int32)
    keep = slot_index[None, :] < live[:, None]
    tiles = jnp.where(keep[:, :, None], tiles, jnp.zeros_like(tiles))
    contrib = jnp.zeros((top_order, right_count), F32)
    contrib = contrib.at[targets.reshape(-1)].add(tiles.reshape(-1, right_count))
    row_part = lax.psum_scatter(contrib, "row", scatter_dimension=0, tiled=True)
    share = lax.psum_scatter(row_part, ("leaf", "col"), scatter_dimension=0, tiled=True)
    updates = lax.all_gather(share, ("leaf", "col"), axis=0, tiled=True)
    reduced = top_rhs - updates
    inverse_all = unit_lower(top_diag.reshape(owned_blocks, block_size, block_size))
    col_global = my_col * col_width + jnp.arange(col_width, dtype=jnp.int32)

    def step(block, solution):
        local = block % owned_blocks
        owner = block // owned_blocks
        factor_rows = jnp.where(
            (col_global < block * block_size)[None, :], top_factor, jnp.zeros_like(top_factor)
        )
        columns = lax.dynamic_slice_in_dim(solution, my_col * col_width, col_width, 0)
        partial_value = jnp.dot(
            factor_rows, columns, precision=highest, preferred_element_type=F32
        )
        block_inverse = lax.dynamic_index_in_dim(inverse_all, local, 0, keepdims=False)
        before = lax.psum(partial_value, "col")
        solved = jnp.dot(
            block_inverse, reduced - before, precision=highest, preferred_element_type=F32
        )
        solved = spread(solved, "row", owner)
        return lax.dynamic_update_slice_in_dim(solution, solved, block * block_size, 0)

    solution = lax.fori_loop(
        0, row_count * owned_blocks, step, jnp.zeros((top_order, right_count), F32)
    )
    top_sol = lax.dynamic_slice_in_dim(solution, my_row * owned_rows, owned_rows, 0)
    return (child_sol, top_sol)


def place():
    return tuple(lax.axis_index(a) for a in ("leaf", "row", "col"))


def split(value):
    high = value.astype(BF16)
    return high, (value - high.astype(F32)).astype(BF16)


def dot3(left, high, low, dims):
    left_high, left_low = split(left)
    rows = left.shape[0]
    both = lax.dot_general(
        jnp.concatenate([left_high, left_low], axis=0), high, dims, preferred_element_type=F32
    )
    cross = lax.dot_general(left_high, low, dims, preferred_element_type=F32)
    return both[:rows] + both[rows:] + cross


def lower(matrix):
    row = lax.broadcasted_iota(jnp.int32, matrix.shape, 0)
    col = lax.broadcasted_iota(jnp.int32, matrix.shape, 1)
    return jnp.where(col <= row, matrix, 0.0)


def turn_kernel(rhs_ref, diag_ref, out_ref, high_ref, low_ref, turned_ref):
    leaf, _, z = place()
    half, piece = turned_ref.shape[0], out_ref.shape[0]
    turned_ref[...] = rhs_ref[:, pl.ds(pl.multiple_of(leaf * half, half), half)].T
    out_ref[...] = turned_ref[pl.ds(pl.multiple_of((z // 2) * piece, piece), piece), :]
    high_ref[...], low_ref[...] = split(lower(diag_ref[...]).T)


def child_kernel(live_hbm, rhs_hbm, diag_hbm, off_hbm, tgt_hbm, sol_hbm, keep_ref, send_ref,
                 live_ref, tgt_ref, rhs_ref, diag_ref, off_ref, sol_ref, tiles_ref, sems):
    leaf, _, _ = place()
    children, slots = off_ref.shape[0], off_ref.shape[1]
    half = keep_ref.shape[0]
    pairs = ((rhs_hbm, rhs_ref), (diag_hbm, diag_ref), (off_hbm, off_ref))
    copies = [
        [pltpu.make_async_copy(source.at[s], target.at[s], sems.at[i, s]) for i, (source, target) in enumerate(pairs)]
        for s in range(children)
    ]
    back = [pltpu.make_async_copy(sol_ref.at[s], sol_hbm.at[s], sems.at[3, s]) for s in range(children)]
    small = [
        pltpu.make_async_copy(live_hbm, live_ref, sems.at[4, 0]),
        pltpu.make_async_copy(tgt_hbm, tgt_ref, sems.at[4, 1]),
    ]
    for s in range(children):
        for copy in copies[s]:
            copy.start()
    for copy in small:
        copy.start()
    for s in range(children):
        copies[s][0].wait()
        copies[s][1].wait()
        rhs = rhs_ref[s]
        sol = rhs + dot3(lower(diag_ref[s]), *split(rhs), NN)
        sol_ref[s] = sol
        back[s].start()
        copies[s][2].wait()
        if s == 0:
            for copy in small:
                copy.wait()
        tiles = dot3(sol.T, *split(off_ref[s]), NT)
        slot = lax.broadcasted_iota(jnp.int32, tiles.shape, 1)
        tiles_ref[:, s * slots:(s + 1) * slots] = jnp.where(slot < live_ref[s], tiles, 0.0)
        send_ref[half:half + 8, s * slots:(s + 1) * slots] = jnp.broadcast_to(
            tgt_ref[s:s + 1, :].astype(F32), (8, slots)
        )
    keep_ref[...] = tiles_ref[pl.ds(pl.multiple_of(leaf * half, half), half), :]
    send_ref[0:half, :] = tiles_ref[pl.ds(pl.multiple_of((1 - leaf) * half, half), half), :]
    for copy in back:
        copy.wait()


def scatter(value, target, size, start):
    index = lax.broadcasted_iota(jnp.int32, (size, value.shape[1]), 0) + start
    hot = jnp.where(index == target, 1.0, 0.0).astype(BF16)
    product = lax.dot_general(value, hot, NT, preferred_element_type=F32)
    half = value.shape[0] // 2
    return product[:half] + product[half:]


def own_kernel(keep_ref, send_ref, *out_refs):
    _, row, _ = place()
    half, size = out_refs[0].shape
    value = jnp.concatenate(split(keep_ref[...]), axis=0)
    target = send_ref[half:half + 1, :].astype(jnp.int32)
    for s, out_ref in enumerate(out_refs):
        out_ref[...] = scatter(value, target, size, jnp.bitwise_xor(row, s) * size)


def other_kernel(recv_ref, *refs):
    _, row, _ = place()
    own_refs, out_refs = refs[:4], refs[4:]
    half, size = out_refs[0].shape
    value = jnp.concatenate(split(recv_ref[0:half, :]), axis=0)
    target = recv_ref[half:half + 1, :].astype(jnp.int32)
    for s, (own_ref, out_ref) in enumerate(zip(own_refs, out_refs)):
        out_ref[...] = own_ref[...] + scatter(value, target, size, jnp.bitwise_xor(row, s) * size)


def pieces_kernel(a_ref, b_ref, c_ref, d_ref, first_ref, second_ref, sum_ref):
    _, _, z = place()
    odd = z % 2
    piece = first_ref.shape[0]
    sum_ref[...] = (a_ref[...] + b_ref[...]) + (c_ref[...] + d_ref[...])
    first_ref[...] = sum_ref[pl.ds(pl.multiple_of(odd * piece, piece), piece), :]
    second_ref[...] = sum_ref[pl.ds(pl.multiple_of((1 - odd) * piece, piece), piece), :]


def factor_kernel(own_ref, near_ref, near_other_ref, on_ref, on_other_ref, *out_refs):
    leaf, row, z = place()
    for block in range(3):
        high_ref, low_ref = out_refs[2 * block], out_refs[2 * block + 1]

        def put(value):
            high_ref[...], low_ref[...] = split(value.T)

        @pl.when((row > block) & (z == 1))
        def _():
            if block == 1:
                put(own_ref[...])
            else:
                put(jnp.where(leaf == block // 2, near_ref[...], near_other_ref[...]))

        @pl.when((row > block) & (z == 2))
        def _():
            if block == 0:
                put(jnp.where(leaf == 1, on_ref[...], on_other_ref[...]))
            elif block == 1:
                put(jnp.where(leaf == 0, near_ref[...], near_other_ref[...]))
            else:
                put(own_ref[...])


def chain_kernel(owner, has_sums, solves, *refs):
    refs = list(refs)
    out_refs = [refs.pop()]
    if has_sums:
        out_refs.insert(0, refs.pop())
    _, row, z = place()
    given_ref = refs[0]
    if has_sums:
        value = given_ref[...] - ((refs[1][...] + refs[2][...]) + (refs[3][...] + refs[4][...]))
        out_refs[0][...] = value
        out_refs[1][...] = value
        refs = refs[5:]
    else:
        out_refs[0][...] = refs[1][...]
        refs = refs[2:]

    @pl.when((row == owner) & ((z == 1) | (z == 2)))
    def _():
        left = out_refs[0][...] if has_sums else given_ref[...]
        used = refs[2:] if solves else refs
        for i in range(0, len(used), 3):
            left = left - dot3(used[i][...], used[i + 1][...], used[i + 2][...], NN)
        if solves:
            left = left + dot3(left, refs[0][...], refs[1][...], NN)
        out_refs[-1][...] = left


def half_kernel(b_ref, a_ref, c_ref, x_ref, out_ref):
    _, _, z = place()
    x, a, b, c = x_ref[...], a_ref[...], b_ref[...], c_ref[...]
    low = jnp.where(z == 0, a, jnp.where(z == 1, x, jnp.where(z == 2, b, c)))
    high = jnp.where(z == 0, c, jnp.where(z == 1, b, jnp.where(z == 2, x, a)))
    out_ref[...] = jnp.concatenate([low, high], axis=0).T


def write_kernel(mine, part_ref, *refs):
    out_hbm, sem = refs[-2:]
    leaf, _, _ = place()
    half = part_ref.shape[1]
    at = leaf if mine else 1 - leaf
    copy = pltpu.make_async_copy(part_ref, out_hbm.at[:, pl.ds(pl.multiple_of(at * half, half), half)], sem)
    copy.start()
    copy.wait()


def call(kernel, ins, outs, scratch=(), outside=(), outs_outside=(), pinned=(), aliases=None, limit=24, flops=0):
    def spec(i, a):
        return ANY if i in outside else SM if a.ndim == 1 else VM

    def shape(i, out):
        dims, dtype = out if isinstance(out[0], tuple) else (out, F32)
        return pltpu.VMEM(dims, dtype) if i in pinned else jax.ShapeDtypeStruct(dims, dtype)

    outs = pl.pallas_call(
        kernel,
        out_shape=[shape(i, out) for i, out in enumerate(outs)],
        in_specs=[spec(i, a) for i, a in enumerate(ins)],
        out_specs=[ANY if i in outs_outside else VM for i in range(len(outs))],
        scratch_shapes=[pltpu.VMEM(s, F32) if isinstance(s, tuple) else s for s in scratch],
        input_output_aliases=aliases or {},
        cost_estimate=pl.CostEstimate(flops=flops, bytes_accessed=4 * sum(a.size for a in ins), transcendentals=0),
        compiler_params=pltpu.CompilerParams(vmem_limit_bytes=limit * 1024 * 1024),
    )(*ins)
    return list(outs)


def central(child_rhs, child_diag, child_off, live, targets, top_rhs, top_factor, top_diag):
    rows, cols = lax.axis_size("row"), lax.axis_size("col")
    size = top_diag.shape[1]
    right = top_rhs.shape[1]
    half, piece = right // 2, right // 4
    children, slots = targets.shape
    shape = (piece, size)
    block = ((size, size), BF16)
    dma = pltpu.SemaphoreType.DMA

    def at(r, c):
        return r * cols + c

    def swap(value):
        return lax.ppermute(value, "leaf", [(0, 1), (1, 0)])

    def along_row(value, step):
        return lax.ppermute(value, "row", [(r, r ^ step) for r in range(rows)])

    def along_col(value, pairs):
        rest = [a for a in range(cols) if a not in [p[0] for p in pairs]]
        open_ends = [b for b in range(cols) if b not in [p[1] for p in pairs]]
        return lax.ppermute(value, "col", pairs + list(zip(rest, open_ends)))

    def plane(value, pairs):
        groups = [[at(k, z) + leaf * rows * cols for leaf in (0, 1) for z in range(cols)] for k in range(rows)]
        for here in groups:
            rest = [a for a in here if a not in [p[0] for p in pairs]]
            ends = [b for b in here if b not in [p[1] for p in pairs]]
            stay = [a for a in rest if a in ends]
            rest, ends = [a for a in rest if a not in stay], [b for b in ends if b not in stay]
            pairs = pairs + [(a, a) for a in stay] + list(zip(rest, ends))
        return lax.ppermute(value, ("leaf", "row", "col"), pairs)

    shift = rows * cols
    near = plane(
        top_factor,
        [(at(k, 0), at(k, 1)) for k in (1, 2, 3)]
        + [(at(k, 1), at(k, 2)) for k in (2, 3)]
        + [(at(3, 2) + shift, at(3, 1) + shift)],
    )
    child_sol, keep, send = call(
        child_kernel,
        [live, child_rhs, child_diag, child_off, targets],
        [child_rhs.shape, (half, children * slots), (half + 8, children * slots)],
        [pltpu.SMEM(live.shape, jnp.int32), pltpu.VMEM(targets.shape, jnp.int32), child_rhs.shape,
         child_diag.shape, child_off.shape, child_rhs.shape, (right, children * slots), dma((5, max(2, children)))],
        outside=(0, 1, 2, 3, 4),
        outs_outside=(0,),
        pinned=(1, 2),
        limit=56,
    )
    sums = call(own_kernel, [keep, send], [(half, size)] * rows)
    sums = call(other_kernel, [swap(send)] + sums, [(half, size)] * rows)
    got = [along_row(sums[s], s) for s in (1, 2, 3)]
    rhs_piece, diag_high, diag_low = call(
        turn_kernel, [top_rhs, top_diag], [shape, block, block], [(half, size)]
    )
    diag = [diag_high, diag_low]
    first, second = call(pieces_kernel, [sums[0]] + got, [shape] * 2, [(half, size)], flops=10 ** 11)
    q = [
        along_col(second, [(0, 2), (3, 1)]),
        along_col(first, [(0, 1), (3, 2)]),
        along_col(first, [(1, 2), (2, 1)]),
    ]

    def chain(owner, ins, has_sums=False, solves=True, flops=0):
        outs = call(
            functools.partial(chain_kernel, owner, has_sums, solves), ins, [shape] * (1 + has_sums), flops=flops
        )
        return outs if has_sums else outs[0]

    res, x = chain(0, [rhs_piece, second] + q + diag, has_sums=True, flops=10 ** 10)
    on = plane(near, [(at(k, 1), at(k, 2) + shift) for k in (1, 2, 3)])
    factor = call(factor_kernel, [top_factor, near, swap(near), on, swap(on)], [block] * 6)
    factor = [factor[0:2], factor[2:4], factor[4:6]]
    to1 = along_row(x, 1)
    to2 = along_row(x, 2)
    x = chain(1, [res, x] + diag + [to1] + factor[0])
    on = along_row(x, 3)
    res = chain(2, [res, res, to2] + factor[0], solves=False)
    x = chain(2, [res, x] + diag + [on] + factor[1])
    to3 = along_row(x, 1)
    late = along_row(x, 2)
    res = chain(3, [res, res, on] + factor[0], solves=False)
    x = chain(3, [res, x] + diag + [late] + factor[1] + [to3] + factor[2])

    both = along_col(x, [(1, 2), (2, 1)])
    step = along_col(x, [(1, 0), (2, 3)])
    over = along_col(x, [(1, 3), (2, 0)])
    (own,) = call(half_kernel, [both, step, over, x], [(size, half)])
    (top_sol,) = call(
        functools.partial(write_kernel, True), [own], [top_rhs.shape], [dma(())], outs_outside=(0,)
    )
    (top_sol,) = call(
        functools.partial(write_kernel, False),
        [swap(own), top_sol],
        [top_rhs.shape],
        [dma(())],
        outside=(1,),
        outs_outside=(0,),
        aliases={1: 0},
    )
    return (child_sol, top_sol)


def solution(mesh):
    in_specs = (
        P(("leaf", "row", "col"), None, None),
        P(("leaf", "row", "col"), None, None),
        P(("leaf", "row", "col"), None, None),
        P(("leaf", "row", "col")),
        P(("leaf", "row", "col"), None),
        P("row", None),
        P("row", "col"),
        P("row", None),
    )
    out_specs = (P(("leaf", "row", "col"), None, None), P("row", None))
    axes = tuple(mesh.shape[a] for a in ("leaf", "row", "col"))

    def shards(*args):
        top_rhs, top_factor, top_diag = args[5:]
        size = top_diag.shape[1]
        fits = axes == (2, 4, 4) and top_rhs.shape[0] == size and top_factor.shape[1] == size
        return (central if fits else any_mesh)(*args)

    return jax.shard_map(shards, mesh=mesh, in_specs=in_specs, out_specs=out_specs, check_vma=False)
```

```python
import functools

import jax
import jax.numpy as jnp
from jax import lax
from jax.experimental import pallas as pl
from jax.experimental.pallas import tpu as pltpu
from jax.sharding import PartitionSpec as P

F32 = jnp.float32
BF16 = jnp.bfloat16
NT = (((1,), (1,)), ((), ()))
NN = (((1,), (0,)), ((), ()))
VM = pl.BlockSpec(memory_space=pltpu.VMEM)
ANY = pl.BlockSpec(memory_space=pl.ANY)
SM = pl.BlockSpec(memory_space=pltpu.SMEM)


def spread(value, axis, source):
    kept = jnp.where(lax.axis_index(axis) == source, value, 0).astype(value.dtype)
    return lax.psum(kept, axis)


def unit_lower(matrix):
    return jnp.tril(matrix) + jnp.eye(matrix.shape[-1], dtype=matrix.dtype)


def any_mesh(child_rhs, child_diag, child_off, live, targets, top_rhs, top_factor, top_diag):
    highest = lax.Precision.HIGHEST
    owned_rows = top_rhs.shape[0]
    right_count = top_rhs.shape[1]
    block_size = top_diag.shape[1]
    owned_blocks = owned_rows // block_size
    row_count = lax.axis_size("row")
    top_order = owned_rows * row_count
    col_width = top_factor.shape[1]
    my_row = lax.axis_index("row")
    my_col = lax.axis_index("col")
    child_sol = jnp.einsum("bij,bjr->bir", unit_lower(child_diag), child_rhs, precision=highest)
    tiles = jnp.einsum("btj,bjr->btr", child_off, child_sol, precision=highest)
    slot_index = jnp.arange(child_off.shape[1], dtype=jnp.int32)
    keep = slot_index[None, :] < live[:, None]
    tiles = jnp.where(keep[:, :, None], tiles, jnp.zeros_like(tiles))
    contrib = jnp.zeros((top_order, right_count), F32)
    contrib = contrib.at[targets.reshape(-1)].add(tiles.reshape(-1, right_count))
    row_part = lax.psum_scatter(contrib, "row", scatter_dimension=0, tiled=True)
    share = lax.psum_scatter(row_part, ("leaf", "col"), scatter_dimension=0, tiled=True)
    updates = lax.all_gather(share, ("leaf", "col"), axis=0, tiled=True)
    reduced = top_rhs - updates
    inverse_all = unit_lower(top_diag.reshape(owned_blocks, block_size, block_size))
    col_global = my_col * col_width + jnp.arange(col_width, dtype=jnp.int32)

    def step(block, solution):
        local = block % owned_blocks
        owner = block // owned_blocks
        factor_rows = jnp.where(
            (col_global < block * block_size)[None, :], top_factor, jnp.zeros_like(top_factor)
        )
        columns = lax.dynamic_slice_in_dim(solution, my_col * col_width, col_width, 0)
        partial_value = jnp.dot(
            factor_rows, columns, precision=highest, preferred_element_type=F32
        )
        block_inverse = lax.dynamic_index_in_dim(inverse_all, local, 0, keepdims=False)
        before = lax.psum(partial_value, "col")
        solved = jnp.dot(
            block_inverse, reduced - before, precision=highest, preferred_element_type=F32
        )
        solved = spread(solved, "row", owner)
        return lax.dynamic_update_slice_in_dim(solution, solved, block * block_size, 0)

    solution = lax.fori_loop(
        0, row_count * owned_blocks, step, jnp.zeros((top_order, right_count), F32)
    )
    top_sol = lax.dynamic_slice_in_dim(solution, my_row * owned_rows, owned_rows, 0)
    return (child_sol, top_sol)


def place():
    return tuple(lax.axis_index(a) for a in ("leaf", "row", "col"))


def split(value):
    high = value.astype(BF16)
    return high, (value - high.astype(F32)).astype(BF16)


def dot3(left, high, low, dims):
    left_high, left_low = split(left)
    rows = left.shape[0]
    both = lax.dot_general(
        jnp.concatenate([left_high, left_low], axis=0), high, dims, preferred_element_type=F32
    )
    cross = lax.dot_general(left_high, low, dims, preferred_element_type=F32)
    return both[:rows] + both[rows:] + cross


def lower(matrix):
    row = lax.broadcasted_iota(jnp.int32, matrix.shape, 0)
    col = lax.broadcasted_iota(jnp.int32, matrix.shape, 1)
    return jnp.where(col <= row, matrix, 0.0)


def turn_kernel(rhs_ref, diag_ref, out_ref, high_ref, low_ref, turned_ref):
    leaf, _, z = place()
    half, piece = turned_ref.shape[0], out_ref.shape[0]
    turned_ref[...] = rhs_ref[:, pl.ds(pl.multiple_of(leaf * half, half), half)].T
    out_ref[...] = turned_ref[pl.ds(pl.multiple_of((z // 2) * piece, piece), piece), :]
    high_ref[...], low_ref[...] = split(lower(diag_ref[...]).T)


def child_kernel(live_hbm, rhs_hbm, diag_hbm, off_hbm, tgt_hbm, sol_hbm, keep_ref, send_ref,
                 live_ref, tgt_ref, rhs_ref, diag_ref, off_ref, sol_ref, tiles_ref, sems):
    leaf, _, _ = place()
    children, slots = off_ref.shape[0], off_ref.shape[1]
    half = keep_ref.shape[0]
    pairs = ((rhs_hbm, rhs_ref), (diag_hbm, diag_ref), (off_hbm, off_ref))
    copies = [
        [pltpu.make_async_copy(source.at[s], target.at[s], sems.at[i, s]) for i, (source, target) in enumerate(pairs)]
        for s in range(children)
    ]
    back = [pltpu.make_async_copy(sol_ref.at[s], sol_hbm.at[s], sems.at[3, s]) for s in range(children)]
    small = [
        pltpu.make_async_copy(live_hbm, live_ref, sems.at[4, 0]),
        pltpu.make_async_copy(tgt_hbm, tgt_ref, sems.at[4, 1]),
    ]
    for s in range(children):
        for copy in copies[s]:
            copy.start()
    for copy in small:
        copy.start()
    for s in range(children):
        copies[s][0].wait()
        copies[s][1].wait()
        rhs = rhs_ref[s]
        sol = rhs + dot3(lower(diag_ref[s]), *split(rhs), NN)
        sol_ref[s] = sol
        back[s].start()
        copies[s][2].wait()
        if s == 0:
            for copy in small:
                copy.wait()
        tiles = dot3(sol.T, *split(off_ref[s]), NT)
        slot = lax.broadcasted_iota(jnp.int32, tiles.shape, 1)
        tiles_ref[:, s * slots:(s + 1) * slots] = jnp.where(slot < live_ref[s], tiles, 0.0)
        send_ref[half:half + 8, s * slots:(s + 1) * slots] = jnp.broadcast_to(
            tgt_ref[s:s + 1, :].astype(F32), (8, slots)
        )
    keep_ref[...] = tiles_ref[pl.ds(pl.multiple_of(leaf * half, half), half), :]
    send_ref[0:half, :] = tiles_ref[pl.ds(pl.multiple_of((1 - leaf) * half, half), half), :]
    for copy in back:
        copy.wait()


def scatter(value, target, size, start):
    index = lax.broadcasted_iota(jnp.int32, (size, value.shape[1]), 0) + start
    hot = jnp.where(index == target, 1.0, 0.0).astype(BF16)
    product = lax.dot_general(value, hot, NT, preferred_element_type=F32)
    half = value.shape[0] // 2
    return product[:half] + product[half:]


def own_kernel(keep_ref, send_ref, *out_refs):
    _, row, _ = place()
    half, size = out_refs[0].shape
    value = jnp.concatenate(split(keep_ref[...]), axis=0)
    target = send_ref[half:half + 1, :].astype(jnp.int32)
    for s, out_ref in enumerate(out_refs):
        out_ref[...] = scatter(value, target, size, jnp.bitwise_xor(row, s) * size)


def other_kernel(recv_ref, *refs):
    _, row, _ = place()
    own_refs, out_refs = refs[:4], refs[4:]
    half, size = out_refs[0].shape
    value = jnp.concatenate(split(recv_ref[0:half, :]), axis=0)
    target = recv_ref[half:half + 1, :].astype(jnp.int32)
    for s, (own_ref, out_ref) in enumerate(zip(own_refs, out_refs)):
        out_ref[...] = own_ref[...] + scatter(value, target, size, jnp.bitwise_xor(row, s) * size)


def pieces_kernel(a_ref, b_ref, c_ref, d_ref, first_ref, second_ref, sum_ref):
    _, _, z = place()
    odd = z % 2
    piece = first_ref.shape[0]
    sum_ref[...] = (a_ref[...] + b_ref[...]) + (c_ref[...] + d_ref[...])
    first_ref[...] = sum_ref[pl.ds(pl.multiple_of(odd * piece, piece), piece), :]
    second_ref[...] = sum_ref[pl.ds(pl.multiple_of((1 - odd) * piece, piece), piece), :]


def factor_kernel(own_ref, near_ref, near_other_ref, on_ref, on_other_ref, *out_refs):
    leaf, row, z = place()
    for block in range(3):
        high_ref, low_ref = out_refs[2 * block], out_refs[2 * block + 1]

        def put(value):
            high_ref[...], low_ref[...] = split(value.T)

        @pl.when((row > block) & (z == 1))
        def _():
            if block == 1:
                put(own_ref[...])
            else:
                put(jnp.where(leaf == block // 2, near_ref[...], near_other_ref[...]))

        @pl.when((row > block) & (z == 2))
        def _():
            if block == 0:
                put(jnp.where(leaf == 1, on_ref[...], on_other_ref[...]))
            elif block == 1:
                put(jnp.where(leaf == 0, near_ref[...], near_other_ref[...]))
            else:
                put(own_ref[...])


def chain_kernel(owner, has_sums, solves, *refs):
    refs = list(refs)
    out_refs = [refs.pop()]
    if has_sums:
        out_refs.insert(0, refs.pop())
    _, row, z = place()
    given_ref = refs[0]
    if has_sums:
        value = given_ref[...] - ((refs[1][...] + refs[2][...]) + (refs[3][...] + refs[4][...]))
        out_refs[0][...] = value
        out_refs[1][...] = value
        refs = refs[5:]
    else:
        out_refs[0][...] = refs[1][...]
        refs = refs[2:]

    @pl.when((row == owner) & ((z == 1) | (z == 2)))
    def _():
        left = out_refs[0][...] if has_sums else given_ref[...]
        used = refs[2:] if solves else refs
        for i in range(0, len(used), 3):
            left = left - dot3(used[i][...], used[i + 1][...], used[i + 2][...], NN)
        if solves:
            left = left + dot3(left, refs[0][...], refs[1][...], NN)
        out_refs[-1][...] = left


def half_kernel(b_ref, a_ref, c_ref, x_ref, out_ref):
    _, _, z = place()
    x, a, b, c = x_ref[...], a_ref[...], b_ref[...], c_ref[...]
    low = jnp.where(z == 0, a, jnp.where(z == 1, x, jnp.where(z == 2, b, c)))
    high = jnp.where(z == 0, c, jnp.where(z == 1, b, jnp.where(z == 2, x, a)))
    out_ref[...] = jnp.concatenate([low, high], axis=0).T


def write_kernel(mine, part_ref, *refs):
    out_hbm, sem = refs[-2:]
    leaf, _, _ = place()
    half = part_ref.shape[1]
    at = leaf if mine else 1 - leaf
    copy = pltpu.make_async_copy(part_ref, out_hbm.at[:, pl.ds(pl.multiple_of(at * half, half), half)], sem)
    copy.start()
    copy.wait()


def call(kernel, ins, outs, scratch=(), outside=(), outs_outside=(), pinned=(), aliases=None, limit=24, flops=0):
    def spec(i, a):
        return ANY if i in outside else SM if a.ndim == 1 else VM

    def shape(i, out):
        dims, dtype = out if isinstance(out[0], tuple) else (out, F32)
        return pltpu.VMEM(dims, dtype) if i in pinned else jax.ShapeDtypeStruct(dims, dtype)

    outs = pl.pallas_call(
        kernel,
        out_shape=[shape(i, out) for i, out in enumerate(outs)],
        in_specs=[spec(i, a) for i, a in enumerate(ins)],
        out_specs=[ANY if i in outs_outside else VM for i in range(len(outs))],
        scratch_shapes=[pltpu.VMEM(s, F32) if isinstance(s, tuple) else s for s in scratch],
        input_output_aliases=aliases or {},
        cost_estimate=pl.CostEstimate(flops=flops, bytes_accessed=4 * sum(a.size for a in ins), transcendentals=0),
        compiler_params=pltpu.CompilerParams(vmem_limit_bytes=limit * 1024 * 1024),
    )(*ins)
    return list(outs)


def central(child_rhs, child_diag, child_off, live, targets, top_rhs, top_factor, top_diag):
    rows, cols = lax.axis_size("row"), lax.axis_size("col")
    size = top_diag.shape[1]
    right = top_rhs.shape[1]
    half, piece = right // 2, right // 4
    children, slots = targets.shape
    shape = (piece, size)
    block = ((size, size), BF16)
    dma = pltpu.SemaphoreType.DMA

    def at(r, c):
        return r * cols + c

    def swap(value):
        return lax.ppermute(value, "leaf", [(0, 1), (1, 0)])

    def along_row(value, step):
        return lax.ppermute(value, "row", [(r, r ^ step) for r in range(rows)])

    def along_col(value, pairs):
        rest = [a for a in range(cols) if a not in [p[0] for p in pairs]]
        open_ends = [b for b in range(cols) if b not in [p[1] for p in pairs]]
        return lax.ppermute(value, "col", pairs + list(zip(rest, open_ends)))

    def filled(pairs):
        for k in range(rows):
            here = [at(k, z) + leaf * shift for leaf in (0, 1) for z in range(cols)]
            rest = [a for a in here if a not in [p[0] for p in pairs]]
            ends = [b for b in here if b not in [p[1] for p in pairs]]
            for a in sorted(rest, key=lambda a: a not in ends):
                b = min(ends, key=lambda b: (a != b, abs(a % cols - b % cols)))
                ends.remove(b)
                pairs = pairs + [(a, b)]
        return pairs

    def everywhere(value, pairs):
        return lax.ppermute(value, ("leaf", "row", "col"), pairs)

    shift = rows * cols
    near = everywhere(
        top_factor,
        filled(
            [(at(k, 0), at(k, 1)) for k in (1, 2, 3)]
            + [(at(k, 1), at(k, 2)) for k in (2, 3)]
            + [(at(3, 2) + shift, at(3, 1) + shift)]
        ),
    )
    child_sol, keep, send = call(
        child_kernel,
        [live, child_rhs, child_diag, child_off, targets],
        [child_rhs.shape, (half, children * slots), (half + 8, children * slots)],
        [pltpu.SMEM(live.shape, jnp.int32), pltpu.VMEM(targets.shape, jnp.int32), child_rhs.shape,
         child_diag.shape, child_off.shape, child_rhs.shape, (right, children * slots), dma((5, max(2, children)))],
        outside=(0, 1, 2, 3, 4),
        outs_outside=(0,),
        pinned=(1, 2),
        limit=56,
    )
    sums = call(own_kernel, [keep, send], [(half, size)] * rows)
    sums = call(other_kernel, [swap(send)] + sums, [(half, size)] * rows)
    got = [along_row(sums[s], s) for s in (1, 2, 3)]
    rhs_piece, diag_high, diag_low = call(
        turn_kernel, [top_rhs, top_diag], [shape, block, block], [(half, size)]
    )
    diag = [diag_high, diag_low]
    first, second = call(pieces_kernel, [sums[0]] + got, [shape] * 2, [(half, size)], flops=10 ** 11)
    q = [
        along_col(second, [(0, 2), (3, 1)]),
        along_col(first, [(0, 1), (3, 2)]),
        along_col(first, [(1, 2), (2, 1)]),
    ]

    def chain(owner, ins, has_sums=False, solves=True, flops=0):
        outs = call(
            functools.partial(chain_kernel, owner, has_sums, solves), ins, [shape] * (1 + has_sums), flops=flops
        )
        return outs if has_sums else outs[0]

    res, x = chain(0, [rhs_piece, second] + q + diag, has_sums=True, flops=10 ** 10)
    on = everywhere(near, [(at(k, 1), at(k, 2) + shift) for k in (1, 2, 3)])
    factor = call(factor_kernel, [top_factor, near, swap(near), on, swap(on)], [block] * 6)
    factor = [factor[0:2], factor[2:4], factor[4:6]]
    to1 = along_row(x, 1)
    to2 = along_row(x, 2)
    x = chain(1, [res, x] + diag + [to1] + factor[0])
    on = along_row(x, 3)
    res = chain(2, [res, res, to2] + factor[0], solves=False)
    x = chain(2, [res, x] + diag + [on] + factor[1])
    to3 = along_row(x, 1)
    late = along_row(x, 2)
    res = chain(3, [res, res, on] + factor[0], solves=False)
    x = chain(3, [res, x] + diag + [late] + factor[1] + [to3] + factor[2])

    both = along_col(x, [(1, 2), (2, 1)])
    step = along_col(x, [(1, 0), (2, 3)])
    over = along_col(x, [(1, 3), (2, 0)])
    (own,) = call(half_kernel, [both, step, over, x], [(size, half)])
    (top_sol,) = call(
        functools.partial(write_kernel, True), [own], [top_rhs.shape], [dma(())], outs_outside=(0,)
    )
    (top_sol,) = call(
        functools.partial(write_kernel, False),
        [swap(own), top_sol],
        [top_rhs.shape],
        [dma(())],
        outside=(1,),
        outs_outside=(0,),
        aliases={1: 0},
    )
    return (child_sol, top_sol)


def solution(mesh):
    in_specs = (
        P(("leaf", "row", "col"), None, None),
        P(("leaf", "row", "col"), None, None),
        P(("leaf", "row", "col"), None, None),
        P(("leaf", "row", "col")),
        P(("leaf", "row", "col"), None),
        P("row", None),
        P("row", "col"),
        P("row", None),
    )
    out_specs = (P(("leaf", "row", "col"), None, None), P("row", None))
    axes = tuple(mesh.shape[a] for a in ("leaf", "row", "col"))

    def shards(*args):
        top_rhs, top_factor, top_diag = args[5:]
        size = top_diag.shape[1]
        fits = axes == (2, 4, 4) and top_rhs.shape[0] == size and top_factor.shape[1] == size
        return (central if fits else any_mesh)(*args)

    return jax.shard_map(shards, mesh=mesh, in_specs=in_specs, out_specs=out_specs, check_vma=False)
```

```python
import functools

import jax
import jax.numpy as jnp
from jax import lax
from jax.experimental import pallas as pl
from jax.experimental.pallas import tpu as pltpu
from jax.sharding import PartitionSpec as P

F32 = jnp.float32
BF16 = jnp.bfloat16
NT = (((1,), (1,)), ((), ()))
NN = (((1,), (0,)), ((), ()))
VM = pl.BlockSpec(memory_space=pltpu.VMEM)
ANY = pl.BlockSpec(memory_space=pl.ANY)
SM = pl.BlockSpec(memory_space=pltpu.SMEM)


def spread(value, axis, source):
    kept = jnp.where(lax.axis_index(axis) == source, value, 0).astype(value.dtype)
    return lax.psum(kept, axis)


def unit_lower(matrix):
    return jnp.tril(matrix) + jnp.eye(matrix.shape[-1], dtype=matrix.dtype)


def any_mesh(child_rhs, child_diag, child_off, live, targets, top_rhs, top_factor, top_diag):
    highest = lax.Precision.HIGHEST
    owned_rows = top_rhs.shape[0]
    right_count = top_rhs.shape[1]
    block_size = top_diag.shape[1]
    owned_blocks = owned_rows // block_size
    row_count = lax.axis_size("row")
    top_order = owned_rows * row_count
    col_width = top_factor.shape[1]
    my_row = lax.axis_index("row")
    my_col = lax.axis_index("col")
    child_sol = jnp.einsum("bij,bjr->bir", unit_lower(child_diag), child_rhs, precision=highest)
    tiles = jnp.einsum("btj,bjr->btr", child_off, child_sol, precision=highest)
    slot_index = jnp.arange(child_off.shape[1], dtype=jnp.int32)
    keep = slot_index[None, :] < live[:, None]
    tiles = jnp.where(keep[:, :, None], tiles, jnp.zeros_like(tiles))
    contrib = jnp.zeros((top_order, right_count), F32)
    contrib = contrib.at[targets.reshape(-1)].add(tiles.reshape(-1, right_count))
    row_part = lax.psum_scatter(contrib, "row", scatter_dimension=0, tiled=True)
    share = lax.psum_scatter(row_part, ("leaf", "col"), scatter_dimension=0, tiled=True)
    updates = lax.all_gather(share, ("leaf", "col"), axis=0, tiled=True)
    reduced = top_rhs - updates
    inverse_all = unit_lower(top_diag.reshape(owned_blocks, block_size, block_size))
    col_global = my_col * col_width + jnp.arange(col_width, dtype=jnp.int32)

    def step(block, solution):
        local = block % owned_blocks
        owner = block // owned_blocks
        factor_rows = jnp.where(
            (col_global < block * block_size)[None, :], top_factor, jnp.zeros_like(top_factor)
        )
        columns = lax.dynamic_slice_in_dim(solution, my_col * col_width, col_width, 0)
        partial_value = jnp.dot(
            factor_rows, columns, precision=highest, preferred_element_type=F32
        )
        block_inverse = lax.dynamic_index_in_dim(inverse_all, local, 0, keepdims=False)
        before = lax.psum(partial_value, "col")
        solved = jnp.dot(
            block_inverse, reduced - before, precision=highest, preferred_element_type=F32
        )
        solved = spread(solved, "row", owner)
        return lax.dynamic_update_slice_in_dim(solution, solved, block * block_size, 0)

    solution = lax.fori_loop(
        0, row_count * owned_blocks, step, jnp.zeros((top_order, right_count), F32)
    )
    top_sol = lax.dynamic_slice_in_dim(solution, my_row * owned_rows, owned_rows, 0)
    return (child_sol, top_sol)


def place():
    return tuple(lax.axis_index(a) for a in ("leaf", "row", "col"))


def split(value):
    high = value.astype(BF16)
    return high, (value - high.astype(F32)).astype(BF16)


def dot3(left, high, low, dims):
    left_high, left_low = split(left)
    rows = left.shape[0]
    both = lax.dot_general(
        jnp.concatenate([left_high, left_low], axis=0), high, dims, preferred_element_type=F32
    )
    cross = lax.dot_general(left_high, low, dims, preferred_element_type=F32)
    return both[:rows] + both[rows:] + cross


def lower(matrix):
    row = lax.broadcasted_iota(jnp.int32, matrix.shape, 0)
    col = lax.broadcasted_iota(jnp.int32, matrix.shape, 1)
    return jnp.where(col <= row, matrix, 0.0)


def turn_kernel(rhs_ref, diag_ref, out_ref, high_ref, low_ref, turned_ref):
    leaf, _, z = place()
    half, piece = turned_ref.shape[0], out_ref.shape[0]
    turned_ref[...] = rhs_ref[:, pl.ds(pl.multiple_of(leaf * half, half), half)].T
    out_ref[...] = turned_ref[pl.ds(pl.multiple_of((z // 2) * piece, piece), piece), :]
    high_ref[...], low_ref[...] = split(lower(diag_ref[...]).T)


def child_kernel(live_hbm, rhs_hbm, diag_hbm, off_hbm, tgt_hbm, sol_hbm, keep_ref, send_ref,
                 live_ref, tgt_ref, rhs_ref, diag_ref, off_ref, sol_ref, tiles_ref, sems):
    leaf, _, _ = place()
    children, slots = off_ref.shape[0], off_ref.shape[1]
    half = keep_ref.shape[0]
    pairs = ((rhs_hbm, rhs_ref), (diag_hbm, diag_ref), (off_hbm, off_ref))
    copies = [
        [pltpu.make_async_copy(source.at[s], target.at[s], sems.at[i, s]) for i, (source, target) in enumerate(pairs)]
        for s in range(children)
    ]
    back = [pltpu.make_async_copy(sol_ref.at[s], sol_hbm.at[s], sems.at[3, s]) for s in range(children)]
    small = [
        pltpu.make_async_copy(live_hbm, live_ref, sems.at[4, 0]),
        pltpu.make_async_copy(tgt_hbm, tgt_ref, sems.at[4, 1]),
    ]
    for s in range(children):
        for copy in copies[s]:
            copy.start()
    for copy in small:
        copy.start()
    for s in range(children):
        copies[s][0].wait()
        copies[s][1].wait()
        rhs = rhs_ref[s]
        sol = rhs + dot3(lower(diag_ref[s]), *split(rhs), NN)
        sol_ref[s] = sol
        back[s].start()
        copies[s][2].wait()
        if s == 0:
            for copy in small:
                copy.wait()
        tiles = dot3(sol.T, *split(off_ref[s]), NT)
        slot = lax.broadcasted_iota(jnp.int32, tiles.shape, 1)
        tiles_ref[:, s * slots:(s + 1) * slots] = jnp.where(slot < live_ref[s], tiles, 0.0)
        send_ref[half:half + 8, s * slots:(s + 1) * slots] = jnp.broadcast_to(
            tgt_ref[s:s + 1, :].astype(F32), (8, slots)
        )
    keep_ref[...] = tiles_ref[pl.ds(pl.multiple_of(leaf * half, half), half), :]
    send_ref[0:half, :] = tiles_ref[pl.ds(pl.multiple_of((1 - leaf) * half, half), half), :]
    for copy in back:
        copy.wait()


def scatter(value, target, size, start):
    index = lax.broadcasted_iota(jnp.int32, (size, value.shape[1]), 0) + start
    hot = jnp.where(index == target, 1.0, 0.0).astype(BF16)
    product = lax.dot_general(value, hot, NT, preferred_element_type=F32)
    half = value.shape[0] // 2
    return product[:half] + product[half:]


def own_kernel(keep_ref, send_ref, *out_refs):
    _, row, _ = place()
    half, size = out_refs[0].shape
    value = jnp.concatenate(split(keep_ref[...]), axis=0)
    target = send_ref[half:half + 1, :].astype(jnp.int32)
    for s, out_ref in enumerate(out_refs):
        out_ref[...] = scatter(value, target, size, jnp.bitwise_xor(row, s) * size)


def other_kernel(recv_ref, *refs):
    _, row, _ = place()
    own_refs, out_refs = refs[:4], refs[4:]
    half, size = out_refs[0].shape
    value = jnp.concatenate(split(recv_ref[0:half, :]), axis=0)
    target = recv_ref[half:half + 1, :].astype(jnp.int32)
    for s, (own_ref, out_ref) in enumerate(zip(own_refs, out_refs)):
        out_ref[...] = own_ref[...] + scatter(value, target, size, jnp.bitwise_xor(row, s) * size)


def pieces_kernel(a_ref, b_ref, c_ref, d_ref, first_ref, second_ref, sum_ref):
    _, _, z = place()
    odd = z % 2
    piece = first_ref.shape[0]
    sum_ref[...] = (a_ref[...] + b_ref[...]) + (c_ref[...] + d_ref[...])
    first_ref[...] = sum_ref[pl.ds(pl.multiple_of(odd * piece, piece), piece), :]
    second_ref[...] = sum_ref[pl.ds(pl.multiple_of((1 - odd) * piece, piece), piece), :]


def factor_kernel(own_ref, sent_ref, other_ref, diag_high_ref, diag_low_ref, *out_refs):
    leaf, row, z = place()
    for block in range(3):
        high_ref, low_ref = out_refs[2 * block], out_refs[2 * block + 1]

        @pl.when((row > block) & ((z == 1) | (z == 2)))
        def _():
            if block == 0:
                value = jnp.where((leaf == 0) == (z == 1), sent_ref[...], other_ref[...])
            else:
                sent = jnp.where((leaf == 0) == (block == 1), sent_ref[...], other_ref[...])
                value = jnp.where(z == block, own_ref[...], sent)
            value = value.T
            value = value + dot3(value, diag_high_ref[...], diag_low_ref[...], NN)
            high_ref[...], low_ref[...] = split(value)


def first_kernel(rhs_ref, a_ref, b_ref, c_ref, d_ref, high_ref, low_ref, out_ref):
    value = rhs_ref[...] - ((a_ref[...] + b_ref[...]) + (c_ref[...] + d_ref[...]))
    out_ref[...] = value + dot3(value, high_ref[...], low_ref[...], NN)


def chain_kernel(owner, given_ref, *refs):
    _, row, z = place()
    used, out_ref = refs[:-1], refs[-1]
    out_ref[...] = given_ref[...]

    @pl.when((row == owner) & ((z == 1) | (z == 2)))
    def _():
        left = given_ref[...]
        for i in range(0, len(used), 3):
            left = left - dot3(used[i][...], used[i + 1][...], used[i + 2][...], NN)
        out_ref[...] = left


def half_kernel(b_ref, a_ref, c_ref, x_ref, out_ref):
    _, _, z = place()
    x, a, b, c = x_ref[...], a_ref[...], b_ref[...], c_ref[...]
    low = jnp.where(z == 0, a, jnp.where(z == 1, x, jnp.where(z == 2, b, c)))
    high = jnp.where(z == 0, c, jnp.where(z == 1, b, jnp.where(z == 2, x, a)))
    out_ref[...] = jnp.concatenate([low, high], axis=0).T


def write_kernel(mine, part_ref, *refs):
    out_hbm, sem = refs[-2:]
    leaf, _, _ = place()
    half = part_ref.shape[1]
    at = leaf if mine else 1 - leaf
    copy = pltpu.make_async_copy(part_ref, out_hbm.at[:, pl.ds(pl.multiple_of(at * half, half), half)], sem)
    copy.start()
    copy.wait()


def call(kernel, ins, outs, scratch=(), outside=(), outs_outside=(), pinned=(), aliases=None, limit=24, flops=0):
    def spec(i, a):
        return ANY if i in outside else SM if a.ndim == 1 else VM

    def shape(i, out):
        dims, dtype = out if isinstance(out[0], tuple) else (out, F32)
        return pltpu.VMEM(dims, dtype) if i in pinned else jax.ShapeDtypeStruct(dims, dtype)

    outs = pl.pallas_call(
        kernel,
        out_shape=[shape(i, out) for i, out in enumerate(outs)],
        in_specs=[spec(i, a) for i, a in enumerate(ins)],
        out_specs=[ANY if i in outs_outside else VM for i in range(len(outs))],
        scratch_shapes=[pltpu.VMEM(s, F32) if isinstance(s, tuple) else s for s in scratch],
        input_output_aliases=aliases or {},
        cost_estimate=pl.CostEstimate(flops=flops, bytes_accessed=4 * sum(a.size for a in ins), transcendentals=0),
        compiler_params=pltpu.CompilerParams(vmem_limit_bytes=limit * 1024 * 1024),
    )(*ins)
    return list(outs)


def central(child_rhs, child_diag, child_off, live, targets, top_rhs, top_factor, top_diag):
    rows, cols = lax.axis_size("row"), lax.axis_size("col")
    size = top_diag.shape[1]
    right = top_rhs.shape[1]
    half, piece = right // 2, right // 4
    children, slots = targets.shape
    shape = (piece, size)
    block = ((size, size), BF16)
    dma = pltpu.SemaphoreType.DMA

    def at(r, c):
        return r * cols + c

    def swap(value):
        return lax.ppermute(value, "leaf", [(0, 1), (1, 0)])

    def along_row(value, step):
        return lax.ppermute(value, "row", [(r, r ^ step) for r in range(rows)])

    def along_col(value, pairs):
        rest = [a for a in range(cols) if a not in [p[0] for p in pairs]]
        open_ends = [b for b in range(cols) if b not in [p[1] for p in pairs]]
        return lax.ppermute(value, "col", pairs + list(zip(rest, open_ends)))

    near = [(at(k, 0), at(k, 1)) for k in (1, 2, 3)] + [(at(k, 1), at(k, 2)) for k in (2, 3)]
    far = [(at(k, 0), at(k, 2)) for k in (1, 2, 3)] + [(at(3, 2), at(3, 1))]
    shift = rows * cols
    pairs = near + [(a + shift, b + shift) for a, b in far]
    for k in range(2 * rows):
        here = range(k * cols, (k + 1) * cols)
        rest = [a for a in here if a not in [p[0] for p in pairs]]
        open_ends = [b for b in here if b not in [p[1] for p in pairs]]
        stay = [a for a in rest if a in open_ends]
        pairs = pairs + [(a, a) for a in stay]
        pairs = pairs + list(zip([a for a in rest if a not in stay], [b for b in open_ends if b not in stay]))
    sent = lax.ppermute(top_factor, ("leaf", "row", "col"), pairs)
    child_sol, keep, send = call(
        child_kernel,
        [live, child_rhs, child_diag, child_off, targets],
        [child_rhs.shape, (half, children * slots), (half + 8, children * slots)],
        [pltpu.SMEM(live.shape, jnp.int32), pltpu.VMEM(targets.shape, jnp.int32), child_rhs.shape,
         child_diag.shape, child_off.shape, child_rhs.shape, (right, children * slots), dma((5, max(2, children)))],
        outside=(0, 1, 2, 3, 4),
        outs_outside=(0,),
        pinned=(1, 2),
        limit=56,
    )
    sums = call(own_kernel, [keep, send], [(half, size)] * rows)
    sums = call(other_kernel, [swap(send)] + sums, [(half, size)] * rows)
    got = [along_row(sums[s], s) for s in (1, 2, 3)]
    rhs_piece, diag_high, diag_low = call(
        turn_kernel, [top_rhs, top_diag], [shape, block, block], [(half, size)]
    )
    diag = [diag_high, diag_low]
    first, second = call(pieces_kernel, [sums[0]] + got, [shape] * 2, [(half, size)])
    q = [
        along_col(second, [(0, 2), (3, 1)]),
        along_col(first, [(0, 1), (3, 2)]),
        along_col(first, [(1, 2), (2, 1)]),
    ]

    factor = call(factor_kernel, [top_factor, sent, swap(sent)] + diag, [block] * 6)
    factor = [factor[0:2], factor[2:4], factor[4:6]]

    def chain(owner, ins):
        (out,) = call(functools.partial(chain_kernel, owner), ins, [shape])
        return out

    (x,) = call(first_kernel, [rhs_piece, second] + q + diag, [shape], flops=10 ** 10)
    to1 = along_row(x, 1)
    to2 = along_row(x, 2)
    x = chain(1, [x, to1] + factor[0])
    on = along_row(x, 3)
    x = chain(2, [x, to2] + factor[0])
    x = chain(2, [x, on] + factor[1])
    to3 = along_row(x, 1)
    late = along_row(x, 2)
    x = chain(3, [x, on] + factor[0])
    x = chain(3, [x, late] + factor[1] + [to3] + factor[2])

    both = along_col(x, [(1, 2), (2, 1)])
    step = along_col(x, [(1, 0), (2, 3)])
    over = along_col(x, [(1, 3), (2, 0)])
    (own,) = call(half_kernel, [both, step, over, x], [(size, half)])
    (top_sol,) = call(
        functools.partial(write_kernel, True), [own], [top_rhs.shape], [dma(())], outs_outside=(0,)
    )
    (top_sol,) = call(
        functools.partial(write_kernel, False),
        [swap(own), top_sol],
        [top_rhs.shape],
        [dma(())],
        outside=(1,),
        outs_outside=(0,),
        aliases={1: 0},
    )
    return (child_sol, top_sol)


def solution(mesh):
    in_specs = (
        P(("leaf", "row", "col"), None, None),
        P(("leaf", "row", "col"), None, None),
        P(("leaf", "row", "col"), None, None),
        P(("leaf", "row", "col")),
        P(("leaf", "row", "col"), None),
        P("row", None),
        P("row", "col"),
        P("row", None),
    )
    out_specs = (P(("leaf", "row", "col"), None, None), P("row", None))
    axes = tuple(mesh.shape[a] for a in ("leaf", "row", "col"))

    def shards(*args):
        top_rhs, top_factor, top_diag = args[5:]
        size = top_diag.shape[1]
        fits = axes == (2, 4, 4) and top_rhs.shape[0] == size and top_factor.shape[1] == size
        return (central if fits else any_mesh)(*args)

    return jax.shard_map(shards, mesh=mesh, in_specs=in_specs, out_specs=out_specs, check_vma=False)
```

```python
import functools

import jax
import jax.numpy as jnp
from jax import lax
from jax.experimental import pallas as pl
from jax.experimental.pallas import tpu as pltpu
from jax.sharding import PartitionSpec as P

F32 = jnp.float32
BF16 = jnp.bfloat16
NT = (((1,), (1,)), ((), ()))
NN = (((1,), (0,)), ((), ()))
VM = pl.BlockSpec(memory_space=pltpu.VMEM)
ANY = pl.BlockSpec(memory_space=pl.ANY)
SM = pl.BlockSpec(memory_space=pltpu.SMEM)


def spread(value, axis, source):
    kept = jnp.where(lax.axis_index(axis) == source, value, 0).astype(value.dtype)
    return lax.psum(kept, axis)


def unit_lower(matrix):
    return jnp.tril(matrix) + jnp.eye(matrix.shape[-1], dtype=matrix.dtype)


def any_mesh(child_rhs, child_diag, child_off, live, targets, top_rhs, top_factor, top_diag):
    highest = lax.Precision.HIGHEST
    owned_rows = top_rhs.shape[0]
    right_count = top_rhs.shape[1]
    block_size = top_diag.shape[1]
    owned_blocks = owned_rows // block_size
    row_count = lax.axis_size("row")
    top_order = owned_rows * row_count
    col_width = top_factor.shape[1]
    my_row = lax.axis_index("row")
    my_col = lax.axis_index("col")
    child_sol = jnp.einsum("bij,bjr->bir", unit_lower(child_diag), child_rhs, precision=highest)
    tiles = jnp.einsum("btj,bjr->btr", child_off, child_sol, precision=highest)
    slot_index = jnp.arange(child_off.shape[1], dtype=jnp.int32)
    keep = slot_index[None, :] < live[:, None]
    tiles = jnp.where(keep[:, :, None], tiles, jnp.zeros_like(tiles))
    contrib = jnp.zeros((top_order, right_count), F32)
    contrib = contrib.at[targets.reshape(-1)].add(tiles.reshape(-1, right_count))
    row_part = lax.psum_scatter(contrib, "row", scatter_dimension=0, tiled=True)
    share = lax.psum_scatter(row_part, ("leaf", "col"), scatter_dimension=0, tiled=True)
    updates = lax.all_gather(share, ("leaf", "col"), axis=0, tiled=True)
    reduced = top_rhs - updates
    inverse_all = unit_lower(top_diag.reshape(owned_blocks, block_size, block_size))
    col_global = my_col * col_width + jnp.arange(col_width, dtype=jnp.int32)

    def step(block, solution):
        local = block % owned_blocks
        owner = block // owned_blocks
        factor_rows = jnp.where(
            (col_global < block * block_size)[None, :], top_factor, jnp.zeros_like(top_factor)
        )
        columns = lax.dynamic_slice_in_dim(solution, my_col * col_width, col_width, 0)
        partial_value = jnp.dot(
            factor_rows, columns, precision=highest, preferred_element_type=F32
        )
        block_inverse = lax.dynamic_index_in_dim(inverse_all, local, 0, keepdims=False)
        before = lax.psum(partial_value, "col")
        solved = jnp.dot(
            block_inverse, reduced - before, precision=highest, preferred_element_type=F32
        )
        solved = spread(solved, "row", owner)
        return lax.dynamic_update_slice_in_dim(solution, solved, block * block_size, 0)

    solution = lax.fori_loop(
        0, row_count * owned_blocks, step, jnp.zeros((top_order, right_count), F32)
    )
    top_sol = lax.dynamic_slice_in_dim(solution, my_row * owned_rows, owned_rows, 0)
    return (child_sol, top_sol)


def place():
    return tuple(lax.axis_index(a) for a in ("leaf", "row", "col"))


def split(value):
    high = value.astype(BF16)
    return high, (value - high.astype(F32)).astype(BF16)


def dot3(left, high, low, dims):
    left_high, left_low = split(left)
    rows = left.shape[0]
    both = lax.dot_general(
        jnp.concatenate([left_high, left_low], axis=0), high, dims, preferred_element_type=F32
    )
    cross = lax.dot_general(left_high, low, dims, preferred_element_type=F32)
    return both[:rows] + both[rows:] + cross


def lower(matrix):
    row = lax.broadcasted_iota(jnp.int32, matrix.shape, 0)
    col = lax.broadcasted_iota(jnp.int32, matrix.shape, 1)
    return jnp.where(col <= row, matrix, 0.0)


def turn_kernel(rhs_ref, diag_ref, out_ref, high_ref, low_ref, turned_ref):
    leaf, _, z = place()
    half, piece = turned_ref.shape[0], out_ref.shape[0]
    turned_ref[...] = rhs_ref[:, pl.ds(pl.multiple_of(leaf * half, half), half)].T
    out_ref[...] = turned_ref[pl.ds(pl.multiple_of((z // 2) * piece, piece), piece), :]
    high_ref[...], low_ref[...] = split(lower(diag_ref[...]).T)


def child_kernel(live_hbm, rhs_hbm, diag_hbm, off_hbm, tgt_hbm, sol_hbm, keep_ref, send_ref,
                 live_ref, tgt_ref, rhs_ref, diag_ref, off_ref, sol_ref, tiles_ref, sems):
    leaf, _, _ = place()
    children, slots = off_ref.shape[0], off_ref.shape[1]
    half = keep_ref.shape[0]
    pairs = ((rhs_hbm, rhs_ref), (diag_hbm, diag_ref), (off_hbm, off_ref))
    copies = [
        [pltpu.make_async_copy(source.at[s], target.at[s], sems.at[i, s]) for i, (source, target) in enumerate(pairs)]
        for s in range(children)
    ]
    back = [pltpu.make_async_copy(sol_ref.at[s], sol_hbm.at[s], sems.at[3, s]) for s in range(children)]
    small = [
        pltpu.make_async_copy(live_hbm, live_ref, sems.at[4, 0]),
        pltpu.make_async_copy(tgt_hbm, tgt_ref, sems.at[4, 1]),
    ]
    for s in range(children):
        for copy in copies[s]:
            copy.start()
    for copy in small:
        copy.start()
    for s in range(children):
        copies[s][0].wait()
        copies[s][1].wait()
        rhs = rhs_ref[s]
        sol = rhs + dot3(lower(diag_ref[s]), *split(rhs), NN)
        sol_ref[s] = sol
        back[s].start()
        copies[s][2].wait()
        if s == 0:
            for copy in small:
                copy.wait()
        tiles = dot3(sol.T, *split(off_ref[s]), NT)
        slot = lax.broadcasted_iota(jnp.int32, tiles.shape, 1)
        tiles_ref[:, s * slots:(s + 1) * slots] = jnp.where(slot < live_ref[s], tiles, 0.0)
        send_ref[half:half + 8, s * slots:(s + 1) * slots] = jnp.broadcast_to(
            tgt_ref[s:s + 1, :].astype(F32), (8, slots)
        )
    keep_ref[...] = tiles_ref[pl.ds(pl.multiple_of(leaf * half, half), half), :]
    send_ref[0:half, :] = tiles_ref[pl.ds(pl.multiple_of((1 - leaf) * half, half), half), :]
    for copy in back:
        copy.wait()


def scatter(value, target, size, start):
    index = lax.broadcasted_iota(jnp.int32, (size, value.shape[1]), 0) + start
    hot = jnp.where(index == target, 1.0, 0.0).astype(BF16)
    product = lax.dot_general(value, hot, NT, preferred_element_type=F32)
    half = value.shape[0] // 2
    return product[:half] + product[half:]


def own_kernel(keep_ref, send_ref, *out_refs):
    _, row, _ = place()
    half, size = out_refs[0].shape
    value = jnp.concatenate(split(keep_ref[...]), axis=0)
    target = send_ref[half:half + 1, :].astype(jnp.int32)
    for s, out_ref in enumerate(out_refs):
        out_ref[...] = scatter(value, target, size, jnp.bitwise_xor(row, s) * size)


def other_kernel(recv_ref, *refs):
    _, row, _ = place()
    own_refs, out_refs = refs[:4], refs[4:]
    half, size = out_refs[0].shape
    value = jnp.concatenate(split(recv_ref[0:half, :]), axis=0)
    target = recv_ref[half:half + 1, :].astype(jnp.int32)
    for s, (own_ref, out_ref) in enumerate(zip(own_refs, out_refs)):
        out_ref[...] = own_ref[...] + scatter(value, target, size, jnp.bitwise_xor(row, s) * size)


def pieces_kernel(a_ref, b_ref, c_ref, d_ref, first_ref, second_ref, sum_ref):
    _, _, z = place()
    odd = z % 2
    piece = first_ref.shape[0]
    sum_ref[...] = (a_ref[...] + b_ref[...]) + (c_ref[...] + d_ref[...])
    first_ref[...] = sum_ref[pl.ds(pl.multiple_of(odd * piece, piece), piece), :]
    second_ref[...] = sum_ref[pl.ds(pl.multiple_of((1 - odd) * piece, piece), piece), :]


def factor_kernel(own_ref, sent_ref, other_ref, diag_high_ref, diag_low_ref, *out_refs):
    leaf, row, z = place()
    for block in range(3):
        high_ref, low_ref = out_refs[2 * block], out_refs[2 * block + 1]

        @pl.when((row > block) & ((z == 1) | (z == 2)))
        def _():
            if block == 0:
                value = jnp.where((leaf == 0) == (z == 1), sent_ref[...], other_ref[...])
            else:
                sent = jnp.where((leaf == 0) == (block == 1), sent_ref[...], other_ref[...])
                value = jnp.where(z == block, own_ref[...], sent)
            value = value.T
            value = value + dot3(value, diag_high_ref[...], diag_low_ref[...], NN)
            high_ref[...], low_ref[...] = split(value)


def first_kernel(rhs_ref, a_ref, b_ref, c_ref, d_ref, high_ref, low_ref, out_ref):
    value = rhs_ref[...] - ((a_ref[...] + b_ref[...]) + (c_ref[...] + d_ref[...]))
    out_ref[...] = value + dot3(value, high_ref[...], low_ref[...], NN)


def chain_kernel(owner, given_ref, *refs):
    _, row, z = place()
    used, out_ref = refs[:-1], refs[-1]
    out_ref[...] = given_ref[...]

    @pl.when((row == owner) & ((z == 1) | (z == 2)))
    def _():
        left = given_ref[...]
        for i in range(0, len(used), 3):
            left = left - dot3(used[i][...], used[i + 1][...], used[i + 2][...], NN)
        out_ref[...] = left


def half_kernel(b_ref, a_ref, c_ref, x_ref, out_ref):
    _, _, z = place()
    x, a, b, c = x_ref[...], a_ref[...], b_ref[...], c_ref[...]
    low = jnp.where(z == 0, a, jnp.where(z == 1, x, jnp.where(z == 2, b, c)))
    high = jnp.where(z == 0, c, jnp.where(z == 1, b, jnp.where(z == 2, x, a)))
    out_ref[...] = jnp.concatenate([low, high], axis=0).T


def write_kernel(mine, part_ref, *refs):
    out_hbm, sem = refs[-2:]
    leaf, _, _ = place()
    half = part_ref.shape[1]
    at = leaf if mine else 1 - leaf
    copy = pltpu.make_async_copy(part_ref, out_hbm.at[:, pl.ds(pl.multiple_of(at * half, half), half)], sem)
    copy.start()
    copy.wait()


def call(kernel, ins, outs, scratch=(), outside=(), outs_outside=(), pinned=(), aliases=None, limit=24, flops=0):
    def spec(i, a):
        return ANY if i in outside else SM if a.ndim == 1 else VM

    def shape(i, out):
        dims, dtype = out if isinstance(out[0], tuple) else (out, F32)
        return pltpu.VMEM(dims, dtype) if i in pinned else jax.ShapeDtypeStruct(dims, dtype)

    outs = pl.pallas_call(
        kernel,
        out_shape=[shape(i, out) for i, out in enumerate(outs)],
        in_specs=[spec(i, a) for i, a in enumerate(ins)],
        out_specs=[ANY if i in outs_outside else VM for i in range(len(outs))],
        scratch_shapes=[pltpu.VMEM(s, F32) if isinstance(s, tuple) else s for s in scratch],
        input_output_aliases=aliases or {},
        cost_estimate=pl.CostEstimate(flops=flops, bytes_accessed=4 * sum(a.size for a in ins), transcendentals=0),
        compiler_params=pltpu.CompilerParams(vmem_limit_bytes=limit * 1024 * 1024),
    )(*ins)
    return list(outs)


def central(child_rhs, child_diag, child_off, live, targets, top_rhs, top_factor, top_diag):
    rows, cols = lax.axis_size("row"), lax.axis_size("col")
    size = top_diag.shape[1]
    right = top_rhs.shape[1]
    half, piece = right // 2, right // 4
    children, slots = targets.shape
    shape = (piece, size)
    block = ((size, size), BF16)
    dma = pltpu.SemaphoreType.DMA

    def at(r, c):
        return r * cols + c

    def swap(value):
        return lax.ppermute(value, "leaf", [(0, 1), (1, 0)])

    def along_row(value, step):
        return lax.ppermute(value, "row", [(r, r ^ step) for r in range(rows)])

    def along_col(value, pairs):
        rest = [a for a in range(cols) if a not in [p[0] for p in pairs]]
        open_ends = [b for b in range(cols) if b not in [p[1] for p in pairs]]
        return lax.ppermute(value, "col", pairs + list(zip(rest, open_ends)))

    near = [(at(k, 0), at(k, 1)) for k in (1, 2, 3)] + [(at(k, 1), at(k, 2)) for k in (2, 3)]
    far = [(at(k, 0), at(k, 2)) for k in (1, 2, 3)] + [(at(3, 2), at(3, 1))]
    shift = rows * cols
    sent = lax.ppermute(
        top_factor, ("leaf", "row", "col"), near + [(a + shift, b + shift) for a, b in far]
    )
    child_sol, keep, send = call(
        child_kernel,
        [live, child_rhs, child_diag, child_off, targets],
        [child_rhs.shape, (half, children * slots), (half + 8, children * slots)],
        [pltpu.SMEM(live.shape, jnp.int32), pltpu.VMEM(targets.shape, jnp.int32), child_rhs.shape,
         child_diag.shape, child_off.shape, child_rhs.shape, (right, children * slots), dma((5, max(2, children)))],
        outside=(0, 1, 2, 3, 4),
        outs_outside=(0,),
        pinned=(1, 2),
        limit=56,
    )
    sums = call(own_kernel, [keep, send], [(half, size)] * rows)
    sums = call(other_kernel, [swap(send)] + sums, [(half, size)] * rows)
    got = [along_row(sums[s], s) for s in (1, 2, 3)]
    rhs_piece, diag_high, diag_low = call(
        turn_kernel, [top_rhs, top_diag], [shape, block, block], [(half, size)]
    )
    diag = [diag_high, diag_low]
    first, second = call(pieces_kernel, [sums[0]] + got, [shape] * 2, [(half, size)])
    q = [
        along_col(second, [(0, 2), (3, 1)]),
        along_col(first, [(0, 1), (3, 2)]),
        along_col(first, [(1, 2), (2, 1)]),
    ]

    factor = call(factor_kernel, [top_factor, sent, swap(sent)] + diag, [block] * 6)
    factor = [factor[0:2], factor[2:4], factor[4:6]]

    def chain(owner, ins):
        (out,) = call(functools.partial(chain_kernel, owner), ins, [shape])
        return out

    (x,) = call(first_kernel, [rhs_piece, second] + q + diag, [shape], flops=10 ** 10)
    to1 = along_row(x, 1)
    to2 = along_row(x, 2)
    x = chain(1, [x, to1] + factor[0])
    on = along_row(x, 3)
    x = chain(2, [x, to2] + factor[0])
    x = chain(2, [x, on] + factor[1])
    to3 = along_row(x, 1)
    late = along_row(x, 2)
    x = chain(3, [x, on] + factor[0])
    x = chain(3, [x, late] + factor[1] + [to3] + factor[2])

    both = along_col(x, [(1, 2), (2, 1)])
    step = along_col(x, [(1, 0), (2, 3)])
    over = along_col(x, [(1, 3), (2, 0)])
    (own,) = call(half_kernel, [both, step, over, x], [(size, half)])
    (top_sol,) = call(
        functools.partial(write_kernel, True), [own], [top_rhs.shape], [dma(())], outs_outside=(0,)
    )
    (top_sol,) = call(
        functools.partial(write_kernel, False),
        [swap(own), top_sol],
        [top_rhs.shape],
        [dma(())],
        outside=(1,),
        outs_outside=(0,),
        aliases={1: 0},
    )
    return (child_sol, top_sol)


def solution(mesh):
    in_specs = (
        P(("leaf", "row", "col"), None, None),
        P(("leaf", "row", "col"), None, None),
        P(("leaf", "row", "col"), None, None),
        P(("leaf", "row", "col")),
        P(("leaf", "row", "col"), None),
        P("row", None),
        P("row", "col"),
        P("row", None),
    )
    out_specs = (P(("leaf", "row", "col"), None, None), P("row", None))
    axes = tuple(mesh.shape[a] for a in ("leaf", "row", "col"))

    def shards(*args):
        top_rhs, top_factor, top_diag = args[5:]
        size = top_diag.shape[1]
        fits = axes == (2, 4, 4) and top_rhs.shape[0] == size and top_factor.shape[1] == size
        return (central if fits else any_mesh)(*args)

    return jax.shard_map(shards, mesh=mesh, in_specs=in_specs, out_specs=out_specs, check_vma=False)
```

```python
import functools

import jax
import jax.numpy as jnp
from jax import lax
from jax.experimental import pallas as pl
from jax.experimental.pallas import tpu as pltpu
from jax.sharding import PartitionSpec as P

F32 = jnp.float32
BF16 = jnp.bfloat16
NT = (((1,), (1,)), ((), ()))
NN = (((1,), (0,)), ((), ()))
VM = pl.BlockSpec(memory_space=pltpu.VMEM)
ANY = pl.BlockSpec(memory_space=pl.ANY)
SM = pl.BlockSpec(memory_space=pltpu.SMEM)


def spread(value, axis, source):
    kept = jnp.where(lax.axis_index(axis) == source, value, 0).astype(value.dtype)
    return lax.psum(kept, axis)


def unit_lower(matrix):
    return jnp.tril(matrix) + jnp.eye(matrix.shape[-1], dtype=matrix.dtype)


def any_mesh(child_rhs, child_diag, child_off, live, targets, top_rhs, top_factor, top_diag):
    highest = lax.Precision.HIGHEST
    owned_rows = top_rhs.shape[0]
    right_count = top_rhs.shape[1]
    block_size = top_diag.shape[1]
    owned_blocks = owned_rows // block_size
    row_count = lax.axis_size("row")
    top_order = owned_rows * row_count
    col_width = top_factor.shape[1]
    my_row = lax.axis_index("row")
    my_col = lax.axis_index("col")
    child_sol = jnp.einsum("bij,bjr->bir", unit_lower(child_diag), child_rhs, precision=highest)
    tiles = jnp.einsum("btj,bjr->btr", child_off, child_sol, precision=highest)
    slot_index = jnp.arange(child_off.shape[1], dtype=jnp.int32)
    keep = slot_index[None, :] < live[:, None]
    tiles = jnp.where(keep[:, :, None], tiles, jnp.zeros_like(tiles))
    contrib = jnp.zeros((top_order, right_count), F32)
    contrib = contrib.at[targets.reshape(-1)].add(tiles.reshape(-1, right_count))
    row_part = lax.psum_scatter(contrib, "row", scatter_dimension=0, tiled=True)
    share = lax.psum_scatter(row_part, ("leaf", "col"), scatter_dimension=0, tiled=True)
    updates = lax.all_gather(share, ("leaf", "col"), axis=0, tiled=True)
    reduced = top_rhs - updates
    inverse_all = unit_lower(top_diag.reshape(owned_blocks, block_size, block_size))
    col_global = my_col * col_width + jnp.arange(col_width, dtype=jnp.int32)

    def step(block, solution):
        local = block % owned_blocks
        owner = block // owned_blocks
        factor_rows = jnp.where(
            (col_global < block * block_size)[None, :], top_factor, jnp.zeros_like(top_factor)
        )
        columns = lax.dynamic_slice_in_dim(solution, my_col * col_width, col_width, 0)
        partial_value = jnp.dot(
            factor_rows, columns, precision=highest, preferred_element_type=F32
        )
        block_inverse = lax.dynamic_index_in_dim(inverse_all, local, 0, keepdims=False)
        before = lax.psum(partial_value, "col")
        solved = jnp.dot(
            block_inverse, reduced - before, precision=highest, preferred_element_type=F32
        )
        solved = spread(solved, "row", owner)
        return lax.dynamic_update_slice_in_dim(solution, solved, block * block_size, 0)

    solution = lax.fori_loop(
        0, row_count * owned_blocks, step, jnp.zeros((top_order, right_count), F32)
    )
    top_sol = lax.dynamic_slice_in_dim(solution, my_row * owned_rows, owned_rows, 0)
    return (child_sol, top_sol)


def place():
    return tuple(lax.axis_index(a) for a in ("leaf", "row", "col"))


def split(value):
    high = value.astype(BF16)
    return high, (value - high.astype(F32)).astype(BF16)


def dot3(left, high, low, dims):
    left_high, left_low = split(left)
    rows = left.shape[0]
    both = lax.dot_general(
        jnp.concatenate([left_high, left_low], axis=0), high, dims, preferred_element_type=F32
    )
    cross = lax.dot_general(left_high, low, dims, preferred_element_type=F32)
    return both[:rows] + both[rows:] + cross


def lower(matrix):
    row = lax.broadcasted_iota(jnp.int32, matrix.shape, 0)
    col = lax.broadcasted_iota(jnp.int32, matrix.shape, 1)
    return jnp.where(col <= row, matrix, 0.0)


def turn_kernel(rhs_ref, diag_ref, out_ref, high_ref, low_ref, turned_ref):
    leaf, _, z = place()
    half, piece = turned_ref.shape[0], out_ref.shape[0]
    turned_ref[...] = rhs_ref[:, pl.ds(pl.multiple_of(leaf * half, half), half)].T
    out_ref[...] = turned_ref[pl.ds(pl.multiple_of((z // 2) * piece, piece), piece), :]
    high_ref[...], low_ref[...] = split(lower(diag_ref[...]).T)


def child_kernel(live_hbm, rhs_hbm, diag_hbm, off_hbm, tgt_hbm, sol_hbm, keep_ref, send_ref,
                 live_ref, tgt_ref, rhs_ref, diag_ref, off_ref, sol_ref, tiles_ref, sems):
    leaf, _, _ = place()
    children, slots = off_ref.shape[0], off_ref.shape[1]
    half = keep_ref.shape[0]
    pairs = ((rhs_hbm, rhs_ref), (diag_hbm, diag_ref), (off_hbm, off_ref))
    copies = [
        [pltpu.make_async_copy(source.at[s], target.at[s], sems.at[i, s]) for i, (source, target) in enumerate(pairs)]
        for s in range(children)
    ]
    back = [pltpu.make_async_copy(sol_ref.at[s], sol_hbm.at[s], sems.at[3, s]) for s in range(children)]
    small = [
        pltpu.make_async_copy(live_hbm, live_ref, sems.at[4, 0]),
        pltpu.make_async_copy(tgt_hbm, tgt_ref, sems.at[4, 1]),
    ]
    for s in range(children):
        for copy in copies[s]:
            copy.start()
    for copy in small:
        copy.start()
    for s in range(children):
        copies[s][0].wait()
        copies[s][1].wait()
        rhs = rhs_ref[s]
        sol = rhs + dot3(lower(diag_ref[s]), *split(rhs), NN)
        sol_ref[s] = sol
        back[s].start()
        copies[s][2].wait()
        if s == 0:
            for copy in small:
                copy.wait()
        tiles = dot3(sol.T, *split(off_ref[s]), NT)
        slot = lax.broadcasted_iota(jnp.int32, tiles.shape, 1)
        tiles_ref[:, s * slots:(s + 1) * slots] = jnp.where(slot < live_ref[s], tiles, 0.0)
        send_ref[half:half + 8, s * slots:(s + 1) * slots] = jnp.broadcast_to(
            tgt_ref[s:s + 1, :].astype(F32), (8, slots)
        )
    keep_ref[...] = tiles_ref[pl.ds(pl.multiple_of(leaf * half, half), half), :]
    send_ref[0:half, :] = tiles_ref[pl.ds(pl.multiple_of((1 - leaf) * half, half), half), :]
    for copy in back:
        copy.wait()


def scatter(value, target, size, start):
    index = lax.broadcasted_iota(jnp.int32, (size, value.shape[1]), 0) + start
    hot = jnp.where(index == target, 1.0, 0.0).astype(BF16)
    product = lax.dot_general(value, hot, NT, preferred_element_type=F32)
    half = value.shape[0] // 2
    return product[:half] + product[half:]


def own_kernel(keep_ref, send_ref, *out_refs):
    _, row, _ = place()
    half, size = out_refs[0].shape
    value = jnp.concatenate(split(keep_ref[...]), axis=0)
    target = send_ref[half:half + 1, :].astype(jnp.int32)
    for s, out_ref in enumerate(out_refs):
        out_ref[...] = scatter(value, target, size, jnp.bitwise_xor(row, s) * size)


def other_kernel(recv_ref, *refs):
    _, row, _ = place()
    own_refs, out_refs = refs[:4], refs[4:]
    half, size = out_refs[0].shape
    value = jnp.concatenate(split(recv_ref[0:half, :]), axis=0)
    target = recv_ref[half:half + 1, :].astype(jnp.int32)
    for s, (own_ref, out_ref) in enumerate(zip(own_refs, out_refs)):
        out_ref[...] = own_ref[...] + scatter(value, target, size, jnp.bitwise_xor(row, s) * size)


def pieces_kernel(a_ref, b_ref, c_ref, d_ref, first_ref, second_ref, sum_ref):
    _, _, z = place()
    odd = z % 2
    piece = first_ref.shape[0]
    sum_ref[...] = (a_ref[...] + b_ref[...]) + (c_ref[...] + d_ref[...])
    first_ref[...] = sum_ref[pl.ds(pl.multiple_of(odd * piece, piece), piece), :]
    second_ref[...] = sum_ref[pl.ds(pl.multiple_of((1 - odd) * piece, piece), piece), :]


def factor_kernel(own_ref, sent_ref, other_ref, diag_high_ref, diag_low_ref, *out_refs):
    leaf, row, z = place()
    for block in range(3):
        high_ref, low_ref = out_refs[2 * block], out_refs[2 * block + 1]

        @pl.when((row > block) & ((z == 1) | (z == 2)))
        def _():
            if block == 0:
                value = jnp.where((leaf == 0) == (z == 1), sent_ref[...], other_ref[...])
            else:
                sent = jnp.where((leaf == 0) == (block == 1), sent_ref[...], other_ref[...])
                value = jnp.where(z == block, own_ref[...], sent)
            value = value.T
            value = value + dot3(value, diag_high_ref[...], diag_low_ref[...], NN)
            high_ref[...], low_ref[...] = split(value)


def first_kernel(rhs_ref, a_ref, b_ref, c_ref, d_ref, high_ref, low_ref, out_ref):
    value = rhs_ref[...] - ((a_ref[...] + b_ref[...]) + (c_ref[...] + d_ref[...]))
    out_ref[...] = value + dot3(value, high_ref[...], low_ref[...], NN)


def chain_kernel(owner, given_ref, *refs):
    _, row, z = place()
    used, out_ref = refs[:-1], refs[-1]
    out_ref[...] = given_ref[...]

    @pl.when((row == owner) & ((z == 1) | (z == 2)))
    def _():
        left = given_ref[...]
        for i in range(0, len(used), 3):
            left = left - dot3(used[i][...], used[i + 1][...], used[i + 2][...], NN)
        out_ref[...] = left


def half_kernel(a_ref, b_ref, c_ref, x_ref, out_ref):
    _, _, z = place()
    x, a, b, c = x_ref[...], a_ref[...], b_ref[...], c_ref[...]
    low = jnp.where(z == 0, a, jnp.where(z == 1, x, jnp.where(z == 2, b, c)))
    high = jnp.where(z == 0, c, jnp.where(z == 1, b, jnp.where(z == 2, x, a)))
    out_ref[...] = jnp.concatenate([low, high], axis=0).T


def write_kernel(mine, part_ref, *refs):
    out_hbm, sem = refs[-2:]
    leaf, _, _ = place()
    half = part_ref.shape[1]
    at = leaf if mine else 1 - leaf
    copy = pltpu.make_async_copy(part_ref, out_hbm.at[:, pl.ds(pl.multiple_of(at * half, half), half)], sem)
    copy.start()
    copy.wait()


def call(kernel, ins, outs, scratch=(), outside=(), outs_outside=(), pinned=(), aliases=None, limit=24, flops=0):
    def spec(i, a):
        return ANY if i in outside else SM if a.ndim == 1 else VM

    def shape(i, out):
        dims, dtype = out if isinstance(out[0], tuple) else (out, F32)
        return pltpu.VMEM(dims, dtype) if i in pinned else jax.ShapeDtypeStruct(dims, dtype)

    outs = pl.pallas_call(
        kernel,
        out_shape=[shape(i, out) for i, out in enumerate(outs)],
        in_specs=[spec(i, a) for i, a in enumerate(ins)],
        out_specs=[ANY if i in outs_outside else VM for i in range(len(outs))],
        scratch_shapes=[pltpu.VMEM(s, F32) if isinstance(s, tuple) else s for s in scratch],
        input_output_aliases=aliases or {},
        cost_estimate=pl.CostEstimate(flops=flops, bytes_accessed=4 * sum(a.size for a in ins), transcendentals=0),
        compiler_params=pltpu.CompilerParams(vmem_limit_bytes=limit * 1024 * 1024),
    )(*ins)
    return list(outs)


def central(child_rhs, child_diag, child_off, live, targets, top_rhs, top_factor, top_diag):
    rows, cols = lax.axis_size("row"), lax.axis_size("col")
    size = top_diag.shape[1]
    right = top_rhs.shape[1]
    half, piece = right // 2, right // 4
    children, slots = targets.shape
    shape = (piece, size)
    block = ((size, size), BF16)
    dma = pltpu.SemaphoreType.DMA

    def at(r, c):
        return r * cols + c

    def swap(value):
        return lax.ppermute(value, "leaf", [(0, 1), (1, 0)])

    def along_row(value, step):
        return lax.ppermute(value, "row", [(r, r ^ step) for r in range(rows)])

    def along_col(value, pairs):
        rest = [a for a in range(cols) if a not in [p[0] for p in pairs]]
        open_ends = [b for b in range(cols) if b not in [p[1] for p in pairs]]
        return lax.ppermute(value, "col", pairs + list(zip(rest, open_ends)))

    near = [(at(k, 0), at(k, 1)) for k in (1, 2, 3)] + [(at(k, 1), at(k, 2)) for k in (2, 3)]
    far = [(at(k, 0), at(k, 2)) for k in (1, 2, 3)] + [(at(3, 2), at(3, 1))]
    shift = rows * cols
    sent = lax.ppermute(
        top_factor, ("leaf", "row", "col"), near + [(a + shift, b + shift) for a, b in far]
    )
    child_sol, keep, send = call(
        child_kernel,
        [live, child_rhs, child_diag, child_off, targets],
        [child_rhs.shape, (half, children * slots), (half + 8, children * slots)],
        [pltpu.SMEM(live.shape, jnp.int32), pltpu.VMEM(targets.shape, jnp.int32), child_rhs.shape,
         child_diag.shape, child_off.shape, child_rhs.shape, (right, children * slots), dma((5, max(2, children)))],
        outside=(0, 1, 2, 3, 4),
        outs_outside=(0,),
        pinned=(1, 2),
        limit=56,
    )
    sums = call(own_kernel, [keep, send], [(half, size)] * rows)
    sums = call(other_kernel, [swap(send)] + sums, [(half, size)] * rows)
    got = [along_row(sums[s], s) for s in (3, 1, 2)]
    rhs_piece, diag_high, diag_low = call(
        turn_kernel, [top_rhs, top_diag], [shape, block, block], [(half, size)]
    )
    diag = [diag_high, diag_low]
    first, second = call(pieces_kernel, [sums[0]] + got, [shape] * 2, [(half, size)])
    q = [
        along_col(second, [(0, 2), (3, 1)]),
        along_col(first, [(0, 1), (3, 2)]),
        along_col(first, [(1, 2), (2, 1)]),
    ]

    factor = call(factor_kernel, [top_factor, sent, swap(sent)] + diag, [block] * 6)
    factor = [factor[0:2], factor[2:4], factor[4:6]]

    def chain(owner, ins):
        (out,) = call(functools.partial(chain_kernel, owner), ins, [shape])
        return out

    (x,) = call(first_kernel, [rhs_piece, second] + q + diag, [shape], flops=10 ** 10)
    to1 = along_row(x, 1)
    to2 = along_row(x, 2)
    x = chain(1, [x, to1] + factor[0])
    on = along_row(x, 3)
    x = chain(2, [x, to2] + factor[0])
    x = chain(2, [x, on] + factor[1])
    to3 = along_row(x, 1)
    late = along_row(x, 2)
    x = chain(3, [x, on] + factor[0])
    x = chain(3, [x, late] + factor[1] + [to3] + factor[2])

    both = along_col(x, [(1, 2), (2, 1)])
    step = along_col(x, [(1, 0), (2, 3)])
    over = along_col(x, [(1, 3), (2, 0)])
    (own,) = call(half_kernel, [step, both, over, x], [(size, half)])
    (top_sol,) = call(
        functools.partial(write_kernel, True), [own], [top_rhs.shape], [dma(())], outs_outside=(0,)
    )
    (top_sol,) = call(
        functools.partial(write_kernel, False),
        [swap(own), top_sol],
        [top_rhs.shape],
        [dma(())],
        outside=(1,),
        outs_outside=(0,),
        aliases={1: 0},
    )
    return (child_sol, top_sol)


def solution(mesh):
    in_specs = (
        P(("leaf", "row", "col"), None, None),
        P(("leaf", "row", "col"), None, None),
        P(("leaf", "row", "col"), None, None),
        P(("leaf", "row", "col")),
        P(("leaf", "row", "col"), None),
        P("row", None),
        P("row", "col"),
        P("row", None),
    )
    out_specs = (P(("leaf", "row", "col"), None, None), P("row", None))
    axes = tuple(mesh.shape[a] for a in ("leaf", "row", "col"))

    def shards(*args):
        top_rhs, top_factor, top_diag = args[5:]
        size = top_diag.shape[1]
        fits = axes == (2, 4, 4) and top_rhs.shape[0] == size and top_factor.shape[1] == size
        return (central if fits else any_mesh)(*args)

    return jax.shard_map(shards, mesh=mesh, in_specs=in_specs, out_specs=out_specs, check_vma=False)
```

```python
import functools

import jax
import jax.numpy as jnp
from jax import lax
from jax.experimental import pallas as pl
from jax.experimental.pallas import tpu as pltpu
from jax.sharding import PartitionSpec as P

F32 = jnp.float32
BF16 = jnp.bfloat16
NT = (((1,), (1,)), ((), ()))
NN = (((1,), (0,)), ((), ()))
VM = pl.BlockSpec(memory_space=pltpu.VMEM)
ANY = pl.BlockSpec(memory_space=pl.ANY)
SM = pl.BlockSpec(memory_space=pltpu.SMEM)


def spread(value, axis, source):
    kept = jnp.where(lax.axis_index(axis) == source, value, 0).astype(value.dtype)
    return lax.psum(kept, axis)


def unit_lower(matrix):
    return jnp.tril(matrix) + jnp.eye(matrix.shape[-1], dtype=matrix.dtype)


def any_mesh(child_rhs, child_diag, child_off, live, targets, top_rhs, top_factor, top_diag):
    highest = lax.Precision.HIGHEST
    owned_rows = top_rhs.shape[0]
    right_count = top_rhs.shape[1]
    block_size = top_diag.shape[1]
    owned_blocks = owned_rows // block_size
    row_count = lax.axis_size("row")
    top_order = owned_rows * row_count
    col_width = top_factor.shape[1]
    my_row = lax.axis_index("row")
    my_col = lax.axis_index("col")
    child_sol = jnp.einsum("bij,bjr->bir", unit_lower(child_diag), child_rhs, precision=highest)
    tiles = jnp.einsum("btj,bjr->btr", child_off, child_sol, precision=highest)
    slot_index = jnp.arange(child_off.shape[1], dtype=jnp.int32)
    keep = slot_index[None, :] < live[:, None]
    tiles = jnp.where(keep[:, :, None], tiles, jnp.zeros_like(tiles))
    contrib = jnp.zeros((top_order, right_count), F32)
    contrib = contrib.at[targets.reshape(-1)].add(tiles.reshape(-1, right_count))
    row_part = lax.psum_scatter(contrib, "row", scatter_dimension=0, tiled=True)
    share = lax.psum_scatter(row_part, ("leaf", "col"), scatter_dimension=0, tiled=True)
    updates = lax.all_gather(share, ("leaf", "col"), axis=0, tiled=True)
    reduced = top_rhs - updates
    inverse_all = unit_lower(top_diag.reshape(owned_blocks, block_size, block_size))
    col_global = my_col * col_width + jnp.arange(col_width, dtype=jnp.int32)

    def step(block, solution):
        local = block % owned_blocks
        owner = block // owned_blocks
        factor_rows = jnp.where(
            (col_global < block * block_size)[None, :], top_factor, jnp.zeros_like(top_factor)
        )
        columns = lax.dynamic_slice_in_dim(solution, my_col * col_width, col_width, 0)
        partial_value = jnp.dot(
            factor_rows, columns, precision=highest, preferred_element_type=F32
        )
        block_inverse = lax.dynamic_index_in_dim(inverse_all, local, 0, keepdims=False)
        before = lax.psum(partial_value, "col")
        solved = jnp.dot(
            block_inverse, reduced - before, precision=highest, preferred_element_type=F32
        )
        solved = spread(solved, "row", owner)
        return lax.dynamic_update_slice_in_dim(solution, solved, block * block_size, 0)

    solution = lax.fori_loop(
        0, row_count * owned_blocks, step, jnp.zeros((top_order, right_count), F32)
    )
    top_sol = lax.dynamic_slice_in_dim(solution, my_row * owned_rows, owned_rows, 0)
    return (child_sol, top_sol)


def place():
    return tuple(lax.axis_index(a) for a in ("leaf", "row", "col"))


def split(value):
    high = value.astype(BF16)
    return high, (value - high.astype(F32)).astype(BF16)


def dot3(left, high, low, dims):
    left_high, left_low = split(left)
    rows = left.shape[0]
    both = lax.dot_general(
        jnp.concatenate([left_high, left_low], axis=0), high, dims, preferred_element_type=F32
    )
    cross = lax.dot_general(left_high, low, dims, preferred_element_type=F32)
    return both[:rows] + both[rows:] + cross


def lower(matrix):
    row = lax.broadcasted_iota(jnp.int32, matrix.shape, 0)
    col = lax.broadcasted_iota(jnp.int32, matrix.shape, 1)
    return jnp.where(col <= row, matrix, 0.0)


def turn_kernel(rhs_ref, diag_ref, out_ref, high_ref, low_ref, turned_ref):
    leaf, _, z = place()
    half, piece = turned_ref.shape[0], out_ref.shape[0]
    turned_ref[...] = rhs_ref[:, pl.ds(pl.multiple_of(leaf * half, half), half)].T
    out_ref[...] = turned_ref[pl.ds(pl.multiple_of((z // 2) * piece, piece), piece), :]
    high_ref[...], low_ref[...] = split(lower(diag_ref[...]).T)


def child_kernel(live_hbm, rhs_hbm, diag_hbm, off_hbm, tgt_hbm, sol_hbm, keep_ref, send_ref,
                 live_ref, tgt_ref, rhs_ref, diag_ref, off_ref, sol_ref, tiles_ref, sems):
    leaf, _, _ = place()
    children, slots = off_ref.shape[0], off_ref.shape[1]
    half = keep_ref.shape[0]
    pairs = ((rhs_hbm, rhs_ref), (diag_hbm, diag_ref), (off_hbm, off_ref))
    copies = [
        [pltpu.make_async_copy(source.at[s], target.at[s], sems.at[i, s]) for i, (source, target) in enumerate(pairs)]
        for s in range(children)
    ]
    back = [pltpu.make_async_copy(sol_ref.at[s], sol_hbm.at[s], sems.at[3, s]) for s in range(children)]
    small = [
        pltpu.make_async_copy(live_hbm, live_ref, sems.at[4, 0]),
        pltpu.make_async_copy(tgt_hbm, tgt_ref, sems.at[4, 1]),
    ]
    for s in range(children):
        for copy in copies[s]:
            copy.start()
    for copy in small:
        copy.start()
    for s in range(children):
        copies[s][0].wait()
        copies[s][1].wait()
        rhs = rhs_ref[s]
        sol = rhs + dot3(lower(diag_ref[s]), *split(rhs), NN)
        sol_ref[s] = sol
        back[s].start()
        copies[s][2].wait()
        if s == 0:
            for copy in small:
                copy.wait()
        tiles = dot3(sol.T, *split(off_ref[s]), NT)
        slot = lax.broadcasted_iota(jnp.int32, tiles.shape, 1)
        tiles_ref[:, s * slots:(s + 1) * slots] = jnp.where(slot < live_ref[s], tiles, 0.0)
        send_ref[half:half + 8, s * slots:(s + 1) * slots] = jnp.broadcast_to(
            tgt_ref[s:s + 1, :].astype(F32), (8, slots)
        )
    keep_ref[...] = tiles_ref[pl.ds(pl.multiple_of(leaf * half, half), half), :]
    send_ref[0:half, :] = tiles_ref[pl.ds(pl.multiple_of((1 - leaf) * half, half), half), :]
    for copy in back:
        copy.wait()


def scatter(value, target, size, start):
    index = lax.broadcasted_iota(jnp.int32, (size, value.shape[1]), 0) + start
    hot = jnp.where(index == target, 1.0, 0.0).astype(BF16)
    product = lax.dot_general(value, hot, NT, preferred_element_type=F32)
    half = value.shape[0] // 2
    return product[:half] + product[half:]


def own_kernel(keep_ref, send_ref, *out_refs):
    _, row, _ = place()
    half, size = out_refs[0].shape
    value = jnp.concatenate(split(keep_ref[...]), axis=0)
    target = send_ref[half:half + 1, :].astype(jnp.int32)
    for s, out_ref in enumerate(out_refs):
        out_ref[...] = scatter(value, target, size, jnp.bitwise_xor(row, s) * size)


def other_kernel(recv_ref, *refs):
    _, row, _ = place()
    own_refs, out_refs = refs[:4], refs[4:]
    half, size = out_refs[0].shape
    value = jnp.concatenate(split(recv_ref[0:half, :]), axis=0)
    target = recv_ref[half:half + 1, :].astype(jnp.int32)
    for s, (own_ref, out_ref) in enumerate(zip(own_refs, out_refs)):
        out_ref[...] = own_ref[...] + scatter(value, target, size, jnp.bitwise_xor(row, s) * size)


def pieces_kernel(a_ref, b_ref, c_ref, d_ref, first_ref, second_ref, sum_ref):
    _, _, z = place()
    odd = z % 2
    piece = first_ref.shape[0]
    sum_ref[...] = (a_ref[...] + b_ref[...]) + (c_ref[...] + d_ref[...])
    first_ref[...] = sum_ref[pl.ds(pl.multiple_of(odd * piece, piece), piece), :]
    second_ref[...] = sum_ref[pl.ds(pl.multiple_of((1 - odd) * piece, piece), piece), :]


def factor_kernel(own_ref, sent_ref, other_ref, diag_high_ref, diag_low_ref, *out_refs):
    leaf, row, z = place()
    for block in range(3):
        high_ref, low_ref = out_refs[2 * block], out_refs[2 * block + 1]

        @pl.when((row > block) & ((z == 1) | (z == 2)))
        def _():
            if block == 0:
                value = jnp.where((leaf == 0) == (z == 1), sent_ref[...], other_ref[...])
            else:
                sent = jnp.where((leaf == 0) == (block == 1), sent_ref[...], other_ref[...])
                value = jnp.where(z == block, own_ref[...], sent)
            value = value.T
            value = value + dot3(value, diag_high_ref[...], diag_low_ref[...], NN)
            high_ref[...], low_ref[...] = split(value)


def first_kernel(rhs_ref, a_ref, b_ref, c_ref, d_ref, high_ref, low_ref, out_ref):
    value = rhs_ref[...] - ((a_ref[...] + b_ref[...]) + (c_ref[...] + d_ref[...]))
    out_ref[...] = value + dot3(value, high_ref[...], low_ref[...], NN)


def chain_kernel(owner, given_ref, *refs):
    _, row, z = place()
    used, out_ref = refs[:-1], refs[-1]
    out_ref[...] = given_ref[...]

    @pl.when((row == owner) & ((z == 1) | (z == 2)))
    def _():
        left = given_ref[...]
        for i in range(0, len(used), 3):
            left = left - dot3(used[i][...], used[i + 1][...], used[i + 2][...], NN)
        out_ref[...] = left


def half_kernel(a_ref, b_ref, c_ref, x_ref, out_ref):
    _, _, z = place()
    x, a, b, c = x_ref[...], a_ref[...], b_ref[...], c_ref[...]
    low = jnp.where(z == 0, a, jnp.where(z == 1, x, jnp.where(z == 2, b, c)))
    high = jnp.where(z == 0, c, jnp.where(z == 1, b, jnp.where(z == 2, x, a)))
    out_ref[...] = jnp.concatenate([low, high], axis=0).T


def write_kernel(mine, part_ref, *refs):
    out_hbm, sem = refs[-2:]
    leaf, _, _ = place()
    half = part_ref.shape[1]
    at = leaf if mine else 1 - leaf
    copy = pltpu.make_async_copy(part_ref, out_hbm.at[:, pl.ds(pl.multiple_of(at * half, half), half)], sem)
    copy.start()
    copy.wait()


def call(kernel, ins, outs, scratch=(), outside=(), outs_outside=(), pinned=(), aliases=None, limit=24, flops=0):
    def spec(i, a):
        return ANY if i in outside else SM if a.ndim == 1 else VM

    def shape(i, out):
        dims, dtype = out if isinstance(out[0], tuple) else (out, F32)
        return pltpu.VMEM(dims, dtype) if i in pinned else jax.ShapeDtypeStruct(dims, dtype)

    outs = pl.pallas_call(
        kernel,
        out_shape=[shape(i, out) for i, out in enumerate(outs)],
        in_specs=[spec(i, a) for i, a in enumerate(ins)],
        out_specs=[ANY if i in outs_outside else VM for i in range(len(outs))],
        scratch_shapes=[pltpu.VMEM(s, F32) if isinstance(s, tuple) else s for s in scratch],
        input_output_aliases=aliases or {},
        cost_estimate=pl.CostEstimate(flops=flops, bytes_accessed=4 * sum(a.size for a in ins), transcendentals=0),
        compiler_params=pltpu.CompilerParams(vmem_limit_bytes=limit * 1024 * 1024),
    )(*ins)
    return list(outs)


def central(child_rhs, child_diag, child_off, live, targets, top_rhs, top_factor, top_diag):
    rows, cols = lax.axis_size("row"), lax.axis_size("col")
    size = top_diag.shape[1]
    right = top_rhs.shape[1]
    half, piece = right // 2, right // 4
    children, slots = targets.shape
    shape = (piece, size)
    block = ((size, size), BF16)
    dma = pltpu.SemaphoreType.DMA

    def at(r, c):
        return r * cols + c

    def swap(value):
        return lax.ppermute(value, "leaf", [(0, 1), (1, 0)])

    def along(axis, value, pairs):
        ends = range(lax.axis_size(axis))
        rest = [a for a in ends if a not in [p[0] for p in pairs]]
        open_ends = [b for b in ends if b not in [p[1] for p in pairs]]
        stay = [a for a in rest if a in open_ends]
        back = zip([a for a in rest if a not in stay], [b for b in open_ends if b not in stay])
        return lax.ppermute(value, axis, pairs + [(a, a) for a in stay] + list(back))

    def along_col(value, pairs):
        return along("col", value, pairs)

    def hop(value, pairs):
        return along("row", value, pairs)

    near = [(at(k, 0), at(k, 1)) for k in (1, 2, 3)] + [(at(k, 1), at(k, 2)) for k in (2, 3)]
    far = [(at(k, 0), at(k, 2)) for k in (1, 2, 3)] + [(at(3, 2), at(3, 1))]
    shift = rows * cols
    sent = lax.ppermute(
        top_factor, ("leaf", "row", "col"), near + [(a + shift, b + shift) for a, b in far]
    )
    child_sol, keep, send = call(
        child_kernel,
        [live, child_rhs, child_diag, child_off, targets],
        [child_rhs.shape, (half, children * slots), (half + 8, children * slots)],
        [pltpu.SMEM(live.shape, jnp.int32), pltpu.VMEM(targets.shape, jnp.int32), child_rhs.shape,
         child_diag.shape, child_off.shape, child_rhs.shape, (right, children * slots), dma((5, max(2, children)))],
        outside=(0, 1, 2, 3, 4),
        outs_outside=(0,),
        pinned=(1, 2),
        limit=56,
    )
    sums = call(own_kernel, [keep, send], [(half, size)] * rows)
    sums = call(other_kernel, [swap(send)] + sums, [(half, size)] * rows)
    got = [hop(sums[s], [(r, r ^ s) for r in range(rows)]) for s in (3, 1, 2)]
    rhs_piece, diag_high, diag_low = call(
        turn_kernel, [top_rhs, top_diag], [shape, block, block], [(half, size)]
    )
    diag = [diag_high, diag_low]
    first, second = call(pieces_kernel, [sums[0]] + got, [shape] * 2, [(half, size)])
    q = [
        along_col(first, [(0, 1), (3, 2)]),
        along_col(second, [(0, 2), (3, 1)]),
        along_col(first, [(1, 2), (2, 1)]),
    ]

    factor = call(factor_kernel, [top_factor, sent, swap(sent)] + diag, [block] * 6)
    factor = [factor[0:2], factor[2:4], factor[4:6]]

    def chain(owner, ins):
        (out,) = call(functools.partial(chain_kernel, owner), ins, [shape])
        return out

    (x,) = call(first_kernel, [rhs_piece, second] + q + diag, [shape], flops=10 ** 10)
    to1 = hop(x, [(0, 1)])
    to2 = hop(x, [(0, 2)])
    x = chain(1, [x, to1] + factor[0])
    on = hop(x, [(1, 2), (0, 3)])
    x = chain(2, [x, to2] + factor[0])
    x = chain(2, [x, on] + factor[1])
    to3 = hop(x, [(2, 3)])
    late = hop(x, [(1, 3)])
    x = chain(3, [x, on] + factor[0])
    x = chain(3, [x, late] + factor[1] + [to3] + factor[2])

    both = along_col(x, [(1, 2), (2, 1)])
    step = along_col(x, [(1, 0), (2, 3)])
    over = along_col(x, [(1, 3), (2, 0)])
    (own,) = call(half_kernel, [step, both, over, x], [(size, half)])
    (top_sol,) = call(
        functools.partial(write_kernel, True), [own], [top_rhs.shape], [dma(())], outs_outside=(0,)
    )
    (top_sol,) = call(
        functools.partial(write_kernel, False),
        [swap(own), top_sol],
        [top_rhs.shape],
        [dma(())],
        outside=(1,),
        outs_outside=(0,),
        aliases={1: 0},
    )
    return (child_sol, top_sol)


def solution(mesh):
    in_specs = (
        P(("leaf", "row", "col"), None, None),
        P(("leaf", "row", "col"), None, None),
        P(("leaf", "row", "col"), None, None),
        P(("leaf", "row", "col")),
        P(("leaf", "row", "col"), None),
        P("row", None),
        P("row", "col"),
        P("row", None),
    )
    out_specs = (P(("leaf", "row", "col"), None, None), P("row", None))
    axes = tuple(mesh.shape[a] for a in ("leaf", "row", "col"))

    def shards(*args):
        top_rhs, top_factor, top_diag = args[5:]
        size = top_diag.shape[1]
        fits = axes == (2, 4, 4) and top_rhs.shape[0] == size and top_factor.shape[1] == size
        return (central if fits else any_mesh)(*args)

    return jax.shard_map(shards, mesh=mesh, in_specs=in_specs, out_specs=out_specs, check_vma=False)
```

```python
import functools

import jax
import jax.numpy as jnp
from jax import lax
from jax.experimental import pallas as pl
from jax.experimental.pallas import tpu as pltpu
from jax.sharding import PartitionSpec as P

F32 = jnp.float32
BF16 = jnp.bfloat16
NT = (((1,), (1,)), ((), ()))
NN = (((1,), (0,)), ((), ()))
VM = pl.BlockSpec(memory_space=pltpu.VMEM)
ANY = pl.BlockSpec(memory_space=pl.ANY)
SM = pl.BlockSpec(memory_space=pltpu.SMEM)


def spread(value, axis, source):
    kept = jnp.where(lax.axis_index(axis) == source, value, 0).astype(value.dtype)
    return lax.psum(kept, axis)


def unit_lower(matrix):
    return jnp.tril(matrix) + jnp.eye(matrix.shape[-1], dtype=matrix.dtype)


def any_mesh(child_rhs, child_diag, child_off, live, targets, top_rhs, top_factor, top_diag):
    highest = lax.Precision.HIGHEST
    owned_rows = top_rhs.shape[0]
    right_count = top_rhs.shape[1]
    block_size = top_diag.shape[1]
    owned_blocks = owned_rows // block_size
    row_count = lax.axis_size("row")
    top_order = owned_rows * row_count
    col_width = top_factor.shape[1]
    my_row = lax.axis_index("row")
    my_col = lax.axis_index("col")
    child_sol = jnp.einsum("bij,bjr->bir", unit_lower(child_diag), child_rhs, precision=highest)
    tiles = jnp.einsum("btj,bjr->btr", child_off, child_sol, precision=highest)
    slot_index = jnp.arange(child_off.shape[1], dtype=jnp.int32)
    keep = slot_index[None, :] < live[:, None]
    tiles = jnp.where(keep[:, :, None], tiles, jnp.zeros_like(tiles))
    contrib = jnp.zeros((top_order, right_count), F32)
    contrib = contrib.at[targets.reshape(-1)].add(tiles.reshape(-1, right_count))
    row_part = lax.psum_scatter(contrib, "row", scatter_dimension=0, tiled=True)
    share = lax.psum_scatter(row_part, ("leaf", "col"), scatter_dimension=0, tiled=True)
    updates = lax.all_gather(share, ("leaf", "col"), axis=0, tiled=True)
    reduced = top_rhs - updates
    inverse_all = unit_lower(top_diag.reshape(owned_blocks, block_size, block_size))
    col_global = my_col * col_width + jnp.arange(col_width, dtype=jnp.int32)

    def step(block, solution):
        local = block % owned_blocks
        owner = block // owned_blocks
        factor_rows = jnp.where(
            (col_global < block * block_size)[None, :], top_factor, jnp.zeros_like(top_factor)
        )
        columns = lax.dynamic_slice_in_dim(solution, my_col * col_width, col_width, 0)
        partial_value = jnp.dot(
            factor_rows, columns, precision=highest, preferred_element_type=F32
        )
        block_inverse = lax.dynamic_index_in_dim(inverse_all, local, 0, keepdims=False)
        before = lax.psum(partial_value, "col")
        solved = jnp.dot(
            block_inverse, reduced - before, precision=highest, preferred_element_type=F32
        )
        solved = spread(solved, "row", owner)
        return lax.dynamic_update_slice_in_dim(solution, solved, block * block_size, 0)

    solution = lax.fori_loop(
        0, row_count * owned_blocks, step, jnp.zeros((top_order, right_count), F32)
    )
    top_sol = lax.dynamic_slice_in_dim(solution, my_row * owned_rows, owned_rows, 0)
    return (child_sol, top_sol)


def place():
    return tuple(lax.axis_index(a) for a in ("leaf", "row", "col"))


def split(value):
    high = value.astype(BF16)
    return high, (value - high.astype(F32)).astype(BF16)


def dot3(left, high, low, dims):
    left_high, left_low = split(left)
    rows = left.shape[0]
    both = lax.dot_general(
        jnp.concatenate([left_high, left_low], axis=0), high, dims, preferred_element_type=F32
    )
    cross = lax.dot_general(left_high, low, dims, preferred_element_type=F32)
    return both[:rows] + both[rows:] + cross


def lower(matrix):
    row = lax.broadcasted_iota(jnp.int32, matrix.shape, 0)
    col = lax.broadcasted_iota(jnp.int32, matrix.shape, 1)
    return jnp.where(col <= row, matrix, 0.0)


def turn_kernel(rhs_ref, diag_ref, out_ref, high_ref, low_ref, turned_ref):
    leaf, _, z = place()
    half, piece = turned_ref.shape[0], out_ref.shape[0]
    turned_ref[...] = rhs_ref[:, pl.ds(pl.multiple_of(leaf * half, half), half)].T
    out_ref[...] = turned_ref[pl.ds(pl.multiple_of((z // 2) * piece, piece), piece), :]
    high_ref[...], low_ref[...] = split(lower(diag_ref[...]).T)


def child_kernel(live_hbm, rhs_hbm, diag_hbm, off_hbm, tgt_hbm, sol_hbm, keep_ref, send_ref,
                 live_ref, tgt_ref, rhs_ref, diag_ref, off_ref, sol_ref, tiles_ref, sems):
    leaf, _, _ = place()
    children, slots = off_ref.shape[0], off_ref.shape[1]
    half = keep_ref.shape[0]
    pairs = ((rhs_hbm, rhs_ref), (diag_hbm, diag_ref), (off_hbm, off_ref))
    copies = [
        [pltpu.make_async_copy(source.at[s], target.at[s], sems.at[i, s]) for i, (source, target) in enumerate(pairs)]
        for s in range(children)
    ]
    back = [pltpu.make_async_copy(sol_ref.at[s], sol_hbm.at[s], sems.at[3, s]) for s in range(children)]
    small = [
        pltpu.make_async_copy(live_hbm, live_ref, sems.at[4, 0]),
        pltpu.make_async_copy(tgt_hbm, tgt_ref, sems.at[4, 1]),
    ]
    for s in range(children):
        for copy in copies[s]:
            copy.start()
    for copy in small:
        copy.start()
    for s in range(children):
        copies[s][0].wait()
        copies[s][1].wait()
        rhs = rhs_ref[s]
        sol = rhs + dot3(lower(diag_ref[s]), *split(rhs), NN)
        sol_ref[s] = sol
        back[s].start()
        copies[s][2].wait()
        if s == 0:
            for copy in small:
                copy.wait()
        tiles = dot3(sol.T, *split(off_ref[s]), NT)
        slot = lax.broadcasted_iota(jnp.int32, tiles.shape, 1)
        tiles_ref[:, s * slots:(s + 1) * slots] = jnp.where(slot < live_ref[s], tiles, 0.0)
        send_ref[half:half + 8, s * slots:(s + 1) * slots] = jnp.broadcast_to(
            tgt_ref[s:s + 1, :].astype(F32), (8, slots)
        )
    keep_ref[...] = tiles_ref[pl.ds(pl.multiple_of(leaf * half, half), half), :]
    send_ref[0:half, :] = tiles_ref[pl.ds(pl.multiple_of((1 - leaf) * half, half), half), :]
    for copy in back:
        copy.wait()


def scatter(value, target, size, start):
    index = lax.broadcasted_iota(jnp.int32, (size, value.shape[1]), 0) + start
    hot = jnp.where(index == target, 1.0, 0.0).astype(BF16)
    product = lax.dot_general(value, hot, NT, preferred_element_type=F32)
    half = value.shape[0] // 2
    return product[:half] + product[half:]


def own_kernel(keep_ref, send_ref, *out_refs):
    _, row, _ = place()
    half, size = out_refs[0].shape
    value = jnp.concatenate(split(keep_ref[...]), axis=0)
    target = send_ref[half:half + 1, :].astype(jnp.int32)
    for s, out_ref in enumerate(out_refs):
        out_ref[...] = scatter(value, target, size, jnp.bitwise_xor(row, s) * size)


def other_kernel(recv_ref, *refs):
    _, row, _ = place()
    own_refs, out_refs = refs[:4], refs[4:]
    half, size = out_refs[0].shape
    value = jnp.concatenate(split(recv_ref[0:half, :]), axis=0)
    target = recv_ref[half:half + 1, :].astype(jnp.int32)
    for s, (own_ref, out_ref) in enumerate(zip(own_refs, out_refs)):
        out_ref[...] = own_ref[...] + scatter(value, target, size, jnp.bitwise_xor(row, s) * size)


def pieces_kernel(a_ref, b_ref, c_ref, d_ref, first_ref, second_ref, sum_ref):
    _, _, z = place()
    odd = z % 2
    piece = first_ref.shape[0]
    sum_ref[...] = (a_ref[...] + b_ref[...]) + (c_ref[...] + d_ref[...])
    first_ref[...] = sum_ref[pl.ds(pl.multiple_of(odd * piece, piece), piece), :]
    second_ref[...] = sum_ref[pl.ds(pl.multiple_of((1 - odd) * piece, piece), piece), :]


def factor_kernel(own_ref, sent_ref, other_ref, diag_high_ref, diag_low_ref, *out_refs):
    leaf, row, z = place()
    for block in range(3):
        high_ref, low_ref = out_refs[2 * block], out_refs[2 * block + 1]

        @pl.when((row > block) & ((z == 1) | (z == 2)))
        def _():
            if block == 0:
                value = jnp.where((leaf == 0) == (z == 1), sent_ref[...], other_ref[...])
            else:
                sent = jnp.where((leaf == 0) == (block == 1), sent_ref[...], other_ref[...])
                value = jnp.where(z == block, own_ref[...], sent)
            value = value.T
            value = value + dot3(value, diag_high_ref[...], diag_low_ref[...], NN)
            high_ref[...], low_ref[...] = split(value)


def first_kernel(rhs_ref, a_ref, b_ref, c_ref, d_ref, high_ref, low_ref, all_ref, *out_refs):
    value = rhs_ref[...] - ((a_ref[...] + b_ref[...]) + (c_ref[...] + d_ref[...]))
    all_ref[...] = value + dot3(value, high_ref[...], low_ref[...], NN)
    rows = out_refs[0].shape[0]
    for i, out_ref in enumerate(out_refs):
        out_ref[...] = all_ref[i * rows:(i + 1) * rows, :]


def joined(refs):
    return jnp.concatenate([ref[...] for ref in refs], axis=0)


def side_kernel(owner, given_a_ref, given_b_ref, x_ref, high_ref, low_ref, *out_refs):
    _, row, z = place()
    rows = given_a_ref.shape[0]
    for given_ref, out_ref in zip((given_a_ref, given_b_ref), out_refs):
        out_ref[...] = given_ref[...]

    @pl.when((row == owner) & ((z == 1) | (z == 2)))
    def _():
        product = dot3(x_ref[...], high_ref[...], low_ref[...], NN)
        for i, out_ref in enumerate(out_refs):
            out_ref[...] = out_ref[...] - product[i * rows:(i + 1) * rows]


def join_kernel(given_a_ref, given_b_ref, *refs):
    _, row, z = place()
    out_ref = refs[-1]
    out_ref[...] = joined((given_a_ref, given_b_ref))

    @pl.when((row == 3) & ((z == 1) | (z == 2)))
    def _():
        left = joined((given_a_ref, given_b_ref))
        for i in range(0, len(refs) - 1, 4):
            left = left - dot3(joined(refs[i:i + 2]), refs[i + 2][...], refs[i + 3][...], NN)
        out_ref[...] = left


def chain_kernel(owner, given_ref, *refs):
    _, row, z = place()
    used, out_ref = refs[:-1], refs[-1]
    out_ref[...] = given_ref[...]

    @pl.when((row == owner) & ((z == 1) | (z == 2)))
    def _():
        left = given_ref[...]
        for i in range(0, len(used), 3):
            left = left - dot3(used[i][...], used[i + 1][...], used[i + 2][...], NN)
        out_ref[...] = left


def half_kernel(a_ref, b_ref, c_ref, x_ref, out_ref):
    _, _, z = place()
    x, a, b, c = x_ref[...], a_ref[...], b_ref[...], c_ref[...]
    low = jnp.where(z == 0, a, jnp.where(z == 1, x, jnp.where(z == 2, b, c)))
    high = jnp.where(z == 0, c, jnp.where(z == 1, b, jnp.where(z == 2, x, a)))
    out_ref[...] = jnp.concatenate([low, high], axis=0).T


def write_kernel(mine, part_ref, *refs):
    out_hbm, sem = refs[-2:]
    leaf, _, _ = place()
    half = part_ref.shape[1]
    at = leaf if mine else 1 - leaf
    copy = pltpu.make_async_copy(part_ref, out_hbm.at[:, pl.ds(pl.multiple_of(at * half, half), half)], sem)
    copy.start()
    copy.wait()


def call(kernel, ins, outs, scratch=(), outside=(), outs_outside=(), pinned=(), aliases=None, limit=24, flops=0):
    def spec(i, a):
        return ANY if i in outside else SM if a.ndim == 1 else VM

    def shape(i, out):
        dims, dtype = out if isinstance(out[0], tuple) else (out, F32)
        return pltpu.VMEM(dims, dtype) if i in pinned else jax.ShapeDtypeStruct(dims, dtype)

    outs = pl.pallas_call(
        kernel,
        out_shape=[shape(i, out) for i, out in enumerate(outs)],
        in_specs=[spec(i, a) for i, a in enumerate(ins)],
        out_specs=[ANY if i in outs_outside else VM for i in range(len(outs))],
        scratch_shapes=[pltpu.VMEM(s, F32) if isinstance(s, tuple) else s for s in scratch],
        input_output_aliases=aliases or {},
        cost_estimate=pl.CostEstimate(flops=flops, bytes_accessed=4 * sum(a.size for a in ins), transcendentals=0),
        compiler_params=pltpu.CompilerParams(vmem_limit_bytes=limit * 1024 * 1024),
    )(*ins)
    return list(outs)


def central(child_rhs, child_diag, child_off, live, targets, top_rhs, top_factor, top_diag):
    rows, cols = lax.axis_size("row"), lax.axis_size("col")
    size = top_diag.shape[1]
    right = top_rhs.shape[1]
    half, piece = right // 2, right // 4
    children, slots = targets.shape
    shape = (piece, size)
    block = ((size, size), BF16)
    dma = pltpu.SemaphoreType.DMA

    def at(r, c):
        return r * cols + c

    def swap(value):
        return lax.ppermute(value, "leaf", [(0, 1), (1, 0)])

    def along_row(value, step):
        return lax.ppermute(value, "row", [(r, r ^ step) for r in range(rows)])

    def along_col(value, pairs):
        rest = [a for a in range(cols) if a not in [p[0] for p in pairs]]
        open_ends = [b for b in range(cols) if b not in [p[1] for p in pairs]]
        return lax.ppermute(value, "col", pairs + list(zip(rest, open_ends)))

    near = [(at(k, 0), at(k, 1)) for k in (1, 2, 3)] + [(at(k, 1), at(k, 2)) for k in (2, 3)]
    far = [(at(k, 0), at(k, 2)) for k in (1, 2, 3)] + [(at(3, 2), at(3, 1))]
    shift = rows * cols
    sent = lax.ppermute(
        top_factor, ("leaf", "row", "col"), near + [(a + shift, b + shift) for a, b in far]
    )
    child_sol, keep, send = call(
        child_kernel,
        [live, child_rhs, child_diag, child_off, targets],
        [child_rhs.shape, (half, children * slots), (half + 8, children * slots)],
        [pltpu.SMEM(live.shape, jnp.int32), pltpu.VMEM(targets.shape, jnp.int32), child_rhs.shape,
         child_diag.shape, child_off.shape, child_rhs.shape, (right, children * slots), dma((5, max(2, children)))],
        outside=(0, 1, 2, 3, 4),
        outs_outside=(0,),
        pinned=(1, 2),
        limit=56,
    )
    sums = call(own_kernel, [keep, send], [(half, size)] * rows)
    sums = call(other_kernel, [swap(send)] + sums, [(half, size)] * rows)
    got = [along_row(sums[s], s) for s in (3, 1, 2)]
    rhs_piece, diag_high, diag_low = call(
        turn_kernel, [top_rhs, top_diag], [shape, block, block], [(half, size)]
    )
    diag = [diag_high, diag_low]
    first, second = call(pieces_kernel, [sums[0]] + got, [shape] * 2, [(half, size)])
    q = [
        along_col(second, [(0, 2), (3, 1)]),
        along_col(first, [(0, 1), (3, 2)]),
        along_col(first, [(1, 2), (2, 1)]),
    ]

    factor = call(factor_kernel, [top_factor, sent, swap(sent)] + diag, [block] * 6)
    factor = [factor[0:2], factor[2:4], factor[4:6]]

    part = (piece // 2, size)

    def chain(owner, ins):
        (out,) = call(functools.partial(chain_kernel, owner), ins, [part])
        return out

    x, *xs = call(first_kernel, [rhs_piece, second] + q + diag, [shape, part, part], flops=10 ** 10)
    to1 = [along_row(v, 1) for v in xs]
    to2 = along_row(x, 2)
    xs = [chain(1, [v, t] + factor[0]) for v, t in zip(xs, to1)]
    on = [along_row(v, 3) for v in xs]
    xs = call(functools.partial(side_kernel, 2), xs + [to2] + factor[0], [part, part])
    xs = [chain(2, [v, t] + factor[1]) for v, t in zip(xs, on)]
    to3 = [along_row(v, 1) for v in xs]
    late = [along_row(v, 2) for v in xs]
    xs = [chain(3, [v, t] + factor[0]) for v, t in zip(xs, on)]
    (x,) = call(join_kernel, xs + late + factor[1] + to3 + factor[2], [shape])

    both = along_col(x, [(1, 2), (2, 1)])
    step = along_col(x, [(1, 0), (2, 3)])
    over = along_col(x, [(1, 3), (2, 0)])
    (own,) = call(half_kernel, [step, both, over, x], [(size, half)])
    (top_sol,) = call(
        functools.partial(write_kernel, True), [own], [top_rhs.shape], [dma(())], outs_outside=(0,)
    )
    (top_sol,) = call(
        functools.partial(write_kernel, False),
        [swap(own), top_sol],
        [top_rhs.shape],
        [dma(())],
        outside=(1,),
        outs_outside=(0,),
        aliases={1: 0},
    )
    return (child_sol, top_sol)


def solution(mesh):
    in_specs = (
        P(("leaf", "row", "col"), None, None),
        P(("leaf", "row", "col"), None, None),
        P(("leaf", "row", "col"), None, None),
        P(("leaf", "row", "col")),
        P(("leaf", "row", "col"), None),
        P("row", None),
        P("row", "col"),
        P("row", None),
    )
    out_specs = (P(("leaf", "row", "col"), None, None), P("row", None))
    axes = tuple(mesh.shape[a] for a in ("leaf", "row", "col"))

    def shards(*args):
        top_rhs, top_factor, top_diag = args[5:]
        size = top_diag.shape[1]
        fits = axes == (2, 4, 4) and top_rhs.shape[0] == size and top_factor.shape[1] == size
        return (central if fits else any_mesh)(*args)

    return jax.shard_map(shards, mesh=mesh, in_specs=in_specs, out_specs=out_specs, check_vma=False)
```

```python
import functools

import jax
import jax.numpy as jnp
from jax import lax
from jax.experimental import pallas as pl
from jax.experimental.pallas import tpu as pltpu
from jax.sharding import PartitionSpec as P

F32 = jnp.float32
BF16 = jnp.bfloat16
NT = (((1,), (1,)), ((), ()))
NN = (((1,), (0,)), ((), ()))
VM = pl.BlockSpec(memory_space=pltpu.VMEM)
ANY = pl.BlockSpec(memory_space=pl.ANY)
SM = pl.BlockSpec(memory_space=pltpu.SMEM)


def spread(value, axis, source):
    kept = jnp.where(lax.axis_index(axis) == source, value, 0).astype(value.dtype)
    return lax.psum(kept, axis)


def unit_lower(matrix):
    return jnp.tril(matrix) + jnp.eye(matrix.shape[-1], dtype=matrix.dtype)


def any_mesh(child_rhs, child_diag, child_off, live, targets, top_rhs, top_factor, top_diag):
    highest = lax.Precision.HIGHEST
    owned_rows = top_rhs.shape[0]
    right_count = top_rhs.shape[1]
    block_size = top_diag.shape[1]
    owned_blocks = owned_rows // block_size
    row_count = lax.axis_size("row")
    top_order = owned_rows * row_count
    col_width = top_factor.shape[1]
    my_row = lax.axis_index("row")
    my_col = lax.axis_index("col")
    child_sol = jnp.einsum("bij,bjr->bir", unit_lower(child_diag), child_rhs, precision=highest)
    tiles = jnp.einsum("btj,bjr->btr", child_off, child_sol, precision=highest)
    slot_index = jnp.arange(child_off.shape[1], dtype=jnp.int32)
    keep = slot_index[None, :] < live[:, None]
    tiles = jnp.where(keep[:, :, None], tiles, jnp.zeros_like(tiles))
    contrib = jnp.zeros((top_order, right_count), F32)
    contrib = contrib.at[targets.reshape(-1)].add(tiles.reshape(-1, right_count))
    row_part = lax.psum_scatter(contrib, "row", scatter_dimension=0, tiled=True)
    share = lax.psum_scatter(row_part, ("leaf", "col"), scatter_dimension=0, tiled=True)
    updates = lax.all_gather(share, ("leaf", "col"), axis=0, tiled=True)
    reduced = top_rhs - updates
    inverse_all = unit_lower(top_diag.reshape(owned_blocks, block_size, block_size))
    col_global = my_col * col_width + jnp.arange(col_width, dtype=jnp.int32)

    def step(block, solution):
        local = block % owned_blocks
        owner = block // owned_blocks
        factor_rows = jnp.where(
            (col_global < block * block_size)[None, :], top_factor, jnp.zeros_like(top_factor)
        )
        columns = lax.dynamic_slice_in_dim(solution, my_col * col_width, col_width, 0)
        partial_value = jnp.dot(
            factor_rows, columns, precision=highest, preferred_element_type=F32
        )
        block_inverse = lax.dynamic_index_in_dim(inverse_all, local, 0, keepdims=False)
        before = lax.psum(partial_value, "col")
        solved = jnp.dot(
            block_inverse, reduced - before, precision=highest, preferred_element_type=F32
        )
        solved = spread(solved, "row", owner)
        return lax.dynamic_update_slice_in_dim(solution, solved, block * block_size, 0)

    solution = lax.fori_loop(
        0, row_count * owned_blocks, step, jnp.zeros((top_order, right_count), F32)
    )
    top_sol = lax.dynamic_slice_in_dim(solution, my_row * owned_rows, owned_rows, 0)
    return (child_sol, top_sol)


def place():
    return tuple(lax.axis_index(a) for a in ("leaf", "row", "col"))


def split(value):
    high = value.astype(BF16)
    return high, (value - high.astype(F32)).astype(BF16)


def dot3(left, high, low, dims):
    left_high, left_low = split(left)
    rows = left.shape[0]
    both = lax.dot_general(
        jnp.concatenate([left_high, left_low], axis=0), high, dims, preferred_element_type=F32
    )
    cross = lax.dot_general(left_high, low, dims, preferred_element_type=F32)
    return both[:rows] + both[rows:] + cross


def lower(matrix):
    row = lax.broadcasted_iota(jnp.int32, matrix.shape, 0)
    col = lax.broadcasted_iota(jnp.int32, matrix.shape, 1)
    return jnp.where(col <= row, matrix, 0.0)


def turn_kernel(rhs_ref, diag_ref, out_ref, high_ref, low_ref, turned_ref):
    leaf, _, z = place()
    half, piece = turned_ref.shape[0], out_ref.shape[0]
    turned_ref[...] = rhs_ref[:, pl.ds(pl.multiple_of(leaf * half, half), half)].T
    out_ref[...] = turned_ref[pl.ds(pl.multiple_of((z // 2) * piece, piece), piece), :]
    high_ref[...], low_ref[...] = split(lower(diag_ref[...]).T)


def child_kernel(live_hbm, rhs_hbm, diag_hbm, off_hbm, tgt_hbm, sol_hbm, keep_ref, send_ref,
                 live_ref, tgt_ref, rhs_ref, diag_ref, off_ref, sol_ref, tiles_ref, sems):
    leaf, _, _ = place()
    children, slots = off_ref.shape[0], off_ref.shape[1]
    half = keep_ref.shape[0]
    pairs = ((rhs_hbm, rhs_ref), (diag_hbm, diag_ref), (off_hbm, off_ref))
    copies = [
        [pltpu.make_async_copy(source.at[s], target.at[s], sems.at[i, s]) for i, (source, target) in enumerate(pairs)]
        for s in range(children)
    ]
    back = [pltpu.make_async_copy(sol_ref.at[s], sol_hbm.at[s], sems.at[3, s]) for s in range(children)]
    small = [
        pltpu.make_async_copy(live_hbm, live_ref, sems.at[4, 0]),
        pltpu.make_async_copy(tgt_hbm, tgt_ref, sems.at[4, 1]),
    ]
    for s in range(children):
        for copy in copies[s]:
            copy.start()
    for copy in small:
        copy.start()
    for s in range(children):
        copies[s][0].wait()
        copies[s][1].wait()
        rhs = rhs_ref[s]
        sol = rhs + dot3(lower(diag_ref[s]), *split(rhs), NN)
        sol_ref[s] = sol
        back[s].start()
        copies[s][2].wait()
        if s == 0:
            for copy in small:
                copy.wait()
        tiles = dot3(sol.T, *split(off_ref[s]), NT)
        slot = lax.broadcasted_iota(jnp.int32, tiles.shape, 1)
        tiles_ref[:, s * slots:(s + 1) * slots] = jnp.where(slot < live_ref[s], tiles, 0.0)
        send_ref[half:half + 8, s * slots:(s + 1) * slots] = jnp.broadcast_to(
            tgt_ref[s:s + 1, :].astype(F32), (8, slots)
        )
    keep_ref[...] = tiles_ref[pl.ds(pl.multiple_of(leaf * half, half), half), :]
    send_ref[0:half, :] = tiles_ref[pl.ds(pl.multiple_of((1 - leaf) * half, half), half), :]
    for copy in back:
        copy.wait()


def scatter(value, target, size, start):
    index = lax.broadcasted_iota(jnp.int32, (size, value.shape[1]), 0) + start
    hot = jnp.where(index == target, 1.0, 0.0).astype(BF16)
    product = lax.dot_general(value, hot, NT, preferred_element_type=F32)
    half = value.shape[0] // 2
    return product[:half] + product[half:]


def own_kernel(keep_ref, send_ref, *out_refs):
    _, row, _ = place()
    half, size = out_refs[0].shape
    value = jnp.concatenate(split(keep_ref[...]), axis=0)
    target = send_ref[half:half + 1, :].astype(jnp.int32)
    for s, out_ref in enumerate(out_refs):
        out_ref[...] = scatter(value, target, size, jnp.bitwise_xor(row, s) * size)


def other_kernel(recv_ref, *refs):
    _, row, _ = place()
    own_refs, out_refs = refs[:4], refs[4:]
    half, size = out_refs[0].shape
    value = jnp.concatenate(split(recv_ref[0:half, :]), axis=0)
    target = recv_ref[half:half + 1, :].astype(jnp.int32)
    for s, (own_ref, out_ref) in enumerate(zip(own_refs, out_refs)):
        out_ref[...] = own_ref[...] + scatter(value, target, size, jnp.bitwise_xor(row, s) * size)


def pieces_kernel(a_ref, b_ref, c_ref, d_ref, first_ref, second_ref, sum_ref):
    _, _, z = place()
    odd = z % 2
    piece = first_ref.shape[0]
    sum_ref[...] = (a_ref[...] + b_ref[...]) + (c_ref[...] + d_ref[...])
    first_ref[...] = sum_ref[pl.ds(pl.multiple_of(odd * piece, piece), piece), :]
    second_ref[...] = sum_ref[pl.ds(pl.multiple_of((1 - odd) * piece, piece), piece), :]


def factor_kernel(own_ref, sent_ref, other_ref, diag_high_ref, diag_low_ref, *out_refs):
    leaf, row, z = place()
    for block in range(3):
        high_ref, low_ref = out_refs[2 * block], out_refs[2 * block + 1]

        @pl.when((row > block) & ((z == 1) | (z == 2)))
        def _():
            if block == 0:
                value = jnp.where((leaf == 0) == (z == 1), sent_ref[...], other_ref[...])
            else:
                sent = jnp.where((leaf == 0) == (block == 1), sent_ref[...], other_ref[...])
                value = jnp.where(z == block, own_ref[...], sent)
            value = value.T
            value = value + dot3(value, diag_high_ref[...], diag_low_ref[...], NN)
            high_ref[...], low_ref[...] = split(value)


def first_kernel(rhs_ref, a_ref, b_ref, c_ref, d_ref, high_ref, low_ref, out_ref):
    value = rhs_ref[...] - ((a_ref[...] + b_ref[...]) + (c_ref[...] + d_ref[...]))
    out_ref[...] = value + dot3(value, high_ref[...], low_ref[...], NN)


def chain_kernel(owner, given_ref, *refs):
    _, row, z = place()
    used, out_ref = refs[:-1], refs[-1]
    out_ref[...] = given_ref[...]

    @pl.when((row == owner) & ((z == 1) | (z == 2)))
    def _():
        left = given_ref[...]
        for i in range(0, len(used), 3):
            left = left - dot3(used[i][...], used[i + 1][...], used[i + 2][...], NN)
        out_ref[...] = left


def half_kernel(a_ref, b_ref, c_ref, x_ref, out_ref):
    _, _, z = place()
    x, a, b, c = x_ref[...], a_ref[...], b_ref[...], c_ref[...]
    low = jnp.where(z == 0, a, jnp.where(z == 1, x, jnp.where(z == 2, b, c)))
    high = jnp.where(z == 0, c, jnp.where(z == 1, b, jnp.where(z == 2, x, a)))
    out_ref[...] = jnp.concatenate([low, high], axis=0).T


def write_kernel(mine, part_ref, *refs):
    out_hbm, sem = refs[-2:]
    leaf, _, _ = place()
    half = part_ref.shape[1]
    at = leaf if mine else 1 - leaf
    copy = pltpu.make_async_copy(part_ref, out_hbm.at[:, pl.ds(pl.multiple_of(at * half, half), half)], sem)
    copy.start()
    copy.wait()


def call(kernel, ins, outs, scratch=(), outside=(), outs_outside=(), pinned=(), aliases=None, limit=24, flops=0):
    def spec(i, a):
        return ANY if i in outside else SM if a.ndim == 1 else VM

    def shape(i, out):
        dims, dtype = out if isinstance(out[0], tuple) else (out, F32)
        return pltpu.VMEM(dims, dtype) if i in pinned else jax.ShapeDtypeStruct(dims, dtype)

    outs = pl.pallas_call(
        kernel,
        out_shape=[shape(i, out) for i, out in enumerate(outs)],
        in_specs=[spec(i, a) for i, a in enumerate(ins)],
        out_specs=[ANY if i in outs_outside else VM for i in range(len(outs))],
        scratch_shapes=[pltpu.VMEM(s, F32) if isinstance(s, tuple) else s for s in scratch],
        input_output_aliases=aliases or {},
        cost_estimate=pl.CostEstimate(flops=flops, bytes_accessed=4 * sum(a.size for a in ins), transcendentals=0),
        compiler_params=pltpu.CompilerParams(vmem_limit_bytes=limit * 1024 * 1024),
    )(*ins)
    return list(outs)


def central(child_rhs, child_diag, child_off, live, targets, top_rhs, top_factor, top_diag):
    rows, cols = lax.axis_size("row"), lax.axis_size("col")
    size = top_diag.shape[1]
    right = top_rhs.shape[1]
    half, piece = right // 2, right // 4
    children, slots = targets.shape
    shape = (piece, size)
    block = ((size, size), BF16)
    dma = pltpu.SemaphoreType.DMA

    def at(r, c):
        return r * cols + c

    def swap(value):
        return lax.ppermute(value, "leaf", [(0, 1), (1, 0)])

    def along_row(value, step):
        return lax.ppermute(value, "row", [(r, r ^ step) for r in range(rows)])

    def along_col(value, pairs):
        rest = [a for a in range(cols) if a not in [p[0] for p in pairs]]
        open_ends = [b for b in range(cols) if b not in [p[1] for p in pairs]]
        return lax.ppermute(value, "col", pairs + list(zip(rest, open_ends)))

    near = [(at(k, 0), at(k, 1)) for k in (1, 2, 3)] + [(at(k, 1), at(k, 2)) for k in (2, 3)]
    far = [(at(k, 0), at(k, 2)) for k in (1, 2, 3)] + [(at(3, 2), at(3, 1))]
    shift = rows * cols
    sent = lax.ppermute(
        top_factor, ("leaf", "row", "col"), near + [(a + shift, b + shift) for a, b in far]
    )
    child_sol, keep, send = call(
        child_kernel,
        [live, child_rhs, child_diag, child_off, targets],
        [child_rhs.shape, (half, children * slots), (half + 8, children * slots)],
        [pltpu.SMEM(live.shape, jnp.int32), pltpu.VMEM(targets.shape, jnp.int32), child_rhs.shape,
         child_diag.shape, child_off.shape, child_rhs.shape, (right, children * slots), dma((5, max(2, children)))],
        outside=(0, 1, 2, 3, 4),
        outs_outside=(0,),
        pinned=(1, 2),
        limit=56,
    )
    sums = call(own_kernel, [keep, send], [(half, size)] * rows)
    sums = call(other_kernel, [swap(send)] + sums, [(half, size)] * rows)
    got = [along_row(sums[s], s) for s in (3, 1, 2)]
    rhs_piece, diag_high, diag_low = call(
        turn_kernel, [top_rhs, top_diag], [shape, block, block], [(half, size)]
    )
    diag = [diag_high, diag_low]
    first, second = call(pieces_kernel, [sums[0]] + got, [shape] * 2, [(half, size)])
    q = [
        along_col(second, [(0, 2), (3, 1)]),
        along_col(first, [(0, 1), (3, 2)]),
        along_col(first, [(1, 2), (2, 1)]),
    ]

    factor = call(factor_kernel, [top_factor, sent, swap(sent)] + diag, [block] * 6)
    factor = [factor[0:2], factor[2:4], factor[4:6]]

    def chain(owner, ins):
        (out,) = call(functools.partial(chain_kernel, owner), ins, [shape])
        return out

    (x,) = call(first_kernel, [rhs_piece, second] + q + diag, [shape], flops=10 ** 10)
    to1 = along_row(x, 1)
    to2 = along_row(x, 2)
    x = chain(1, [x, to1] + factor[0])
    on = along_row(x, 3)
    x = chain(2, [x, to2] + factor[0])
    x = chain(2, [x, on] + factor[1])
    to3 = along_row(x, 1)
    late = lax.ppermute(x, "row", [(1, 3)])
    x = chain(3, [x, on] + factor[0])
    x = chain(3, [x, late] + factor[1] + [to3] + factor[2])

    both = along_col(x, [(1, 2), (2, 1)])
    step = along_col(x, [(1, 0), (2, 3)])
    over = along_col(x, [(1, 3), (2, 0)])
    (own,) = call(half_kernel, [step, both, over, x], [(size, half)])
    (top_sol,) = call(
        functools.partial(write_kernel, True), [own], [top_rhs.shape], [dma(())], outs_outside=(0,)
    )
    (top_sol,) = call(
        functools.partial(write_kernel, False),
        [swap(own), top_sol],
        [top_rhs.shape],
        [dma(())],
        outside=(1,),
        outs_outside=(0,),
        aliases={1: 0},
    )
    return (child_sol, top_sol)


def solution(mesh):
    in_specs = (
        P(("leaf", "row", "col"), None, None),
        P(("leaf", "row", "col"), None, None),
        P(("leaf", "row", "col"), None, None),
        P(("leaf", "row", "col")),
        P(("leaf", "row", "col"), None),
        P("row", None),
        P("row", "col"),
        P("row", None),
    )
    out_specs = (P(("leaf", "row", "col"), None, None), P("row", None))
    axes = tuple(mesh.shape[a] for a in ("leaf", "row", "col"))

    def shards(*args):
        top_rhs, top_factor, top_diag = args[5:]
        size = top_diag.shape[1]
        fits = axes == (2, 4, 4) and top_rhs.shape[0] == size and top_factor.shape[1] == size
        return (central if fits else any_mesh)(*args)

    return jax.shard_map(shards, mesh=mesh, in_specs=in_specs, out_specs=out_specs, check_vma=False)
```

```python
import functools

import jax
import jax.numpy as jnp
from jax import lax
from jax.experimental import pallas as pl
from jax.experimental.pallas import tpu as pltpu
from jax.sharding import PartitionSpec as P

F32 = jnp.float32
BF16 = jnp.bfloat16
NT = (((1,), (1,)), ((), ()))
NN = (((1,), (0,)), ((), ()))
VM = pl.BlockSpec(memory_space=pltpu.VMEM)
ANY = pl.BlockSpec(memory_space=pl.ANY)
SM = pl.BlockSpec(memory_space=pltpu.SMEM)


def spread(value, axis, source):
    kept = jnp.where(lax.axis_index(axis) == source, value, 0).astype(value.dtype)
    return lax.psum(kept, axis)


def unit_lower(matrix):
    return jnp.tril(matrix) + jnp.eye(matrix.shape[-1], dtype=matrix.dtype)


def any_mesh(child_rhs, child_diag, child_off, live, targets, top_rhs, top_factor, top_diag):
    highest = lax.Precision.HIGHEST
    owned_rows = top_rhs.shape[0]
    right_count = top_rhs.shape[1]
    block_size = top_diag.shape[1]
    owned_blocks = owned_rows // block_size
    row_count = lax.axis_size("row")
    top_order = owned_rows * row_count
    col_width = top_factor.shape[1]
    my_row = lax.axis_index("row")
    my_col = lax.axis_index("col")
    child_sol = jnp.einsum("bij,bjr->bir", unit_lower(child_diag), child_rhs, precision=highest)
    tiles = jnp.einsum("btj,bjr->btr", child_off, child_sol, precision=highest)
    slot_index = jnp.arange(child_off.shape[1], dtype=jnp.int32)
    keep = slot_index[None, :] < live[:, None]
    tiles = jnp.where(keep[:, :, None], tiles, jnp.zeros_like(tiles))
    contrib = jnp.zeros((top_order, right_count), F32)
    contrib = contrib.at[targets.reshape(-1)].add(tiles.reshape(-1, right_count))
    row_part = lax.psum_scatter(contrib, "row", scatter_dimension=0, tiled=True)
    share = lax.psum_scatter(row_part, ("leaf", "col"), scatter_dimension=0, tiled=True)
    updates = lax.all_gather(share, ("leaf", "col"), axis=0, tiled=True)
    reduced = top_rhs - updates
    inverse_all = unit_lower(top_diag.reshape(owned_blocks, block_size, block_size))
    col_global = my_col * col_width + jnp.arange(col_width, dtype=jnp.int32)

    def step(block, solution):
        local = block % owned_blocks
        owner = block // owned_blocks
        factor_rows = jnp.where(
            (col_global < block * block_size)[None, :], top_factor, jnp.zeros_like(top_factor)
        )
        columns = lax.dynamic_slice_in_dim(solution, my_col * col_width, col_width, 0)
        partial_value = jnp.dot(
            factor_rows, columns, precision=highest, preferred_element_type=F32
        )
        block_inverse = lax.dynamic_index_in_dim(inverse_all, local, 0, keepdims=False)
        before = lax.psum(partial_value, "col")
        solved = jnp.dot(
            block_inverse, reduced - before, precision=highest, preferred_element_type=F32
        )
        solved = spread(solved, "row", owner)
        return lax.dynamic_update_slice_in_dim(solution, solved, block * block_size, 0)

    solution = lax.fori_loop(
        0, row_count * owned_blocks, step, jnp.zeros((top_order, right_count), F32)
    )
    top_sol = lax.dynamic_slice_in_dim(solution, my_row * owned_rows, owned_rows, 0)
    return (child_sol, top_sol)


def place():
    return tuple(lax.axis_index(a) for a in ("leaf", "row", "col"))


def split(value):
    high = value.astype(BF16)
    return high, (value - high.astype(F32)).astype(BF16)


def dot3(left, high, low, dims):
    left_high, left_low = split(left)
    rows = left.shape[0]
    both = lax.dot_general(
        jnp.concatenate([left_high, left_low], axis=0), high, dims, preferred_element_type=F32
    )
    cross = lax.dot_general(left_high, low, dims, preferred_element_type=F32)
    return both[:rows] + both[rows:] + cross


def lower(matrix):
    row = lax.broadcasted_iota(jnp.int32, matrix.shape, 0)
    col = lax.broadcasted_iota(jnp.int32, matrix.shape, 1)
    return jnp.where(col <= row, matrix, 0.0)


def turn_kernel(rhs_ref, diag_ref, out_ref, high_ref, low_ref, turned_ref):
    leaf, _, z = place()
    half, piece = turned_ref.shape[0], out_ref.shape[0]
    turned_ref[...] = rhs_ref[:, pl.ds(pl.multiple_of(leaf * half, half), half)].T
    out_ref[...] = turned_ref[pl.ds(pl.multiple_of((z // 2) * piece, piece), piece), :]
    high_ref[...], low_ref[...] = split(lower(diag_ref[...]).T)


def child_kernel(live_hbm, rhs_hbm, diag_hbm, off_hbm, tgt_hbm, sol_hbm, keep_ref, send_ref,
                 live_ref, tgt_ref, rhs_ref, diag_ref, off_ref, sol_ref, tiles_ref, sems):
    leaf, _, _ = place()
    children, slots = off_ref.shape[0], off_ref.shape[1]
    half = keep_ref.shape[0]
    pairs = ((rhs_hbm, rhs_ref), (diag_hbm, diag_ref), (off_hbm, off_ref))
    copies = [
        [pltpu.make_async_copy(source.at[s], target.at[s], sems.at[i, s]) for i, (source, target) in enumerate(pairs)]
        for s in range(children)
    ]
    back = [pltpu.make_async_copy(sol_ref.at[s], sol_hbm.at[s], sems.at[3, s]) for s in range(children)]
    small = [
        pltpu.make_async_copy(live_hbm, live_ref, sems.at[4, 0]),
        pltpu.make_async_copy(tgt_hbm, tgt_ref, sems.at[4, 1]),
    ]
    for s in range(children):
        for copy in copies[s]:
            copy.start()
    for copy in small:
        copy.start()
    for s in range(children):
        copies[s][0].wait()
        copies[s][1].wait()
        rhs = rhs_ref[s]
        sol = rhs + dot3(lower(diag_ref[s]), *split(rhs), NN)
        sol_ref[s] = sol
        back[s].start()
        copies[s][2].wait()
        if s == 0:
            for copy in small:
                copy.wait()
        tiles = dot3(sol.T, *split(off_ref[s]), NT)
        slot = lax.broadcasted_iota(jnp.int32, tiles.shape, 1)
        tiles_ref[:, s * slots:(s + 1) * slots] = jnp.where(slot < live_ref[s], tiles, 0.0)
        send_ref[half:half + 8, s * slots:(s + 1) * slots] = jnp.broadcast_to(
            tgt_ref[s:s + 1, :].astype(F32), (8, slots)
        )
    keep_ref[...] = tiles_ref[pl.ds(pl.multiple_of(leaf * half, half), half), :]
    send_ref[0:half, :] = tiles_ref[pl.ds(pl.multiple_of((1 - leaf) * half, half), half), :]
    for copy in back:
        copy.wait()


def scatter(value, target, size, start):
    index = lax.broadcasted_iota(jnp.int32, (size, value.shape[1]), 0) + start
    hot = jnp.where(index == target, 1.0, 0.0).astype(BF16)
    product = lax.dot_general(value, hot, NT, preferred_element_type=F32)
    half = value.shape[0] // 2
    return product[:half] + product[half:]


def own_kernel(keep_ref, send_ref, *out_refs):
    _, row, _ = place()
    half, size = out_refs[0].shape
    value = jnp.concatenate(split(keep_ref[...]), axis=0)
    target = send_ref[half:half + 1, :].astype(jnp.int32)
    for s, out_ref in enumerate(out_refs):
        out_ref[...] = scatter(value, target, size, jnp.bitwise_xor(row, s) * size)


def other_kernel(recv_ref, *refs):
    _, row, _ = place()
    own_refs, out_refs = refs[:4], refs[4:]
    half, size = out_refs[0].shape
    value = jnp.concatenate(split(recv_ref[0:half, :]), axis=0)
    target = recv_ref[half:half + 1, :].astype(jnp.int32)
    for s, (own_ref, out_ref) in enumerate(zip(own_refs, out_refs)):
        out_ref[...] = own_ref[...] + scatter(value, target, size, jnp.bitwise_xor(row, s) * size)


def pieces_kernel(a_ref, b_ref, c_ref, d_ref, first_ref, second_ref, sum_ref):
    _, _, z = place()
    odd = z % 2
    piece = first_ref.shape[0]
    sum_ref[...] = (a_ref[...] + b_ref[...]) + (c_ref[...] + d_ref[...])
    first_ref[...] = sum_ref[pl.ds(pl.multiple_of(odd * piece, piece), piece), :]
    second_ref[...] = sum_ref[pl.ds(pl.multiple_of((1 - odd) * piece, piece), piece), :]


def factor_kernel(own_ref, sent_ref, other_ref, diag_high_ref, diag_low_ref, *out_refs):
    leaf, row, z = place()
    for block in range(3):
        high_ref, low_ref = out_refs[2 * block], out_refs[2 * block + 1]

        @pl.when((row > block) & ((z == 1) | (z == 2)))
        def _():
            if block == 0:
                value = jnp.where((leaf == 0) == (z == 1), sent_ref[...], other_ref[...])
            else:
                sent = jnp.where((leaf == 0) == (block == 1), sent_ref[...], other_ref[...])
                value = jnp.where(z == block, own_ref[...], sent)
            value = value.T
            value = value + dot3(value, diag_high_ref[...], diag_low_ref[...], NN)
            high_ref[...], low_ref[...] = split(value)


def first_kernel(rhs_ref, a_ref, b_ref, c_ref, d_ref, high_ref, low_ref, out_ref):
    value = rhs_ref[...] - ((a_ref[...] + b_ref[...]) + (c_ref[...] + d_ref[...]))
    out_ref[...] = value + dot3(value, high_ref[...], low_ref[...], NN)


def chain_kernel(owner, given_ref, *refs):
    _, row, z = place()
    used, out_ref = refs[:-1], refs[-1]
    out_ref[...] = given_ref[...]

    @pl.when((row == owner) & ((z == 1) | (z == 2)))
    def _():
        left = given_ref[...]
        for i in range(0, len(used), 3):
            left = left - dot3(used[i][...], used[i + 1][...], used[i + 2][...], NN)
        out_ref[...] = left


def half_kernel(a_ref, b_ref, c_ref, x_ref, out_ref):
    _, _, z = place()
    x, a, b, c = x_ref[...], a_ref[...], b_ref[...], c_ref[...]
    low = jnp.where(z == 0, a, jnp.where(z == 1, x, jnp.where(z == 2, b, c)))
    high = jnp.where(z == 0, c, jnp.where(z == 1, b, jnp.where(z == 2, x, a)))
    out_ref[...] = jnp.concatenate([low, high], axis=0).T


def write_kernel(mine, part_ref, *refs):
    out_hbm, sem = refs[-2:]
    leaf, _, _ = place()
    half = part_ref.shape[1]
    at = leaf if mine else 1 - leaf
    copy = pltpu.make_async_copy(part_ref, out_hbm.at[:, pl.ds(pl.multiple_of(at * half, half), half)], sem)
    copy.start()
    copy.wait()


def call(kernel, ins, outs, scratch=(), outside=(), outs_outside=(), pinned=(), aliases=None, limit=24, flops=0):
    def spec(i, a):
        return ANY if i in outside else SM if a.ndim == 1 else VM

    def shape(i, out):
        dims, dtype = out if isinstance(out[0], tuple) else (out, F32)
        return pltpu.VMEM(dims, dtype) if i in pinned else jax.ShapeDtypeStruct(dims, dtype)

    outs = pl.pallas_call(
        kernel,
        out_shape=[shape(i, out) for i, out in enumerate(outs)],
        in_specs=[spec(i, a) for i, a in enumerate(ins)],
        out_specs=[ANY if i in outs_outside else VM for i in range(len(outs))],
        scratch_shapes=[pltpu.VMEM(s, F32) if isinstance(s, tuple) else s for s in scratch],
        input_output_aliases=aliases or {},
        cost_estimate=pl.CostEstimate(flops=flops, bytes_accessed=4 * sum(a.size for a in ins), transcendentals=0),
        compiler_params=pltpu.CompilerParams(vmem_limit_bytes=limit * 1024 * 1024),
    )(*ins)
    return list(outs)


def central(child_rhs, child_diag, child_off, live, targets, top_rhs, top_factor, top_diag):
    rows, cols = lax.axis_size("row"), lax.axis_size("col")
    size = top_diag.shape[1]
    right = top_rhs.shape[1]
    half, piece = right // 2, right // 4
    children, slots = targets.shape
    shape = (piece, size)
    block = ((size, size), BF16)
    dma = pltpu.SemaphoreType.DMA

    def at(r, c):
        return r * cols + c

    def swap(value):
        return lax.ppermute(value, "leaf", [(0, 1), (1, 0)])

    def along_row(value, step):
        return lax.ppermute(value, "row", [(r, r ^ step) for r in range(rows)])

    def along_col(value, pairs):
        rest = [a for a in range(cols) if a not in [p[0] for p in pairs]]
        open_ends = [b for b in range(cols) if b not in [p[1] for p in pairs]]
        return lax.ppermute(value, "col", pairs + list(zip(rest, open_ends)))

    near = [(at(k, 0), at(k, 1)) for k in (1, 2, 3)] + [(at(k, 1), at(k, 2)) for k in (2, 3)]
    far = [(at(k, 0), at(k, 2)) for k in (1, 2, 3)] + [(at(3, 2), at(3, 1))]
    shift = rows * cols
    sent = lax.ppermute(
        top_factor, ("leaf", "row", "col"), near + [(a + shift, b + shift) for a, b in far]
    )
    child_sol, keep, send = call(
        child_kernel,
        [live, child_rhs, child_diag, child_off, targets],
        [child_rhs.shape, (half, children * slots), (half + 8, children * slots)],
        [pltpu.SMEM(live.shape, jnp.int32), pltpu.VMEM(targets.shape, jnp.int32), child_rhs.shape,
         child_diag.shape, child_off.shape, child_rhs.shape, (right, children * slots), dma((5, max(2, children)))],
        outside=(0, 1, 2, 3, 4),
        outs_outside=(0,),
        pinned=(1, 2),
        limit=56,
    )
    sums = call(own_kernel, [keep, send], [(half, size)] * rows)
    sums = call(other_kernel, [swap(send)] + sums, [(half, size)] * rows)
    got = [along_row(sums[s], s) for s in (3, 1, 2)]
    rhs_piece, diag_high, diag_low = call(
        turn_kernel, [top_rhs, top_diag], [shape, block, block], [(half, size)]
    )
    diag = [diag_high, diag_low]
    first, second = call(pieces_kernel, [sums[0]] + got, [shape] * 2, [(half, size)])
    q = [
        along_col(second, [(0, 2), (3, 1)]),
        along_col(first, [(0, 1), (3, 2)]),
        along_col(first, [(1, 2), (2, 1)]),
    ]

    factor = call(factor_kernel, [top_factor, sent, swap(sent)] + diag, [block] * 6)
    factor = [factor[0:2], factor[2:4], factor[4:6]]

    def chain(owner, ins):
        (out,) = call(functools.partial(chain_kernel, owner), ins, [shape])
        return out

    (x,) = call(first_kernel, [rhs_piece, second] + q + diag, [shape], flops=10 ** 10)
    to1 = along_row(x, 1)
    to2 = along_row(x, 2)
    x = chain(1, [x, to1] + factor[0])
    on = along_row(x, 3)
    late = lax.ppermute(x, "row", [(1, 3)])
    x = chain(2, [x, to2] + factor[0])
    x = chain(2, [x, on] + factor[1])
    to3 = along_row(x, 1)
    x = chain(3, [x, on] + factor[0] + [late] + factor[1])
    x = chain(3, [x, to3] + factor[2])

    both = along_col(x, [(1, 2), (2, 1)])
    step = along_col(x, [(1, 0), (2, 3)])
    over = along_col(x, [(1, 3), (2, 0)])
    (own,) = call(half_kernel, [step, both, over, x], [(size, half)])
    (top_sol,) = call(
        functools.partial(write_kernel, True), [own], [top_rhs.shape], [dma(())], outs_outside=(0,)
    )
    (top_sol,) = call(
        functools.partial(write_kernel, False),
        [swap(own), top_sol],
        [top_rhs.shape],
        [dma(())],
        outside=(1,),
        outs_outside=(0,),
        aliases={1: 0},
    )
    return (child_sol, top_sol)


def solution(mesh):
    in_specs = (
        P(("leaf", "row", "col"), None, None),
        P(("leaf", "row", "col"), None, None),
        P(("leaf", "row", "col"), None, None),
        P(("leaf", "row", "col")),
        P(("leaf", "row", "col"), None),
        P("row", None),
        P("row", "col"),
        P("row", None),
    )
    out_specs = (P(("leaf", "row", "col"), None, None), P("row", None))
    axes = tuple(mesh.shape[a] for a in ("leaf", "row", "col"))

    def shards(*args):
        top_rhs, top_factor, top_diag = args[5:]
        size = top_diag.shape[1]
        fits = axes == (2, 4, 4) and top_rhs.shape[0] == size and top_factor.shape[1] == size
        return (central if fits else any_mesh)(*args)

    return jax.shard_map(shards, mesh=mesh, in_specs=in_specs, out_specs=out_specs, check_vma=False)
```

```python
import functools

import jax
import jax.numpy as jnp
from jax import lax
from jax.experimental import pallas as pl
from jax.experimental.pallas import tpu as pltpu
from jax.sharding import PartitionSpec as P

F32 = jnp.float32
BF16 = jnp.bfloat16
NT = (((1,), (1,)), ((), ()))
NN = (((1,), (0,)), ((), ()))
VM = pl.BlockSpec(memory_space=pltpu.VMEM)
ANY = pl.BlockSpec(memory_space=pl.ANY)
SM = pl.BlockSpec(memory_space=pltpu.SMEM)


def spread(value, axis, source):
    kept = jnp.where(lax.axis_index(axis) == source, value, 0).astype(value.dtype)
    return lax.psum(kept, axis)


def unit_lower(matrix):
    return jnp.tril(matrix) + jnp.eye(matrix.shape[-1], dtype=matrix.dtype)


def any_mesh(child_rhs, child_diag, child_off, live, targets, top_rhs, top_factor, top_diag):
    highest = lax.Precision.HIGHEST
    owned_rows = top_rhs.shape[0]
    right_count = top_rhs.shape[1]
    block_size = top_diag.shape[1]
    owned_blocks = owned_rows // block_size
    row_count = lax.axis_size("row")
    top_order = owned_rows * row_count
    col_width = top_factor.shape[1]
    my_row = lax.axis_index("row")
    my_col = lax.axis_index("col")
    child_sol = jnp.einsum("bij,bjr->bir", unit_lower(child_diag), child_rhs, precision=highest)
    tiles = jnp.einsum("btj,bjr->btr", child_off, child_sol, precision=highest)
    slot_index = jnp.arange(child_off.shape[1], dtype=jnp.int32)
    keep = slot_index[None, :] < live[:, None]
    tiles = jnp.where(keep[:, :, None], tiles, jnp.zeros_like(tiles))
    contrib = jnp.zeros((top_order, right_count), F32)
    contrib = contrib.at[targets.reshape(-1)].add(tiles.reshape(-1, right_count))
    row_part = lax.psum_scatter(contrib, "row", scatter_dimension=0, tiled=True)
    share = lax.psum_scatter(row_part, ("leaf", "col"), scatter_dimension=0, tiled=True)
    updates = lax.all_gather(share, ("leaf", "col"), axis=0, tiled=True)
    reduced = top_rhs - updates
    inverse_all = unit_lower(top_diag.reshape(owned_blocks, block_size, block_size))
    col_global = my_col * col_width + jnp.arange(col_width, dtype=jnp.int32)

    def step(block, solution):
        local = block % owned_blocks
        owner = block // owned_blocks
        factor_rows = jnp.where(
            (col_global < block * block_size)[None, :], top_factor, jnp.zeros_like(top_factor)
        )
        columns = lax.dynamic_slice_in_dim(solution, my_col * col_width, col_width, 0)
        partial_value = jnp.dot(
            factor_rows, columns, precision=highest, preferred_element_type=F32
        )
        block_inverse = lax.dynamic_index_in_dim(inverse_all, local, 0, keepdims=False)
        before = lax.psum(partial_value, "col")
        solved = jnp.dot(
            block_inverse, reduced - before, precision=highest, preferred_element_type=F32
        )
        solved = spread(solved, "row", owner)
        return lax.dynamic_update_slice_in_dim(solution, solved, block * block_size, 0)

    solution = lax.fori_loop(
        0, row_count * owned_blocks, step, jnp.zeros((top_order, right_count), F32)
    )
    top_sol = lax.dynamic_slice_in_dim(solution, my_row * owned_rows, owned_rows, 0)
    return (child_sol, top_sol)


def place():
    return tuple(lax.axis_index(a) for a in ("leaf", "row", "col"))


def split(value):
    high = value.astype(BF16)
    return high, (value - high.astype(F32)).astype(BF16)


def dot3(left, high, low, dims):
    left_high, left_low = split(left)
    rows = left.shape[0]
    both = lax.dot_general(
        jnp.concatenate([left_high, left_low], axis=0), high, dims, preferred_element_type=F32
    )
    cross = lax.dot_general(left_high, low, dims, preferred_element_type=F32)
    return both[:rows] + both[rows:] + cross


def lower(matrix):
    row = lax.broadcasted_iota(jnp.int32, matrix.shape, 0)
    col = lax.broadcasted_iota(jnp.int32, matrix.shape, 1)
    return jnp.where(col <= row, matrix, 0.0)


def turn_kernel(rhs_ref, diag_ref, out_ref, high_ref, low_ref, turned_ref):
    leaf, _, z = place()
    half, piece = turned_ref.shape[0], out_ref.shape[0]
    turned_ref[...] = rhs_ref[:, pl.ds(pl.multiple_of(leaf * half, half), half)].T
    out_ref[...] = turned_ref[pl.ds(pl.multiple_of((z // 2) * piece, piece), piece), :]
    high_ref[...], low_ref[...] = split(lower(diag_ref[...]).T)


def child_kernel(live_hbm, rhs_hbm, diag_hbm, off_hbm, tgt_hbm, sol_hbm, keep_ref, send_ref,
                 live_ref, tgt_ref, rhs_ref, diag_ref, off_ref, sol_ref, tiles_ref, sems):
    leaf, _, _ = place()
    children, slots = off_ref.shape[0], off_ref.shape[1]
    half = keep_ref.shape[0]
    pairs = ((rhs_hbm, rhs_ref), (diag_hbm, diag_ref), (off_hbm, off_ref))
    copies = [
        [pltpu.make_async_copy(source.at[s], target.at[s], sems.at[i, s]) for i, (source, target) in enumerate(pairs)]
        for s in range(children)
    ]
    back = [pltpu.make_async_copy(sol_ref.at[s], sol_hbm.at[s], sems.at[3, s]) for s in range(children)]
    small = [
        pltpu.make_async_copy(live_hbm, live_ref, sems.at[4, 0]),
        pltpu.make_async_copy(tgt_hbm, tgt_ref, sems.at[4, 1]),
    ]
    for s in range(children):
        for copy in copies[s]:
            copy.start()
    for copy in small:
        copy.start()
    for s in range(children):
        copies[s][0].wait()
        copies[s][1].wait()
        rhs = rhs_ref[s]
        sol = rhs + dot3(lower(diag_ref[s]), *split(rhs), NN)
        sol_ref[s] = sol
        back[s].start()
        copies[s][2].wait()
        if s == 0:
            for copy in small:
                copy.wait()
        tiles = dot3(sol.T, *split(off_ref[s]), NT)
        slot = lax.broadcasted_iota(jnp.int32, tiles.shape, 1)
        tiles_ref[:, s * slots:(s + 1) * slots] = jnp.where(slot < live_ref[s], tiles, 0.0)
        send_ref[half:half + 8, s * slots:(s + 1) * slots] = jnp.broadcast_to(
            tgt_ref[s:s + 1, :].astype(F32), (8, slots)
        )
    keep_ref[...] = tiles_ref[pl.ds(pl.multiple_of(leaf * half, half), half), :]
    send_ref[0:half, :] = tiles_ref[pl.ds(pl.multiple_of((1 - leaf) * half, half), half), :]
    for copy in back:
        copy.wait()


def scatter(value, target, size, start):
    index = lax.broadcasted_iota(jnp.int32, (size, value.shape[1]), 0) + start
    hot = jnp.where(index == target, 1.0, 0.0).astype(BF16)
    product = lax.dot_general(value, hot, NT, preferred_element_type=F32)
    half = value.shape[0] // 2
    return product[:half] + product[half:]


def own_kernel(keep_ref, send_ref, *out_refs):
    _, row, _ = place()
    half, size = out_refs[0].shape
    value = jnp.concatenate(split(keep_ref[...]), axis=0)
    target = send_ref[half:half + 1, :].astype(jnp.int32)
    for s, out_ref in enumerate(out_refs):
        out_ref[...] = scatter(value, target, size, jnp.bitwise_xor(row, s) * size)


def other_kernel(recv_ref, *refs):
    _, row, _ = place()
    own_refs, out_refs = refs[:4], refs[4:]
    half, size = out_refs[0].shape
    value = jnp.concatenate(split(recv_ref[0:half, :]), axis=0)
    target = recv_ref[half:half + 1, :].astype(jnp.int32)
    for s, (own_ref, out_ref) in enumerate(zip(own_refs, out_refs)):
        out_ref[...] = own_ref[...] + scatter(value, target, size, jnp.bitwise_xor(row, s) * size)


def pieces_kernel(a_ref, b_ref, c_ref, d_ref, first_ref, second_ref, sum_ref):
    _, _, z = place()
    odd = z % 2
    piece = first_ref.shape[0]
    sum_ref[...] = (a_ref[...] + b_ref[...]) + (c_ref[...] + d_ref[...])
    first_ref[...] = sum_ref[pl.ds(pl.multiple_of(odd * piece, piece), piece), :]
    second_ref[...] = sum_ref[pl.ds(pl.multiple_of((1 - odd) * piece, piece), piece), :]


def factor_kernel(own_ref, sent_ref, other_ref, diag_high_ref, diag_low_ref, *out_refs):
    leaf, row, z = place()
    for block in range(3):
        high_ref, low_ref = out_refs[2 * block], out_refs[2 * block + 1]

        @pl.when((row > block) & ((z == 1) | (z == 2)))
        def _():
            if block == 0:
                value = jnp.where((leaf == 0) == (z == 1), sent_ref[...], other_ref[...])
            else:
                sent = jnp.where((leaf == 0) == (block == 1), sent_ref[...], other_ref[...])
                value = jnp.where(z == block, own_ref[...], sent)
            value = value.T
            value = value + dot3(value, diag_high_ref[...], diag_low_ref[...], NN)
            high_ref[...], low_ref[...] = split(value)


def first_kernel(rhs_ref, a_ref, b_ref, c_ref, d_ref, high_ref, low_ref, out_ref):
    value = rhs_ref[...] - ((a_ref[...] + b_ref[...]) + (c_ref[...] + d_ref[...]))
    out_ref[...] = value + dot3(value, high_ref[...], low_ref[...], NN)


def chain_kernel(owner, given_ref, *refs):
    _, row, z = place()
    used, out_ref = refs[:-1], refs[-1]
    out_ref[...] = given_ref[...]

    @pl.when((row == owner) & ((z == 1) | (z == 2)))
    def _():
        left = given_ref[...]
        for i in range(0, len(used), 3):
            left = left - dot3(used[i][...], used[i + 1][...], used[i + 2][...], NN)
        out_ref[...] = left


def half_kernel(a_ref, b_ref, c_ref, x_ref, out_ref):
    _, _, z = place()
    x, a, b, c = x_ref[...], a_ref[...], b_ref[...], c_ref[...]
    low = jnp.where(z == 0, a, jnp.where(z == 1, x, jnp.where(z == 2, b, c)))
    high = jnp.where(z == 0, c, jnp.where(z == 1, b, jnp.where(z == 2, x, a)))
    out_ref[...] = jnp.concatenate([low, high], axis=0).T


def write_kernel(mine, part_ref, *refs):
    out_hbm, sem = refs[-2:]
    leaf, _, _ = place()
    half = part_ref.shape[1]
    at = leaf if mine else 1 - leaf
    copy = pltpu.make_async_copy(part_ref, out_hbm.at[:, pl.ds(pl.multiple_of(at * half, half), half)], sem)
    copy.start()
    copy.wait()


def call(kernel, ins, outs, scratch=(), outside=(), outs_outside=(), pinned=(), aliases=None, limit=24, flops=0):
    def spec(i, a):
        return ANY if i in outside else SM if a.ndim == 1 else VM

    def shape(i, out):
        dims, dtype = out if isinstance(out[0], tuple) else (out, F32)
        return pltpu.VMEM(dims, dtype) if i in pinned else jax.ShapeDtypeStruct(dims, dtype)

    outs = pl.pallas_call(
        kernel,
        out_shape=[shape(i, out) for i, out in enumerate(outs)],
        in_specs=[spec(i, a) for i, a in enumerate(ins)],
        out_specs=[ANY if i in outs_outside else VM for i in range(len(outs))],
        scratch_shapes=[pltpu.VMEM(s, F32) if isinstance(s, tuple) else s for s in scratch],
        input_output_aliases=aliases or {},
        cost_estimate=pl.CostEstimate(flops=flops, bytes_accessed=4 * sum(a.size for a in ins), transcendentals=0),
        compiler_params=pltpu.CompilerParams(vmem_limit_bytes=limit * 1024 * 1024),
    )(*ins)
    return list(outs)


def central(child_rhs, child_diag, child_off, live, targets, top_rhs, top_factor, top_diag):
    rows, cols = lax.axis_size("row"), lax.axis_size("col")
    size = top_diag.shape[1]
    right = top_rhs.shape[1]
    half, piece = right // 2, right // 4
    children, slots = targets.shape
    shape = (piece, size)
    block = ((size, size), BF16)
    dma = pltpu.SemaphoreType.DMA

    def at(r, c):
        return r * cols + c

    def swap(value):
        return lax.ppermute(value, "leaf", [(0, 1), (1, 0)])

    def along_row(value, step):
        return lax.ppermute(value, "row", [(r, r ^ step) for r in range(rows)])

    def along_col(value, pairs):
        rest = [a for a in range(cols) if a not in [p[0] for p in pairs]]
        open_ends = [b for b in range(cols) if b not in [p[1] for p in pairs]]
        return lax.ppermute(value, "col", pairs + list(zip(rest, open_ends)))

    def exchange(axis, value, a, b):
        count = lax.axis_size(axis)
        pairs = [(a, b), (b, a), (a + count, b + count), (b + count, a + count)]
        for other in range(count):
            if other not in (a, b):
                pairs += [(other, other + count), (other + count, other)]
        return lax.ppermute(value, ("leaf", axis), pairs)

    near = [(at(k, 0), at(k, 1)) for k in (1, 2, 3)] + [(at(k, 1), at(k, 2)) for k in (2, 3)]
    far = [(at(k, 0), at(k, 2)) for k in (1, 2, 3)] + [(at(3, 2), at(3, 1))]
    shift = rows * cols
    sent = lax.ppermute(
        top_factor, ("leaf", "row", "col"), near + [(a + shift, b + shift) for a, b in far]
    )
    child_sol, keep, send = call(
        child_kernel,
        [live, child_rhs, child_diag, child_off, targets],
        [child_rhs.shape, (half, children * slots), (half + 8, children * slots)],
        [pltpu.SMEM(live.shape, jnp.int32), pltpu.VMEM(targets.shape, jnp.int32), child_rhs.shape,
         child_diag.shape, child_off.shape, child_rhs.shape, (right, children * slots), dma((5, max(2, children)))],
        outside=(0, 1, 2, 3, 4),
        outs_outside=(0,),
        pinned=(1, 2),
        limit=56,
    )
    sums = call(own_kernel, [keep, send], [(half, size)] * rows)
    sums = call(other_kernel, [swap(send)] + sums, [(half, size)] * rows)
    got = [along_row(sums[s], s) for s in (3, 1, 2)]
    rhs_piece, diag_high, diag_low = call(
        turn_kernel, [top_rhs, top_diag], [shape, block, block], [(half, size)]
    )
    diag = [diag_high, diag_low]
    first, second = call(pieces_kernel, [sums[0]] + got, [shape] * 2, [(half, size)])
    q = [
        along_col(second, [(0, 2), (3, 1)]),
        along_col(first, [(0, 1), (3, 2)]),
        exchange("col", first, 1, 2),
    ]

    factor = call(factor_kernel, [top_factor, sent, swap(sent)] + diag, [block] * 6)
    factor = [factor[0:2], factor[2:4], factor[4:6]]

    def chain(owner, ins):
        (out,) = call(functools.partial(chain_kernel, owner), ins, [shape])
        return out

    (x,) = call(first_kernel, [rhs_piece, second] + q + diag, [shape], flops=10 ** 10)
    to1 = exchange("row", x, 0, 1)
    to2 = exchange("row", x, 0, 2)
    x = chain(1, [x, to1] + factor[0])
    on = along_row(x, 3)
    late = exchange("row", x, 1, 3)
    x = chain(2, [x, to2] + factor[0])
    x = chain(2, [x, on] + factor[1])
    to3 = exchange("row", x, 2, 3)
    x = chain(3, [x, on] + factor[0] + [late] + factor[1])
    x = chain(3, [x, to3] + factor[2])

    both = exchange("col", x, 1, 2)
    step = along_col(x, [(1, 0), (2, 3)])
    over = along_col(x, [(1, 3), (2, 0)])
    (own,) = call(half_kernel, [step, both, over, x], [(size, half)])
    (top_sol,) = call(
        functools.partial(write_kernel, True), [own], [top_rhs.shape], [dma(())], outs_outside=(0,)
    )
    (top_sol,) = call(
        functools.partial(write_kernel, False),
        [swap(own), top_sol],
        [top_rhs.shape],
        [dma(())],
        outside=(1,),
        outs_outside=(0,),
        aliases={1: 0},
    )
    return (child_sol, top_sol)


def solution(mesh):
    in_specs = (
        P(("leaf", "row", "col"), None, None),
        P(("leaf", "row", "col"), None, None),
        P(("leaf", "row", "col"), None, None),
        P(("leaf", "row", "col")),
        P(("leaf", "row", "col"), None),
        P("row", None),
        P("row", "col"),
        P("row", None),
    )
    out_specs = (P(("leaf", "row", "col"), None, None), P("row", None))
    axes = tuple(mesh.shape[a] for a in ("leaf", "row", "col"))

    def shards(*args):
        top_rhs, top_factor, top_diag = args[5:]
        size = top_diag.shape[1]
        fits = axes == (2, 4, 4) and top_rhs.shape[0] == size and top_factor.shape[1] == size
        return (central if fits else any_mesh)(*args)

    return jax.shard_map(shards, mesh=mesh, in_specs=in_specs, out_specs=out_specs, check_vma=False)
```

```python
import functools

import jax
import jax.numpy as jnp
from jax import lax
from jax.experimental import pallas as pl
from jax.experimental.pallas import tpu as pltpu
from jax.sharding import PartitionSpec as P

F32 = jnp.float32
BF16 = jnp.bfloat16
NT = (((1,), (1,)), ((), ()))
NN = (((1,), (0,)), ((), ()))
VM = pl.BlockSpec(memory_space=pltpu.VMEM)
ANY = pl.BlockSpec(memory_space=pl.ANY)
SM = pl.BlockSpec(memory_space=pltpu.SMEM)


def spread(value, axis, source):
    kept = jnp.where(lax.axis_index(axis) == source, value, 0).astype(value.dtype)
    return lax.psum(kept, axis)


def unit_lower(matrix):
    return jnp.tril(matrix) + jnp.eye(matrix.shape[-1], dtype=matrix.dtype)


def any_mesh(child_rhs, child_diag, child_off, live, targets, top_rhs, top_factor, top_diag):
    highest = lax.Precision.HIGHEST
    owned_rows = top_rhs.shape[0]
    right_count = top_rhs.shape[1]
    block_size = top_diag.shape[1]
    owned_blocks = owned_rows // block_size
    row_count = lax.axis_size("row")
    top_order = owned_rows * row_count
    col_width = top_factor.shape[1]
    my_row = lax.axis_index("row")
    my_col = lax.axis_index("col")
    child_sol = jnp.einsum("bij,bjr->bir", unit_lower(child_diag), child_rhs, precision=highest)
    tiles = jnp.einsum("btj,bjr->btr", child_off, child_sol, precision=highest)
    slot_index = jnp.arange(child_off.shape[1], dtype=jnp.int32)
    keep = slot_index[None, :] < live[:, None]
    tiles = jnp.where(keep[:, :, None], tiles, jnp.zeros_like(tiles))
    contrib = jnp.zeros((top_order, right_count), F32)
    contrib = contrib.at[targets.reshape(-1)].add(tiles.reshape(-1, right_count))
    row_part = lax.psum_scatter(contrib, "row", scatter_dimension=0, tiled=True)
    share = lax.psum_scatter(row_part, ("leaf", "col"), scatter_dimension=0, tiled=True)
    updates = lax.all_gather(share, ("leaf", "col"), axis=0, tiled=True)
    reduced = top_rhs - updates
    inverse_all = unit_lower(top_diag.reshape(owned_blocks, block_size, block_size))
    col_global = my_col * col_width + jnp.arange(col_width, dtype=jnp.int32)

    def step(block, solution):
        local = block % owned_blocks
        owner = block // owned_blocks
        factor_rows = jnp.where(
            (col_global < block * block_size)[None, :], top_factor, jnp.zeros_like(top_factor)
        )
        columns = lax.dynamic_slice_in_dim(solution, my_col * col_width, col_width, 0)
        partial_value = jnp.dot(
            factor_rows, columns, precision=highest, preferred_element_type=F32
        )
        block_inverse = lax.dynamic_index_in_dim(inverse_all, local, 0, keepdims=False)
        before = lax.psum(partial_value, "col")
        solved = jnp.dot(
            block_inverse, reduced - before, precision=highest, preferred_element_type=F32
        )
        solved = spread(solved, "row", owner)
        return lax.dynamic_update_slice_in_dim(solution, solved, block * block_size, 0)

    solution = lax.fori_loop(
        0, row_count * owned_blocks, step, jnp.zeros((top_order, right_count), F32)
    )
    top_sol = lax.dynamic_slice_in_dim(solution, my_row * owned_rows, owned_rows, 0)
    return (child_sol, top_sol)


def place():
    return tuple(lax.axis_index(a) for a in ("leaf", "row", "col"))


def split(value):
    high = value.astype(BF16)
    return high, (value - high.astype(F32)).astype(BF16)


def dot3(left, high, low, dims):
    left_high, left_low = split(left)
    rows = left.shape[0]
    both = lax.dot_general(
        jnp.concatenate([left_high, left_low], axis=0), high, dims, preferred_element_type=F32
    )
    cross = lax.dot_general(left_high, low, dims, preferred_element_type=F32)
    return both[:rows] + both[rows:] + cross


def lower(matrix):
    row = lax.broadcasted_iota(jnp.int32, matrix.shape, 0)
    col = lax.broadcasted_iota(jnp.int32, matrix.shape, 1)
    return jnp.where(col <= row, matrix, 0.0)


def turn_kernel(rhs_ref, diag_ref, out_ref, high_ref, low_ref, turned_ref):
    leaf, _, z = place()
    half, piece = turned_ref.shape[0], out_ref.shape[0]
    turned_ref[...] = rhs_ref[:, pl.ds(pl.multiple_of(leaf * half, half), half)].T
    out_ref[...] = turned_ref[pl.ds(pl.multiple_of((z // 2) * piece, piece), piece), :]
    high_ref[...], low_ref[...] = split(lower(diag_ref[...]).T)


def child_kernel(live_hbm, rhs_hbm, diag_hbm, off_hbm, tgt_hbm, sol_hbm, keep_ref, send_ref,
                 live_ref, tgt_ref, rhs_ref, diag_ref, off_ref, sol_ref, tiles_ref, sems):
    leaf, _, _ = place()
    children, slots = off_ref.shape[0], off_ref.shape[1]
    half = keep_ref.shape[0]
    pairs = ((rhs_hbm, rhs_ref), (diag_hbm, diag_ref), (off_hbm, off_ref))
    copies = [
        [pltpu.make_async_copy(source.at[s], target.at[s], sems.at[i, s]) for i, (source, target) in enumerate(pairs)]
        for s in range(children)
    ]
    back = [pltpu.make_async_copy(sol_ref.at[s], sol_hbm.at[s], sems.at[3, s]) for s in range(children)]
    small = [
        pltpu.make_async_copy(live_hbm, live_ref, sems.at[4, 0]),
        pltpu.make_async_copy(tgt_hbm, tgt_ref, sems.at[4, 1]),
    ]
    for s in range(children):
        for copy in copies[s]:
            copy.start()
    for copy in small:
        copy.start()
    for s in range(children):
        copies[s][0].wait()
        copies[s][1].wait()
        rhs = rhs_ref[s]
        sol = rhs + dot3(lower(diag_ref[s]), *split(rhs), NN)
        sol_ref[s] = sol
        back[s].start()
        copies[s][2].wait()
        if s == 0:
            for copy in small:
                copy.wait()
        tiles = dot3(sol.T, *split(off_ref[s]), NT)
        slot = lax.broadcasted_iota(jnp.int32, tiles.shape, 1)
        tiles_ref[:, s * slots:(s + 1) * slots] = jnp.where(slot < live_ref[s], tiles, 0.0)
        send_ref[half:half + 8, s * slots:(s + 1) * slots] = jnp.broadcast_to(
            tgt_ref[s:s + 1, :].astype(F32), (8, slots)
        )
    keep_ref[...] = tiles_ref[pl.ds(pl.multiple_of(leaf * half, half), half), :]
    send_ref[0:half, :] = tiles_ref[pl.ds(pl.multiple_of((1 - leaf) * half, half), half), :]
    for copy in back:
        copy.wait()


def scatter(value, target, size, start):
    index = lax.broadcasted_iota(jnp.int32, (size, value.shape[1]), 0) + start
    hot = jnp.where(index == target, 1.0, 0.0).astype(BF16)
    product = lax.dot_general(value, hot, NT, preferred_element_type=F32)
    half = value.shape[0] // 2
    return product[:half] + product[half:]


def own_kernel(keep_ref, send_ref, *out_refs):
    _, row, _ = place()
    half, size = out_refs[0].shape
    value = jnp.concatenate(split(keep_ref[...]), axis=0)
    target = send_ref[half:half + 1, :].astype(jnp.int32)
    for s, out_ref in enumerate(out_refs):
        out_ref[...] = scatter(value, target, size, jnp.bitwise_xor(row, s) * size)


def other_kernel(recv_ref, *refs):
    _, row, _ = place()
    own_refs, out_refs = refs[:4], refs[4:]
    half, size = out_refs[0].shape
    value = jnp.concatenate(split(recv_ref[0:half, :]), axis=0)
    target = recv_ref[half:half + 1, :].astype(jnp.int32)
    for s, (own_ref, out_ref) in enumerate(zip(own_refs, out_refs)):
        out_ref[...] = own_ref[...] + scatter(value, target, size, jnp.bitwise_xor(row, s) * size)


def pieces_kernel(a_ref, b_ref, c_ref, d_ref, first_ref, second_ref, sum_ref):
    _, _, z = place()
    odd = z % 2
    piece = first_ref.shape[0]
    sum_ref[...] = (a_ref[...] + b_ref[...]) + (c_ref[...] + d_ref[...])
    first_ref[...] = sum_ref[pl.ds(pl.multiple_of(odd * piece, piece), piece), :]
    second_ref[...] = sum_ref[pl.ds(pl.multiple_of((1 - odd) * piece, piece), piece), :]


def factor_kernel(own_ref, sent_ref, other_ref, diag_high_ref, diag_low_ref, *out_refs):
    leaf, row, z = place()
    for block in range(3):
        high_ref, low_ref = out_refs[2 * block], out_refs[2 * block + 1]

        @pl.when((row > block) & ((z == 1) | (z == 2)))
        def _():
            if block == 0:
                value = jnp.where((leaf == 0) == (z == 1), sent_ref[...], other_ref[...])
            else:
                sent = jnp.where((leaf == 0) == (block == 1), sent_ref[...], other_ref[...])
                value = jnp.where(z == block, own_ref[...], sent)
            value = value.T
            value = value + dot3(value, diag_high_ref[...], diag_low_ref[...], NN)
            high_ref[...], low_ref[...] = split(value)


def first_kernel(rhs_ref, a_ref, b_ref, c_ref, d_ref, high_ref, low_ref, out_ref):
    value = rhs_ref[...] - ((a_ref[...] + b_ref[...]) + (c_ref[...] + d_ref[...]))
    out_ref[...] = value + dot3(value, high_ref[...], low_ref[...], NN)


def chain_kernel(owner, given_ref, *refs):
    _, row, z = place()
    used, out_ref = refs[:-1], refs[-1]
    out_ref[...] = given_ref[...]

    @pl.when((row == owner) & ((z == 1) | (z == 2)))
    def _():
        left = given_ref[...]
        for i in range(0, len(used), 3):
            left = left - dot3(used[i][...], used[i + 1][...], used[i + 2][...], NN)
        out_ref[...] = left


def half_kernel(b_ref, a_ref, c_ref, x_ref, out_ref):
    _, _, z = place()
    x, a, b, c = x_ref[...], a_ref[...], b_ref[...], c_ref[...]
    low = jnp.where(z == 0, a, jnp.where(z == 1, x, jnp.where(z == 2, b, c)))
    high = jnp.where(z == 0, c, jnp.where(z == 1, b, jnp.where(z == 2, x, a)))
    out_ref[...] = jnp.concatenate([low, high], axis=0).T


def write_kernel(mine, part_ref, *refs):
    out_hbm, sem = refs[-2:]
    leaf, _, _ = place()
    half = part_ref.shape[1]
    at = leaf if mine else 1 - leaf
    copy = pltpu.make_async_copy(part_ref, out_hbm.at[:, pl.ds(pl.multiple_of(at * half, half), half)], sem)
    copy.start()
    copy.wait()


def call(kernel, ins, outs, scratch=(), outside=(), outs_outside=(), pinned=(), aliases=None, limit=24, flops=0):
    def spec(i, a):
        return ANY if i in outside else SM if a.ndim == 1 else VM

    def shape(i, out):
        dims, dtype = out if isinstance(out[0], tuple) else (out, F32)
        return pltpu.VMEM(dims, dtype) if i in pinned else jax.ShapeDtypeStruct(dims, dtype)

    outs = pl.pallas_call(
        kernel,
        out_shape=[shape(i, out) for i, out in enumerate(outs)],
        in_specs=[spec(i, a) for i, a in enumerate(ins)],
        out_specs=[ANY if i in outs_outside else VM for i in range(len(outs))],
        scratch_shapes=[pltpu.VMEM(s, F32) if isinstance(s, tuple) else s for s in scratch],
        input_output_aliases=aliases or {},
        cost_estimate=pl.CostEstimate(flops=flops, bytes_accessed=4 * sum(a.size for a in ins), transcendentals=0),
        compiler_params=pltpu.CompilerParams(vmem_limit_bytes=limit * 1024 * 1024),
    )(*ins)
    return list(outs)


def central(child_rhs, child_diag, child_off, live, targets, top_rhs, top_factor, top_diag):
    rows, cols = lax.axis_size("row"), lax.axis_size("col")
    size = top_diag.shape[1]
    right = top_rhs.shape[1]
    half, piece = right // 2, right // 4
    children, slots = targets.shape
    shape = (piece, size)
    block = ((size, size), BF16)
    dma = pltpu.SemaphoreType.DMA

    def at(r, c):
        return r * cols + c

    def swap(value):
        return lax.ppermute(value, "leaf", [(0, 1), (1, 0)])

    def along_row(value, step):
        return lax.ppermute(value, "row", [(r, r ^ step) for r in range(rows)])

    def along_col(value, pairs):
        rest = [a for a in range(cols) if a not in [p[0] for p in pairs]]
        open_ends = [b for b in range(cols) if b not in [p[1] for p in pairs]]
        return lax.ppermute(value, "col", pairs + list(zip(rest, open_ends)))

    def exchange(axis, value, a, b):
        count = lax.axis_size(axis)
        pairs = [(a, b), (b, a), (a + count, b + count), (b + count, a + count)]
        for other in range(count):
            if other not in (a, b):
                pairs += [(other, other + count), (other + count, other)]
        return lax.ppermute(value, ("leaf", axis), pairs)

    near = [(at(k, 0), at(k, 1)) for k in (1, 2, 3)] + [(at(k, 1), at(k, 2)) for k in (2, 3)]
    far = [(at(k, 0), at(k, 2)) for k in (1, 2, 3)] + [(at(3, 2), at(3, 1))]
    shift = rows * cols
    sent = lax.ppermute(
        top_factor, ("leaf", "row", "col"), near + [(a + shift, b + shift) for a, b in far]
    )
    child_sol, keep, send = call(
        child_kernel,
        [live, child_rhs, child_diag, child_off, targets],
        [child_rhs.shape, (half, children * slots), (half + 8, children * slots)],
        [pltpu.SMEM(live.shape, jnp.int32), pltpu.VMEM(targets.shape, jnp.int32), child_rhs.shape,
         child_diag.shape, child_off.shape, child_rhs.shape, (right, children * slots), dma((5, max(2, children)))],
        outside=(0, 1, 2, 3, 4),
        outs_outside=(0,),
        pinned=(1, 2),
        limit=56,
    )
    sums = call(own_kernel, [keep, send], [(half, size)] * rows)
    sums = call(other_kernel, [swap(send)] + sums, [(half, size)] * rows)
    got = [along_row(sums[s], s) for s in (3, 1, 2)]
    rhs_piece, diag_high, diag_low = call(
        turn_kernel, [top_rhs, top_diag], [shape, block, block], [(half, size)]
    )
    diag = [diag_high, diag_low]
    first, second = call(pieces_kernel, [sums[0]] + got, [shape] * 2, [(half, size)])
    q = [
        along_col(second, [(0, 2), (3, 1)]),
        along_col(first, [(0, 1), (3, 2)]),
        exchange("col", first, 1, 2),
    ]

    factor = call(factor_kernel, [top_factor, sent, swap(sent)] + diag, [block] * 6)
    factor = [factor[0:2], factor[2:4], factor[4:6]]

    def chain(owner, ins):
        (out,) = call(functools.partial(chain_kernel, owner), ins, [shape])
        return out

    (x,) = call(first_kernel, [rhs_piece, second] + q + diag, [shape], flops=10 ** 10)
    to1 = exchange("row", x, 0, 1)
    to2 = exchange("row", x, 0, 2)
    x = chain(1, [x, to1] + factor[0])
    on = along_row(x, 3)
    late = exchange("row", x, 1, 3)
    x = chain(2, [x, to2] + factor[0])
    x = chain(2, [x, on] + factor[1])
    to3 = exchange("row", x, 2, 3)
    x = chain(3, [x, on] + factor[0] + [late] + factor[1])
    x = chain(3, [x, to3] + factor[2])

    both = exchange("col", x, 1, 2)
    step = along_col(x, [(1, 0), (2, 3)])
    over = along_col(x, [(1, 3), (2, 0)])
    (own,) = call(half_kernel, [both, step, over, x], [(size, half)])
    (top_sol,) = call(
        functools.partial(write_kernel, True), [own], [top_rhs.shape], [dma(())], outs_outside=(0,)
    )
    (top_sol,) = call(
        functools.partial(write_kernel, False),
        [swap(own), top_sol],
        [top_rhs.shape],
        [dma(())],
        outside=(1,),
        outs_outside=(0,),
        aliases={1: 0},
    )
    return (child_sol, top_sol)


def solution(mesh):
    in_specs = (
        P(("leaf", "row", "col"), None, None),
        P(("leaf", "row", "col"), None, None),
        P(("leaf", "row", "col"), None, None),
        P(("leaf", "row", "col")),
        P(("leaf", "row", "col"), None),
        P("row", None),
        P("row", "col"),
        P("row", None),
    )
    out_specs = (P(("leaf", "row", "col"), None, None), P("row", None))
    axes = tuple(mesh.shape[a] for a in ("leaf", "row", "col"))

    def shards(*args):
        top_rhs, top_factor, top_diag = args[5:]
        size = top_diag.shape[1]
        fits = axes == (2, 4, 4) and top_rhs.shape[0] == size and top_factor.shape[1] == size
        return (central if fits else any_mesh)(*args)

    return jax.shard_map(shards, mesh=mesh, in_specs=in_specs, out_specs=out_specs, check_vma=False)
```

```python
import functools

import jax
import jax.numpy as jnp
from jax import lax
from jax.experimental import pallas as pl
from jax.experimental.pallas import tpu as pltpu
from jax.sharding import PartitionSpec as P

F32 = jnp.float32
BF16 = jnp.bfloat16
NT = (((1,), (1,)), ((), ()))
NN = (((1,), (0,)), ((), ()))
VM = pl.BlockSpec(memory_space=pltpu.VMEM)
ANY = pl.BlockSpec(memory_space=pl.ANY)
SM = pl.BlockSpec(memory_space=pltpu.SMEM)


def spread(value, axis, source):
    kept = jnp.where(lax.axis_index(axis) == source, value, 0).astype(value.dtype)
    return lax.psum(kept, axis)


def unit_lower(matrix):
    return jnp.tril(matrix) + jnp.eye(matrix.shape[-1], dtype=matrix.dtype)


def any_mesh(child_rhs, child_diag, child_off, live, targets, top_rhs, top_factor, top_diag):
    highest = lax.Precision.HIGHEST
    owned_rows = top_rhs.shape[0]
    right_count = top_rhs.shape[1]
    block_size = top_diag.shape[1]
    owned_blocks = owned_rows // block_size
    row_count = lax.axis_size("row")
    top_order = owned_rows * row_count
    col_width = top_factor.shape[1]
    my_row = lax.axis_index("row")
    my_col = lax.axis_index("col")
    child_sol = jnp.einsum("bij,bjr->bir", unit_lower(child_diag), child_rhs, precision=highest)
    tiles = jnp.einsum("btj,bjr->btr", child_off, child_sol, precision=highest)
    slot_index = jnp.arange(child_off.shape[1], dtype=jnp.int32)
    keep = slot_index[None, :] < live[:, None]
    tiles = jnp.where(keep[:, :, None], tiles, jnp.zeros_like(tiles))
    contrib = jnp.zeros((top_order, right_count), F32)
    contrib = contrib.at[targets.reshape(-1)].add(tiles.reshape(-1, right_count))
    row_part = lax.psum_scatter(contrib, "row", scatter_dimension=0, tiled=True)
    share = lax.psum_scatter(row_part, ("leaf", "col"), scatter_dimension=0, tiled=True)
    updates = lax.all_gather(share, ("leaf", "col"), axis=0, tiled=True)
    reduced = top_rhs - updates
    inverse_all = unit_lower(top_diag.reshape(owned_blocks, block_size, block_size))
    col_global = my_col * col_width + jnp.arange(col_width, dtype=jnp.int32)

    def step(block, solution):
        local = block % owned_blocks
        owner = block // owned_blocks
        factor_rows = jnp.where(
            (col_global < block * block_size)[None, :], top_factor, jnp.zeros_like(top_factor)
        )
        columns = lax.dynamic_slice_in_dim(solution, my_col * col_width, col_width, 0)
        partial_value = jnp.dot(
            factor_rows, columns, precision=highest, preferred_element_type=F32
        )
        block_inverse = lax.dynamic_index_in_dim(inverse_all, local, 0, keepdims=False)
        before = lax.psum(partial_value, "col")
        solved = jnp.dot(
            block_inverse, reduced - before, precision=highest, preferred_element_type=F32
        )
        solved = spread(solved, "row", owner)
        return lax.dynamic_update_slice_in_dim(solution, solved, block * block_size, 0)

    solution = lax.fori_loop(
        0, row_count * owned_blocks, step, jnp.zeros((top_order, right_count), F32)
    )
    top_sol = lax.dynamic_slice_in_dim(solution, my_row * owned_rows, owned_rows, 0)
    return (child_sol, top_sol)


def place():
    return tuple(lax.axis_index(a) for a in ("leaf", "row", "col"))


def split(value):
    high = value.astype(BF16)
    return high, (value - high.astype(F32)).astype(BF16)


def dot3(left, high, low, dims):
    left_high, left_low = split(left)
    rows = left.shape[0]
    both = lax.dot_general(
        jnp.concatenate([left_high, left_low], axis=0), high, dims, preferred_element_type=F32
    )
    cross = lax.dot_general(left_high, low, dims, preferred_element_type=F32)
    return both[:rows] + both[rows:] + cross


def lower(matrix):
    row = lax.broadcasted_iota(jnp.int32, matrix.shape, 0)
    col = lax.broadcasted_iota(jnp.int32, matrix.shape, 1)
    return jnp.where(col <= row, matrix, 0.0)


def turn_kernel(rhs_ref, diag_ref, out_ref, high_ref, low_ref, turned_ref):
    leaf, _, z = place()
    half, piece = turned_ref.shape[0], out_ref.shape[0]
    turned_ref[...] = rhs_ref[:, pl.ds(pl.multiple_of(leaf * half, half), half)].T
    out_ref[...] = turned_ref[pl.ds(pl.multiple_of((z // 2) * piece, piece), piece), :]
    high_ref[...], low_ref[...] = split(lower(diag_ref[...]).T)


def child_kernel(live_hbm, rhs_hbm, diag_hbm, off_hbm, tgt_hbm, sol_hbm, keep_ref, send_ref,
                 live_ref, tgt_ref, rhs_ref, diag_ref, off_ref, sol_ref, tiles_ref, sems):
    leaf, _, _ = place()
    children, slots = off_ref.shape[0], off_ref.shape[1]
    half = keep_ref.shape[0]
    pairs = ((rhs_hbm, rhs_ref), (diag_hbm, diag_ref), (off_hbm, off_ref))
    copies = [
        [pltpu.make_async_copy(source.at[s], target.at[s], sems.at[i, s]) for i, (source, target) in enumerate(pairs)]
        for s in range(children)
    ]
    back = [pltpu.make_async_copy(sol_ref.at[s], sol_hbm.at[s], sems.at[3, s]) for s in range(children)]
    small = [
        pltpu.make_async_copy(live_hbm, live_ref, sems.at[4, 0]),
        pltpu.make_async_copy(tgt_hbm, tgt_ref, sems.at[4, 1]),
    ]
    for s in range(children):
        for copy in copies[s]:
            copy.start()
    for copy in small:
        copy.start()
    for s in range(children):
        copies[s][0].wait()
        copies[s][1].wait()
        rhs = rhs_ref[s]
        sol = rhs + dot3(lower(diag_ref[s]), *split(rhs), NN)
        sol_ref[s] = sol
        back[s].start()
        copies[s][2].wait()
        if s == 0:
            for copy in small:
                copy.wait()
        tiles = dot3(sol.T, *split(off_ref[s]), NT)
        slot = lax.broadcasted_iota(jnp.int32, tiles.shape, 1)
        tiles_ref[:, s * slots:(s + 1) * slots] = jnp.where(slot < live_ref[s], tiles, 0.0)
        send_ref[half:half + 8, s * slots:(s + 1) * slots] = jnp.broadcast_to(
            tgt_ref[s:s + 1, :].astype(F32), (8, slots)
        )
    keep_ref[...] = tiles_ref[pl.ds(pl.multiple_of(leaf * half, half), half), :]
    send_ref[0:half, :] = tiles_ref[pl.ds(pl.multiple_of((1 - leaf) * half, half), half), :]
    for copy in back:
        copy.wait()


def scatter(value, target, size, start):
    index = lax.broadcasted_iota(jnp.int32, (size, value.shape[1]), 0) + start
    hot = jnp.where(index == target, 1.0, 0.0).astype(BF16)
    product = lax.dot_general(value, hot, NT, preferred_element_type=F32)
    half = value.shape[0] // 2
    return product[:half] + product[half:]


def own_kernel(keep_ref, send_ref, *out_refs):
    _, row, _ = place()
    half, size = out_refs[0].shape
    value = jnp.concatenate(split(keep_ref[...]), axis=0)
    target = send_ref[half:half + 1, :].astype(jnp.int32)
    for s, out_ref in enumerate(out_refs):
        out_ref[...] = scatter(value, target, size, jnp.bitwise_xor(row, s) * size)


def other_kernel(recv_ref, *refs):
    _, row, _ = place()
    own_refs, out_refs = refs[:4], refs[4:]
    half, size = out_refs[0].shape
    value = jnp.concatenate(split(recv_ref[0:half, :]), axis=0)
    target = recv_ref[half:half + 1, :].astype(jnp.int32)
    for s, (own_ref, out_ref) in enumerate(zip(own_refs, out_refs)):
        out_ref[...] = own_ref[...] + scatter(value, target, size, jnp.bitwise_xor(row, s) * size)


def pieces_kernel(a_ref, b_ref, c_ref, d_ref, first_ref, second_ref, sum_ref):
    _, _, z = place()
    odd = z % 2
    piece = first_ref.shape[0]
    sum_ref[...] = (a_ref[...] + b_ref[...]) + (c_ref[...] + d_ref[...])
    first_ref[...] = sum_ref[pl.ds(pl.multiple_of(odd * piece, piece), piece), :]
    second_ref[...] = sum_ref[pl.ds(pl.multiple_of((1 - odd) * piece, piece), piece), :]


def factor_kernel(own_ref, sent_ref, other_ref, diag_high_ref, diag_low_ref, *out_refs):
    leaf, row, z = place()
    for block in range(3):
        high_ref, low_ref = out_refs[2 * block], out_refs[2 * block + 1]

        @pl.when((row > block) & ((z == 1) | (z == 2)))
        def _():
            if block == 0:
                value = jnp.where((leaf == 0) == (z == 1), sent_ref[...], other_ref[...])
            else:
                sent = jnp.where((leaf == 0) == (block == 1), sent_ref[...], other_ref[...])
                value = jnp.where(z == block, own_ref[...], sent)
            value = value.T
            value = value + dot3(value, diag_high_ref[...], diag_low_ref[...], NN)
            high_ref[...], low_ref[...] = split(value)


def first_kernel(rhs_ref, a_ref, b_ref, c_ref, d_ref, high_ref, low_ref, out_ref):
    value = rhs_ref[...] - ((a_ref[...] + b_ref[...]) + (c_ref[...] + d_ref[...]))
    out_ref[...] = value + dot3(value, high_ref[...], low_ref[...], NN)


def chain_kernel(owner, given_ref, *refs):
    _, row, z = place()
    used, out_ref = refs[:-1], refs[-1]
    out_ref[...] = given_ref[...]

    @pl.when((row == owner) & ((z == 1) | (z == 2)))
    def _():
        left = given_ref[...]
        for i in range(0, len(used), 3):
            left = left - dot3(used[i][...], used[i + 1][...], used[i + 2][...], NN)
        out_ref[...] = left


def half_kernel(b_ref, a_ref, c_ref, x_ref, out_ref):
    _, _, z = place()
    x, a, b, c = x_ref[...], a_ref[...], b_ref[...], c_ref[...]
    low = jnp.where(z == 0, a, jnp.where(z == 1, x, jnp.where(z == 2, b, c)))
    high = jnp.where(z == 0, c, jnp.where(z == 1, b, jnp.where(z == 2, x, a)))
    out_ref[...] = jnp.concatenate([low, high], axis=0).T


def write_kernel(mine, part_ref, *refs):
    out_hbm, sem = refs[-2:]
    leaf, _, _ = place()
    half = part_ref.shape[1]
    at = leaf if mine else 1 - leaf
    copy = pltpu.make_async_copy(part_ref, out_hbm.at[:, pl.ds(pl.multiple_of(at * half, half), half)], sem)
    copy.start()
    copy.wait()


def call(kernel, ins, outs, scratch=(), outside=(), outs_outside=(), pinned=(), aliases=None, limit=24, flops=0):
    def spec(i, a):
        return ANY if i in outside else SM if a.ndim == 1 else VM

    def shape(i, out):
        dims, dtype = out if isinstance(out[0], tuple) else (out, F32)
        return pltpu.VMEM(dims, dtype) if i in pinned else jax.ShapeDtypeStruct(dims, dtype)

    outs = pl.pallas_call(
        kernel,
        out_shape=[shape(i, out) for i, out in enumerate(outs)],
        in_specs=[spec(i, a) for i, a in enumerate(ins)],
        out_specs=[ANY if i in outs_outside else VM for i in range(len(outs))],
        scratch_shapes=[pltpu.VMEM(s, F32) if isinstance(s, tuple) else s for s in scratch],
        input_output_aliases=aliases or {},
        cost_estimate=pl.CostEstimate(flops=flops, bytes_accessed=4 * sum(a.size for a in ins), transcendentals=0),
        compiler_params=pltpu.CompilerParams(vmem_limit_bytes=limit * 1024 * 1024),
    )(*ins)
    return list(outs)


def central(child_rhs, child_diag, child_off, live, targets, top_rhs, top_factor, top_diag):
    rows, cols = lax.axis_size("row"), lax.axis_size("col")
    size = top_diag.shape[1]
    right = top_rhs.shape[1]
    half, piece = right // 2, right // 4
    children, slots = targets.shape
    shape = (piece, size)
    block = ((size, size), BF16)
    dma = pltpu.SemaphoreType.DMA

    def at(r, c):
        return r * cols + c

    def swap(value):
        return lax.ppermute(value, "leaf", [(0, 1), (1, 0)])

    def along_row(value, step):
        return lax.ppermute(value, "row", [(r, r ^ step) for r in range(rows)])

    def along_col(value, pairs):
        rest = [a for a in range(cols) if a not in [p[0] for p in pairs]]
        open_ends = [b for b in range(cols) if b not in [p[1] for p in pairs]]
        return lax.ppermute(value, "col", pairs + list(zip(rest, open_ends)))

    def exchange(axis, value, a, b):
        count = lax.axis_size(axis)
        pairs = [(a, b), (b, a), (a + count, b + count), (b + count, a + count)]
        for other in range(count):
            if other not in (a, b):
                pairs += [(other, other + count), (other + count, other)]
        return lax.ppermute(value, ("leaf", axis), pairs)

    near = [(at(k, 0), at(k, 1)) for k in (1, 2, 3)] + [(at(k, 1), at(k, 2)) for k in (2, 3)]
    far = [(at(k, 0), at(k, 2)) for k in (1, 2, 3)] + [(at(3, 2), at(3, 1))]
    shift = rows * cols
    sent = lax.ppermute(
        top_factor, ("leaf", "row", "col"), near + [(a + shift, b + shift) for a, b in far]
    )
    child_sol, keep, send = call(
        child_kernel,
        [live, child_rhs, child_diag, child_off, targets],
        [child_rhs.shape, (half, children * slots), (half + 8, children * slots)],
        [pltpu.SMEM(live.shape, jnp.int32), pltpu.VMEM(targets.shape, jnp.int32), child_rhs.shape,
         child_diag.shape, child_off.shape, child_rhs.shape, (right, children * slots), dma((5, max(2, children)))],
        outside=(0, 1, 2, 3, 4),
        outs_outside=(0,),
        pinned=(1, 2),
        limit=56,
    )
    sums = call(own_kernel, [keep, send], [(half, size)] * rows)
    sums = call(other_kernel, [swap(send)] + sums, [(half, size)] * rows)
    got = [along_row(sums[s], s) for s in (3, 1, 2)]
    rhs_piece, diag_high, diag_low = call(
        turn_kernel, [top_rhs, top_diag], [shape, block, block], [(half, size)]
    )
    diag = [diag_high, diag_low]
    first, second = call(pieces_kernel, [sums[0]] + got, [shape] * 2, [(half, size)])
    q = [
        along_col(second, [(0, 2), (3, 1)]),
        exchange("col", first, 1, 2),
        along_col(first, [(0, 1), (3, 2)]),
    ]

    factor = call(factor_kernel, [top_factor, sent, swap(sent)] + diag, [block] * 6)
    factor = [factor[0:2], factor[2:4], factor[4:6]]

    def chain(owner, ins):
        (out,) = call(functools.partial(chain_kernel, owner), ins, [shape])
        return out

    (x,) = call(first_kernel, [rhs_piece, second] + q + diag, [shape], flops=10 ** 10)
    to1 = exchange("row", x, 0, 1)
    to2 = exchange("row", x, 0, 2)
    x = chain(1, [x, to1] + factor[0])
    on = along_row(x, 3)
    late = exchange("row", x, 1, 3)
    x = chain(2, [x, to2] + factor[0])
    x = chain(2, [x, on] + factor[1])
    to3 = exchange("row", x, 2, 3)
    x = chain(3, [x, on] + factor[0] + [late] + factor[1])
    x = chain(3, [x, to3] + factor[2])

    both = exchange("col", x, 1, 2)
    step = along_col(x, [(1, 0), (2, 3)])
    over = along_col(x, [(1, 3), (2, 0)])
    (own,) = call(half_kernel, [both, step, over, x], [(size, half)])
    (top_sol,) = call(
        functools.partial(write_kernel, True), [own], [top_rhs.shape], [dma(())], outs_outside=(0,)
    )
    (top_sol,) = call(
        functools.partial(write_kernel, False),
        [swap(own), top_sol],
        [top_rhs.shape],
        [dma(())],
        outside=(1,),
        outs_outside=(0,),
        aliases={1: 0},
    )
    return (child_sol, top_sol)


def solution(mesh):
    in_specs = (
        P(("leaf", "row", "col"), None, None),
        P(("leaf", "row", "col"), None, None),
        P(("leaf", "row", "col"), None, None),
        P(("leaf", "row", "col")),
        P(("leaf", "row", "col"), None),
        P("row", None),
        P("row", "col"),
        P("row", None),
    )
    out_specs = (P(("leaf", "row", "col"), None, None), P("row", None))
    axes = tuple(mesh.shape[a] for a in ("leaf", "row", "col"))

    def shards(*args):
        top_rhs, top_factor, top_diag = args[5:]
        size = top_diag.shape[1]
        fits = axes == (2, 4, 4) and top_rhs.shape[0] == size and top_factor.shape[1] == size
        return (central if fits else any_mesh)(*args)

    return jax.shard_map(shards, mesh=mesh, in_specs=in_specs, out_specs=out_specs, check_vma=False)
```

```python
import functools

import jax
import jax.numpy as jnp
from jax import lax
from jax.experimental import pallas as pl
from jax.experimental.pallas import tpu as pltpu
from jax.sharding import PartitionSpec as P

F32 = jnp.float32
BF16 = jnp.bfloat16
NT = (((1,), (1,)), ((), ()))
NN = (((1,), (0,)), ((), ()))
VM = pl.BlockSpec(memory_space=pltpu.VMEM)
ANY = pl.BlockSpec(memory_space=pl.ANY)
SM = pl.BlockSpec(memory_space=pltpu.SMEM)


def spread(value, axis, source):
    kept = jnp.where(lax.axis_index(axis) == source, value, 0).astype(value.dtype)
    return lax.psum(kept, axis)


def unit_lower(matrix):
    return jnp.tril(matrix) + jnp.eye(matrix.shape[-1], dtype=matrix.dtype)


def any_mesh(child_rhs, child_diag, child_off, live, targets, top_rhs, top_factor, top_diag):
    highest = lax.Precision.HIGHEST
    owned_rows = top_rhs.shape[0]
    right_count = top_rhs.shape[1]
    block_size = top_diag.shape[1]
    owned_blocks = owned_rows // block_size
    row_count = lax.axis_size("row")
    top_order = owned_rows * row_count
    col_width = top_factor.shape[1]
    my_row = lax.axis_index("row")
    my_col = lax.axis_index("col")
    child_sol = jnp.einsum("bij,bjr->bir", unit_lower(child_diag), child_rhs, precision=highest)
    tiles = jnp.einsum("btj,bjr->btr", child_off, child_sol, precision=highest)
    slot_index = jnp.arange(child_off.shape[1], dtype=jnp.int32)
    keep = slot_index[None, :] < live[:, None]
    tiles = jnp.where(keep[:, :, None], tiles, jnp.zeros_like(tiles))
    contrib = jnp.zeros((top_order, right_count), F32)
    contrib = contrib.at[targets.reshape(-1)].add(tiles.reshape(-1, right_count))
    row_part = lax.psum_scatter(contrib, "row", scatter_dimension=0, tiled=True)
    share = lax.psum_scatter(row_part, ("leaf", "col"), scatter_dimension=0, tiled=True)
    updates = lax.all_gather(share, ("leaf", "col"), axis=0, tiled=True)
    reduced = top_rhs - updates
    inverse_all = unit_lower(top_diag.reshape(owned_blocks, block_size, block_size))
    col_global = my_col * col_width + jnp.arange(col_width, dtype=jnp.int32)

    def step(block, solution):
        local = block % owned_blocks
        owner = block // owned_blocks
        factor_rows = jnp.where(
            (col_global < block * block_size)[None, :], top_factor, jnp.zeros_like(top_factor)
        )
        columns = lax.dynamic_slice_in_dim(solution, my_col * col_width, col_width, 0)
        partial_value = jnp.dot(
            factor_rows, columns, precision=highest, preferred_element_type=F32
        )
        block_inverse = lax.dynamic_index_in_dim(inverse_all, local, 0, keepdims=False)
        before = lax.psum(partial_value, "col")
        solved = jnp.dot(
            block_inverse, reduced - before, precision=highest, preferred_element_type=F32
        )
        solved = spread(solved, "row", owner)
        return lax.dynamic_update_slice_in_dim(solution, solved, block * block_size, 0)

    solution = lax.fori_loop(
        0, row_count * owned_blocks, step, jnp.zeros((top_order, right_count), F32)
    )
    top_sol = lax.dynamic_slice_in_dim(solution, my_row * owned_rows, owned_rows, 0)
    return (child_sol, top_sol)


def place():
    return tuple(lax.axis_index(a) for a in ("leaf", "row", "col"))


def split(value):
    high = value.astype(BF16)
    return high, (value - high.astype(F32)).astype(BF16)


def dot3(left, high, low, dims):
    left_high, left_low = split(left)
    rows = left.shape[0]
    both = lax.dot_general(
        jnp.concatenate([left_high, left_low], axis=0), high, dims, preferred_element_type=F32
    )
    cross = lax.dot_general(left_high, low, dims, preferred_element_type=F32)
    return both[:rows] + both[rows:] + cross


def lower(matrix):
    row = lax.broadcasted_iota(jnp.int32, matrix.shape, 0)
    col = lax.broadcasted_iota(jnp.int32, matrix.shape, 1)
    return jnp.where(col <= row, matrix, 0.0)


def turn_kernel(rhs_ref, diag_ref, out_ref, high_ref, low_ref, turned_ref):
    leaf, _, z = place()
    half, piece = turned_ref.shape[0], out_ref.shape[0]
    turned_ref[...] = rhs_ref[:, pl.ds(pl.multiple_of(leaf * half, half), half)].T
    out_ref[...] = turned_ref[pl.ds(pl.multiple_of((z // 2) * piece, piece), piece), :]
    high_ref[...], low_ref[...] = split(lower(diag_ref[...]).T)


def child_kernel(live_hbm, rhs_hbm, diag_hbm, off_hbm, tgt_hbm, sol_hbm, keep_ref, send_ref,
                 live_ref, tgt_ref, rhs_ref, diag_ref, off_ref, sol_ref, tiles_ref, sems):
    leaf, _, _ = place()
    children, slots = off_ref.shape[0], off_ref.shape[1]
    half = keep_ref.shape[0]
    pairs = ((rhs_hbm, rhs_ref), (diag_hbm, diag_ref), (off_hbm, off_ref))
    copies = [
        [pltpu.make_async_copy(source.at[s], target.at[s], sems.at[i, s]) for i, (source, target) in enumerate(pairs)]
        for s in range(children)
    ]
    back = [pltpu.make_async_copy(sol_ref.at[s], sol_hbm.at[s], sems.at[3, s]) for s in range(children)]
    small = [
        pltpu.make_async_copy(live_hbm, live_ref, sems.at[4, 0]),
        pltpu.make_async_copy(tgt_hbm, tgt_ref, sems.at[4, 1]),
    ]
    for copy in small:
        copy.start()
    for s in range(children):
        for copy in copies[s]:
            copy.start()
    for s in range(children):
        copies[s][0].wait()
        copies[s][1].wait()
        rhs = rhs_ref[s]
        sol = rhs + dot3(lower(diag_ref[s]), *split(rhs), NN)
        sol_ref[s] = sol
        back[s].start()
        copies[s][2].wait()
        if s == 0:
            for copy in small:
                copy.wait()
        tiles = dot3(sol.T, *split(off_ref[s]), NT)
        slot = lax.broadcasted_iota(jnp.int32, tiles.shape, 1)
        tiles_ref[:, s * slots:(s + 1) * slots] = jnp.where(slot < live_ref[s], tiles, 0.0)
        send_ref[half:half + 8, s * slots:(s + 1) * slots] = jnp.broadcast_to(
            tgt_ref[s:s + 1, :].astype(F32), (8, slots)
        )
    keep_ref[...] = tiles_ref[pl.ds(pl.multiple_of(leaf * half, half), half), :]
    send_ref[0:half, :] = tiles_ref[pl.ds(pl.multiple_of((1 - leaf) * half, half), half), :]
    for copy in back:
        copy.wait()


def scatter(value, target, size, start):
    index = lax.broadcasted_iota(jnp.int32, (size, value.shape[1]), 0) + start
    hot = jnp.where(index == target, 1.0, 0.0).astype(BF16)
    product = lax.dot_general(value, hot, NT, preferred_element_type=F32)
    half = value.shape[0] // 2
    return product[:half] + product[half:]


def own_kernel(keep_ref, send_ref, *out_refs):
    _, row, _ = place()
    half, size = out_refs[0].shape
    value = jnp.concatenate(split(keep_ref[...]), axis=0)
    target = send_ref[half:half + 1, :].astype(jnp.int32)
    for s, out_ref in enumerate(out_refs):
        out_ref[...] = scatter(value, target, size, jnp.bitwise_xor(row, s) * size)


def other_kernel(recv_ref, *refs):
    _, row, _ = place()
    own_refs, out_refs = refs[:4], refs[4:]
    half, size = out_refs[0].shape
    value = jnp.concatenate(split(recv_ref[0:half, :]), axis=0)
    target = recv_ref[half:half + 1, :].astype(jnp.int32)
    for s, (own_ref, out_ref) in enumerate(zip(own_refs, out_refs)):
        out_ref[...] = own_ref[...] + scatter(value, target, size, jnp.bitwise_xor(row, s) * size)


def pieces_kernel(a_ref, b_ref, c_ref, d_ref, first_ref, second_ref, sum_ref):
    _, _, z = place()
    odd = z % 2
    piece = first_ref.shape[0]
    sum_ref[...] = (a_ref[...] + b_ref[...]) + (c_ref[...] + d_ref[...])
    first_ref[...] = sum_ref[pl.ds(pl.multiple_of(odd * piece, piece), piece), :]
    second_ref[...] = sum_ref[pl.ds(pl.multiple_of((1 - odd) * piece, piece), piece), :]


def factor_kernel(own_ref, sent_ref, other_ref, diag_high_ref, diag_low_ref, *out_refs):
    leaf, row, z = place()
    for block in range(3):
        high_ref, low_ref = out_refs[2 * block], out_refs[2 * block + 1]

        @pl.when((row > block) & ((z == 1) | (z == 2)))
        def _():
            if block == 0:
                value = jnp.where((leaf == 0) == (z == 1), sent_ref[...], other_ref[...])
            else:
                sent = jnp.where((leaf == 0) == (block == 1), sent_ref[...], other_ref[...])
                value = jnp.where(z == block, own_ref[...], sent)
            value = value.T
            value = value + dot3(value, diag_high_ref[...], diag_low_ref[...], NN)
            high_ref[...], low_ref[...] = split(value)


def first_kernel(rhs_ref, a_ref, b_ref, c_ref, d_ref, high_ref, low_ref, out_ref):
    value = rhs_ref[...] - ((a_ref[...] + b_ref[...]) + (c_ref[...] + d_ref[...]))
    out_ref[...] = value + dot3(value, high_ref[...], low_ref[...], NN)


def chain_kernel(owner, given_ref, *refs):
    _, row, z = place()
    used, out_ref = refs[:-1], refs[-1]
    out_ref[...] = given_ref[...]

    @pl.when((row == owner) & ((z == 1) | (z == 2)))
    def _():
        left = given_ref[...]
        for i in range(0, len(used), 3):
            left = left - dot3(used[i][...], used[i + 1][...], used[i + 2][...], NN)
        out_ref[...] = left


def half_kernel(b_ref, a_ref, c_ref, x_ref, out_ref):
    _, _, z = place()
    x, a, b, c = x_ref[...], a_ref[...], b_ref[...], c_ref[...]
    low = jnp.where(z == 0, a, jnp.where(z == 1, x, jnp.where(z == 2, b, c)))
    high = jnp.where(z == 0, c, jnp.where(z == 1, b, jnp.where(z == 2, x, a)))
    out_ref[...] = jnp.concatenate([low, high], axis=0).T


def write_kernel(mine, part_ref, *refs):
    out_hbm, sem = refs[-2:]
    leaf, _, _ = place()
    half = part_ref.shape[1]
    at = leaf if mine else 1 - leaf
    copy = pltpu.make_async_copy(part_ref, out_hbm.at[:, pl.ds(pl.multiple_of(at * half, half), half)], sem)
    copy.start()
    copy.wait()


def call(kernel, ins, outs, scratch=(), outside=(), outs_outside=(), pinned=(), aliases=None, limit=24, flops=0):
    def spec(i, a):
        return ANY if i in outside else SM if a.ndim == 1 else VM

    def shape(i, out):
        dims, dtype = out if isinstance(out[0], tuple) else (out, F32)
        return pltpu.VMEM(dims, dtype) if i in pinned else jax.ShapeDtypeStruct(dims, dtype)

    outs = pl.pallas_call(
        kernel,
        out_shape=[shape(i, out) for i, out in enumerate(outs)],
        in_specs=[spec(i, a) for i, a in enumerate(ins)],
        out_specs=[ANY if i in outs_outside else VM for i in range(len(outs))],
        scratch_shapes=[pltpu.VMEM(s, F32) if isinstance(s, tuple) else s for s in scratch],
        input_output_aliases=aliases or {},
        cost_estimate=pl.CostEstimate(flops=flops, bytes_accessed=4 * sum(a.size for a in ins), transcendentals=0),
        compiler_params=pltpu.CompilerParams(vmem_limit_bytes=limit * 1024 * 1024),
    )(*ins)
    return list(outs)


def central(child_rhs, child_diag, child_off, live, targets, top_rhs, top_factor, top_diag):
    rows, cols = lax.axis_size("row"), lax.axis_size("col")
    size = top_diag.shape[1]
    right = top_rhs.shape[1]
    half, piece = right // 2, right // 4
    children, slots = targets.shape
    shape = (piece, size)
    block = ((size, size), BF16)
    dma = pltpu.SemaphoreType.DMA

    def at(r, c):
        return r * cols + c

    def swap(value):
        return lax.ppermute(value, "leaf", [(0, 1), (1, 0)])

    def along_row(value, step):
        return lax.ppermute(value, "row", [(r, r ^ step) for r in range(rows)])

    def along_col(value, pairs):
        rest = [a for a in range(cols) if a not in [p[0] for p in pairs]]
        open_ends = [b for b in range(cols) if b not in [p[1] for p in pairs]]
        return lax.ppermute(value, "col", pairs + list(zip(rest, open_ends)))

    def exchange(axis, value, a, b):
        count = lax.axis_size(axis)
        pairs = [(a, b), (b, a), (a + count, b + count), (b + count, a + count)]
        for other in range(count):
            if other not in (a, b):
                pairs += [(other, other + count), (other + count, other)]
        return lax.ppermute(value, ("leaf", axis), pairs)

    near = [(at(k, 0), at(k, 1)) for k in (1, 2, 3)] + [(at(k, 1), at(k, 2)) for k in (2, 3)]
    far = [(at(k, 0), at(k, 2)) for k in (1, 2, 3)] + [(at(3, 2), at(3, 1))]
    shift = rows * cols
    sent = lax.ppermute(
        top_factor, ("leaf", "row", "col"), near + [(a + shift, b + shift) for a, b in far]
    )
    child_sol, keep, send = call(
        child_kernel,
        [live, child_rhs, child_diag, child_off, targets],
        [child_rhs.shape, (half, children * slots), (half + 8, children * slots)],
        [pltpu.SMEM(live.shape, jnp.int32), pltpu.VMEM(targets.shape, jnp.int32), child_rhs.shape,
         child_diag.shape, child_off.shape, child_rhs.shape, (right, children * slots), dma((5, max(2, children)))],
        outside=(0, 1, 2, 3, 4),
        outs_outside=(0,),
        pinned=(1, 2),
        limit=56,
    )
    sums = call(own_kernel, [keep, send], [(half, size)] * rows)
    sums = call(other_kernel, [swap(send)] + sums, [(half, size)] * rows)
    got = [along_row(sums[s], s) for s in (3, 1, 2)]
    rhs_piece, diag_high, diag_low = call(
        turn_kernel, [top_rhs, top_diag], [shape, block, block], [(half, size)]
    )
    diag = [diag_high, diag_low]
    first, second = call(pieces_kernel, [sums[0]] + got, [shape] * 2, [(half, size)])
    q = [
        along_col(second, [(0, 2), (3, 1)]),
        exchange("col", first, 1, 2),
        along_col(first, [(0, 1), (3, 2)]),
    ]

    factor = call(factor_kernel, [top_factor, sent, swap(sent)] + diag, [block] * 6)
    factor = [factor[0:2], factor[2:4], factor[4:6]]

    def chain(owner, ins):
        (out,) = call(functools.partial(chain_kernel, owner), ins, [shape])
        return out

    (x,) = call(first_kernel, [rhs_piece, second] + q + diag, [shape], flops=10 ** 10)
    to1 = exchange("row", x, 0, 1)
    to2 = exchange("row", x, 0, 2)
    x = chain(1, [x, to1] + factor[0])
    on = along_row(x, 3)
    late = exchange("row", x, 1, 3)
    x = chain(2, [x, to2] + factor[0])
    x = chain(2, [x, on] + factor[1])
    to3 = exchange("row", x, 2, 3)
    x = chain(3, [x, on] + factor[0] + [late] + factor[1])
    x = chain(3, [x, to3] + factor[2])

    both = exchange("col", x, 1, 2)
    step = along_col(x, [(1, 0), (2, 3)])
    over = along_col(x, [(1, 3), (2, 0)])
    (own,) = call(half_kernel, [both, step, over, x], [(size, half)])
    (top_sol,) = call(
        functools.partial(write_kernel, True), [own], [top_rhs.shape], [dma(())], outs_outside=(0,)
    )
    (top_sol,) = call(
        functools.partial(write_kernel, False),
        [swap(own), top_sol],
        [top_rhs.shape],
        [dma(())],
        outside=(1,),
        outs_outside=(0,),
        aliases={1: 0},
    )
    return (child_sol, top_sol)


def solution(mesh):
    in_specs = (
        P(("leaf", "row", "col"), None, None),
        P(("leaf", "row", "col"), None, None),
        P(("leaf", "row", "col"), None, None),
        P(("leaf", "row", "col")),
        P(("leaf", "row", "col"), None),
        P("row", None),
        P("row", "col"),
        P("row", None),
    )
    out_specs = (P(("leaf", "row", "col"), None, None), P("row", None))
    axes = tuple(mesh.shape[a] for a in ("leaf", "row", "col"))

    def shards(*args):
        top_rhs, top_factor, top_diag = args[5:]
        size = top_diag.shape[1]
        fits = axes == (2, 4, 4) and top_rhs.shape[0] == size and top_factor.shape[1] == size
        return (central if fits else any_mesh)(*args)

    return jax.shard_map(shards, mesh=mesh, in_specs=in_specs, out_specs=out_specs, check_vma=False)
```

```python
import functools

import jax
import jax.numpy as jnp
from jax import lax
from jax.experimental import pallas as pl
from jax.experimental.pallas import tpu as pltpu
from jax.sharding import PartitionSpec as P

F32 = jnp.float32
BF16 = jnp.bfloat16
NT = (((1,), (1,)), ((), ()))
NN = (((1,), (0,)), ((), ()))
VM = pl.BlockSpec(memory_space=pltpu.VMEM)
ANY = pl.BlockSpec(memory_space=pl.ANY)
SM = pl.BlockSpec(memory_space=pltpu.SMEM)


def spread(value, axis, source):
    kept = jnp.where(lax.axis_index(axis) == source, value, 0).astype(value.dtype)
    return lax.psum(kept, axis)


def unit_lower(matrix):
    return jnp.tril(matrix) + jnp.eye(matrix.shape[-1], dtype=matrix.dtype)


def any_mesh(child_rhs, child_diag, child_off, live, targets, top_rhs, top_factor, top_diag):
    highest = lax.Precision.HIGHEST
    owned_rows = top_rhs.shape[0]
    right_count = top_rhs.shape[1]
    block_size = top_diag.shape[1]
    owned_blocks = owned_rows // block_size
    row_count = lax.axis_size("row")
    top_order = owned_rows * row_count
    col_width = top_factor.shape[1]
    my_row = lax.axis_index("row")
    my_col = lax.axis_index("col")
    child_sol = jnp.einsum("bij,bjr->bir", unit_lower(child_diag), child_rhs, precision=highest)
    tiles = jnp.einsum("btj,bjr->btr", child_off, child_sol, precision=highest)
    slot_index = jnp.arange(child_off.shape[1], dtype=jnp.int32)
    keep = slot_index[None, :] < live[:, None]
    tiles = jnp.where(keep[:, :, None], tiles, jnp.zeros_like(tiles))
    contrib = jnp.zeros((top_order, right_count), F32)
    contrib = contrib.at[targets.reshape(-1)].add(tiles.reshape(-1, right_count))
    row_part = lax.psum_scatter(contrib, "row", scatter_dimension=0, tiled=True)
    share = lax.psum_scatter(row_part, ("leaf", "col"), scatter_dimension=0, tiled=True)
    updates = lax.all_gather(share, ("leaf", "col"), axis=0, tiled=True)
    reduced = top_rhs - updates
    inverse_all = unit_lower(top_diag.reshape(owned_blocks, block_size, block_size))
    col_global = my_col * col_width + jnp.arange(col_width, dtype=jnp.int32)

    def step(block, solution):
        local = block % owned_blocks
        owner = block // owned_blocks
        factor_rows = jnp.where(
            (col_global < block * block_size)[None, :], top_factor, jnp.zeros_like(top_factor)
        )
        columns = lax.dynamic_slice_in_dim(solution, my_col * col_width, col_width, 0)
        partial_value = jnp.dot(
            factor_rows, columns, precision=highest, preferred_element_type=F32
        )
        block_inverse = lax.dynamic_index_in_dim(inverse_all, local, 0, keepdims=False)
        before = lax.psum(partial_value, "col")
        solved = jnp.dot(
            block_inverse, reduced - before, precision=highest, preferred_element_type=F32
        )
        solved = spread(solved, "row", owner)
        return lax.dynamic_update_slice_in_dim(solution, solved, block * block_size, 0)

    solution = lax.fori_loop(
        0, row_count * owned_blocks, step, jnp.zeros((top_order, right_count), F32)
    )
    top_sol = lax.dynamic_slice_in_dim(solution, my_row * owned_rows, owned_rows, 0)
    return (child_sol, top_sol)


def place():
    return tuple(lax.axis_index(a) for a in ("leaf", "row", "col"))


def split(value):
    high = value.astype(BF16)
    return high, (value - high.astype(F32)).astype(BF16)


def dot3(left, high, low, dims):
    left_high, left_low = split(left)
    rows = left.shape[0]
    both = lax.dot_general(
        jnp.concatenate([left_high, left_low], axis=0), high, dims, preferred_element_type=F32
    )
    cross = lax.dot_general(left_high, low, dims, preferred_element_type=F32)
    return both[:rows] + both[rows:] + cross


def lower(matrix):
    row = lax.broadcasted_iota(jnp.int32, matrix.shape, 0)
    col = lax.broadcasted_iota(jnp.int32, matrix.shape, 1)
    return jnp.where(col <= row, matrix, 0.0)


def turn_kernel(rhs_ref, diag_ref, out_ref, high_ref, low_ref, turned_ref):
    leaf, _, z = place()
    half, piece = turned_ref.shape[0], out_ref.shape[0]
    turned_ref[...] = rhs_ref[:, pl.ds(pl.multiple_of(leaf * half, half), half)].T
    out_ref[...] = turned_ref[pl.ds(pl.multiple_of((z // 2) * piece, piece), piece), :]
    high_ref[...], low_ref[...] = split(lower(diag_ref[...]).T)


def child_kernel(live_hbm, rhs_hbm, diag_hbm, off_hbm, tgt_hbm, sol_hbm, keep_ref, send_ref,
                 live_ref, tgt_ref, rhs_ref, diag_ref, off_ref, sol_ref, tiles_ref, sems):
    leaf, _, _ = place()
    children, slots = off_ref.shape[0], off_ref.shape[1]
    half = keep_ref.shape[0]
    pairs = ((rhs_hbm, rhs_ref), (diag_hbm, diag_ref), (off_hbm, off_ref))
    copies = [
        [pltpu.make_async_copy(source.at[s], target.at[s], sems.at[i, s]) for i, (source, target) in enumerate(pairs)]
        for s in range(children)
    ]
    back = [pltpu.make_async_copy(sol_ref.at[s], sol_hbm.at[s], sems.at[3, s]) for s in range(children)]
    small = [
        pltpu.make_async_copy(live_hbm, live_ref, sems.at[4, 0]),
        pltpu.make_async_copy(tgt_hbm, tgt_ref, sems.at[4, 1]),
    ]
    for s in range(children):
        for copy in copies[s]:
            copy.start()
    for copy in small:
        copy.start()
    for s in range(children):
        copies[s][0].wait()
        copies[s][1].wait()
        rhs = rhs_ref[s]
        sol = rhs + dot3(lower(diag_ref[s]), *split(rhs), NN)
        sol_ref[s] = sol
        back[s].start()
        copies[s][2].wait()
        if s == 0:
            for copy in small:
                copy.wait()
        tiles = dot3(sol.T, *split(off_ref[s]), NT)
        slot = lax.broadcasted_iota(jnp.int32, tiles.shape, 1)
        tiles_ref[:, s * slots:(s + 1) * slots] = jnp.where(slot < live_ref[s], tiles, 0.0)
        send_ref[half:half + 8, s * slots:(s + 1) * slots] = jnp.broadcast_to(
            tgt_ref[s:s + 1, :].astype(F32), (8, slots)
        )
    keep_ref[...] = tiles_ref[pl.ds(pl.multiple_of(leaf * half, half), half), :]
    send_ref[0:half, :] = tiles_ref[pl.ds(pl.multiple_of((1 - leaf) * half, half), half), :]
    for copy in back:
        copy.wait()


def scatter(value, target, size, start):
    index = lax.broadcasted_iota(jnp.int32, (size, value.shape[1]), 0) + start
    hot = jnp.where(index == target, 1.0, 0.0).astype(BF16)
    product = lax.dot_general(value, hot, NT, preferred_element_type=F32)
    half = value.shape[0] // 2
    return product[:half] + product[half:]


def own_kernel(keep_ref, send_ref, *out_refs):
    _, row, _ = place()
    half, size = out_refs[0].shape
    value = jnp.concatenate(split(keep_ref[...]), axis=0)
    target = send_ref[half:half + 1, :].astype(jnp.int32)
    for s, out_ref in enumerate(out_refs):
        out_ref[...] = scatter(value, target, size, jnp.bitwise_xor(row, s) * size)


def other_kernel(recv_ref, *refs):
    _, row, _ = place()
    own_refs, out_refs = refs[:4], refs[4:]
    half, size = out_refs[0].shape
    value = jnp.concatenate(split(recv_ref[0:half, :]), axis=0)
    target = recv_ref[half:half + 1, :].astype(jnp.int32)
    for s, (own_ref, out_ref) in enumerate(zip(own_refs, out_refs)):
        out_ref[...] = own_ref[...] + scatter(value, target, size, jnp.bitwise_xor(row, s) * size)


def pieces_kernel(a_ref, b_ref, c_ref, d_ref, first_ref, second_ref, sum_ref):
    _, _, z = place()
    odd = z % 2
    piece = first_ref.shape[0]
    sum_ref[...] = (a_ref[...] + b_ref[...]) + (c_ref[...] + d_ref[...])
    first_ref[...] = sum_ref[pl.ds(pl.multiple_of(odd * piece, piece), piece), :]
    second_ref[...] = sum_ref[pl.ds(pl.multiple_of((1 - odd) * piece, piece), piece), :]


def factor_kernel(own_ref, sent_ref, other_ref, diag_high_ref, diag_low_ref, *out_refs):
    leaf, row, z = place()
    for block in range(3):
        high_ref, low_ref = out_refs[2 * block], out_refs[2 * block + 1]

        @pl.when((row > block) & ((z == 1) | (z == 2)))
        def _():
            if block == 0:
                value = jnp.where((leaf == 0) == (z == 1), sent_ref[...], other_ref[...])
            else:
                sent = jnp.where((leaf == 0) == (block == 1), sent_ref[...], other_ref[...])
                value = jnp.where(z == block, own_ref[...], sent)
            value = value.T
            value = value + dot3(value, diag_high_ref[...], diag_low_ref[...], NN)
            high_ref[...], low_ref[...] = split(value)


def first_kernel(rhs_ref, a_ref, b_ref, c_ref, d_ref, high_ref, low_ref, out_ref):
    value = rhs_ref[...] - ((a_ref[...] + b_ref[...]) + (c_ref[...] + d_ref[...]))
    out_ref[...] = value + dot3(value, high_ref[...], low_ref[...], NN)


def chain_kernel(owner, given_ref, *refs):
    _, row, z = place()
    used, out_ref = refs[:-1], refs[-1]
    out_ref[...] = given_ref[...]

    @pl.when((row == owner) & ((z == 1) | (z == 2)))
    def _():
        left = given_ref[...]
        for i in range(0, len(used), 3):
            left = left - dot3(used[i][...], used[i + 1][...], used[i + 2][...], NN)
        out_ref[...] = left


def half_kernel(b_ref, a_ref, c_ref, x_ref, out_ref):
    _, _, z = place()
    x, a, b, c = x_ref[...], a_ref[...], b_ref[...], c_ref[...]
    low = jnp.where(z == 0, a, jnp.where(z == 1, x, jnp.where(z == 2, b, c)))
    high = jnp.where(z == 0, c, jnp.where(z == 1, b, jnp.where(z == 2, x, a)))
    out_ref[...] = jnp.concatenate([low, high], axis=0).T


def write_kernel(mine, part_ref, *refs):
    out_hbm, sem = refs[-2:]
    leaf, _, _ = place()
    half = part_ref.shape[1]
    at = leaf if mine else 1 - leaf
    copy = pltpu.make_async_copy(part_ref, out_hbm.at[:, pl.ds(pl.multiple_of(at * half, half), half)], sem)
    copy.start()
    copy.wait()


def call(kernel, ins, outs, scratch=(), outside=(), outs_outside=(), pinned=(), aliases=None, limit=24, flops=0):
    def spec(i, a):
        return ANY if i in outside else SM if a.ndim == 1 else VM

    def shape(i, out):
        dims, dtype = out if isinstance(out[0], tuple) else (out, F32)
        return pltpu.VMEM(dims, dtype) if i in pinned else jax.ShapeDtypeStruct(dims, dtype)

    outs = pl.pallas_call(
        kernel,
        out_shape=[shape(i, out) for i, out in enumerate(outs)],
        in_specs=[spec(i, a) for i, a in enumerate(ins)],
        out_specs=[ANY if i in outs_outside else VM for i in range(len(outs))],
        scratch_shapes=[pltpu.VMEM(s, F32) if isinstance(s, tuple) else s for s in scratch],
        input_output_aliases=aliases or {},
        cost_estimate=pl.CostEstimate(flops=flops, bytes_accessed=4 * sum(a.size for a in ins), transcendentals=0),
        compiler_params=pltpu.CompilerParams(vmem_limit_bytes=limit * 1024 * 1024),
    )(*ins)
    return list(outs)


def central(child_rhs, child_diag, child_off, live, targets, top_rhs, top_factor, top_diag):
    rows, cols = lax.axis_size("row"), lax.axis_size("col")
    size = top_diag.shape[1]
    right = top_rhs.shape[1]
    half, piece = right // 2, right // 4
    children, slots = targets.shape
    shape = (piece, size)
    block = ((size, size), BF16)
    dma = pltpu.SemaphoreType.DMA

    def at(r, c):
        return r * cols + c

    def swap(value):
        return lax.ppermute(value, "leaf", [(0, 1), (1, 0)])

    def along_row(value, step):
        return lax.ppermute(value, "row", [(r, r ^ step) for r in range(rows)])

    def along_col(value, pairs):
        rest = [a for a in range(cols) if a not in [p[0] for p in pairs]]
        open_ends = [b for b in range(cols) if b not in [p[1] for p in pairs]]
        return lax.ppermute(value, "col", pairs + list(zip(rest, open_ends)))

    def exchange(axis, value, a, b):
        count = lax.axis_size(axis)
        pairs = [(a, b), (b, a), (a + count, b + count), (b + count, a + count)]
        for other in range(count):
            if other not in (a, b):
                pairs += [(other, other + count), (other + count, other)]
        return lax.ppermute(value, ("leaf", axis), pairs)

    near = [(at(k, 0), at(k, 1)) for k in (1, 2, 3)] + [(at(k, 1), at(k, 2)) for k in (2, 3)]
    far = [(at(k, 0), at(k, 2)) for k in (1, 2, 3)] + [(at(3, 2), at(3, 1))]
    shift = rows * cols
    sent = lax.ppermute(
        top_factor, ("leaf", "row", "col"), near + [(a + shift, b + shift) for a, b in far]
    )
    child_sol, keep, send = call(
        child_kernel,
        [live, child_rhs, child_diag, child_off, targets],
        [child_rhs.shape, (half, children * slots), (half + 8, children * slots)],
        [pltpu.SMEM(live.shape, jnp.int32), pltpu.VMEM(targets.shape, jnp.int32), child_rhs.shape,
         child_diag.shape, child_off.shape, child_rhs.shape, (right, children * slots), dma((5, max(2, children)))],
        outside=(0, 1, 2, 3, 4),
        outs_outside=(0,),
        pinned=(1, 2),
        limit=56,
    )
    sums = call(own_kernel, [keep, send], [(half, size)] * rows)
    sums = call(other_kernel, [swap(send)] + sums, [(half, size)] * rows)
    got = [along_row(sums[s], s) for s in (1, 2, 3)]
    rhs_piece, diag_high, diag_low = call(
        turn_kernel, [top_rhs, top_diag], [shape, block, block], [(half, size)]
    )
    diag = [diag_high, diag_low]
    first, second = call(pieces_kernel, [sums[0]] + got, [shape] * 2, [(half, size)])
    q = [
        along_col(second, [(0, 2), (3, 1)]),
        exchange("col", first, 1, 2),
        along_col(first, [(0, 1), (3, 2)]),
    ]

    factor = call(factor_kernel, [top_factor, sent, swap(sent)] + diag, [block] * 6)
    factor = [factor[0:2], factor[2:4], factor[4:6]]

    def chain(owner, ins):
        (out,) = call(functools.partial(chain_kernel, owner), ins, [shape])
        return out

    (x,) = call(first_kernel, [rhs_piece, second] + q + diag, [shape], flops=10 ** 10)
    to1 = exchange("row", x, 0, 1)
    to2 = exchange("row", x, 0, 2)
    x = chain(1, [x, to1] + factor[0])
    on = along_row(x, 3)
    late = exchange("row", x, 1, 3)
    x = chain(2, [x, to2] + factor[0])
    x = chain(2, [x, on] + factor[1])
    to3 = exchange("row", x, 2, 3)
    x = chain(3, [x, on] + factor[0] + [late] + factor[1])
    x = chain(3, [x, to3] + factor[2])

    both = exchange("col", x, 1, 2)
    step = along_col(x, [(1, 0), (2, 3)])
    over = along_col(x, [(1, 3), (2, 0)])
    (own,) = call(half_kernel, [both, step, over, x], [(size, half)])
    (top_sol,) = call(
        functools.partial(write_kernel, True), [own], [top_rhs.shape], [dma(())], outs_outside=(0,)
    )
    (top_sol,) = call(
        functools.partial(write_kernel, False),
        [swap(own), top_sol],
        [top_rhs.shape],
        [dma(())],
        outside=(1,),
        outs_outside=(0,),
        aliases={1: 0},
    )
    return (child_sol, top_sol)


def solution(mesh):
    in_specs = (
        P(("leaf", "row", "col"), None, None),
        P(("leaf", "row", "col"), None, None),
        P(("leaf", "row", "col"), None, None),
        P(("leaf", "row", "col")),
        P(("leaf", "row", "col"), None),
        P("row", None),
        P("row", "col"),
        P("row", None),
    )
    out_specs = (P(("leaf", "row", "col"), None, None), P("row", None))
    axes = tuple(mesh.shape[a] for a in ("leaf", "row", "col"))

    def shards(*args):
        top_rhs, top_factor, top_diag = args[5:]
        size = top_diag.shape[1]
        fits = axes == (2, 4, 4) and top_rhs.shape[0] == size and top_factor.shape[1] == size
        return (central if fits else any_mesh)(*args)

    return jax.shard_map(shards, mesh=mesh, in_specs=in_specs, out_specs=out_specs, check_vma=False)
```
